32 devices in a mesh: fsdp: 4 (over z), context: 4 (over y, x), tensor: 2 (over core).
Axes of the slice: x: 2, y: 2, z: 4, core: 2. Of those that a mesh axis runs over, the one named last changes fastest.
Arguments:
- tokens: bfloat16 [8192, 1024], P(('fsdp', 'context')), may hold values from -6 to 6
- segments: int32 [4, 2048], P('fsdp'), may hold values from 0 to 2, never falling along the last dimension, each value on 1 to 1024 neighbouring positions
- deal: int32 [4, 8], P('fsdp'), may hold values from 0 to 7, as said below
- gain_mix: float32 [1024], replicated, may hold values from 0.5 to 1.5
- w_query: bfloat16 [1024, 512], P('fsdp', 'tensor'), may hold values from -0.1875 to 0.1875
- w_keyval: bfloat16 [1024, 256], P('fsdp', 'tensor'), may hold values from -0.1875 to 0.1875
- w_attn_out: bfloat16 [1024, 512], P('fsdp', 'tensor'), may hold values from -1.5 to 1.5
- w_gate_z: bfloat16 [1024, 1536], P('fsdp', 'tensor'), may hold values from -0.1875 to 0.1875
- w_in_x: bfloat16 [1024, 1536], P('fsdp', 'tensor'), may hold values from -0.1875 to 0.1875
- w_bc: bfloat16 [1024, 256], P('fsdp'), may hold values from -0.1875 to 0.1875
- w_step: bfloat16 [1024, 24], P('fsdp', 'tensor'), may hold values from -0.1875 to 0.1875
- conv_x: float32 [4, 1536], P(None, 'tensor'), may hold values from -0.5 to 0.5
- conv_bc: float32 [4, 256], replicated, may hold values from -0.5 to 0.5
- step_bias: float32 [24], P('tensor'), may hold values from -5 to -1
- decay_log: float32 [24], P('tensor'), may hold values from -4 to 1
- skip: float32 [24], P('tensor'), may hold values from 0.5 to 1.5
- w_ssm_out: bfloat16 [1024, 1536], P('fsdp', 'tensor'), may hold values from -0.15625 to 0.15625
- gain_ffn: float32 [1024], replicated, may hold values from 0.5 to 1.5
- w_ffn_gate: bfloat16 [1024, 2048], P('fsdp', 'tensor'), may hold values from -0.1875 to 0.1875
- w_ffn_up: bfloat16 [1024, 2048], P('fsdp', 'tensor'), may hold values from -0.1875 to 0.1875
- w_ffn_down: bfloat16 [1024, 2048], P('fsdp', 'tensor'), may hold values from -0.125 to 0.125
- cotangent: bfloat16 [8192, 1024], P(('fsdp', 'context')), may hold values from -6 to 6
Outputs:
- mixed_out: bfloat16 [8192, 1024], P(('fsdp', 'context'))
- tokens_grad: bfloat16 [8192, 1024], P(('fsdp', 'context'))
- gain_mix_grad: float32 [1024], replicated
- w_query_grad: float32 [1024, 512], P('fsdp', 'tensor')
- w_keyval_grad: float32 [1024, 256], P('fsdp', 'tensor')
- w_attn_out_grad: float32 [1024, 512], P('fsdp', 'tensor')
- w_gate_z_grad: float32 [1024, 1536], P('fsdp', 'tensor')
- w_in_x_grad: float32 [1024, 1536], P('fsdp', 'tensor')
- w_bc_grad: float32 [1024, 256], P('fsdp')
- w_step_grad: float32 [1024, 24], P('fsdp', 'tensor')
- conv_x_grad: float32 [4, 1536], P(None, 'tensor')
- conv_bc_grad: float32 [4, 256], replicated
- step_bias_grad: float32 [24], P('tensor')
- decay_log_grad: float32 [24], P('tensor')
- skip_grad: float32 [24], P('tensor')
- w_ssm_out_grad: float32 [1024, 1536], P('fsdp', 'tensor')
- gain_ffn_grad: float32 [1024], replicated
- w_ffn_gate_grad: float32 [1024, 2048], P('fsdp', 'tensor')
- w_ffn_up_grad: float32 [1024, 2048], P('fsdp', 'tensor')
- w_ffn_down_grad: float32 [1024, 2048], P('fsdp', 'tensor')
The draws below stay inside these ranges and needn't reach their ends.
Inputs may be any that keep to these rules, and one draw needn't show every extreme that they name: `segments`: in each stream document numbers start at 0 and never fall; every one of the 3 documents is present, none is longer than 1024 tokens and one is exactly that long. `deal`: each row names every half-block once. Half-blocks h and 7 - h never stand in slots 2 c and 2 c + 1 of one c: for each such pair one stands in slot 2 c or 2 c + 1 and the other in slot 2 c' or 2 c' + 1 with c' = (c - 1) mod (4).
All inputs are finite; a program needn't handle non-finite values.
Results may differ from the reference program's by a relative error of at most 0.014.
Values may be sent and summed in bfloat16 or wider, within the bound.
A program may use at most 192 MiB of HBM per device.

```python
import math
import jax
import jax.numpy as jnp
import numpy as np
from jax import lax

D = 1024
FF = 2048
QHEADS = 8
KVHEADS = 2
HEAD_DIM = 64
SSM_HEADS = 24
SSM_DIM = 64
STATE = 128
CONV = 4
SPAN = 256
QBLOCK = 512
DOCS = 3
HALF = 256
HALVES = 8
LEN = 2048
GROUPS = 4
TOKENS = 8192
SSM_INNER = 1536


def draw_deal(key, part):
    pair_count = HALVES // 2

    def one_stream(stream_index):
        stream_key = jax.random.fold_in(jax.random.fold_in(key, 7001), stream_index)
        pair_order = jax.random.permutation(jax.random.fold_in(stream_key, 1), pair_count).astype(jnp.int32)
        sides = jax.random.randint(jax.random.fold_in(stream_key, 2), (pair_count,), 0, 2).astype(jnp.int32)
        flips = jax.random.randint(jax.random.fold_in(stream_key, 3), (pair_count,), 0, 2).astype(jnp.int32)
        next_order = jnp.roll(pair_order, -1)
        next_sides = jnp.roll(sides, -1)
        leading = jnp.where(sides == 0, pair_order, HALVES - 1 - pair_order)
        trailing = jnp.where(next_sides == 0, HALVES - 1 - next_order, next_order)
        slot_zero = jnp.where(flips == 0, leading, trailing)
        slot_one = jnp.where(flips == 0, trailing, leading)
        return jnp.stack([slot_zero, slot_one], axis=1).reshape(HALVES).astype(jnp.int32)
    return jax.vmap(one_stream)(jnp.arange(GROUPS, dtype=jnp.int32))


def block_levels(rng, shape, shards, low, top_value):
    factor_of = 1.0
    for position, parts in shards:
        draws = jax.random.uniform(jax.random.fold_in(jax.random.fold_in(rng, 6), position), (parts,), jnp.float32, low / len(shards), top_value / len(shards))
        factor_of = factor_of * jnp.repeat(jnp.exp(draws), shape[position] // parts).reshape((-1,) + (1,) * (len(shape) - 1 - position))
    return factor_of


def split_up(number_of, total, limit, slope):
    weights = [(1 << 20) // math.isqrt(grade ** slope) + 1 for grade in range(2, number_of + 1)]
    rest, counts = total - limit - (number_of - 1), [1] * (number_of - 1)
    while rest > 0:
        candidates = [i for i in range(number_of - 1) if counts[i] < limit]
        whole, budget = sum([weights[i] for i in candidates]), rest
        for i in candidates:
            addition = min(limit - counts[i], max(1, budget * weights[i] // whole), rest)
            counts[i] = counts[i] + addition
            rest = rest - addition
    return np.array([limit] + counts)


def ragged(key, count, total, reach, slope):
    if count == 2:
        one = jax.random.randint(key, (), max(1, total - reach), min(reach, total - 1) + 1)
        return jnp.stack([one, total - one])
    lengths = jnp.asarray(split_up(count, total, reach, slope), jnp.int32)
    couples = (count - 1) // 2
    source_of, taker = lengths[1:1 + 2 * couples:2], lengths[2:2 + 2 * couples:2]
    room = jnp.minimum(source_of - 1, reach - taker)
    moved = jax.random.randint(jax.random.fold_in(key, 1), (couples,), 0, 1 << 20) % (room + 1)
    lengths = lengths.at[1:1 + 2 * couples:2].set(source_of - moved).at[2:2 + 2 * couples:2].set(taker + moved)
    return lengths[jax.random.permutation(jax.random.fold_in(key, 2), count)]


def scatter_about(own_key, extent, scale, reach, split=(), held_as=jnp.bfloat16):
    drawn = scale * jax.random.normal(own_key, extent, jnp.float32)
    if split:
        drawn = drawn * block_levels(own_key, extent, split, -0.22, 0.18)
    return jnp.clip(drawn, -reach, reach).astype(held_as)


def setup_inputs(seed: int = 0) -> dict:
    splits = jax.random.split(jax.random.key(seed), 23)
    tokens = scatter_about(splits[0], (TOKENS, D), 1.0, 6.0, ((0, 16),))
    segments = jax.vmap(lambda own: jnp.searchsorted(jnp.cumsum(ragged(own, DOCS, LEN, LEN // 2, 1)), jnp.arange(LEN), side="right"))(jax.random.split(splits[1], GROUPS)).reshape((GROUPS, LEN)).astype(jnp.int32)
    deal = draw_deal(jax.random.fold_in(splits[22], 71), 0)
    gain_mix = jnp.clip(1.0 + 0.1 * jax.random.normal(splits[3], (D,), jnp.float32), 0.5, 1.5)
    w_query = scatter_about(splits[4], (D, QHEADS * HEAD_DIM), D ** -0.5, 0.1875, ((0, 4), (1, 2)))
    w_keyval = scatter_about(splits[5], (D, 2 * KVHEADS * HEAD_DIM), D ** -0.5, 0.1875, ((0, 4), (1, 2)))
    w_attn_out = scatter_about(splits[6], (D, QHEADS * HEAD_DIM), (QHEADS * HEAD_DIM // 32) ** -0.5, 1.5, ((0, 4), (1, 2)))
    w_gate_z = scatter_about(splits[7], (D, SSM_INNER), D ** -0.5, 0.1875, ((0, 4), (1, 2)))
    w_in_x = scatter_about(splits[8], (D, SSM_INNER), D ** -0.5, 0.1875, ((0, 4), (1, 2)))
    w_bc = scatter_about(splits[9], (D, 2 * STATE), D ** -0.5, 0.1875, ((0, 4),))
    w_step = scatter_about(splits[10], (D, SSM_HEADS), D ** -0.5, 0.1875, ((0, 4), (1, 2)))
    conv_x = jnp.clip(jax.random.uniform(splits[11], (CONV, SSM_INNER), jnp.float32, -0.5, 0.5) * block_levels(splits[11], (CONV, SSM_INNER), ((1, 2),), -0.4, 0.0), -0.5, 0.5)
    conv_bc = jnp.clip(jax.random.uniform(splits[12], (CONV, 2 * STATE), jnp.float32, -0.5, 0.5), -0.5, 0.5)
    step_bias = jnp.clip(-5.0 + 4.0 * jax.random.uniform(splits[13], (SSM_HEADS,), jnp.float32) ** block_levels(splits[13], (SSM_HEADS,), ((0, 2),), -0.2, 0.2), -5.0, -1.0)
    decay_log = jnp.clip(-4.0 + 5.0 * jax.random.uniform(splits[14], (SSM_HEADS,), jnp.float32) ** block_levels(splits[14], (SSM_HEADS,), ((0, 2),), -0.2, 0.2), -4.0, 1.0)
    skip = jnp.clip(0.5 + 1.0 * jax.random.uniform(splits[15], (SSM_HEADS,), jnp.float32) ** block_levels(splits[15], (SSM_HEADS,), ((0, 2),), -0.2, 0.2), 0.5, 1.5)
    w_ssm_out = scatter_about(splits[16], (D, SSM_INNER), SSM_INNER ** -0.5, 0.15625, ((0, 4), (1, 2)))
    gain_ffn = jnp.clip(1.0 + 0.1 * jax.random.normal(splits[17], (D,), jnp.float32), 0.5, 1.5)
    w_ffn_gate = scatter_about(splits[18], (D, FF), D ** -0.5, 0.1875, ((0, 4), (1, 2)))
    w_ffn_up = scatter_about(splits[19], (D, FF), D ** -0.5, 0.1875, ((0, 4), (1, 2)))
    w_ffn_down = scatter_about(splits[20], (D, FF), FF ** -0.5, 0.125, ((0, 4), (1, 2)))
    cotangent = scatter_about(splits[21], (TOKENS, D), 1.0, 6.0, ((0, 16),))
    return {"tokens": tokens, "segments": segments, "deal": deal, "gain_mix": gain_mix, "w_query": w_query, "w_keyval": w_keyval, "w_attn_out": w_attn_out, "w_gate_z": w_gate_z, "w_in_x": w_in_x, "w_bc": w_bc, "w_step": w_step, "conv_x": conv_x, "conv_bc": conv_bc, "step_bias": step_bias, "decay_log": decay_log, "skip": skip, "w_ssm_out": w_ssm_out, "gain_ffn": gain_ffn, "w_ffn_gate": w_ffn_gate, "w_ffn_up": w_ffn_up, "w_ffn_down": w_ffn_down, "cotangent": cotangent}


exact = lax.Precision.HIGHEST
epsilon = 1e-05
masked = -1e+30

@jax.custom_vjp
def low(v):
    return lax.optimization_barrier(v.astype(jnp.bfloat16)).astype(jnp.float32)

@jax.custom_vjp
def low_back(v):
    return v

def low_keep(v):
    return (low(v), None)

def low_pass(kept, grad):
    return (grad,)

def back_keep(v):
    return (v, None)

def back_low(kept, grad):
    return (low(grad),)
low.defvjp(low_keep, low_pass)
low_back.defvjp(back_keep, back_low)

def matmul(left, right):
    return jnp.dot(left, right, precision=exact)

def project_out(left, stored):
    return jnp.dot(left, stored.T, precision=exact)

def norm_rows(values, gain):
    scale = lax.rsqrt(lax.optimization_barrier(jnp.mean(values * values, axis=-1, keepdims=True)) + epsilon)
    return values * scale * gain

def positions(segment_ids):
    count = segment_ids.shape[0]
    order = jnp.arange(count, dtype=jnp.int32)
    before = jnp.concatenate([jnp.full((1,), -1, jnp.int32), segment_ids[:-1]])
    starts = jnp.where(segment_ids != before, order, jnp.zeros_like(order))
    return (order - lax.cummax(starts, axis=0)).astype(jnp.float32)

def rotate(values, where_at):
    half = values.shape[-1] // 2
    freqs = 10000.0 ** (-jnp.arange(half, dtype=jnp.float32) / half)
    angles = where_at[:, None] * freqs[None, :]
    cosine = jnp.cos(angles)[:, None, :]
    sine = jnp.sin(angles)[:, None, :]
    first = values[..., :half]
    second = values[..., half:]
    return jnp.concatenate([first * cosine - second * sine, second * cosine + first * sine], axis=-1)

def attend_block(query, keys, values, query_ids, key_ids, query_order, key_order):
    count = query.shape[0]
    kv_heads = keys.shape[1]
    groups = query.shape[1] // kv_heads
    width = query.shape[2]
    grouped = query.reshape(count, kv_heads, groups, width)
    scores = jnp.einsum('rkgd,skd->kgrs', grouped, keys, precision=exact) / math.sqrt(width)
    allowed = (key_order[None, :] <= query_order[:, None]) & (key_ids[None, :] == query_ids[:, None])
    scores = jnp.where(allowed[None, None], scores, masked)
    highest = lax.optimization_barrier(jnp.max(scores, axis=-1, keepdims=True))
    weights = jnp.exp(scores - highest)
    probs = low(weights / lax.optimization_barrier(jnp.sum(weights, axis=-1, keepdims=True)))
    result = jnp.einsum('kgrs,skd->rkgd', probs, values, precision=exact)
    return result.reshape(count, kv_heads * groups * width)

def attention(query, keys, values, query_ids, key_ids, query_order, key_order, block):
    count = query.shape[0]
    blocks = count // block

    def one_block(pieces):
        return attend_block(pieces[0], keys, values, pieces[1], key_ids, pieces[2], key_order)
    result = lax.map(jax.checkpoint(one_block), (query.reshape((blocks, block) + query.shape[1:]), query_ids.reshape(blocks, block), query_order.reshape(blocks, block)))
    return result.reshape(count, -1)

def causal_conv(values, rim_rows, taps, segment_ids, rim_ids):
    count = values.shape[0]
    width = taps.shape[0]
    padded = jnp.concatenate([rim_rows, values], axis=0)
    padded_ids = jnp.concatenate([rim_ids, segment_ids])
    result = jnp.zeros_like(values)
    for tap_index in range(width):
        window = padded[tap_index:tap_index + count]
        alike = (padded_ids[tap_index:tap_index + count] == segment_ids).astype(jnp.float32)
        result = result + taps[tap_index][None, :] * window * alike[:, None]
    return result

def ssd_block(state, pieces):
    inner_x, b_rows, c_rows, step, rate, segment_ids, before_id = pieces
    count = inner_x.shape[0]
    totals = jnp.cumsum(-rate, axis=0)
    order = jnp.arange(count, dtype=jnp.int32)
    alike = (segment_ids[:, None] == segment_ids[None, :]) & (order[None, :] <= order[:, None])
    gaps = totals[:, None, :] - totals[None, :, :]
    decays = jnp.exp(jnp.where(alike[:, :, None], gaps, masked))
    inner = jnp.dot(c_rows, b_rows.T, precision=exact)
    weights = decays * inner[:, :, None] * step[None, :, :]
    result = jnp.einsum('tsh,shp->thp', weights, inner_x, precision=exact)
    carry_on = (segment_ids == before_id).astype(jnp.float32)
    factor = jnp.exp(totals) * carry_on[:, None]
    result = result + factor[:, :, None] * jnp.einsum('hpn,tn->thp', state, c_rows, precision=exact)
    keep_last = (segment_ids == segment_ids[count - 1]).astype(jnp.float32)
    tails = jnp.exp(totals[count - 1][None, :] - totals) * keep_last[:, None] * step
    carried = (jnp.exp(totals[count - 1]) * carry_on[count - 1])[:, None, None] * state
    new_state = carried + jnp.einsum('sh,shp,sn->hpn', tails, inner_x, b_rows, precision=exact)
    return (new_state, result)

def ssd(inner_x, b_rows, c_rows, step, rate, segment_ids, first_before, state, span):
    count = inner_x.shape[0]
    blocks = count // span
    lasts = segment_ids[span - 1::span]
    befores = jnp.concatenate([jnp.reshape(first_before, (1,)).astype(jnp.int32), lasts[:blocks - 1]])

    def shaped(values):
        return values.reshape((blocks, span) + values.shape[1:])
    final, result = lax.scan(jax.checkpoint(ssd_block), state, (shaped(inner_x), shaped(b_rows), shaped(c_rows), shaped(step), shaped(rate), shaped(segment_ids), befores))
    return (result.reshape(inner_x.shape), final)

def layer(block_rows, segment_ids, params):
    gain_one, query_w, keyval_w, attn_w, gate_w, inner_w, bc_w, step_w, taps_x, taps_bc, step_shift, decay_logs, skip_gain, ssm_w, gain_two, ffn_gate_w, ffn_up_w, ffn_down_w = params
    count = block_rows.shape[0]
    order = jnp.arange(count, dtype=jnp.int32)
    where_at = positions(segment_ids)
    normed = low(norm_rows(block_rows, gain_one))
    query = low_back(low(rotate(matmul(normed, query_w).reshape(count, QHEADS, HEAD_DIM), where_at)))
    pairs = matmul(normed, keyval_w).reshape(count, KVHEADS, 2, HEAD_DIM)
    keys = low_back(low(rotate(pairs[:, :, 0], where_at)))
    values = low_back(low(pairs[:, :, 1]))
    attended = low_back(low(attention(query, keys, values, segment_ids, segment_ids, order, order, QBLOCK)))
    gate_z = matmul(normed, gate_w)
    inner_x = matmul(normed, inner_w)
    bc_raw = matmul(normed, bc_w)
    step_raw = matmul(normed, step_w)
    joined = jnp.concatenate([inner_x, bc_raw], axis=1)
    taps = jnp.concatenate([taps_x, taps_bc], axis=1)
    rim_rows = jnp.zeros((CONV - 1, joined.shape[1]), jnp.float32)
    rim_ids = jnp.full((CONV - 1,), -1, jnp.int32)
    convolved = jax.nn.silu(causal_conv(joined, rim_rows, taps, segment_ids, rim_ids))
    ssm_x = low(convolved[:, :SSM_INNER]).reshape(count, SSM_HEADS, SSM_DIM)
    ssm_b = low(convolved[:, SSM_INNER:SSM_INNER + STATE])
    ssm_c = low(convolved[:, SSM_INNER + STATE:])
    step = jax.nn.softplus(step_raw + step_shift)
    rate = step * jnp.exp(decay_logs)
    start_state = jnp.zeros((SSM_HEADS, SSM_DIM, STATE), jnp.float32)
    ssm_y = ssd(ssm_x, ssm_b, ssm_c, step, rate, segment_ids, jnp.array(-1, jnp.int32), start_state, SPAN)[0]
    ssm_y = ssm_y + skip_gain[None, :, None] * ssm_x
    gated = low_back(low(ssm_y.reshape(count, SSM_INNER) * jax.nn.silu(gate_z)))
    mixed_rows = block_rows + project_out(attended, attn_w) + project_out(gated, ssm_w)
    normed_ffn = low(norm_rows(mixed_rows, gain_two))
    gate = low_back(matmul(normed_ffn, ffn_gate_w))
    upper = low_back(matmul(normed_ffn, ffn_up_w))
    hidden = low_back(low(jax.nn.silu(gate) * upper))
    return mixed_rows + project_out(hidden, ffn_down_w)

def reference(tokens, segments, deal, gain_mix, w_query, w_keyval, w_attn_out, w_gate_z, w_in_x, w_bc, w_step, conv_x, conv_bc, step_bias, decay_log, skip, w_ssm_out, gain_ffn, w_ffn_gate, w_ffn_up, w_ffn_down, cotangent):
    params = tuple((item.astype(jnp.float32) for item in (gain_mix, w_query, w_keyval, w_attn_out, w_gate_z, w_in_x, w_bc, w_step, conv_x, conv_bc, step_bias, decay_log, skip, w_ssm_out, gain_ffn, w_ffn_gate, w_ffn_up, w_ffn_down)))
    inputs = tokens.astype(jnp.float32)

    def forward(inputs, params):
        stacked = inputs.reshape(GROUPS, HALVES, HALF, D)

        def one_group(pieces):
            rows, segment_ids, dealt = pieces
            inverse = jnp.argsort(dealt).astype(jnp.int32)
            stream = jnp.take(rows, inverse, axis=0).reshape(LEN, D)
            result = layer(stream, segment_ids, params).reshape(HALVES, HALF, D)
            return jnp.take(result, dealt.astype(jnp.int32), axis=0)
        result = lax.map(jax.checkpoint(one_group), (stacked, segments, deal))
        return result.reshape(GROUPS * LEN, D)
    output, pull = jax.vjp(forward, inputs, params)
    grad_inputs, grads = pull(cotangent.astype(jnp.float32))
    return (output.astype(jnp.bfloat16), grad_inputs.astype(jnp.bfloat16), grads[0], grads[1], grads[2], grads[3], grads[4], grads[5], grads[6], grads[7], grads[8], grads[9], grads[10], grads[11], grads[12], grads[13], grads[14], grads[15], grads[16], grads[17])
```

```python
import functools

import jax
import jax.numpy as jnp
from jax import lax
from jax.experimental import pallas as pl
from jax.experimental.pallas import tpu as pltpu
from jax.sharding import PartitionSpec as P

HEAD_DIM = 64
SSM_DIM = 64
STATE = 128
CONV = 4
HALF = 256
WINDOW = 4

epsilon = 1e-05
masked = -1e30
F32 = jnp.float32
BF16 = jnp.bfloat16
exact = lax.Precision.HIGHEST


def dot(left, right, left_dim=1, right_dim=0, precision=None):
    return lax.dot_general(
        left,
        right,
        (((left_dim,), (right_dim,)), ((), ())),
        precision=precision,
        preferred_element_type=F32,
    )


def sigmoid(v):
    return 1.0 / (1.0 + jnp.exp(-v))


def softplus(v):
    return jnp.maximum(v, 0.0) + jnp.log1p(jnp.exp(-jnp.abs(v)))


def swap_halves(v):
    half = v.shape[1] // 2
    return jnp.concatenate([v[:, half:], v[:, :half]], axis=1)


def iotas(rows, columns):
    return (
        lax.broadcasted_iota(jnp.int32, (rows, columns), 0),
        lax.broadcasted_iota(jnp.int32, (rows, columns), 1),
    )


def state_scale(last_row, carry_last, heads):
    pieces = [
        jnp.broadcast_to(last_row[:, h * SSM_DIM : h * SSM_DIM + 1], (SSM_DIM, STATE))
        for h in range(heads)
    ]
    return jnp.exp(jnp.concatenate(pieces, axis=0)) * carry_last


def block_decays(step_raw, heads_ref, lane_pos, heads):
    rows = step_raw.shape[0]
    inner = heads * SSM_DIM
    raw = step_raw + heads_ref[0:1, :inner]
    step = softplus(raw)
    rate = step * jnp.exp(heads_ref[1:2, :inner])
    row, col = iotas(rows, rows)
    lower = jnp.where(col <= row, 1.0, 0.0).astype(F32)
    totals = dot(lower, -rate, precision=exact)
    last_row = totals[rows - 1 : rows]
    pos_last = lane_pos[rows - 1 : rows, 0:1]
    local = lax.broadcasted_iota(jnp.int32, (rows, 1), 0).astype(F32)
    carry_on = (lane_pos[:, 0:1] > local).astype(F32)
    keep_last = (local >= (rows - 1) - pos_last).astype(F32)
    carry_last = (pos_last > rows - 1).astype(F32)
    factor = jnp.exp(totals) * carry_on
    tails = jnp.exp(last_row - totals) * keep_last
    return raw, step, rate, totals, last_row, carry_last, factor, tails


def local_mask(lane_pos, rows):
    row, col = iotas(rows, rows)
    gap = (row - col).astype(F32)
    return (gap >= 0) & (gap <= lane_pos[:, 0:1])


def key_window(block):
    start = jnp.maximum(block - WINDOW, 0)
    return start, (block - start) * HALF


def window_mask(lane_pos, offset, rows, keys):
    row, col = iotas(rows, keys)
    gap = (row - col + offset).astype(F32)
    return (gap >= 0) & (gap <= lane_pos[:, 0:1])


def head_decay(totals, totals_t, h, allowed):
    gap = totals[:, h * SSM_DIM : h * SSM_DIM + 1] - totals_t[h * SSM_DIM : h * SSM_DIM + 1, :]
    return jnp.exp(jnp.where(allowed, gap, masked))


def mixer_forward_kernel(
    slots_ref, u_ref, table_ref, heads_ref, taps_ref, ag_ref, y_ref, conv_ref, state_in_ref, kv_ref,
    ext, state, keyval,
):
    block = pl.program_id(0)
    heads = state.shape[0] // SSM_DIM
    inner = heads * SSM_DIM
    width = ext.shape[1]
    rows = u_ref.shape[0]

    @pl.when(block == 0)
    def _():
        ext[0:8, :] = jnp.zeros((8, width), F32)
        state[...] = jnp.zeros(state.shape, F32)
        keyval[...] = jnp.zeros(keyval.shape, BF16)

    lane_pos = table_ref[:, 128:256]
    cosine = table_ref[:, 0:64]
    sine = table_ref[:, 64:128]
    q_at = inner
    u = u_ref[:, :width].astype(F32)
    ext[8 : 8 + rows, :] = u
    conv = u * taps_ref[CONV - 1 : CONV, :]
    for back in range(1, CONV):
        reach = lane_pos[:, 0:1] >= back
        shifted = ext[8 - back : 8 - back + rows, :]
        conv = conv + jnp.where(reach, shifted, 0.0) * taps_ref[CONV - 1 - back : CONV - back, :]
    ext[0:8, :] = u[rows - 8 : rows]
    act = conv * sigmoid(conv)
    ssm_x = act[:, :inner].astype(BF16)
    ssm_b = act[:, 256:384].astype(BF16)
    ssm_c = act[:, 384:512].astype(BF16)
    conv_ref[:, 0:256] = conv[:, 0:256]
    conv_ref[:, 256:512] = conv[:, 256:512]
    query = u[:, q_at : q_at + HEAD_DIM]
    query = (query * cosine + swap_halves(query) * sine).astype(BF16)
    conv_ref[:, q_at : q_at + HEAD_DIM] = query.astype(F32)
    key = u_ref[:, 512 + inner : 512 + inner + HEAD_DIM].astype(F32)
    key = key * cosine + swap_halves(key) * sine
    value = u_ref[:, 768 + inner : 768 + inner + HEAD_DIM].astype(F32)
    pair = jnp.concatenate([key, value], axis=1).astype(BF16)
    kv_ref[...] = pair
    keyval[pl.ds(pl.multiple_of(block * rows, rows), rows), :] = pair
    first, offset = key_window(block)
    span = (WINDOW + 1) * HALF
    window = keyval[pl.ds(pl.multiple_of(first * rows, rows), span), :]
    scores = dot(query * 0.125, window[:, :HEAD_DIM], 1, 1)
    scores = jnp.where(window_mask(lane_pos, offset, rows, span), scores, masked)
    highest = jnp.max(scores, axis=1, keepdims=True)
    weights = jnp.exp(scores - highest)
    total = jnp.sum(weights, axis=1, keepdims=True)
    probs = (weights * (1.0 / total)).astype(BF16)
    attended = dot(probs, window[:, HEAD_DIM:])
    _, step, _, totals, last_row, carry_last, factor, tails = block_decays(
        u_ref[:, 768 : 768 + inner].astype(F32), heads_ref, lane_pos, heads
    )
    totals_t = totals.T
    allowed = local_mask(lane_pos, rows)
    cross = dot(ssm_c, ssm_b, 1, 1)
    x_f = ssm_x.astype(F32)
    stepped = step * x_f
    stepped_low = stepped.astype(BF16)
    parts = []
    for h in range(heads):
        lanes = slice(h * SSM_DIM, (h + 1) * SSM_DIM)
        mix = (head_decay(totals, totals_t, h, allowed) * cross).astype(BF16)
        parts.append(dot(mix, stepped_low[:, lanes]))
    held = state[...]
    state_in_ref[...] = held
    y_pure = jnp.concatenate(parts, axis=1) + factor * dot(ssm_c, held.astype(BF16), 1, 1)
    tailed = (tails * stepped_low.astype(F32)).astype(BF16)
    state[...] = state_scale(last_row, carry_last, heads) * held + dot(tailed, ssm_b, 0, 0)
    y_ref[:, :inner] = y_pure
    y_ref[:, inner : inner + HEAD_DIM] = jnp.broadcast_to(
        highest + jnp.log(total), (rows, HEAD_DIM)
    )
    y_full = y_pure + heads_ref[2:3, :inner] * x_f
    gate = u_ref[:, 512 : 512 + inner].astype(F32)
    gated = y_full * (gate * sigmoid(gate))
    ag_ref[...] = jnp.concatenate([gated, attended], axis=1).astype(BF16)


def mixer_backward_kernel(
    slots_ref, dag_ref, ag_ref, u_ref, table_ref, heads_ref, taps_ref, y_ref, conv_ref, state_in_ref,
    state_out_ref, kv_ref, du_ref, stats_ref, dext, dpos, dstate, dkey_t, dvalue_t,
):
    turn = pl.program_id(0)
    blocks = pl.num_programs(0)
    block = blocks - 1 - turn
    heads = dstate.shape[0] // SSM_DIM
    inner = heads * SSM_DIM
    rows = u_ref.shape[0]
    width = dext.shape[1]

    @pl.when(turn == 0)
    def _():
        dext[rows : rows + 8, :] = jnp.zeros((8, width), F32)
        dpos[rows : rows + 8, :] = jnp.full((8, dpos.shape[1]), -1.0, F32)
        dstate[...] = jnp.zeros(dstate.shape, F32)
        dkey_t[...] = jnp.zeros(dkey_t.shape, F32)
        dvalue_t[...] = jnp.zeros(dvalue_t.shape, F32)
        stats_ref[...] = jnp.zeros(stats_ref.shape, F32)

    lane_pos = table_ref[:, 128:256]
    cosine = table_ref[:, 0:64]
    sine = table_ref[:, 64:128]
    first, offset = key_window(block)
    span = (WINDOW + 1) * HALF
    begin = pl.multiple_of(first * rows, rows)
    window = kv_ref[pl.ds(begin, span), :]
    keys = window[:, :HEAD_DIM]
    values = window[:, HEAD_DIM:]
    query = conv_ref[:, inner : inner + HEAD_DIM] * 0.125
    query_low = query.astype(BF16)
    datt = dag_ref[:, inner : inner + HEAD_DIM]
    datt_f = datt.astype(F32)
    lse = y_ref[:, inner : inner + 1]
    scores = dot(query_low, keys, 1, 1)
    allowed_all = window_mask(lane_pos, offset, rows, span)
    probs = jnp.exp(jnp.where(allowed_all, scores, masked) - lse)
    inward = jnp.sum(datt_f * ag_ref[:, inner : inner + HEAD_DIM].astype(F32), axis=1, keepdims=True)
    dscores = (probs * (dot(datt, values, 1, 1) - inward)).astype(BF16)
    dquery = dot(dscores, keys) * 0.125
    dkey_t[:, pl.ds(begin, span)] += dot(query.T.astype(BF16), dscores)
    dvalue_t[:, pl.ds(begin, span)] += dot(datt_f.T.astype(BF16), probs.astype(BF16))
    here = pl.ds(pl.multiple_of(block * rows, rows), rows)
    dkey = dkey_t[:, here].T
    dvalue = dvalue_t[:, here].T
    dquery = dquery * cosine - swap_halves(dquery) * sine
    dkey = dkey * cosine - swap_halves(dkey) * sine
    conv = conv_ref[...]
    gate_conv = sigmoid(conv)
    act = conv * gate_conv
    dact = gate_conv * (1.0 + conv * (1.0 - gate_conv))
    ssm_x = act[:, :inner].astype(BF16)
    ssm_b = act[:, 256:384].astype(BF16)
    ssm_c = act[:, 384:512].astype(BF16)
    x_f = ssm_x.astype(F32)
    raw, step, rate, totals, last_row, carry_last, factor, tails = block_decays(
        u_ref[:, 768 : 768 + inner].astype(F32), heads_ref, lane_pos, heads
    )
    totals_t = totals.T
    allowed = local_mask(lane_pos, rows)
    cross = dot(ssm_c, ssm_b, 1, 1)
    gate = u_ref[:, 512 : 512 + inner].astype(F32)
    sig = sigmoid(gate)
    y_pure = y_ref[:, :inner]
    dgated = dag_ref[:, :inner].astype(F32)
    skip = heads_ref[2:3, :inner]
    dy = dgated * (gate * sig)
    dgate = dgated * (y_pure + skip * x_f) * (sig * (1.0 + gate * (1.0 - sig)))
    dy_low = dy.astype(BF16)
    dy_r = dy_low.astype(F32)
    dy_t = dy.T.astype(BF16)
    stepped_low = (step * x_f).astype(BF16)
    stepped_r = stepped_low.astype(F32)
    tailed = (tails * stepped_r).astype(BF16)
    dcross = jnp.zeros((rows, rows), F32)
    parts = []
    for h in range(heads):
        lanes = slice(h * SSM_DIM, (h + 1) * SSM_DIM)
        decay = head_decay(totals, totals_t, h, allowed)
        mix = (decay * cross).astype(BF16)
        parts.append(dot(dy_t[lanes, :], mix))
        dcross = dcross + dot(dy_low[:, lanes], stepped_low[:, lanes], 1, 1) * decay
    dstep_x = jnp.concatenate(parts, axis=0).T
    dcross_low = dcross.astype(BF16)
    held = state_in_ref[...].astype(BF16)
    dheld = dstate[...]
    dheld_low = dheld.astype(BF16)
    dfactored = (factor * dy).astype(BF16)
    from_state = dot(ssm_b, dheld_low, 1, 1)
    dssm_c = dot(dcross_low, ssm_b) + dot(dfactored, held)
    dssm_b = dot(dcross_low, ssm_c, 0, 0) + dot(tailed, dheld_low)
    dtotals = dy_r * y_pure - stepped_r * dstep_x - tailed.astype(F32) * from_state
    dstep_x = dstep_x + tails * from_state
    end_term = dot(
        jnp.ones((8, STATE), F32), dheld_low.astype(F32) * state_out_ref[...], 1, 1, exact
    )[0:1]
    end_term = jnp.where(turn == 0, jnp.zeros_like(end_term), end_term)
    row, col = iotas(rows, rows)
    upper = jnp.where(col >= row, 1.0, 0.0).astype(F32)
    drate = -(dot(upper, dtotals, precision=exact) + end_term)
    dstate[...] = state_scale(last_row, carry_last, heads) * dheld + dot(dfactored, ssm_c, 0, 0)
    dssm_x = step * dstep_x + skip * dy
    dstep = x_f * dstep_x + jnp.exp(heads_ref[1:2, :inner]) * drate
    draw = dstep * sigmoid(raw)
    none = jnp.zeros((rows, HEAD_DIM), F32)
    dconv = jnp.concatenate([dssm_x, none, dssm_b, dssm_c], axis=1) * dact
    dext[0:rows, :] = dconv
    dpos[0:rows, :] = lane_pos
    u = u_ref[:, :width].astype(F32)
    du = dconv * taps_ref[CONV - 1 : CONV, :]
    stats_ref[CONV - 1 : CONV, :] += jnp.sum(dconv * u, axis=0, keepdims=True)
    for ahead in range(1, CONV):
        reach = dpos[ahead : ahead + rows, 0:1] >= ahead
        shifted = jnp.where(reach, dext[ahead : ahead + rows, :], 0.0)
        tap = CONV - 1 - ahead
        du = du + shifted * taps_ref[tap : tap + 1, :]
        stats_ref[tap : tap + 1, :] += jnp.sum(shifted * u, axis=0, keepdims=True)
    dext[rows : rows + 8, :] = dconv[0:8]
    dpos[rows : rows + 8, :] = lane_pos[0:8]
    stats_ref[4:5, :inner] += jnp.sum(dy * x_f, axis=0, keepdims=True)
    stats_ref[5:6, :inner] += jnp.sum(draw, axis=0, keepdims=True)
    stats_ref[6:7, :inner] += jnp.sum(drate * rate, axis=0, keepdims=True)
    summed = [
        jnp.sum(draw[:, h * SSM_DIM : (h + 1) * SSM_DIM], axis=1, keepdims=True)
        for h in range(heads)
    ]
    lane = lax.broadcasted_iota(jnp.int32, (rows, HEAD_DIM), 1)
    dstep_all = jnp.zeros((rows, HEAD_DIM), F32)
    for h in range(heads):
        dstep_all = jnp.where(lane == h, summed[h], dstep_all)
    du_ref[:, 0:256] = jnp.concatenate([du[:, :inner], dquery], axis=1).astype(BF16)
    du_ref[:, 256:512] = du[:, 256:512].astype(BF16)
    du_ref[:, 512:768] = jnp.concatenate([dgate, dkey], axis=1).astype(BF16)
    du_ref[:, 768:896] = jnp.concatenate([dvalue, dstep_all], axis=1).astype(BF16)


def mixer_forward(u, table, head_rows, taps, slot_of):
    count = u.shape[0]
    blocks = count // HALF
    heads = 3
    inner = heads * SSM_DIM
    width = taps.shape[1]
    at_slot = lambda i, slots: (slots[i], 0)
    in_order = lambda i, slots: (i, 0)
    whole = lambda i, slots: (0, 0)
    return pl.pallas_call(
        mixer_forward_kernel,
        out_shape=(
            jax.ShapeDtypeStruct((count, inner + HEAD_DIM), BF16),
            jax.ShapeDtypeStruct((count, inner + HEAD_DIM), F32),
            jax.ShapeDtypeStruct((count, width), F32),
            jax.ShapeDtypeStruct((blocks * inner, STATE), F32),
            jax.ShapeDtypeStruct((count, 2 * HEAD_DIM), BF16),
        ),
        grid_spec=pltpu.PrefetchScalarGridSpec(
            num_scalar_prefetch=1,
            grid=(blocks,),
            in_specs=[
                pl.BlockSpec((HALF, u.shape[1]), at_slot),
                pl.BlockSpec((HALF, table.shape[1]), in_order),
                pl.BlockSpec(head_rows.shape, whole),
                pl.BlockSpec(taps.shape, whole),
            ],
            out_specs=(
                pl.BlockSpec((HALF, inner + HEAD_DIM), at_slot),
                pl.BlockSpec((HALF, inner + HEAD_DIM), in_order),
                pl.BlockSpec((HALF, width), in_order),
                pl.BlockSpec((inner, STATE), in_order),
                pl.BlockSpec((HALF, 2 * HEAD_DIM), in_order),
            ),
            scratch_shapes=[
                pltpu.VMEM((8 + HALF, width), F32),
                pltpu.VMEM((inner, STATE), F32),
                pltpu.VMEM((count, 2 * HEAD_DIM), BF16),
            ],
        ),
        compiler_params=pltpu.CompilerParams(vmem_limit_bytes=48 << 20),
    )(slot_of, u, table, head_rows, taps)


def mixer_backward(dag, ag, u, table, head_rows, taps, y, conv, states, keyval, slot_of):
    count = u.shape[0]
    blocks = count // HALF
    heads = 3
    inner = heads * SSM_DIM
    width = taps.shape[1]
    last = blocks - 1
    at_slot = lambda i, slots: (slots[last - i], 0)
    in_order = lambda i, slots: (last - i, 0)
    after = lambda i, slots: (jnp.minimum(last - i + 1, last), 0)
    whole = lambda i, slots: (0, 0)
    columns = inner + HEAD_DIM
    return pl.pallas_call(
        mixer_backward_kernel,
        out_shape=(
            jax.ShapeDtypeStruct((count, 896), BF16),
            jax.ShapeDtypeStruct((8, width), F32),
        ),
        grid_spec=pltpu.PrefetchScalarGridSpec(
            num_scalar_prefetch=1,
            grid=(blocks,),
            in_specs=[
                pl.BlockSpec((HALF, columns), at_slot),
                pl.BlockSpec((HALF, columns), at_slot),
                pl.BlockSpec((HALF, u.shape[1]), at_slot),
                pl.BlockSpec((HALF, table.shape[1]), in_order),
                pl.BlockSpec(head_rows.shape, whole),
                pl.BlockSpec(taps.shape, whole),
                pl.BlockSpec((HALF, columns), in_order),
                pl.BlockSpec((HALF, width), in_order),
                pl.BlockSpec((inner, STATE), in_order),
                pl.BlockSpec((inner, STATE), after),
                pl.BlockSpec((count, 2 * HEAD_DIM), whole),
            ],
            out_specs=(
                pl.BlockSpec((HALF, 896), at_slot),
                pl.BlockSpec((8, width), whole),
            ),
            scratch_shapes=[
                pltpu.VMEM((HALF + 8, width), F32),
                pltpu.VMEM((HALF + 8, 128), F32),
                pltpu.VMEM((inner, STATE), F32),
                pltpu.VMEM((HEAD_DIM, count), F32),
                pltpu.VMEM((HEAD_DIM, count), F32),
            ],
        ),
        compiler_params=pltpu.CompilerParams(vmem_limit_bytes=56 << 20),
    )(slot_of, dag, ag, u, table, head_rows, taps, y, conv, states, states, keyval)


GROUP = ("context", "tensor")


def low_dot(left, right, left_dim=1, right_dim=0):
    return dot(left.astype(BF16), right.astype(BF16), left_dim, right_dim)


def inverse_rms(values):
    return lax.rsqrt(jnp.mean(values * values, axis=-1, keepdims=True) + epsilon)


def norm_back(values, gain, grad):
    scale = inverse_rms(values)
    pull = jnp.mean(grad * gain * values, axis=-1, keepdims=True)
    gain_grad = jnp.sum(grad * values * scale, axis=0)
    return scale * (grad * gain - values * scale * scale * pull), gain_grad


def stream_table(segment_ids):
    count = segment_ids.shape[0]
    order = jnp.arange(count, dtype=jnp.int32)
    starts = jnp.sum((segment_ids[None, :] < segment_ids[:, None]).astype(jnp.int32), axis=1)
    pos = (order - starts).astype(F32)
    half = HEAD_DIM // 2
    freqs = 10000.0 ** (-jnp.arange(half, dtype=F32) / half)
    angles = pos[:, None] * freqs[None, :]
    cosine, sine = jnp.cos(angles), jnp.sin(angles)
    return jnp.concatenate(
        [cosine, cosine, -sine, sine, jnp.broadcast_to(pos[:, None], (count, 128))], axis=1
    )


def per_device(
    tokens, segments, deal, gain_mix, w_query, w_keyval, w_attn_out, w_gate_z, w_in_x, w_bc, w_step,
    conv_x, conv_bc, step_bias, decay_log, skip, w_ssm_out, gain_ffn, w_ffn_gate, w_ffn_up,
    w_ffn_down, cotangent,
):
    ctx = lax.axis_size("context")
    c = lax.axis_index("context")
    t = lax.axis_index("tensor")
    heads = skip.shape[0] // ctx
    inner = heads * SSM_DIM
    qd = w_query.shape[1] // ctx
    hid = w_ffn_gate.shape[1] // ctx
    ddt = cotangent.dtype

    def part(array, width):
        return lax.dynamic_slice_in_dim(array, c * width, width, axis=1)

    keys_w, values_w = w_keyval[:, :HEAD_DIM], w_keyval[:, HEAD_DIM:]
    pad = HEAD_DIM - heads
    mine = jnp.concatenate(
        [
            part(w_in_x, inner), part(w_query, qd), w_bc, part(w_gate_z, inner), keys_w, values_w,
            jnp.pad(part(w_step, heads), ((0, 0), (0, pad))),
        ],
        axis=1,
    )
    mine_out = jnp.concatenate([part(w_ssm_out, inner), part(w_attn_out, qd)], axis=1)
    mine_ffn = jnp.concatenate(
        [part(w_ffn_gate, hid), part(w_ffn_up, hid), part(w_ffn_down, hid)], axis=1
    )
    w_all = lax.all_gather(mine, "fsdp", axis=0, tiled=True)
    wout_all = lax.all_gather(mine_out, "fsdp", axis=0, tiled=True)
    wffn_all = lax.all_gather(mine_ffn, "fsdp", axis=0, tiled=True)
    at_step = 896 - HEAD_DIM
    w_wide = jnp.concatenate(
        [
            w_all[:, :768],
            jnp.repeat(w_all[:, at_step : at_step + heads], SSM_DIM, axis=1),
            w_all[:, 768 : 768 + HEAD_DIM],
        ],
        axis=1,
    )
    w_gate, w_up, w_down = wffn_all[:, :hid], wffn_all[:, hid : 2 * hid], wffn_all[:, 2 * hid :]

    order = deal[0]
    ids = jnp.arange(order.shape[0], dtype=jnp.int32)
    slot_of = jnp.sum(jnp.where(order[None, :] == ids[:, None], ids[None, :], 0), axis=1)
    table = stream_table(segments[0])

    def lanes(values):
        return jnp.repeat(lax.dynamic_slice_in_dim(values, c * heads, heads), SSM_DIM)

    head_rows = jnp.zeros((8, 256), F32)
    head_rows = head_rows.at[0, :inner].set(lanes(step_bias))
    head_rows = head_rows.at[1, :inner].set(lanes(decay_log))
    head_rows = head_rows.at[2, :inner].set(lanes(skip))
    taps = jnp.concatenate(
        [part(conv_x, inner), jnp.zeros((CONV, qd), F32), conv_bc], axis=1
    )

    x_all = lax.all_gather(tokens, "context", axis=0, tiled=True)
    cot_all = lax.all_gather(cotangent, "context", axis=0, tiled=True)
    row_count = tokens.shape[0]
    half = row_count // 2
    x_own = lax.dynamic_slice_in_dim(tokens, t * half, half, axis=0).astype(F32)
    cot_own = lax.dynamic_slice_in_dim(cotangent, t * half, half, axis=0).astype(F32)

    xf = x_all.astype(F32)
    normed = (xf * inverse_rms(xf) * gain_mix).astype(BF16)
    u = low_dot(normed, w_wide)
    ag, y, conv, states, keyval = mixer_forward(u, table, head_rows, taps, slot_of)

    def scatter(values):
        return lax.psum_scatter(
            values.astype(BF16), GROUP, scatter_dimension=0, tiled=True
        ).astype(F32)

    mixed = x_own + scatter(low_dot(ag, wout_all, 1, 1))
    nffn_own = (mixed * inverse_rms(mixed) * gain_ffn).astype(BF16)
    nffn = lax.all_gather(nffn_own, GROUP, axis=0, tiled=True)
    gate = low_dot(nffn, w_gate)
    up = low_dot(nffn, w_up)
    sig = sigmoid(gate)
    hidden = (gate * sig * up).astype(BF16)
    out_own = mixed + scatter(low_dot(hidden, w_down, 1, 1))
    dhidden = low_dot(cot_all, w_down).astype(BF16).astype(F32)
    dgate = (dhidden * up * (sig * (1.0 + gate * (1.0 - sig)))).astype(BF16)
    dup = (dhidden * gate * sig).astype(BF16)
    dnffn = scatter(low_dot(dgate, w_gate, 1, 1) + low_dot(dup, w_up, 1, 1))
    dm_norm, dgain_ffn = norm_back(mixed, gain_ffn, dnffn)
    dmixed = cot_own + dm_norm
    dm_all = lax.all_gather(dmixed.astype(BF16), GROUP, axis=0, tiled=True)
    dag = low_dot(dm_all, wout_all).astype(BF16)
    du, stats = mixer_backward(dag, ag, u, table, head_rows, taps, y, conv, states, keyval, slot_of)
    dnormed = scatter(low_dot(du, w_all, 1, 1))
    dx_norm, dgain_mix = norm_back(x_own, gain_mix, dnormed)
    dx_own = dmixed + dx_norm

    mixed_out = lax.all_gather(out_own.astype(BF16), "tensor", axis=0, tiled=True)
    tokens_grad = lax.all_gather(dx_own.astype(BF16), "tensor", axis=0, tiled=True)

    dw = jnp.concatenate(
        [
            low_dot(normed, du, 0, 0),
            low_dot(dm_all, ag, 0, 0),
            low_dot(nffn, dgate, 0, 0),
            low_dot(nffn, dup, 0, 0),
            low_dot(cot_all, hidden, 0, 0),
        ],
        axis=1,
    ).astype(BF16)
    dw = lax.psum_scatter(dw, "fsdp", scatter_dimension=0, tiled=True)
    dw_all = lax.all_gather(dw, "context", axis=0, tiled=False).astype(F32)

    def spread(begin, width):
        piece = dw_all[:, :, begin : begin + width]
        return piece.transpose(1, 0, 2).reshape(piece.shape[1], -1)

    summed = jnp.sum(dw_all, axis=0)
    dbc = lax.psum(summed[:, 256:512], "tensor")
    dkv = summed[:, 768 - HEAD_DIM : 768 + HEAD_DIM]

    def place(values, full, axis_start):
        zero = jnp.zeros(full, F32)
        return lax.dynamic_update_slice(zero, values, axis_start).reshape(-1)

    total_heads = skip.shape[0] * lax.axis_size("tensor")
    at_head = t * skip.shape[0] + c * heads

    def head_sum(row):
        return jnp.sum(row[:inner].reshape(heads, SSM_DIM), axis=1)

    x_width = conv_x.shape[1] * lax.axis_size("tensor")
    small = [
        dgain_mix,
        dgain_ffn,
        place(stats[0:CONV, :inner], (CONV, x_width), (0, t * conv_x.shape[1] + c * inner)),
        stats[0:CONV, 256:512].reshape(-1),
        place(stats[5, :inner].reshape(heads, SSM_DIM)[:, 0], (total_heads,), (at_head,)),
        place(head_sum(stats[6]), (total_heads,), (at_head,)),
        place(head_sum(stats[4]), (total_heads,), (at_head,)),
    ]
    small[4] = place(head_sum(stats[5]), (total_heads,), (at_head,))
    sizes = [s.shape[0] for s in small]
    joined = lax.psum(jnp.concatenate(small), ("fsdp", "context", "tensor"))
    pieces = []
    at = 0
    for size in sizes:
        pieces.append(joined[at : at + size])
        at += size

    def own(values, width, axis):
        return lax.dynamic_slice_in_dim(values, t * width, width, axis=axis)

    return (
        mixed_out,
        tokens_grad,
        pieces[0],
        spread(inner, qd),
        dkv,
        spread(896 + inner, qd),
        spread(512, inner),
        spread(0, inner),
        dbc,
        spread(at_step, heads),
        own(pieces[2].reshape(CONV, x_width), conv_x.shape[1], 1),
        pieces[3].reshape(CONV, -1),
        own(pieces[4], skip.shape[0], 0),
        own(pieces[5], skip.shape[0], 0),
        own(pieces[6], skip.shape[0], 0),
        spread(896, inner),
        pieces[1],
        spread(1152, hid),
        spread(1152 + hid, hid),
        spread(1152 + 2 * hid, hid),
    )


def solution(mesh):
    in_specs = (
        P(("fsdp", "context"), None),
        P("fsdp", None),
        P("fsdp", None),
        P(),
        P("fsdp", "tensor"),
        P("fsdp", "tensor"),
        P("fsdp", "tensor"),
        P("fsdp", "tensor"),
        P("fsdp", "tensor"),
        P("fsdp", None),
        P("fsdp", "tensor"),
        P(None, "tensor"),
        P(),
        P("tensor"),
        P("tensor"),
        P("tensor"),
        P("fsdp", "tensor"),
        P(),
        P("fsdp", "tensor"),
        P("fsdp", "tensor"),
        P("fsdp", "tensor"),
        P(("fsdp", "context"), None),
    )
    out_specs = (
        P(("fsdp", "context"), None),
        P(("fsdp", "context"), None),
        P(),
        P("fsdp", "tensor"),
        P("fsdp", "tensor"),
        P("fsdp", "tensor"),
        P("fsdp", "tensor"),
        P("fsdp", "tensor"),
        P("fsdp", None),
        P("fsdp", "tensor"),
        P(None, "tensor"),
        P(),
        P("tensor"),
        P("tensor"),
        P("tensor"),
        P("fsdp", "tensor"),
        P(),
        P("fsdp", "tensor"),
        P("fsdp", "tensor"),
        P("fsdp", "tensor"),
    )
    return jax.shard_map(
        per_device, mesh=mesh, in_specs=in_specs, out_specs=out_specs, check_vma=False
    )
```

```python
import functools

import jax
import jax.numpy as jnp
from jax import lax
from jax.experimental import pallas as pl
from jax.experimental.pallas import tpu as pltpu
from jax.sharding import PartitionSpec as P

HEAD_DIM = 64
SSM_DIM = 64
STATE = 128
CONV = 4
HALF = 256
WINDOW = 4

epsilon = 1e-05
masked = -1e30
F32 = jnp.float32
BF16 = jnp.bfloat16
exact = lax.Precision.HIGHEST


def dot(left, right, left_dim=1, right_dim=0, precision=None):
    return lax.dot_general(
        left,
        right,
        (((left_dim,), (right_dim,)), ((), ())),
        precision=precision,
        preferred_element_type=F32,
    )


def sigmoid(v):
    return 1.0 / (1.0 + jnp.exp(-v))


def softplus(v):
    return jnp.maximum(v, 0.0) + jnp.log1p(jnp.exp(-jnp.abs(v)))


def swap_halves(v):
    half = v.shape[1] // 2
    return jnp.concatenate([v[:, half:], v[:, :half]], axis=1)


def iotas(rows, columns):
    return (
        lax.broadcasted_iota(jnp.int32, (rows, columns), 0),
        lax.broadcasted_iota(jnp.int32, (rows, columns), 1),
    )


def state_scale(last_row, carry_last, heads):
    pieces = [
        jnp.broadcast_to(last_row[:, h * SSM_DIM : h * SSM_DIM + 1], (SSM_DIM, STATE))
        for h in range(heads)
    ]
    return jnp.exp(jnp.concatenate(pieces, axis=0)) * carry_last


def block_decays(step_raw, heads_ref, lane_pos, heads):
    rows = step_raw.shape[0]
    inner = heads * SSM_DIM
    raw = step_raw + heads_ref[0:1, :inner]
    step = softplus(raw)
    rate = step * jnp.exp(heads_ref[1:2, :inner])
    row, col = iotas(rows, rows)
    lower = jnp.where(col <= row, 1.0, 0.0).astype(F32)
    totals = dot(lower, -rate, precision=exact)
    last_row = totals[rows - 1 : rows]
    pos_last = lane_pos[rows - 1 : rows, 0:1]
    local = lax.broadcasted_iota(jnp.int32, (rows, 1), 0).astype(F32)
    carry_on = (lane_pos[:, 0:1] > local).astype(F32)
    keep_last = (local >= (rows - 1) - pos_last).astype(F32)
    carry_last = (pos_last > rows - 1).astype(F32)
    factor = jnp.exp(totals) * carry_on
    tails = jnp.exp(last_row - totals) * keep_last
    return raw, step, rate, totals, last_row, carry_last, factor, tails


def local_mask(lane_pos, rows):
    row, col = iotas(rows, rows)
    gap = (row - col).astype(F32)
    return (gap >= 0) & (gap <= lane_pos[:, 0:1])


def key_window(block):
    start = jnp.maximum(block - WINDOW, 0)
    return start, (block - start) * HALF


def window_mask(lane_pos, offset, rows, keys):
    row, col = iotas(rows, keys)
    gap = (row - col + offset).astype(F32)
    return (gap >= 0) & (gap <= lane_pos[:, 0:1])


def head_decay(totals, totals_t, h, allowed):
    gap = totals[:, h * SSM_DIM : h * SSM_DIM + 1] - totals_t[h * SSM_DIM : h * SSM_DIM + 1, :]
    return jnp.exp(jnp.where(allowed, gap, masked))


def mixer_forward_kernel(
    slots_ref, u_ref, table_ref, heads_ref, taps_ref, ag_ref, y_ref, conv_ref, state_in_ref, kv_ref,
    ext, state, keyval,
):
    block = pl.program_id(0)
    heads = state.shape[0] // SSM_DIM
    inner = heads * SSM_DIM
    width = ext.shape[1]
    rows = u_ref.shape[0]

    @pl.when(block == 0)
    def _():
        ext[0:8, :] = jnp.zeros((8, width), F32)
        state[...] = jnp.zeros(state.shape, F32)
        keyval[...] = jnp.zeros(keyval.shape, BF16)

    lane_pos = table_ref[:, 128:256]
    cosine = table_ref[:, 0:64]
    sine = table_ref[:, 64:128]
    q_at = inner
    u = u_ref[:, :width].astype(F32)
    ext[8 : 8 + rows, :] = u
    conv = u * taps_ref[CONV - 1 : CONV, :]
    for back in range(1, CONV):
        reach = lane_pos[:, 0:1] >= back
        shifted = ext[8 - back : 8 - back + rows, :]
        conv = conv + jnp.where(reach, shifted, 0.0) * taps_ref[CONV - 1 - back : CONV - back, :]
    ext[0:8, :] = u[rows - 8 : rows]
    act = conv * sigmoid(conv)
    ssm_x = act[:, :inner].astype(BF16)
    ssm_b = act[:, 256:384].astype(BF16)
    ssm_c = act[:, 384:512].astype(BF16)
    conv_ref[:, 0:256] = conv[:, 0:256]
    conv_ref[:, 256:512] = conv[:, 256:512]
    query = u[:, q_at : q_at + HEAD_DIM]
    query = (query * cosine + swap_halves(query) * sine).astype(BF16)
    conv_ref[:, q_at : q_at + HEAD_DIM] = query.astype(F32)
    key = u_ref[:, 512 + inner : 512 + inner + HEAD_DIM].astype(F32)
    key = key * cosine + swap_halves(key) * sine
    value = u_ref[:, 768 + inner : 768 + inner + HEAD_DIM].astype(F32)
    pair = jnp.concatenate([key, value], axis=1).astype(BF16)
    kv_ref[...] = pair
    keyval[pl.ds(pl.multiple_of(block * rows, rows), rows), :] = pair
    first, offset = key_window(block)
    span = (WINDOW + 1) * HALF
    window = keyval[pl.ds(pl.multiple_of(first * rows, rows), span), :]
    scores = dot(query * 0.125, window[:, :HEAD_DIM], 1, 1)
    scores = jnp.where(window_mask(lane_pos, offset, rows, span), scores, masked)
    highest = jnp.max(scores, axis=1, keepdims=True)
    weights = jnp.exp(scores - highest)
    total = jnp.sum(weights, axis=1, keepdims=True)
    probs = (weights * (1.0 / total)).astype(BF16)
    attended = dot(probs, window[:, HEAD_DIM:])
    _, step, _, totals, last_row, carry_last, factor, tails = block_decays(
        u_ref[:, 768 : 768 + inner].astype(F32), heads_ref, lane_pos, heads
    )
    totals_t = totals.T
    allowed = local_mask(lane_pos, rows)
    cross = dot(ssm_c, ssm_b, 1, 1)
    x_f = ssm_x.astype(F32)
    stepped = step * x_f
    stepped_low = stepped.astype(BF16)
    parts = []
    for h in range(heads):
        lanes = slice(h * SSM_DIM, (h + 1) * SSM_DIM)
        mix = (head_decay(totals, totals_t, h, allowed) * cross).astype(BF16)
        parts.append(dot(mix, stepped_low[:, lanes]))
    held = state[...]
    state_in_ref[...] = held
    y_pure = jnp.concatenate(parts, axis=1) + factor * dot(ssm_c, held.astype(BF16), 1, 1)
    tailed = (tails * stepped_low.astype(F32)).astype(BF16)
    state[...] = state_scale(last_row, carry_last, heads) * held + dot(tailed, ssm_b, 0, 0)
    y_ref[:, :inner] = y_pure
    y_ref[:, inner : inner + HEAD_DIM] = jnp.broadcast_to(
        highest + jnp.log(total), (rows, HEAD_DIM)
    )
    y_full = y_pure + heads_ref[2:3, :inner] * x_f
    gate = u_ref[:, 512 : 512 + inner].astype(F32)
    gated = y_full * (gate * sigmoid(gate))
    ag_ref[...] = jnp.concatenate([gated, attended], axis=1).astype(BF16)


def mixer_backward_kernel(
    slots_ref, dag_ref, ag_ref, u_ref, table_ref, heads_ref, taps_ref, y_ref, conv_ref, state_in_ref,
    state_out_ref, kv_ref, du_ref, stats_ref, dext, dpos, dstate, dkey_t, dvalue_t,
):
    turn = pl.program_id(0)
    blocks = pl.num_programs(0)
    block = blocks - 1 - turn
    heads = dstate.shape[0] // SSM_DIM
    inner = heads * SSM_DIM
    rows = u_ref.shape[0]
    width = dext.shape[1]

    @pl.when(turn == 0)
    def _():
        dext[rows : rows + 8, :] = jnp.zeros((8, width), F32)
        dpos[rows : rows + 8, :] = jnp.full((8, dpos.shape[1]), -1.0, F32)
        dstate[...] = jnp.zeros(dstate.shape, F32)
        dkey_t[...] = jnp.zeros(dkey_t.shape, F32)
        dvalue_t[...] = jnp.zeros(dvalue_t.shape, F32)
        stats_ref[...] = jnp.zeros(stats_ref.shape, F32)

    lane_pos = table_ref[:, 128:256]
    cosine = table_ref[:, 0:64]
    sine = table_ref[:, 64:128]
    first, offset = key_window(block)
    span = (WINDOW + 1) * HALF
    begin = pl.multiple_of(first * rows, rows)
    window = kv_ref[pl.ds(begin, span), :]
    keys = window[:, :HEAD_DIM]
    values = window[:, HEAD_DIM:]
    query = conv_ref[:, inner : inner + HEAD_DIM] * 0.125
    query_low = query.astype(BF16)
    datt = dag_ref[:, inner : inner + HEAD_DIM]
    datt_f = datt.astype(F32)
    lse = y_ref[:, inner : inner + 1]
    scores = dot(query_low, keys, 1, 1)
    allowed_all = window_mask(lane_pos, offset, rows, span)
    probs = jnp.exp(jnp.where(allowed_all, scores, masked) - lse)
    inward = jnp.sum(datt_f * ag_ref[:, inner : inner + HEAD_DIM].astype(F32), axis=1, keepdims=True)
    dscores = (probs * (dot(datt, values, 1, 1) - inward)).astype(BF16)
    dquery = dot(dscores, keys) * 0.125
    dkey_t[:, pl.ds(begin, span)] += dot(query.T.astype(BF16), dscores)
    dvalue_t[:, pl.ds(begin, span)] += dot(datt_f.T.astype(BF16), probs.astype(BF16))
    here = pl.ds(pl.multiple_of(block * rows, rows), rows)
    dkey = dkey_t[:, here].T
    dvalue = dvalue_t[:, here].T
    dquery = dquery * cosine - swap_halves(dquery) * sine
    dkey = dkey * cosine - swap_halves(dkey) * sine
    conv = conv_ref[...]
    gate_conv = sigmoid(conv)
    act = conv * gate_conv
    dact = gate_conv * (1.0 + conv * (1.0 - gate_conv))
    ssm_x = act[:, :inner].astype(BF16)
    ssm_b = act[:, 256:384].astype(BF16)
    ssm_c = act[:, 384:512].astype(BF16)
    x_f = ssm_x.astype(F32)
    raw, step, rate, totals, last_row, carry_last, factor, tails = block_decays(
        u_ref[:, 768 : 768 + inner].astype(F32), heads_ref, lane_pos, heads
    )
    totals_t = totals.T
    allowed = local_mask(lane_pos, rows)
    cross = dot(ssm_c, ssm_b, 1, 1)
    gate = u_ref[:, 512 : 512 + inner].astype(F32)
    sig = sigmoid(gate)
    y_pure = y_ref[:, :inner]
    dgated = dag_ref[:, :inner].astype(F32)
    skip = heads_ref[2:3, :inner]
    dy = dgated * (gate * sig)
    dgate = dgated * (y_pure + skip * x_f) * (sig * (1.0 + gate * (1.0 - sig)))
    dy_low = dy.astype(BF16)
    dy_r = dy_low.astype(F32)
    dy_t = dy.T.astype(BF16)
    stepped_low = (step * x_f).astype(BF16)
    stepped_r = stepped_low.astype(F32)
    tailed = (tails * stepped_r).astype(BF16)
    dcross = jnp.zeros((rows, rows), F32)
    parts = []
    for h in range(heads):
        lanes = slice(h * SSM_DIM, (h + 1) * SSM_DIM)
        decay = head_decay(totals, totals_t, h, allowed)
        mix = (decay * cross).astype(BF16)
        parts.append(dot(dy_t[lanes, :], mix))
        dcross = dcross + dot(dy_low[:, lanes], stepped_low[:, lanes], 1, 1) * decay
    dstep_x = jnp.concatenate(parts, axis=0).T
    dcross_low = dcross.astype(BF16)
    held = state_in_ref[...].astype(BF16)
    dheld = dstate[...]
    dheld_low = dheld.astype(BF16)
    dfactored = (factor * dy).astype(BF16)
    from_state = dot(ssm_b, dheld_low, 1, 1)
    dssm_c = dot(dcross_low, ssm_b) + dot(dfactored, held)
    dssm_b = dot(dcross_low, ssm_c, 0, 0) + dot(tailed, dheld_low)
    dtotals = dy_r * y_pure - stepped_r * dstep_x - tailed.astype(F32) * from_state
    dstep_x = dstep_x + tails * from_state
    end_term = dot(
        jnp.ones((8, STATE), F32), dheld_low.astype(F32) * state_out_ref[...], 1, 1, exact
    )[0:1]
    end_term = jnp.where(turn == 0, jnp.zeros_like(end_term), end_term)
    row, col = iotas(rows, rows)
    upper = jnp.where(col >= row, 1.0, 0.0).astype(F32)
    drate = -(dot(upper, dtotals, precision=exact) + end_term)
    dstate[...] = state_scale(last_row, carry_last, heads) * dheld + dot(dfactored, ssm_c, 0, 0)
    dssm_x = step * dstep_x + skip * dy
    dstep = x_f * dstep_x + jnp.exp(heads_ref[1:2, :inner]) * drate
    draw = dstep * sigmoid(raw)
    none = jnp.zeros((rows, HEAD_DIM), F32)
    dconv = jnp.concatenate([dssm_x, none, dssm_b, dssm_c], axis=1) * dact
    dext[0:rows, :] = dconv
    dpos[0:rows, :] = lane_pos
    u = u_ref[:, :width].astype(F32)
    du = dconv * taps_ref[CONV - 1 : CONV, :]
    stats_ref[CONV - 1 : CONV, :] += jnp.sum(dconv * u, axis=0, keepdims=True)
    for ahead in range(1, CONV):
        reach = dpos[ahead : ahead + rows, 0:1] >= ahead
        shifted = jnp.where(reach, dext[ahead : ahead + rows, :], 0.0)
        tap = CONV - 1 - ahead
        du = du + shifted * taps_ref[tap : tap + 1, :]
        stats_ref[tap : tap + 1, :] += jnp.sum(shifted * u, axis=0, keepdims=True)
    dext[rows : rows + 8, :] = dconv[0:8]
    dpos[rows : rows + 8, :] = lane_pos[0:8]
    stats_ref[4:5, :inner] += jnp.sum(dy * x_f, axis=0, keepdims=True)
    stats_ref[5:6, :inner] += jnp.sum(draw, axis=0, keepdims=True)
    stats_ref[6:7, :inner] += jnp.sum(drate * rate, axis=0, keepdims=True)
    summed = [
        jnp.sum(draw[:, h * SSM_DIM : (h + 1) * SSM_DIM], axis=1, keepdims=True)
        for h in range(heads)
    ]
    lane = lax.broadcasted_iota(jnp.int32, (rows, HEAD_DIM), 1)
    dstep_all = jnp.zeros((rows, HEAD_DIM), F32)
    for h in range(heads):
        dstep_all = jnp.where(lane == h, summed[h], dstep_all)
    du_ref[:, 0:256] = jnp.concatenate([du[:, :inner], dquery], axis=1).astype(BF16)
    du_ref[:, 256:512] = du[:, 256:512].astype(BF16)
    du_ref[:, 512:768] = jnp.concatenate([dgate, dkey], axis=1).astype(BF16)
    du_ref[:, 768:896] = jnp.concatenate([dvalue, dstep_all], axis=1).astype(BF16)


def mixer_forward(u, table, head_rows, taps, slot_of):
    count = u.shape[0]
    blocks = count // HALF
    heads = 3
    inner = heads * SSM_DIM
    width = taps.shape[1]
    at_slot = lambda i, slots: (slots[i], 0)
    in_order = lambda i, slots: (i, 0)
    whole = lambda i, slots: (0, 0)
    return pl.pallas_call(
        mixer_forward_kernel,
        out_shape=(
            jax.ShapeDtypeStruct((count, inner + HEAD_DIM), BF16),
            jax.ShapeDtypeStruct((count, inner + HEAD_DIM), F32),
            jax.ShapeDtypeStruct((count, width), F32),
            jax.ShapeDtypeStruct((blocks * inner, STATE), F32),
            jax.ShapeDtypeStruct((count, 2 * HEAD_DIM), BF16),
        ),
        grid_spec=pltpu.PrefetchScalarGridSpec(
            num_scalar_prefetch=1,
            grid=(blocks,),
            in_specs=[
                pl.BlockSpec((HALF, u.shape[1]), at_slot),
                pl.BlockSpec((HALF, table.shape[1]), in_order),
                pl.BlockSpec(head_rows.shape, whole),
                pl.BlockSpec(taps.shape, whole),
            ],
            out_specs=(
                pl.BlockSpec((HALF, inner + HEAD_DIM), at_slot),
                pl.BlockSpec((HALF, inner + HEAD_DIM), in_order),
                pl.BlockSpec((HALF, width), in_order),
                pl.BlockSpec((inner, STATE), in_order),
                pl.BlockSpec((HALF, 2 * HEAD_DIM), in_order),
            ),
            scratch_shapes=[
                pltpu.VMEM((8 + HALF, width), F32),
                pltpu.VMEM((inner, STATE), F32),
                pltpu.VMEM((count, 2 * HEAD_DIM), BF16),
            ],
        ),
        compiler_params=pltpu.CompilerParams(vmem_limit_bytes=48 << 20),
    )(slot_of, u, table, head_rows, taps)


def mixer_backward(dag, ag, u, table, head_rows, taps, y, conv, states, keyval, slot_of):
    count = u.shape[0]
    blocks = count // HALF
    heads = 3
    inner = heads * SSM_DIM
    width = taps.shape[1]
    last = blocks - 1
    at_slot = lambda i, slots: (slots[last - i], 0)
    in_order = lambda i, slots: (last - i, 0)
    after = lambda i, slots: (jnp.minimum(last - i + 1, last), 0)
    whole = lambda i, slots: (0, 0)
    columns = inner + HEAD_DIM
    return pl.pallas_call(
        mixer_backward_kernel,
        out_shape=(
            jax.ShapeDtypeStruct((count, 896), BF16),
            jax.ShapeDtypeStruct((8, width), F32),
        ),
        grid_spec=pltpu.PrefetchScalarGridSpec(
            num_scalar_prefetch=1,
            grid=(blocks,),
            in_specs=[
                pl.BlockSpec((HALF, columns), at_slot),
                pl.BlockSpec((HALF, columns), at_slot),
                pl.BlockSpec((HALF, u.shape[1]), at_slot),
                pl.BlockSpec((HALF, table.shape[1]), in_order),
                pl.BlockSpec(head_rows.shape, whole),
                pl.BlockSpec(taps.shape, whole),
                pl.BlockSpec((HALF, columns), in_order),
                pl.BlockSpec((HALF, width), in_order),
                pl.BlockSpec((inner, STATE), in_order),
                pl.BlockSpec((inner, STATE), after),
                pl.BlockSpec((count, 2 * HEAD_DIM), whole),
            ],
            out_specs=(
                pl.BlockSpec((HALF, 896), at_slot),
                pl.BlockSpec((8, width), whole),
            ),
            scratch_shapes=[
                pltpu.VMEM((HALF + 8, width), F32),
                pltpu.VMEM((HALF + 8, 128), F32),
                pltpu.VMEM((inner, STATE), F32),
                pltpu.VMEM((HEAD_DIM, count), F32),
                pltpu.VMEM((HEAD_DIM, count), F32),
            ],
        ),
        compiler_params=pltpu.CompilerParams(vmem_limit_bytes=56 << 20),
    )(slot_of, dag, ag, u, table, head_rows, taps, y, conv, states, states, keyval)


MESH = pl.DeviceIdType.MESH


class Place:
    def __init__(self):
        self.c = lax.axis_index("context")
        self.t = lax.axis_index("tensor")
        count = lax.axis_size("context")
        self.chips = [
            self.c,
            self.c + 1 - 2 * (self.c % 2),
            (self.c + count // 2) % count,
            count - 1 - self.c,
        ]

    def slot(self, mask, sibling=False):
        core = 1 - self.t if sibling else self.t
        return self.chips[mask] * 2 + core

    def target(self, mask):
        if mask == 4:
            return {"tensor": 1 - self.t}
        return {"context": self.chips[mask]}

    def greet(self, masks=(1, 2, 4)):
        barrier = pltpu.get_barrier_semaphore()
        for mask in masks:
            pl.semaphore_signal(
                barrier, inc=1, device_id=self.target(mask), device_id_type=MESH
            )
        pl.semaphore_wait(barrier, len(masks))


class Wire:
    def __init__(self, place, sems):
        self.place = place
        self.sems = sems
        self.sent = []

    def copy(self, source, target, index, mask):
        return pltpu.make_async_remote_copy(
            src_ref=source,
            dst_ref=target,
            send_sem=self.sems.at[0, index],
            recv_sem=self.sems.at[1, index],
            device_id=self.place.target(mask),
            device_id_type=MESH,
        )

    def send(self, source, target, index, mask):
        made = self.copy(source, target, index, mask)
        made.start()
        self.sent.append(made)

    def arrive(self, target, index, mask):
        self.copy(target, target, index, mask).wait_recv()

    def finish(self):
        for made in self.sent:
            made.wait_send()
        self.sent = []


ROWS = HALF
PART = HALF // 2
TOP, END = pl.ds(0, PART), pl.ds(PART, PART)
SCATTER_SEMS = 10
GATHER_SEMS = 14


def scatter_scratch(columns):
    return [
        pltpu.VMEM((4, ROWS, columns), BF16),
        pltpu.VMEM((4, ROWS, columns), BF16),
        pltpu.VMEM((6, PART, columns), BF16),
        pltpu.VMEM((ROWS, columns), F32),
        pltpu.SemaphoreType.DMA((2, SCATTER_SEMS)),
    ]


SCATTER_ORDER = (3, 1, 2, 0)


class Scatter:
    def __init__(self, place, scratch):
        self.place = place
        self.core_in, self.out, self.chip_in, self.kept, sems = scratch
        self.wire = Wire(place, sems)

    def to_core(self, mask, source):
        index = SCATTER_ORDER.index(mask)
        self.wire.send(source, self.core_in.at[index], index, 4)

    def from_core(self, mask):
        index = SCATTER_ORDER.index(mask)
        self.wire.arrive(self.core_in.at[index], index, 4)
        return self.core_in[index].astype(F32)

    def first(self, mine, total, between=None):
        wire, out, kept = self.wire, self.out, self.kept
        both = mine(3) + self.from_core(3)
        out[0] = both.astype(BF16)
        wire.send(out.at[0, TOP], self.chip_in.at[0], 4, 1)
        wire.send(out.at[0, END], self.chip_in.at[1], 5, 2)
        both = mine(1) + self.from_core(1)
        out[1] = both.astype(BF16)
        wire.send(out.at[1, TOP], self.chip_in.at[2], 6, 1)
        kept[END] = both[PART:]
        both = mine(2) + self.from_core(2)
        out[2] = both.astype(BF16)
        wire.send(out.at[2, END], self.chip_in.at[3], 7, 2)
        kept[TOP] = both[:PART]
        total[...] = mine(0) + self.from_core(0)

    def second(self):
        wire, out, kept, came = self.wire, self.out, self.kept, self.chip_in
        wire.arrive(came.at[0], 4, 1)
        out[3, TOP] = (kept[TOP] + came[0].astype(F32)).astype(BF16)
        wire.send(out.at[3, TOP], came.at[4], 8, 2)
        wire.arrive(came.at[1], 5, 2)
        out[3, END] = (kept[END] + came[1].astype(F32)).astype(BF16)
        wire.send(out.at[3, END], came.at[5], 9, 1)

    def last(self, total):
        wire, came = self.wire, self.chip_in
        wire.arrive(came.at[2], 6, 1)
        wire.arrive(came.at[4], 8, 2)
        total[TOP] += came[2].astype(F32) + came[4].astype(F32)
        wire.arrive(came.at[3], 7, 2)
        wire.arrive(came.at[5], 9, 1)
        total[END] += came[3].astype(F32) + came[5].astype(F32)
        wire.finish()


class Gather:
    def __init__(self, place, whole, sems):
        self.place = place
        self.whole = whole
        self.wire = Wire(place, sems)

    def rows(self, mask, sibling=False, half=None):
        begin = self.place.slot(mask, sibling) * ROWS
        if half is None:
            return self.whole.at[pl.ds(pl.multiple_of(begin, ROWS), ROWS)]
        return self.whole.at[pl.ds(pl.multiple_of(begin + half * PART, PART), PART)]

    def start(self):
        wire = self.wire
        for half, mask, index in ((0, 1, 0), (1, 2, 1), (1, 1, 2), (0, 2, 3)):
            wire.send(self.rows(0, half=half), self.rows(0, half=half), index, mask)
        wire.send(self.rows(0), self.rows(0), 6, 4)

    def relay(self):
        wire = self.wire
        wire.arrive(self.rows(1, half=0), 0, 1)
        wire.send(self.rows(1, half=0), self.rows(1, half=0), 4, 2)
        wire.arrive(self.rows(2, half=1), 1, 2)
        wire.send(self.rows(2, half=1), self.rows(2, half=1), 5, 1)

    def near(self):
        wire = self.wire
        wire.arrive(self.rows(1, half=1), 2, 1)
        wire.send(self.rows(1), self.rows(1), 7, 4)
        wire.arrive(self.rows(2, half=0), 3, 2)
        wire.send(self.rows(2), self.rows(2), 8, 4)

    def far(self):
        wire = self.wire
        wire.arrive(self.rows(3, half=0), 4, 2)
        wire.arrive(self.rows(3, half=1), 5, 1)
        wire.send(self.rows(3), self.rows(3), 9, 4)

    def core(self, mask):
        index = (6, 7, 8, 9)[mask]
        self.wire.arrive(self.rows(mask, sibling=True), index, 4)

    def finish(self):
        self.wire.finish()


def slot_rows(slot):
    return pl.ds(pl.multiple_of(slot * ROWS, ROWS), ROWS)


def norm_scale(values):
    return lax.rsqrt(jnp.mean(values * values, axis=1, keepdims=True) + epsilon)


def middle_kernel(
    ag_ref, wout_ref, wffn_ref, x_ref, cot_ref, cot_all_ref, gain_ref,
    nffn_ref, hidden_ref, dgu_ref, dm_ref, dag_ref, outp_ref, mixed_ref, dmixed_ref, dgain_ref, dw_ref,
    part, *scratch,
):
    place = Place()
    first = Scatter(place, scratch[0:5])
    back = Scatter(place, scratch[5:10])
    forth = Gather(place, nffn_ref, scratch[10])
    home = Gather(place, dm_ref, scratch[11])
    hid = hidden_ref.shape[1]
    place.greet()

    def block(mask, sibling=False):
        return dot(ag_ref[slot_rows(place.slot(mask, sibling)), :], wout_ref[...], 1, 1)

    for mask in SCATTER_ORDER:
        rows = slot_rows(place.slot(mask, True))
        part[rows, :] = block(mask, True).astype(BF16)
        first.to_core(mask, part.at[rows])
    first.first(block, mixed_ref)
    first.second()
    mixed_ref[...] += x_ref[...].astype(F32)
    first.last(mixed_ref)
    mixed = mixed_ref[...]
    gain = gain_ref[...]
    scale = norm_scale(mixed)
    own = slot_rows(place.slot(0))
    nffn_ref[own, :] = (mixed * scale * gain).astype(BF16)
    forth.start()

    def work(slot):
        rows = slot_rows(slot)
        normed = nffn_ref[rows, :]
        gate_up = dot(normed, wffn_ref[:, : 2 * hid])
        dhidden = dot(cot_all_ref[rows, :], wffn_ref[:, 2 * hid :]).astype(BF16).astype(F32)
        gate, up = gate_up[:, :hid], gate_up[:, hid:]
        sig = sigmoid(gate)
        silu = gate * sig
        dgate = dhidden * up * (sig * (1.0 + gate * (1.0 - sig)))
        hidden_ref[rows, :] = (silu * up).astype(BF16)
        dgu_ref[rows, :hid] = dgate.astype(BF16)
        dgu_ref[rows, hid:] = (dhidden * silu).astype(BF16)
        part[rows, :] = dot(dgu_ref[rows, :], wffn_ref[:, : 2 * hid], 1, 1).astype(BF16)

    def hand_over(mask):
        slot = place.slot(mask, True)
        work(slot)
        back.to_core(mask, part.at[slot_rows(slot)])

    work(place.slot(0))
    forth.relay()
    forth.core(0)
    hand_over(0)
    forth.near()
    forth.core(1)
    hand_over(1)
    forth.core(2)
    hand_over(2)
    work(place.slot(1))
    forth.far()
    work(place.slot(2))
    forth.core(3)
    hand_over(3)
    work(place.slot(3))
    forth.finish()

    def ready(mask):
        return part[slot_rows(place.slot(mask)), :].astype(F32)

    back.first(ready, dmixed_ref)

    def out_block(slot, carry):
        rows = slot_rows(slot)
        outp_ref[rows, :] = dot(hidden_ref[rows, :], wffn_ref[:, 2 * hid :], 1, 1).astype(BF16)
        return carry

    lax.fori_loop(0, 8, out_block, 0)
    back.second()
    dw_ref[:, : 2 * hid] = dot(nffn_ref[...], dgu_ref[...], 0, 0).astype(BF16)
    back.last(dmixed_ref)
    dnffn = dmixed_ref[...]
    mixed = mixed_ref[...]
    scale = norm_scale(mixed)
    spread = dnffn * gain
    pull = jnp.mean(spread * mixed, axis=1, keepdims=True)
    dgain_ref[...] = jnp.broadcast_to(
        jnp.sum(dnffn * mixed * scale, axis=0, keepdims=True), dgain_ref.shape
    )
    dmixed = cot_ref[...].astype(F32) + scale * (spread - mixed * (scale * scale * pull))
    dmixed_ref[...] = dmixed
    dm_ref[own, :] = dmixed.astype(BF16)
    home.start()

    def pull_back(slot):
        rows = slot_rows(slot)
        dag_ref[rows, :] = dot(dm_ref[rows, :], wout_ref[...]).astype(BF16)

    pull_back(place.slot(0))
    home.relay()
    dw_ref[:, 2 * hid : 3 * hid] = dot(cot_all_ref[...], hidden_ref[...], 0, 0).astype(BF16)
    home.core(0)
    pull_back(place.slot(0, True))
    home.near()
    pull_back(place.slot(1))
    pull_back(place.slot(2))
    home.far()
    pull_back(place.slot(3))
    for mask in (1, 2, 3):
        home.core(mask)
        pull_back(place.slot(mask, True))
    dw_ref[:, 3 * hid :] = dot(dm_ref[...], ag_ref[...], 0, 0).astype(BF16)
    home.finish()


def middle(ag, wout, wffn, x_own, cot_own, cot_all, gain):
    count, model = cot_all.shape
    hid = wffn.shape[1] // 3
    columns = ag.shape[1]
    vmem = pl.BlockSpec(memory_space=pltpu.VMEM)
    shape = jax.ShapeDtypeStruct
    return pl.pallas_call(
        middle_kernel,
        out_shape=(
            shape((count, model), BF16),
            shape((count, hid), BF16),
            shape((count, 2 * hid), BF16),
            shape((count, model), BF16),
            shape((count, columns), BF16),
            shape((count, model), BF16),
            shape((ROWS, model), F32),
            shape((ROWS, model), F32),
            shape((8, model), F32),
            shape((model, 3 * hid + columns), BF16),
        ),
        in_specs=[vmem] * 7,
        out_specs=(vmem,) * 10,
        scratch_shapes=[pltpu.VMEM((count, model), BF16)]
        + scatter_scratch(model)
        + scatter_scratch(model)
        + [pltpu.SemaphoreType.DMA((2, GATHER_SEMS))] * 2,
        compiler_params=pltpu.CompilerParams(
            collective_id=1, has_side_effects=True, vmem_limit_bytes=60 << 20
        ),
        cost_estimate=pl.CostEstimate(
            flops=20 * count * model * hid, bytes_accessed=40 << 20, transcendentals=count * hid
        ),
    )(ag, wout, wffn, x_own, cot_own, cot_all, gain.reshape(1, -1))


GROUP = ("context", "tensor")


def low_dot(left, right, left_dim=1, right_dim=0):
    return dot(left.astype(BF16), right.astype(BF16), left_dim, right_dim)


def inverse_rms(values):
    return lax.rsqrt(jnp.mean(values * values, axis=-1, keepdims=True) + epsilon)


def norm_back(values, gain, grad):
    scale = inverse_rms(values)
    pull = jnp.mean(grad * gain * values, axis=-1, keepdims=True)
    gain_grad = jnp.sum(grad * values * scale, axis=0)
    return scale * (grad * gain - values * scale * scale * pull), gain_grad


def stream_table(segment_ids):
    count = segment_ids.shape[0]
    order = jnp.arange(count, dtype=jnp.int32)
    starts = jnp.sum((segment_ids[None, :] < segment_ids[:, None]).astype(jnp.int32), axis=1)
    pos = (order - starts).astype(F32)
    half = HEAD_DIM // 2
    freqs = 10000.0 ** (-jnp.arange(half, dtype=F32) / half)
    angles = pos[:, None] * freqs[None, :]
    cosine, sine = jnp.cos(angles), jnp.sin(angles)
    return jnp.concatenate(
        [cosine, cosine, -sine, sine, jnp.broadcast_to(pos[:, None], (count, 128))], axis=1
    )


def per_device(
    tokens, segments, deal, gain_mix, w_query, w_keyval, w_attn_out, w_gate_z, w_in_x, w_bc, w_step,
    conv_x, conv_bc, step_bias, decay_log, skip, w_ssm_out, gain_ffn, w_ffn_gate, w_ffn_up,
    w_ffn_down, cotangent,
):
    ctx = lax.axis_size("context")
    c = lax.axis_index("context")
    t = lax.axis_index("tensor")
    heads = skip.shape[0] // ctx
    inner = heads * SSM_DIM
    qd = w_query.shape[1] // ctx
    hid = w_ffn_gate.shape[1] // ctx
    ddt = cotangent.dtype

    def part(array, width):
        return lax.dynamic_slice_in_dim(array, c * width, width, axis=1)

    keys_w, values_w = w_keyval[:, :HEAD_DIM], w_keyval[:, HEAD_DIM:]
    pad = HEAD_DIM - heads
    mine = jnp.concatenate(
        [
            part(w_in_x, inner), part(w_query, qd), w_bc, part(w_gate_z, inner), keys_w, values_w,
            jnp.pad(part(w_step, heads), ((0, 0), (0, pad))),
        ],
        axis=1,
    )
    mine_out = jnp.concatenate([part(w_ssm_out, inner), part(w_attn_out, qd)], axis=1)
    mine_ffn = jnp.concatenate(
        [part(w_ffn_gate, hid), part(w_ffn_up, hid), part(w_ffn_down, hid)], axis=1
    )
    w_all = lax.all_gather(mine, "fsdp", axis=0, tiled=True)
    wout_all = lax.all_gather(mine_out, "fsdp", axis=0, tiled=True)
    wffn_all = lax.all_gather(mine_ffn, "fsdp", axis=0, tiled=True)
    at_step = 896 - HEAD_DIM
    w_wide = jnp.concatenate(
        [
            w_all[:, :768],
            jnp.repeat(w_all[:, at_step : at_step + heads], SSM_DIM, axis=1),
            w_all[:, 768 : 768 + HEAD_DIM],
        ],
        axis=1,
    )

    order = deal[0]
    ids = jnp.arange(order.shape[0], dtype=jnp.int32)
    slot_of = jnp.sum(jnp.where(order[None, :] == ids[:, None], ids[None, :], 0), axis=1)
    table = stream_table(segments[0])

    def lanes(values):
        return jnp.repeat(lax.dynamic_slice_in_dim(values, c * heads, heads), SSM_DIM)

    head_rows = jnp.zeros((8, 256), F32)
    head_rows = head_rows.at[0, :inner].set(lanes(step_bias))
    head_rows = head_rows.at[1, :inner].set(lanes(decay_log))
    head_rows = head_rows.at[2, :inner].set(lanes(skip))
    taps = jnp.concatenate(
        [part(conv_x, inner), jnp.zeros((CONV, qd), F32), conv_bc], axis=1
    )

    x_all = lax.all_gather(tokens, "context", axis=0, tiled=True)
    cot_all = lax.all_gather(cotangent, "context", axis=0, tiled=True)
    row_count = tokens.shape[0]
    half = row_count // 2
    x_own = lax.dynamic_slice_in_dim(tokens, t * half, half, axis=0)
    cot_own = lax.dynamic_slice_in_dim(cotangent, t * half, half, axis=0)

    xf = x_all.astype(F32)
    normed = (xf * inverse_rms(xf) * gain_mix).astype(BF16)
    u = low_dot(normed, w_wide)
    ag, y, conv, states, keyval = mixer_forward(u, table, head_rows, taps, slot_of)

    def scatter(values):
        return lax.psum_scatter(
            values.astype(BF16), GROUP, scatter_dimension=0, tiled=True
        ).astype(F32)

    nffn, hidden, dgu, dm_all, dag, out_part, mixed, dmixed, dgain_rows, dw_mid = middle(
        ag, wout_all, wffn_all, x_own, cot_own, cot_all, gain_ffn
    )
    dgain_ffn = dgain_rows[0]
    out_own = mixed + scatter(out_part)
    du, stats = mixer_backward(dag, ag, u, table, head_rows, taps, y, conv, states, keyval, slot_of)
    dnormed = scatter(low_dot(du, w_all, 1, 1))
    dx_norm, dgain_mix = norm_back(x_own.astype(F32), gain_mix, dnormed)
    dx_own = dmixed + dx_norm

    mixed_out = lax.all_gather(out_own.astype(BF16), "tensor", axis=0, tiled=True)
    tokens_grad = lax.all_gather(dx_own.astype(BF16), "tensor", axis=0, tiled=True)

    dw_mid = lax.psum_scatter(dw_mid, "fsdp", scatter_dimension=0, tiled=True)
    dw = lax.psum_scatter(
        low_dot(normed, du, 0, 0).astype(BF16), "fsdp", scatter_dimension=0, tiled=True
    )
    dw = jnp.concatenate([dw, dw_mid[:, 3 * hid :], dw_mid[:, : 3 * hid]], axis=1)
    dw_all = lax.all_gather(dw, "context", axis=0, tiled=False).astype(F32)

    def spread(begin, width):
        piece = dw_all[:, :, begin : begin + width]
        return piece.transpose(1, 0, 2).reshape(piece.shape[1], -1)

    summed = jnp.sum(dw_all, axis=0)
    dbc = lax.psum(summed[:, 256:512], "tensor")
    dkv = summed[:, 768 - HEAD_DIM : 768 + HEAD_DIM]

    def place(values, full, axis_start):
        zero = jnp.zeros(full, F32)
        return lax.dynamic_update_slice(zero, values, axis_start).reshape(-1)

    total_heads = skip.shape[0] * lax.axis_size("tensor")
    at_head = t * skip.shape[0] + c * heads

    def head_sum(row):
        return jnp.sum(row[:inner].reshape(heads, SSM_DIM), axis=1)

    x_width = conv_x.shape[1] * lax.axis_size("tensor")
    small = [
        dgain_mix,
        dgain_ffn,
        place(stats[0:CONV, :inner], (CONV, x_width), (0, t * conv_x.shape[1] + c * inner)),
        stats[0:CONV, 256:512].reshape(-1),
        place(stats[5, :inner].reshape(heads, SSM_DIM)[:, 0], (total_heads,), (at_head,)),
        place(head_sum(stats[6]), (total_heads,), (at_head,)),
        place(head_sum(stats[4]), (total_heads,), (at_head,)),
    ]
    small[4] = place(head_sum(stats[5]), (total_heads,), (at_head,))
    sizes = [s.shape[0] for s in small]
    joined = lax.psum(jnp.concatenate(small), ("fsdp", "context", "tensor"))
    pieces = []
    at = 0
    for size in sizes:
        pieces.append(joined[at : at + size])
        at += size

    def own(values, width, axis):
        return lax.dynamic_slice_in_dim(values, t * width, width, axis=axis)

    return (
        mixed_out,
        tokens_grad,
        pieces[0],
        spread(inner, qd),
        dkv,
        spread(896 + inner, qd),
        spread(512, inner),
        spread(0, inner),
        dbc,
        spread(at_step, heads),
        own(pieces[2].reshape(CONV, x_width), conv_x.shape[1], 1),
        pieces[3].reshape(CONV, -1),
        own(pieces[4], skip.shape[0], 0),
        own(pieces[5], skip.shape[0], 0),
        own(pieces[6], skip.shape[0], 0),
        spread(896, inner),
        pieces[1],
        spread(1152, hid),
        spread(1152 + hid, hid),
        spread(1152 + 2 * hid, hid),
    )


def solution(mesh):
    in_specs = (
        P(("fsdp", "context"), None),
        P("fsdp", None),
        P("fsdp", None),
        P(),
        P("fsdp", "tensor"),
        P("fsdp", "tensor"),
        P("fsdp", "tensor"),
        P("fsdp", "tensor"),
        P("fsdp", "tensor"),
        P("fsdp", None),
        P("fsdp", "tensor"),
        P(None, "tensor"),
        P(),
        P("tensor"),
        P("tensor"),
        P("tensor"),
        P("fsdp", "tensor"),
        P(),
        P("fsdp", "tensor"),
        P("fsdp", "tensor"),
        P("fsdp", "tensor"),
        P(("fsdp", "context"), None),
    )
    out_specs = (
        P(("fsdp", "context"), None),
        P(("fsdp", "context"), None),
        P(),
        P("fsdp", "tensor"),
        P("fsdp", "tensor"),
        P("fsdp", "tensor"),
        P("fsdp", "tensor"),
        P("fsdp", "tensor"),
        P("fsdp", None),
        P("fsdp", "tensor"),
        P(None, "tensor"),
        P(),
        P("tensor"),
        P("tensor"),
        P("tensor"),
        P("fsdp", "tensor"),
        P(),
        P("fsdp", "tensor"),
        P("fsdp", "tensor"),
        P("fsdp", "tensor"),
    )
    return jax.shard_map(
        per_device, mesh=mesh, in_specs=in_specs, out_specs=out_specs, check_vma=False
    )
```

```python
import functools

import jax
import jax.numpy as jnp
from jax import lax
from jax.experimental import pallas as pl
from jax.experimental.pallas import tpu as pltpu
from jax.sharding import PartitionSpec as P

HEAD_DIM = 64
SSM_DIM = 64
STATE = 128
CONV = 4
HALF = 256
WINDOW = 4

epsilon = 1e-05
masked = -1e30
F32 = jnp.float32
BF16 = jnp.bfloat16
exact = lax.Precision.HIGHEST


def dot(left, right, left_dim=1, right_dim=0, precision=None):
    return lax.dot_general(
        left,
        right,
        (((left_dim,), (right_dim,)), ((), ())),
        precision=precision,
        preferred_element_type=F32,
    )


def sigmoid(v):
    return 1.0 / (1.0 + jnp.exp(-v))


def softplus(v):
    return jnp.maximum(v, 0.0) + jnp.log1p(jnp.exp(-jnp.abs(v)))


def swap_halves(v):
    half = v.shape[1] // 2
    return jnp.concatenate([v[:, half:], v[:, :half]], axis=1)


def iotas(rows, columns):
    return (
        lax.broadcasted_iota(jnp.int32, (rows, columns), 0),
        lax.broadcasted_iota(jnp.int32, (rows, columns), 1),
    )


def state_scale(last_row, carry_last, heads):
    pieces = [
        jnp.broadcast_to(last_row[:, h * SSM_DIM : h * SSM_DIM + 1], (SSM_DIM, STATE))
        for h in range(heads)
    ]
    return jnp.exp(jnp.concatenate(pieces, axis=0)) * carry_last


def block_decays(step_raw, heads_ref, lane_pos, heads):
    rows = step_raw.shape[0]
    inner = heads * SSM_DIM
    raw = step_raw + heads_ref[0:1, :inner]
    step = softplus(raw)
    rate = step * jnp.exp(heads_ref[1:2, :inner])
    row, col = iotas(rows, rows)
    lower = jnp.where(col <= row, 1.0, 0.0).astype(F32)
    totals = dot(lower, -rate, precision=exact)
    last_row = totals[rows - 1 : rows]
    pos_last = lane_pos[rows - 1 : rows, 0:1]
    local = lax.broadcasted_iota(jnp.int32, (rows, 1), 0).astype(F32)
    carry_on = (lane_pos[:, 0:1] > local).astype(F32)
    keep_last = (local >= (rows - 1) - pos_last).astype(F32)
    carry_last = (pos_last > rows - 1).astype(F32)
    factor = jnp.exp(totals) * carry_on
    tails = jnp.exp(last_row - totals) * keep_last
    return raw, step, rate, totals, last_row, carry_last, factor, tails


def local_mask(lane_pos, rows):
    row, col = iotas(rows, rows)
    gap = (row - col).astype(F32)
    return (gap >= 0) & (gap <= lane_pos[:, 0:1])


def key_window(block):
    start = jnp.maximum(block - WINDOW, 0)
    return start, (block - start) * HALF


def window_mask(lane_pos, offset, rows, keys):
    row, col = iotas(rows, keys)
    gap = (row - col + offset).astype(F32)
    return (gap >= 0) & (gap <= lane_pos[:, 0:1])


def head_decay(totals, totals_t, h, allowed):
    gap = totals[:, h * SSM_DIM : h * SSM_DIM + 1] - totals_t[h * SSM_DIM : h * SSM_DIM + 1, :]
    return jnp.exp(jnp.where(allowed, gap, masked))


def mixer_forward_kernel(
    slots_ref, u_ref, table_ref, heads_ref, taps_ref, ag_ref, y_ref, conv_ref, state_in_ref, kv_ref,
    ext, state, keyval,
):
    block = pl.program_id(0)
    heads = state.shape[0] // SSM_DIM
    inner = heads * SSM_DIM
    width = ext.shape[1]
    rows = u_ref.shape[0]

    @pl.when(block == 0)
    def _():
        ext[0:8, :] = jnp.zeros((8, width), F32)
        state[...] = jnp.zeros(state.shape, F32)
        keyval[...] = jnp.zeros(keyval.shape, BF16)

    lane_pos = table_ref[:, 128:256]
    cosine = table_ref[:, 0:64]
    sine = table_ref[:, 64:128]
    q_at = inner
    u = u_ref[:, :width].astype(F32)
    ext[8 : 8 + rows, :] = u
    conv = u * taps_ref[CONV - 1 : CONV, :]
    for back in range(1, CONV):
        reach = lane_pos[:, 0:1] >= back
        shifted = ext[8 - back : 8 - back + rows, :]
        conv = conv + jnp.where(reach, shifted, 0.0) * taps_ref[CONV - 1 - back : CONV - back, :]
    ext[0:8, :] = u[rows - 8 : rows]
    act = conv * sigmoid(conv)
    ssm_x = act[:, :inner].astype(BF16)
    ssm_b = act[:, 256:384].astype(BF16)
    ssm_c = act[:, 384:512].astype(BF16)
    conv_ref[:, 0:256] = conv[:, 0:256]
    conv_ref[:, 256:512] = conv[:, 256:512]
    query = u[:, q_at : q_at + HEAD_DIM]
    query = (query * cosine + swap_halves(query) * sine).astype(BF16)
    conv_ref[:, q_at : q_at + HEAD_DIM] = query.astype(F32)
    key = u_ref[:, 512 + inner : 512 + inner + HEAD_DIM].astype(F32)
    key = key * cosine + swap_halves(key) * sine
    value = u_ref[:, 768 + inner : 768 + inner + HEAD_DIM].astype(F32)
    pair = jnp.concatenate([key, value], axis=1).astype(BF16)
    kv_ref[...] = pair
    keyval[pl.ds(pl.multiple_of(block * rows, rows), rows), :] = pair
    first, offset = key_window(block)
    span = (WINDOW + 1) * HALF
    window = keyval[pl.ds(pl.multiple_of(first * rows, rows), span), :]
    scores = dot(query * 0.125, window[:, :HEAD_DIM], 1, 1)
    scores = jnp.where(window_mask(lane_pos, offset, rows, span), scores, masked)
    highest = jnp.max(scores, axis=1, keepdims=True)
    weights = jnp.exp(scores - highest)
    total = jnp.sum(weights, axis=1, keepdims=True)
    probs = (weights * (1.0 / total)).astype(BF16)
    attended = dot(probs, window[:, HEAD_DIM:])
    _, step, _, totals, last_row, carry_last, factor, tails = block_decays(
        u_ref[:, 768 : 768 + inner].astype(F32), heads_ref, lane_pos, heads
    )
    totals_t = totals.T
    allowed = local_mask(lane_pos, rows)
    cross = dot(ssm_c, ssm_b, 1, 1)
    x_f = ssm_x.astype(F32)
    stepped = step * x_f
    stepped_low = stepped.astype(BF16)
    parts = []
    for h in range(heads):
        lanes = slice(h * SSM_DIM, (h + 1) * SSM_DIM)
        mix = (head_decay(totals, totals_t, h, allowed) * cross).astype(BF16)
        parts.append(dot(mix, stepped_low[:, lanes]))
    held = state[...]
    state_in_ref[...] = held
    y_pure = jnp.concatenate(parts, axis=1) + factor * dot(ssm_c, held.astype(BF16), 1, 1)
    tailed = (tails * stepped_low.astype(F32)).astype(BF16)
    state[...] = state_scale(last_row, carry_last, heads) * held + dot(tailed, ssm_b, 0, 0)
    y_ref[:, :inner] = y_pure
    y_ref[:, inner : inner + HEAD_DIM] = jnp.broadcast_to(
        highest + jnp.log(total), (rows, HEAD_DIM)
    )
    y_full = y_pure + heads_ref[2:3, :inner] * x_f
    gate = u_ref[:, 512 : 512 + inner].astype(F32)
    gated = y_full * (gate * sigmoid(gate))
    ag_ref[...] = jnp.concatenate([gated, attended], axis=1).astype(BF16)


def mixer_backward_kernel(
    slots_ref, dag_ref, ag_ref, u_ref, table_ref, heads_ref, taps_ref, y_ref, conv_ref, state_in_ref,
    state_out_ref, kv_ref, du_ref, stats_ref, dext, dpos, dstate, dkey_t, dvalue_t,
):
    turn = pl.program_id(0)
    blocks = pl.num_programs(0)
    block = blocks - 1 - turn
    heads = dstate.shape[0] // SSM_DIM
    inner = heads * SSM_DIM
    rows = u_ref.shape[0]
    width = dext.shape[1]

    @pl.when(turn == 0)
    def _():
        dext[rows : rows + 8, :] = jnp.zeros((8, width), F32)
        dpos[rows : rows + 8, :] = jnp.full((8, dpos.shape[1]), -1.0, F32)
        dstate[...] = jnp.zeros(dstate.shape, F32)
        dkey_t[...] = jnp.zeros(dkey_t.shape, F32)
        dvalue_t[...] = jnp.zeros(dvalue_t.shape, F32)
        stats_ref[...] = jnp.zeros(stats_ref.shape, F32)

    lane_pos = table_ref[:, 128:256]
    cosine = table_ref[:, 0:64]
    sine = table_ref[:, 64:128]
    first, offset = key_window(block)
    span = (WINDOW + 1) * HALF
    begin = pl.multiple_of(first * rows, rows)
    window = kv_ref[pl.ds(begin, span), :]
    keys = window[:, :HEAD_DIM]
    values = window[:, HEAD_DIM:]
    query = conv_ref[:, inner : inner + HEAD_DIM] * 0.125
    query_low = query.astype(BF16)
    datt = dag_ref[:, inner : inner + HEAD_DIM]
    datt_f = datt.astype(F32)
    lse = y_ref[:, inner : inner + 1]
    scores = dot(query_low, keys, 1, 1)
    allowed_all = window_mask(lane_pos, offset, rows, span)
    probs = jnp.exp(jnp.where(allowed_all, scores, masked) - lse)
    inward = jnp.sum(datt_f * ag_ref[:, inner : inner + HEAD_DIM].astype(F32), axis=1, keepdims=True)
    dscores = (probs * (dot(datt, values, 1, 1) - inward)).astype(BF16)
    dquery = dot(dscores, keys) * 0.125
    dkey_t[:, pl.ds(begin, span)] += dot(query.T.astype(BF16), dscores)
    dvalue_t[:, pl.ds(begin, span)] += dot(datt_f.T.astype(BF16), probs.astype(BF16))
    here = pl.ds(pl.multiple_of(block * rows, rows), rows)
    dkey = dkey_t[:, here].T
    dvalue = dvalue_t[:, here].T
    dquery = dquery * cosine - swap_halves(dquery) * sine
    dkey = dkey * cosine - swap_halves(dkey) * sine
    conv = conv_ref[...]
    gate_conv = sigmoid(conv)
    act = conv * gate_conv
    dact = gate_conv * (1.0 + conv * (1.0 - gate_conv))
    ssm_x = act[:, :inner].astype(BF16)
    ssm_b = act[:, 256:384].astype(BF16)
    ssm_c = act[:, 384:512].astype(BF16)
    x_f = ssm_x.astype(F32)
    raw, step, rate, totals, last_row, carry_last, factor, tails = block_decays(
        u_ref[:, 768 : 768 + inner].astype(F32), heads_ref, lane_pos, heads
    )
    totals_t = totals.T
    allowed = local_mask(lane_pos, rows)
    cross = dot(ssm_c, ssm_b, 1, 1)
    gate = u_ref[:, 512 : 512 + inner].astype(F32)
    sig = sigmoid(gate)
    y_pure = y_ref[:, :inner]
    dgated = dag_ref[:, :inner].astype(F32)
    skip = heads_ref[2:3, :inner]
    dy = dgated * (gate * sig)
    dgate = dgated * (y_pure + skip * x_f) * (sig * (1.0 + gate * (1.0 - sig)))
    dy_low = dy.astype(BF16)
    dy_r = dy_low.astype(F32)
    dy_t = dy.T.astype(BF16)
    stepped_low = (step * x_f).astype(BF16)
    stepped_r = stepped_low.astype(F32)
    tailed = (tails * stepped_r).astype(BF16)
    dcross = jnp.zeros((rows, rows), F32)
    parts = []
    for h in range(heads):
        lanes = slice(h * SSM_DIM, (h + 1) * SSM_DIM)
        decay = head_decay(totals, totals_t, h, allowed)
        mix = (decay * cross).astype(BF16)
        parts.append(dot(dy_t[lanes, :], mix))
        dcross = dcross + dot(dy_low[:, lanes], stepped_low[:, lanes], 1, 1) * decay
    dstep_x = jnp.concatenate(parts, axis=0).T
    dcross_low = dcross.astype(BF16)
    held = state_in_ref[...].astype(BF16)
    dheld = dstate[...]
    dheld_low = dheld.astype(BF16)
    dfactored = (factor * dy).astype(BF16)
    from_state = dot(ssm_b, dheld_low, 1, 1)
    dssm_c = dot(dcross_low, ssm_b) + dot(dfactored, held)
    dssm_b = dot(dcross_low, ssm_c, 0, 0) + dot(tailed, dheld_low)
    dtotals = dy_r * y_pure - stepped_r * dstep_x - tailed.astype(F32) * from_state
    dstep_x = dstep_x + tails * from_state
    end_term = dot(
        jnp.ones((8, STATE), F32), dheld_low.astype(F32) * state_out_ref[...], 1, 1, exact
    )[0:1]
    end_term = jnp.where(turn == 0, jnp.zeros_like(end_term), end_term)
    row, col = iotas(rows, rows)
    upper = jnp.where(col >= row, 1.0, 0.0).astype(F32)
    drate = -(dot(upper, dtotals, precision=exact) + end_term)
    dstate[...] = state_scale(last_row, carry_last, heads) * dheld + dot(dfactored, ssm_c, 0, 0)
    dssm_x = step * dstep_x + skip * dy
    dstep = x_f * dstep_x + jnp.exp(heads_ref[1:2, :inner]) * drate
    draw = dstep * sigmoid(raw)
    none = jnp.zeros((rows, HEAD_DIM), F32)
    dconv = jnp.concatenate([dssm_x, none, dssm_b, dssm_c], axis=1) * dact
    dext[0:rows, :] = dconv
    dpos[0:rows, :] = lane_pos
    u = u_ref[:, :width].astype(F32)
    du = dconv * taps_ref[CONV - 1 : CONV, :]
    stats_ref[CONV - 1 : CONV, :] += jnp.sum(dconv * u, axis=0, keepdims=True)
    for ahead in range(1, CONV):
        reach = dpos[ahead : ahead + rows, 0:1] >= ahead
        shifted = jnp.where(reach, dext[ahead : ahead + rows, :], 0.0)
        tap = CONV - 1 - ahead
        du = du + shifted * taps_ref[tap : tap + 1, :]
        stats_ref[tap : tap + 1, :] += jnp.sum(shifted * u, axis=0, keepdims=True)
    dext[rows : rows + 8, :] = dconv[0:8]
    dpos[rows : rows + 8, :] = lane_pos[0:8]
    stats_ref[4:5, :inner] += jnp.sum(dy * x_f, axis=0, keepdims=True)
    stats_ref[5:6, :inner] += jnp.sum(draw, axis=0, keepdims=True)
    stats_ref[6:7, :inner] += jnp.sum(drate * rate, axis=0, keepdims=True)
    summed = [
        jnp.sum(draw[:, h * SSM_DIM : (h + 1) * SSM_DIM], axis=1, keepdims=True)
        for h in range(heads)
    ]
    lane = lax.broadcasted_iota(jnp.int32, (rows, HEAD_DIM), 1)
    dstep_all = jnp.zeros((rows, HEAD_DIM), F32)
    for h in range(heads):
        dstep_all = jnp.where(lane == h, summed[h], dstep_all)
    du_ref[:, 0:256] = jnp.concatenate([du[:, :inner], dquery], axis=1).astype(BF16)
    du_ref[:, 256:512] = du[:, 256:512].astype(BF16)
    du_ref[:, 512:768] = jnp.concatenate([dgate, dkey], axis=1).astype(BF16)
    du_ref[:, 768:896] = jnp.concatenate([dvalue, dstep_all], axis=1).astype(BF16)


def mixer_forward(u, table, head_rows, taps, slot_of):
    count = u.shape[0]
    blocks = count // HALF
    heads = 3
    inner = heads * SSM_DIM
    width = taps.shape[1]
    at_slot = lambda i, slots: (slots[i], 0)
    in_order = lambda i, slots: (i, 0)
    whole = lambda i, slots: (0, 0)
    return pl.pallas_call(
        mixer_forward_kernel,
        out_shape=(
            jax.ShapeDtypeStruct((count, inner + HEAD_DIM), BF16),
            jax.ShapeDtypeStruct((count, inner + HEAD_DIM), F32),
            jax.ShapeDtypeStruct((count, width), F32),
            jax.ShapeDtypeStruct((blocks * inner, STATE), F32),
            jax.ShapeDtypeStruct((count, 2 * HEAD_DIM), BF16),
        ),
        grid_spec=pltpu.PrefetchScalarGridSpec(
            num_scalar_prefetch=1,
            grid=(blocks,),
            in_specs=[
                pl.BlockSpec((HALF, u.shape[1]), at_slot),
                pl.BlockSpec((HALF, table.shape[1]), in_order),
                pl.BlockSpec(head_rows.shape, whole),
                pl.BlockSpec(taps.shape, whole),
            ],
            out_specs=(
                pl.BlockSpec((HALF, inner + HEAD_DIM), at_slot),
                pl.BlockSpec((HALF, inner + HEAD_DIM), in_order),
                pl.BlockSpec((HALF, width), in_order),
                pl.BlockSpec((inner, STATE), in_order),
                pl.BlockSpec((HALF, 2 * HEAD_DIM), in_order),
            ),
            scratch_shapes=[
                pltpu.VMEM((8 + HALF, width), F32),
                pltpu.VMEM((inner, STATE), F32),
                pltpu.VMEM((count, 2 * HEAD_DIM), BF16),
            ],
        ),
        compiler_params=pltpu.CompilerParams(vmem_limit_bytes=48 << 20),
    )(slot_of, u, table, head_rows, taps)


def mixer_backward(dag, ag, u, table, head_rows, taps, y, conv, states, keyval, slot_of):
    count = u.shape[0]
    blocks = count // HALF
    heads = 3
    inner = heads * SSM_DIM
    width = taps.shape[1]
    last = blocks - 1
    at_slot = lambda i, slots: (slots[last - i], 0)
    in_order = lambda i, slots: (last - i, 0)
    after = lambda i, slots: (jnp.minimum(last - i + 1, last), 0)
    whole = lambda i, slots: (0, 0)
    columns = inner + HEAD_DIM
    return pl.pallas_call(
        mixer_backward_kernel,
        out_shape=(
            jax.ShapeDtypeStruct((count, 896), BF16),
            jax.ShapeDtypeStruct((8, width), F32),
        ),
        grid_spec=pltpu.PrefetchScalarGridSpec(
            num_scalar_prefetch=1,
            grid=(blocks,),
            in_specs=[
                pl.BlockSpec((HALF, columns), at_slot),
                pl.BlockSpec((HALF, columns), at_slot),
                pl.BlockSpec((HALF, u.shape[1]), at_slot),
                pl.BlockSpec((HALF, table.shape[1]), in_order),
                pl.BlockSpec(head_rows.shape, whole),
                pl.BlockSpec(taps.shape, whole),
                pl.BlockSpec((HALF, columns), in_order),
                pl.BlockSpec((HALF, width), in_order),
                pl.BlockSpec((inner, STATE), in_order),
                pl.BlockSpec((inner, STATE), after),
                pl.BlockSpec((count, 2 * HEAD_DIM), whole),
            ],
            out_specs=(
                pl.BlockSpec((HALF, 896), at_slot),
                pl.BlockSpec((8, width), whole),
            ),
            scratch_shapes=[
                pltpu.VMEM((HALF + 8, width), F32),
                pltpu.VMEM((HALF + 8, 128), F32),
                pltpu.VMEM((inner, STATE), F32),
                pltpu.VMEM((HEAD_DIM, count), F32),
                pltpu.VMEM((HEAD_DIM, count), F32),
            ],
        ),
        compiler_params=pltpu.CompilerParams(vmem_limit_bytes=56 << 20),
    )(slot_of, dag, ag, u, table, head_rows, taps, y, conv, states, states, keyval)


MESH = pl.DeviceIdType.MESH


class Place:
    def __init__(self):
        self.c = lax.axis_index("context")
        self.t = lax.axis_index("tensor")
        count = lax.axis_size("context")
        self.chips = [
            self.c,
            self.c + 1 - 2 * (self.c % 2),
            (self.c + count // 2) % count,
            count - 1 - self.c,
        ]

    def slot(self, mask, sibling=False):
        core = 1 - self.t if sibling else self.t
        return self.chips[mask] * 2 + core

    def target(self, mask):
        if mask == 4:
            return {"tensor": 1 - self.t}
        return {"context": self.chips[mask]}

    def greet(self, line=None):
        barrier = pltpu.get_barrier_semaphore()
        targets = [self.target(mask) for mask in (1, 2, 4)]
        if line is not None:
            targets += [line.target(step) for step in range(1, line.count)]
        for target in targets:
            pl.semaphore_signal(barrier, inc=1, device_id=target, device_id_type=MESH)
        pl.semaphore_wait(barrier, len(targets))


class Wire:
    def __init__(self, place, sems):
        self.place = place
        self.sems = sems
        self.sent = []

    def copy(self, source, target, index, mask):
        return pltpu.make_async_remote_copy(
            src_ref=source,
            dst_ref=target,
            send_sem=self.sems.at[0, index],
            recv_sem=self.sems.at[1, index],
            device_id=self.place.target(mask),
            device_id_type=MESH,
        )

    def send(self, source, target, index, mask):
        made = self.copy(source, target, index, mask)
        made.start()
        self.sent.append(made)

    def arrive(self, target, index, mask):
        self.copy(target, target, index, mask).wait_recv()

    def finish(self):
        for made in self.sent:
            made.wait_send()
        self.sent = []


ROWS = HALF
PART = HALF // 2
TOP, END = pl.ds(0, PART), pl.ds(PART, PART)
SCATTER_SEMS = 10
GATHER_SEMS = 14


def scatter_scratch(columns):
    return [
        pltpu.VMEM((4, ROWS, columns), BF16),
        pltpu.VMEM((4, ROWS, columns), BF16),
        pltpu.VMEM((6, PART, columns), BF16),
        pltpu.VMEM((ROWS, columns), F32),
        pltpu.SemaphoreType.DMA((2, SCATTER_SEMS)),
    ]


SCATTER_ORDER = (3, 1, 2, 0)


class Scatter:
    def __init__(self, place, scratch):
        self.place = place
        self.core_in, self.out, self.chip_in, self.kept, sems = scratch
        self.wire = Wire(place, sems)

    def to_core(self, mask, source):
        index = SCATTER_ORDER.index(mask)
        self.wire.send(source, self.core_in.at[index], index, 4)

    def from_core(self, mask):
        index = SCATTER_ORDER.index(mask)
        self.wire.arrive(self.core_in.at[index], index, 4)
        return self.core_in[index].astype(F32)

    def first(self, mine, total, between=None):
        wire, out, kept = self.wire, self.out, self.kept
        both = mine(3) + self.from_core(3)
        out[0] = both.astype(BF16)
        wire.send(out.at[0, TOP], self.chip_in.at[0], 4, 1)
        wire.send(out.at[0, END], self.chip_in.at[1], 5, 2)
        both = mine(1) + self.from_core(1)
        out[1] = both.astype(BF16)
        wire.send(out.at[1, TOP], self.chip_in.at[2], 6, 1)
        kept[END] = both[PART:]
        both = mine(2) + self.from_core(2)
        out[2] = both.astype(BF16)
        wire.send(out.at[2, END], self.chip_in.at[3], 7, 2)
        kept[TOP] = both[:PART]
        total[...] = mine(0) + self.from_core(0)

    def second(self):
        wire, out, kept, came = self.wire, self.out, self.kept, self.chip_in
        wire.arrive(came.at[0], 4, 1)
        out[3, TOP] = (kept[TOP] + came[0].astype(F32)).astype(BF16)
        wire.send(out.at[3, TOP], came.at[4], 8, 2)
        wire.arrive(came.at[1], 5, 2)
        out[3, END] = (kept[END] + came[1].astype(F32)).astype(BF16)
        wire.send(out.at[3, END], came.at[5], 9, 1)

    def last(self, total):
        wire, came = self.wire, self.chip_in
        wire.arrive(came.at[2], 6, 1)
        wire.arrive(came.at[4], 8, 2)
        total[TOP] += came[2].astype(F32) + came[4].astype(F32)
        wire.arrive(came.at[3], 7, 2)
        wire.arrive(came.at[5], 9, 1)
        total[END] += came[3].astype(F32) + came[5].astype(F32)
        wire.finish()


class Gather:
    def __init__(self, place, whole, sems, rows=ROWS, cores=True):
        self.place = place
        self.whole = whole
        self.size = rows
        self.cores = cores
        self.wire = Wire(place, sems)

    def rows(self, mask, sibling=False, half=None):
        place, size = self.place, self.size
        block = place.slot(mask, sibling) if self.cores else place.chips[mask]
        begin = block * size
        if half is None:
            return self.whole.at[pl.ds(pl.multiple_of(begin, size), size)]
        return self.whole.at[pl.ds(pl.multiple_of(begin + half * (size // 2), size // 2), size // 2)]

    def start(self, core=True):
        wire = self.wire
        for half, mask, index in ((0, 1, 0), (1, 2, 1), (1, 1, 2), (0, 2, 3)):
            wire.send(self.rows(0, half=half), self.rows(0, half=half), index, mask)
        if self.cores and core:
            wire.send(self.rows(0), self.rows(0), 6, 4)

    def relay(self):
        wire = self.wire
        wire.arrive(self.rows(1, half=0), 0, 1)
        wire.send(self.rows(1, half=0), self.rows(1, half=0), 4, 2)
        wire.arrive(self.rows(2, half=1), 1, 2)
        wire.send(self.rows(2, half=1), self.rows(2, half=1), 5, 1)

    def near(self):
        wire = self.wire
        wire.arrive(self.rows(1, half=1), 2, 1)
        if self.cores:
            wire.send(self.rows(1), self.rows(1), 7, 4)
        wire.arrive(self.rows(2, half=0), 3, 2)
        if self.cores:
            wire.send(self.rows(2), self.rows(2), 8, 4)

    def far(self):
        wire = self.wire
        wire.arrive(self.rows(3, half=0), 4, 2)
        wire.arrive(self.rows(3, half=1), 5, 1)
        if self.cores:
            wire.send(self.rows(3), self.rows(3), 9, 4)

    def core(self, mask):
        index = (6, 7, 8, 9)[mask]
        self.wire.arrive(self.rows(mask, sibling=True), index, 4)

    def finish(self):
        self.wire.finish()


class Line:
    def __init__(self):
        self.f = lax.axis_index("fsdp")
        self.count = lax.axis_size("fsdp")

    def target(self, step):
        return {"fsdp": (self.f + step) % self.count}

    def copy(self, source, target, sems, step):
        return pltpu.make_async_remote_copy(
            src_ref=source,
            dst_ref=target,
            send_sem=sems.at[0, step],
            recv_sem=sems.at[1, step],
            device_id=self.target(step),
            device_id_type=MESH,
        )


def slot_rows(slot):
    return pl.ds(pl.multiple_of(slot * ROWS, ROWS), ROWS)


def norm_scale(values):
    return lax.rsqrt(jnp.mean(values * values, axis=1, keepdims=True) + epsilon)


def middle_kernel(
    ag_ref, wout_ref, wffn_ref, x_ref, cot_ref, cot_all_ref, gain_ref,
    nffn_ref, hidden_ref, dgu_ref, dm_ref, dag_ref, outp_ref, mixed_ref, dmixed_ref, dgain_ref, dw_ref,
    part, *scratch,
):
    place = Place()
    first = Scatter(place, scratch[0:5])
    back = Scatter(place, scratch[5:10])
    forth = Gather(place, nffn_ref, scratch[10])
    home = Gather(place, dm_ref, scratch[11])
    hid = hidden_ref.shape[1]
    place.greet()

    def block(mask, sibling=False):
        return dot(ag_ref[slot_rows(place.slot(mask, sibling)), :], wout_ref[...], 1, 1)

    for mask in SCATTER_ORDER:
        rows = slot_rows(place.slot(mask, True))
        part[rows, :] = block(mask, True).astype(BF16)
        first.to_core(mask, part.at[rows])
    first.first(block, mixed_ref)
    first.second()
    mixed_ref[...] += x_ref[...].astype(F32)
    first.last(mixed_ref)
    mixed = mixed_ref[...]
    gain = gain_ref[...]
    scale = norm_scale(mixed)
    own = slot_rows(place.slot(0))
    nffn_ref[own, :] = (mixed * scale * gain).astype(BF16)
    forth.start()

    def work(slot):
        rows = slot_rows(slot)
        normed = nffn_ref[rows, :]
        gate_up = dot(normed, wffn_ref[:, : 2 * hid])
        dhidden = dot(cot_all_ref[rows, :], wffn_ref[:, 2 * hid :]).astype(BF16).astype(F32)
        gate, up = gate_up[:, :hid], gate_up[:, hid:]
        sig = sigmoid(gate)
        silu = gate * sig
        dgate = dhidden * up * (sig * (1.0 + gate * (1.0 - sig)))
        hidden_ref[rows, :] = (silu * up).astype(BF16)
        dgu_ref[rows, :hid] = dgate.astype(BF16)
        dgu_ref[rows, hid:] = (dhidden * silu).astype(BF16)
        part[rows, :] = dot(dgu_ref[rows, :], wffn_ref[:, : 2 * hid], 1, 1).astype(BF16)

    def hand_over(mask):
        slot = place.slot(mask, True)
        work(slot)
        back.to_core(mask, part.at[slot_rows(slot)])

    work(place.slot(0))
    forth.relay()
    forth.core(0)
    hand_over(0)
    forth.near()
    forth.core(1)
    hand_over(1)
    forth.core(2)
    hand_over(2)
    work(place.slot(1))
    forth.far()
    work(place.slot(2))
    forth.core(3)
    hand_over(3)
    work(place.slot(3))
    forth.finish()

    def ready(mask):
        return part[slot_rows(place.slot(mask)), :].astype(F32)

    back.first(ready, dmixed_ref)

    def out_block(slot, carry):
        rows = slot_rows(slot)
        outp_ref[rows, :] = dot(hidden_ref[rows, :], wffn_ref[:, 2 * hid :], 1, 1).astype(BF16)
        return carry

    lax.fori_loop(0, 8, out_block, 0)
    back.second()
    dw_ref[:, : 2 * hid] = dot(nffn_ref[...], dgu_ref[...], 0, 0).astype(BF16)
    back.last(dmixed_ref)
    dnffn = dmixed_ref[...]
    mixed = mixed_ref[...]
    scale = norm_scale(mixed)
    spread = dnffn * gain
    pull = jnp.mean(spread * mixed, axis=1, keepdims=True)
    dgain_ref[...] = jnp.broadcast_to(
        jnp.sum(dnffn * mixed * scale, axis=0, keepdims=True), dgain_ref.shape
    )
    dmixed = cot_ref[...].astype(F32) + scale * (spread - mixed * (scale * scale * pull))
    dmixed_ref[...] = dmixed
    dm_ref[own, :] = dmixed.astype(BF16)
    home.start()

    def pull_back(slot):
        rows = slot_rows(slot)
        dag_ref[rows, :] = dot(dm_ref[rows, :], wout_ref[...]).astype(BF16)

    pull_back(place.slot(0))
    home.relay()
    dw_ref[:, 2 * hid : 3 * hid] = dot(cot_all_ref[...], hidden_ref[...], 0, 0).astype(BF16)
    home.core(0)
    pull_back(place.slot(0, True))
    home.near()
    pull_back(place.slot(1))
    pull_back(place.slot(2))
    home.far()
    pull_back(place.slot(3))
    for mask in (1, 2, 3):
        home.core(mask)
        pull_back(place.slot(mask, True))
    dw_ref[:, 3 * hid :] = dot(dm_ref[...], ag_ref[...], 0, 0).astype(BF16)
    home.finish()


def middle(ag, wout, wffn, x_own, cot_own, cot_all, gain):
    count, model = cot_all.shape
    hid = wffn.shape[1] // 3
    columns = ag.shape[1]
    vmem = pl.BlockSpec(memory_space=pltpu.VMEM)
    shape = jax.ShapeDtypeStruct
    return pl.pallas_call(
        middle_kernel,
        out_shape=(
            shape((count, model), BF16),
            shape((count, hid), BF16),
            shape((count, 2 * hid), BF16),
            shape((count, model), BF16),
            shape((count, columns), BF16),
            shape((count, model), BF16),
            shape((ROWS, model), F32),
            shape((ROWS, model), F32),
            shape((8, model), F32),
            shape((model, 3 * hid + columns), BF16),
        ),
        in_specs=[vmem] * 7,
        out_specs=(vmem,) * 10,
        scratch_shapes=[pltpu.VMEM((count, model), BF16)]
        + scatter_scratch(model)
        + scatter_scratch(model)
        + [pltpu.SemaphoreType.DMA((2, GATHER_SEMS))] * 2,
        compiler_params=pltpu.CompilerParams(
            collective_id=1, has_side_effects=True, vmem_limit_bytes=60 << 20
        ),
        cost_estimate=pl.CostEstimate(
            flops=20 * count * model * hid, bytes_accessed=40 << 20, transcendentals=count * hid
        ),
    )(ag, wout, wffn, x_own, cot_own, cot_all, gain.reshape(1, -1))


def ending_kernel(
    du_ref, w_ref, normed_ref, x_ref, dmixed_ref, gain_ref, mixed_ref, outp_ref, mid_ref, stats_ref,
    dgain_ref,
    grad_ref, out_ref, last_ref, mids_ref, small_ref,
    total, part, dw, arrived, bc_out, bc_in, small_in, *scratch,
):
    place = Place()
    line = Line()
    back = Scatter(place, scratch[0:5])
    final = Scatter(place, scratch[5:10])
    share = mid_ref.shape[0]
    last_all = Gather(place, last_ref, scratch[10], share, False)
    mid_all = Gather(place, mids_ref, scratch[11], share, False)
    small_rows = small_in.shape[1]
    small_all = Gather(place, small_ref, scratch[12], small_rows)
    line_sems, small_sems, pair_sems = scratch[13], scratch[14], scratch[15]
    pair = Wire(place, pair_sems)
    place.greet(line)
    sent = []

    chunk = dw.shape[0] // 4
    for k in range(4):
        dw[k * chunk : (k + 1) * chunk, :] = dot(
            normed_ref[:, k * chunk : (k + 1) * chunk], du_ref[...], 0, 0
        ).astype(BF16)
    for step in range(1, line.count):
        rows = pl.ds(pl.multiple_of((line.f + step) % line.count * share, share), share)
        made = line.copy(dw.at[rows], arrived.at[step], line_sems, step)
        made.start()
        sent.append(made)

    def block(mask, sibling=False):
        return dot(du_ref[slot_rows(place.slot(mask, sibling)), :], w_ref[...], 1, 1)

    for mask in SCATTER_ORDER:
        rows = slot_rows(place.slot(mask, True))
        part[rows, :] = block(mask, True).astype(BF16)
        back.to_core(mask, part.at[rows])
    back.first(block, total)
    mids_ref[pl.ds(pl.multiple_of(place.c * share, share), share), :] = mid_ref[...]
    mid_all.start()
    for mask in SCATTER_ORDER:
        final.to_core(mask, outp_ref.at[slot_rows(place.slot(mask, True))])
    back.second()
    mid_all.relay()
    back.last(total)
    dnormed = total[...]
    x = x_ref[...].astype(F32)
    gain = gain_ref[...]
    scale = norm_scale(x)
    spread = dnormed * gain
    pull = jnp.mean(spread * x, axis=1, keepdims=True)
    grad = dmixed_ref[...] + scale * (spread - x * (scale * scale * pull))
    half = pl.ds(pl.multiple_of(place.t * ROWS, ROWS), ROWS)
    grad_ref[half, :] = grad.astype(BF16)
    pair.send(grad_ref.at[half], grad_ref.at[half], 0, 4)
    small_in[0] = jnp.zeros(small_in.shape[1:], F32)
    small_in[0, 0:1, :] = jnp.sum(dnormed * x * scale, axis=0, keepdims=True)
    small_in[0, 1:2, :] = dgain_ref[0:1, :]
    small_in[0, 8:16, : stats_ref.shape[1]] = stats_ref[...]
    for step in range(1, line.count):
        made = line.copy(small_in.at[0], small_in.at[step], small_sems, step)
        made.start()
        sent.append(made)

    def ready(mask):
        return outp_ref[slot_rows(place.slot(mask)), :].astype(F32)

    final.first(ready, total)
    mid_all.near()
    final.second()
    total[...] += mixed_ref[...]
    mid_all.far()
    final.last(total)
    out_ref[half, :] = total[...].astype(BF16)
    pair.send(out_ref.at[half], out_ref.at[half], 1, 4)

    for step in range(1, line.count):
        line.copy(small_in.at[0], small_in.at[step], small_sems, step).wait_recv()
    summed = small_in[line.f % line.count]
    for other in range(1, line.count):
        summed = summed + small_in[(line.f + line.count - other) % line.count]
    mine = pl.ds(pl.multiple_of(place.slot(0) * small_rows, small_rows), small_rows)
    small_ref[mine, :] = summed
    small_all.start()

    own = pl.ds(pl.multiple_of(line.f * share, share), share)
    for step in range(1, line.count):
        line.copy(arrived.at[step], arrived.at[step], line_sems, step).wait_recv()
    sums = dw[own, :].astype(F32)
    for step in range(1, line.count):
        sums = sums + arrived[step].astype(F32)
    here = pl.ds(pl.multiple_of(place.c * share, share), share)
    bc_out[...] = sums[:, 256:512].astype(BF16)
    pair.send(bc_out, bc_in, 2, 4)
    last_ref[here, 0:256] = sums[:, 0:256].astype(BF16)
    last_ref[here, 512:] = sums[:, 512:].astype(BF16)
    small_all.relay()
    pair.arrive(bc_in, 2, 4)
    last_ref[here, 256:512] = (bc_out[...].astype(F32) + bc_in[...].astype(F32)).astype(BF16)
    last_all.start()
    small_all.near()
    last_all.relay()
    small_all.far()
    last_all.near()
    last_all.far()
    for mask in range(4):
        small_all.core(mask)
    other = pl.ds(pl.multiple_of((1 - place.t) * ROWS, ROWS), ROWS)
    pair.arrive(grad_ref.at[other], 0, 4)
    pair.arrive(out_ref.at[other], 1, 4)
    for made in sent:
        made.wait_send()
    pair.finish()
    mid_all.finish()
    small_all.finish()
    last_all.finish()


def ending(du, w, normed, x_own, dmixed, gain, mixed, outp, mid, stats, dgain, fsdp):
    count, model = normed.shape
    share = mid.shape[0]
    columns = w.shape[1]
    chips = lax.axis_size("context")
    vmem = pl.BlockSpec(memory_space=pltpu.VMEM)
    shape = jax.ShapeDtypeStruct
    dma = pltpu.SemaphoreType.DMA
    return pl.pallas_call(
        ending_kernel,
        out_shape=(
            shape((2 * ROWS, model), BF16),
            shape((2 * ROWS, model), BF16),
            shape((chips * share, columns), BF16),
            shape((chips * share, mid.shape[1]), BF16),
            shape((2 * chips * 16, model), F32),
        ),
        in_specs=[vmem] * 11,
        out_specs=(vmem,) * 5,
        scratch_shapes=[
            pltpu.VMEM((ROWS, model), F32),
            pltpu.VMEM((count, model), BF16),
            pltpu.VMEM((model, columns), BF16),
            pltpu.VMEM((fsdp, share, columns), BF16),
            pltpu.VMEM((share, 256), BF16),
            pltpu.VMEM((share, 256), BF16),
            pltpu.VMEM((fsdp, 16, model), F32),
        ]
        + scatter_scratch(model)
        + scatter_scratch(model)
        + [dma((2, GATHER_SEMS))] * 3
        + [dma((2, fsdp)), dma((2, fsdp)), dma((2, 3))],
        compiler_params=pltpu.CompilerParams(
            collective_id=2, has_side_effects=True, vmem_limit_bytes=60 << 20
        ),
        cost_estimate=pl.CostEstimate(
            flops=4 * count * model * columns, bytes_accessed=30 << 20, transcendentals=0
        ),
    )(du, w, normed, x_own, dmixed, gain.reshape(1, -1), mixed, outp, mid, stats, dgain)


def assemble_kernel(
    last_ref, mid_ref, dx_ref, out_in_ref,
    out_ref, grad_ref, query_ref, keyval_ref, attn_ref, gate_ref, x_ref, bc_ref, step_ref, ssm_ref,
    ffn_gate_ref, ffn_up_ref, ffn_down_ref,
):
    chips = last_ref.shape[0]
    heads = step_ref.shape[1] // chips
    inner = heads * SSM_DIM
    hid = ffn_gate_ref.shape[1] // chips

    def spread(source, begin, width):
        return jnp.concatenate(
            [source[k, :, begin : begin + width].astype(F32) for k in range(chips)], axis=1
        )

    def summed(begin, end):
        total = last_ref[0, :, begin:end].astype(F32)
        for k in range(1, chips):
            total = total + last_ref[k, :, begin:end].astype(F32)
        return total

    out_ref[...] = out_in_ref[...]
    grad_ref[...] = dx_ref[...]
    x_ref[...] = spread(last_ref, 0, inner)
    query_ref[...] = spread(last_ref, inner, HEAD_DIM)
    bc_ref[...] = summed(256, 512)
    gate_ref[...] = spread(last_ref, 512, inner)
    both = summed(640, 896)
    keyval_ref[...] = both[:, HEAD_DIM : 3 * HEAD_DIM]
    step_ref[...] = spread(last_ref, 896 - HEAD_DIM, heads)
    ffn_gate_ref[...] = spread(mid_ref, 0, hid)
    ffn_up_ref[...] = spread(mid_ref, hid, hid)
    ffn_down_ref[...] = spread(mid_ref, 2 * hid, hid)
    ssm_ref[...] = spread(mid_ref, 3 * hid, inner)
    attn_ref[...] = spread(mid_ref, 3 * hid + inner, HEAD_DIM)


def assemble(last, mid, dx, out, widths):
    chips = lax.axis_size("context")
    share = last.shape[0] // chips
    turns = 2
    rows = share // turns
    shape = jax.ShapeDtypeStruct
    block = lambda height, width: pl.BlockSpec((height, width), lambda i: (i, 0))
    slab = lambda width: pl.BlockSpec((chips, rows, width), lambda i: (0, i, 0))
    token_rows = dx.shape[0] // turns
    model = dx.shape[1]
    return pl.pallas_call(
        assemble_kernel,
        grid=(turns,),
        out_shape=(shape(out.shape, BF16), shape(dx.shape, BF16))
        + tuple(shape((share, width), F32) for width in widths),
        in_specs=[
            slab(last.shape[1]), slab(mid.shape[1]), block(token_rows, model),
            block(token_rows, model),
        ],
        out_specs=(block(token_rows, model), block(token_rows, model))
        + tuple(block(rows, width) for width in widths),
        compiler_params=pltpu.CompilerParams(vmem_limit_bytes=40 << 20),
    )(last.reshape(chips, share, -1), mid.reshape(chips, share, -1), dx, out)


GROUP = ("context", "tensor")


def low_dot(left, right, left_dim=1, right_dim=0):
    return dot(left.astype(BF16), right.astype(BF16), left_dim, right_dim)


def inverse_rms(values):
    return lax.rsqrt(jnp.mean(values * values, axis=-1, keepdims=True) + epsilon)


def norm_back(values, gain, grad):
    scale = inverse_rms(values)
    pull = jnp.mean(grad * gain * values, axis=-1, keepdims=True)
    gain_grad = jnp.sum(grad * values * scale, axis=0)
    return scale * (grad * gain - values * scale * scale * pull), gain_grad


def stream_table(segment_ids):
    count = segment_ids.shape[0]
    order = jnp.arange(count, dtype=jnp.int32)
    starts = jnp.sum((segment_ids[None, :] < segment_ids[:, None]).astype(jnp.int32), axis=1)
    pos = (order - starts).astype(F32)
    half = HEAD_DIM // 2
    freqs = 10000.0 ** (-jnp.arange(half, dtype=F32) / half)
    angles = pos[:, None] * freqs[None, :]
    cosine, sine = jnp.cos(angles), jnp.sin(angles)
    return jnp.concatenate(
        [cosine, cosine, -sine, sine, jnp.broadcast_to(pos[:, None], (count, 128))], axis=1
    )


def per_device(
    tokens, segments, deal, gain_mix, w_query, w_keyval, w_attn_out, w_gate_z, w_in_x, w_bc, w_step,
    conv_x, conv_bc, step_bias, decay_log, skip, w_ssm_out, gain_ffn, w_ffn_gate, w_ffn_up,
    w_ffn_down, cotangent,
):
    ctx = lax.axis_size("context")
    c = lax.axis_index("context")
    t = lax.axis_index("tensor")
    heads = skip.shape[0] // ctx
    inner = heads * SSM_DIM
    qd = w_query.shape[1] // ctx
    hid = w_ffn_gate.shape[1] // ctx
    ddt = cotangent.dtype

    def part(array, width):
        return lax.dynamic_slice_in_dim(array, c * width, width, axis=1)

    keys_w, values_w = w_keyval[:, :HEAD_DIM], w_keyval[:, HEAD_DIM:]
    pad = HEAD_DIM - heads
    mine = jnp.concatenate(
        [
            part(w_in_x, inner), part(w_query, qd), w_bc, part(w_gate_z, inner), keys_w, values_w,
            jnp.pad(part(w_step, heads), ((0, 0), (0, pad))),
        ],
        axis=1,
    )
    mine_out = jnp.concatenate([part(w_ssm_out, inner), part(w_attn_out, qd)], axis=1)
    mine_ffn = jnp.concatenate(
        [part(w_ffn_gate, hid), part(w_ffn_up, hid), part(w_ffn_down, hid)], axis=1
    )
    w_all = lax.all_gather(mine, "fsdp", axis=0, tiled=True)
    wout_all = lax.all_gather(mine_out, "fsdp", axis=0, tiled=True)
    wffn_all = lax.all_gather(mine_ffn, "fsdp", axis=0, tiled=True)
    at_step = 896 - HEAD_DIM
    w_wide = jnp.concatenate(
        [
            w_all[:, :768],
            jnp.repeat(w_all[:, at_step : at_step + heads], SSM_DIM, axis=1),
            w_all[:, 768 : 768 + HEAD_DIM],
        ],
        axis=1,
    )

    order = deal[0]
    ids = jnp.arange(order.shape[0], dtype=jnp.int32)
    slot_of = jnp.sum(jnp.where(order[None, :] == ids[:, None], ids[None, :], 0), axis=1)
    table = stream_table(segments[0])

    def lanes(values):
        return jnp.repeat(lax.dynamic_slice_in_dim(values, c * heads, heads), SSM_DIM)

    head_rows = jnp.zeros((8, 256), F32)
    head_rows = head_rows.at[0, :inner].set(lanes(step_bias))
    head_rows = head_rows.at[1, :inner].set(lanes(decay_log))
    head_rows = head_rows.at[2, :inner].set(lanes(skip))
    taps = jnp.concatenate(
        [part(conv_x, inner), jnp.zeros((CONV, qd), F32), conv_bc], axis=1
    )

    x_all = lax.all_gather(tokens, "context", axis=0, tiled=True)
    cot_all = lax.all_gather(cotangent, "context", axis=0, tiled=True)
    row_count = tokens.shape[0]
    half = row_count // 2
    x_own = lax.dynamic_slice_in_dim(tokens, t * half, half, axis=0)
    cot_own = lax.dynamic_slice_in_dim(cotangent, t * half, half, axis=0)

    xf = x_all.astype(F32)
    normed = (xf * inverse_rms(xf) * gain_mix).astype(BF16)
    u = low_dot(normed, w_wide)
    ag, y, conv, states, keyval = mixer_forward(u, table, head_rows, taps, slot_of)

    nffn, hidden, dgu, dm_all, dag, out_part, mixed, dmixed, dgain_rows, dw_mid = middle(
        ag, wout_all, wffn_all, x_own, cot_own, cot_all, gain_ffn
    )
    du, stats = mixer_backward(dag, ag, u, table, head_rows, taps, y, conv, states, keyval, slot_of)
    dw_mid = lax.psum_scatter(dw_mid, "fsdp", scatter_dimension=0, tiled=True)
    dx, out, last, mids, small = ending(
        du, w_all, normed, x_own, dmixed, gain_mix, mixed, out_part, dw_mid, stats, dgain_rows,
        lax.axis_size("fsdp"),
    )
    cores = lax.axis_size("tensor")
    weights = (
        w_query, w_keyval, w_attn_out, w_gate_z, w_in_x, w_bc, w_step, w_ssm_out, w_ffn_gate,
        w_ffn_up, w_ffn_down,
    )
    grads = assemble(last, mids, dx, out, [w.shape[1] for w in weights])
    small = small.reshape(ctx, cores, 16, -1)
    everywhere = jnp.sum(small[:, :, 0:2] , axis=(0, 1))
    dconv_bc = jnp.sum(small[:, :, 8 : 8 + CONV, 256:512], axis=(0, 1))
    own = lax.dynamic_index_in_dim(small, t, axis=1, keepdims=False)
    dconv_x = own[:, 8 : 8 + CONV, :inner].transpose(1, 0, 2).reshape(CONV, -1)
    by_head = own[:, 12:15, :inner].reshape(ctx, 3, heads, SSM_DIM)
    dskip = jnp.sum(by_head[:, 0], axis=2).reshape(-1)
    dbias = jnp.sum(by_head[:, 1], axis=2).reshape(-1)
    ddecay = jnp.sum(by_head[:, 2], axis=2).reshape(-1)
    return (
        grads[0],
        grads[1],
        everywhere[0],
        *grads[2:9],
        dconv_x,
        dconv_bc,
        dbias,
        ddecay,
        dskip,
        grads[9],
        everywhere[1],
        *grads[10:13],
    )


def solution(mesh):
    in_specs = (
        P(("fsdp", "context"), None),
        P("fsdp", None),
        P("fsdp", None),
        P(),
        P("fsdp", "tensor"),
        P("fsdp", "tensor"),
        P("fsdp", "tensor"),
        P("fsdp", "tensor"),
        P("fsdp", "tensor"),
        P("fsdp", None),
        P("fsdp", "tensor"),
        P(None, "tensor"),
        P(),
        P("tensor"),
        P("tensor"),
        P("tensor"),
        P("fsdp", "tensor"),
        P(),
        P("fsdp", "tensor"),
        P("fsdp", "tensor"),
        P("fsdp", "tensor"),
        P(("fsdp", "context"), None),
    )
    out_specs = (
        P(("fsdp", "context"), None),
        P(("fsdp", "context"), None),
        P(),
        P("fsdp", "tensor"),
        P("fsdp", "tensor"),
        P("fsdp", "tensor"),
        P("fsdp", "tensor"),
        P("fsdp", "tensor"),
        P("fsdp", None),
        P("fsdp", "tensor"),
        P(None, "tensor"),
        P(),
        P("tensor"),
        P("tensor"),
        P("tensor"),
        P("fsdp", "tensor"),
        P(),
        P("fsdp", "tensor"),
        P("fsdp", "tensor"),
        P("fsdp", "tensor"),
    )
    return jax.shard_map(
        per_device, mesh=mesh, in_specs=in_specs, out_specs=out_specs, check_vma=False
    )
```

```python
import math

import jax
import jax.numpy as jnp
from jax import lax
from jax.experimental import pallas as pl
from jax.experimental.pallas import tpu as pltpu
from jax.sharding import PartitionSpec as P

HEAD_DIM = 64
SSM_DIM = 64
STATE = 128
CONV = 4
HALF = 256
WINDOW = 4

epsilon = 1e-05
masked = -1e30
F32 = jnp.float32
BF16 = jnp.bfloat16
exact = lax.Precision.HIGHEST


def dot(left, right, left_dim=1, right_dim=0, precision=None):
    return lax.dot_general(
        left,
        right,
        (((left_dim,), (right_dim,)), ((), ())),
        precision=precision,
        preferred_element_type=F32,
    )


def sigmoid(v):
    return 1.0 / (1.0 + jnp.exp(-v))


def softplus(v):
    return jnp.maximum(v, 0.0) + jnp.log1p(jnp.exp(-jnp.abs(v)))


def swap_halves(v):
    half = v.shape[1] // 2
    return jnp.concatenate([v[:, half:], v[:, :half]], axis=1)


def iotas(rows, columns):
    return (
        lax.broadcasted_iota(jnp.int32, (rows, columns), 0),
        lax.broadcasted_iota(jnp.int32, (rows, columns), 1),
    )


def state_scale(last_row, carry_last, heads):
    pieces = [
        jnp.broadcast_to(last_row[:, h * SSM_DIM : h * SSM_DIM + 1], (SSM_DIM, STATE))
        for h in range(heads)
    ]
    return jnp.exp(jnp.concatenate(pieces, axis=0)) * carry_last


def block_decays(step_raw, heads_ref, lane_pos, heads):
    rows = step_raw.shape[0]
    inner = heads * SSM_DIM
    raw = step_raw + heads_ref[0:1, :inner]
    step = softplus(raw)
    rate = step * jnp.exp(heads_ref[1:2, :inner])
    row, col = iotas(rows, rows)
    lower = jnp.where(col <= row, 1.0, 0.0).astype(F32)
    totals = dot(lower, -rate, precision=exact)
    last_row = totals[rows - 1 : rows]
    pos_last = lane_pos[rows - 1 : rows, 0:1]
    local = lax.broadcasted_iota(jnp.int32, (rows, 1), 0).astype(F32)
    carry_on = (lane_pos[:, 0:1] > local).astype(F32)
    keep_last = (local >= (rows - 1) - pos_last).astype(F32)
    carry_last = (pos_last > rows - 1).astype(F32)
    factor = jnp.exp(totals) * carry_on
    tails = jnp.exp(last_row - totals) * keep_last
    return raw, step, rate, totals, last_row, carry_last, factor, tails


def local_mask(lane_pos, rows):
    row, col = iotas(rows, rows)
    gap = (row - col).astype(F32)
    return (gap >= 0) & (gap <= lane_pos[:, 0:1])


def key_window(block):
    start = jnp.maximum(block - WINDOW, 0)
    return start, (block - start) * HALF


def window_mask(lane_pos, offset, rows, keys):
    row, col = iotas(rows, keys)
    gap = (row - col + offset).astype(F32)
    return (gap >= 0) & (gap <= lane_pos[:, 0:1])


def head_decay(totals, totals_t, h, allowed):
    gap = totals[:, h * SSM_DIM : h * SSM_DIM + 1] - totals_t[h * SSM_DIM : h * SSM_DIM + 1, :]
    return jnp.exp(jnp.where(allowed, gap, masked))


def mixer_forward_kernel(
    slots_ref, u_ref, table_ref, heads_ref, taps_ref, ag_ref, y_ref, conv_ref, state_in_ref, kv_ref,
    ext, state, keyval,
):
    block = pl.program_id(0)
    heads = state.shape[0] // SSM_DIM
    inner = heads * SSM_DIM
    width = ext.shape[1]
    rows = u_ref.shape[0]

    @pl.when(block == 0)
    def _():
        ext[0:8, :] = jnp.zeros((8, width), F32)
        state[...] = jnp.zeros(state.shape, F32)
        keyval[...] = jnp.zeros(keyval.shape, BF16)

    lane_pos = table_ref[:, 128:256]
    cosine = table_ref[:, 0:64]
    sine = table_ref[:, 64:128]
    q_at = inner
    u = u_ref[:, :width].astype(F32)
    ext[8 : 8 + rows, :] = u
    conv = u * taps_ref[CONV - 1 : CONV, :]
    for back in range(1, CONV):
        reach = lane_pos[:, 0:1] >= back
        shifted = ext[8 - back : 8 - back + rows, :]
        conv = conv + jnp.where(reach, shifted, 0.0) * taps_ref[CONV - 1 - back : CONV - back, :]
    ext[0:8, :] = u[rows - 8 : rows]
    act = conv * sigmoid(conv)
    ssm_x = act[:, :inner].astype(BF16)
    ssm_b = act[:, 256:384].astype(BF16)
    ssm_c = act[:, 384:512].astype(BF16)
    conv_ref[:, 0:256] = conv[:, 0:256]
    conv_ref[:, 256:512] = conv[:, 256:512]
    query = u[:, q_at : q_at + HEAD_DIM]
    query = (query * cosine + swap_halves(query) * sine).astype(BF16)
    conv_ref[:, q_at : q_at + HEAD_DIM] = query.astype(F32)
    key = u_ref[:, 512 + inner : 512 + inner + HEAD_DIM].astype(F32)
    key = key * cosine + swap_halves(key) * sine
    value = u_ref[:, 768 + inner : 768 + inner + HEAD_DIM].astype(F32)
    pair = jnp.concatenate([key, value], axis=1).astype(BF16)
    kv_ref[...] = pair
    keyval[pl.ds(pl.multiple_of(block * rows, rows), rows), :] = pair
    first, offset = key_window(block)
    span = (WINDOW + 1) * HALF
    window = keyval[pl.ds(pl.multiple_of(first * rows, rows), span), :]
    scores = dot(query * 0.125, window[:, :HEAD_DIM], 1, 1)
    scores = jnp.where(window_mask(lane_pos, offset, rows, span), scores, masked)
    highest = jnp.max(scores, axis=1, keepdims=True)
    weights = jnp.exp(scores - highest)
    total = jnp.sum(weights, axis=1, keepdims=True)
    probs = (weights * (1.0 / total)).astype(BF16)
    attended = dot(probs, window[:, HEAD_DIM:])
    _, step, _, totals, last_row, carry_last, factor, tails = block_decays(
        u_ref[:, 768 : 768 + inner].astype(F32), heads_ref, lane_pos, heads
    )
    totals_t = totals.T
    allowed = local_mask(lane_pos, rows)
    cross = dot(ssm_c, ssm_b, 1, 1)
    x_f = ssm_x.astype(F32)
    stepped = step * x_f
    stepped_low = stepped.astype(BF16)
    parts = []
    for h in range(heads):
        lanes = slice(h * SSM_DIM, (h + 1) * SSM_DIM)
        mix = (head_decay(totals, totals_t, h, allowed) * cross).astype(BF16)
        parts.append(dot(mix, stepped_low[:, lanes]))
    held = state[...]
    state_in_ref[...] = held
    y_pure = jnp.concatenate(parts, axis=1) + factor * dot(ssm_c, held.astype(BF16), 1, 1)
    tailed = (tails * stepped_low.astype(F32)).astype(BF16)
    state[...] = state_scale(last_row, carry_last, heads) * held + dot(tailed, ssm_b, 0, 0)
    y_ref[:, :inner] = y_pure
    y_ref[:, inner : inner + HEAD_DIM] = jnp.broadcast_to(
        highest + jnp.log(total), (rows, HEAD_DIM)
    )
    y_full = y_pure + heads_ref[2:3, :inner] * x_f
    gate = u_ref[:, 512 : 512 + inner].astype(F32)
    gated = y_full * (gate * sigmoid(gate))
    ag_ref[...] = jnp.concatenate([gated, attended], axis=1).astype(BF16)


def mixer_backward_kernel(
    slots_ref, dag_ref, ag_ref, u_ref, table_ref, heads_ref, taps_ref, y_ref, conv_ref, state_in_ref,
    state_out_ref, kv_ref, du_ref, stats_ref, dext, dpos, dstate, dkey_t, dvalue_t,
):
    turn = pl.program_id(0)
    blocks = pl.num_programs(0)
    block = blocks - 1 - turn
    heads = dstate.shape[0] // SSM_DIM
    inner = heads * SSM_DIM
    rows = u_ref.shape[0]
    width = dext.shape[1]

    @pl.when(turn == 0)
    def _():
        dext[rows : rows + 8, :] = jnp.zeros((8, width), F32)
        dpos[rows : rows + 8, :] = jnp.full((8, dpos.shape[1]), -1.0, F32)
        dstate[...] = jnp.zeros(dstate.shape, F32)
        dkey_t[...] = jnp.zeros(dkey_t.shape, F32)
        dvalue_t[...] = jnp.zeros(dvalue_t.shape, F32)
        stats_ref[...] = jnp.zeros(stats_ref.shape, F32)

    lane_pos = table_ref[:, 128:256]
    cosine = table_ref[:, 0:64]
    sine = table_ref[:, 64:128]
    first, offset = key_window(block)
    span = (WINDOW + 1) * HALF
    begin = pl.multiple_of(first * rows, rows)
    window = kv_ref[pl.ds(begin, span), :]
    keys = window[:, :HEAD_DIM]
    values = window[:, HEAD_DIM:]
    query = conv_ref[:, inner : inner + HEAD_DIM] * 0.125
    query_low = query.astype(BF16)
    datt = dag_ref[:, inner : inner + HEAD_DIM]
    datt_f = datt.astype(F32)
    lse = y_ref[:, inner : inner + 1]
    scores = dot(query_low, keys, 1, 1)
    allowed_all = window_mask(lane_pos, offset, rows, span)
    probs = jnp.exp(jnp.where(allowed_all, scores, masked) - lse)
    inward = jnp.sum(datt_f * ag_ref[:, inner : inner + HEAD_DIM].astype(F32), axis=1, keepdims=True)
    dscores = (probs * (dot(datt, values, 1, 1) - inward)).astype(BF16)
    dquery = dot(dscores, keys) * 0.125
    dkey_t[:, pl.ds(begin, span)] += dot(query.T.astype(BF16), dscores)
    dvalue_t[:, pl.ds(begin, span)] += dot(datt_f.T.astype(BF16), probs.astype(BF16))
    here = pl.ds(pl.multiple_of(block * rows, rows), rows)
    dkey = dkey_t[:, here].T
    dvalue = dvalue_t[:, here].T
    dquery = dquery * cosine - swap_halves(dquery) * sine
    dkey = dkey * cosine - swap_halves(dkey) * sine
    conv = conv_ref[...]
    gate_conv = sigmoid(conv)
    act = conv * gate_conv
    dact = gate_conv * (1.0 + conv * (1.0 - gate_conv))
    ssm_x = act[:, :inner].astype(BF16)
    ssm_b = act[:, 256:384].astype(BF16)
    ssm_c = act[:, 384:512].astype(BF16)
    x_f = ssm_x.astype(F32)
    raw, step, rate, totals, last_row, carry_last, factor, tails = block_decays(
        u_ref[:, 768 : 768 + inner].astype(F32), heads_ref, lane_pos, heads
    )
    totals_t = totals.T
    allowed = local_mask(lane_pos, rows)
    cross = dot(ssm_c, ssm_b, 1, 1)
    gate = u_ref[:, 512 : 512 + inner].astype(F32)
    sig = sigmoid(gate)
    y_pure = y_ref[:, :inner]
    dgated = dag_ref[:, :inner].astype(F32)
    skip = heads_ref[2:3, :inner]
    dy = dgated * (gate * sig)
    dgate = dgated * (y_pure + skip * x_f) * (sig * (1.0 + gate * (1.0 - sig)))
    dy_low = dy.astype(BF16)
    dy_r = dy_low.astype(F32)
    dy_t = dy.T.astype(BF16)
    stepped_low = (step * x_f).astype(BF16)
    stepped_r = stepped_low.astype(F32)
    tailed = (tails * stepped_r).astype(BF16)
    dcross = jnp.zeros((rows, rows), F32)
    parts = []
    for h in range(heads):
        lanes = slice(h * SSM_DIM, (h + 1) * SSM_DIM)
        decay = head_decay(totals, totals_t, h, allowed)
        mix = (decay * cross).astype(BF16)
        parts.append(dot(dy_t[lanes, :], mix))
        dcross = dcross + dot(dy_low[:, lanes], stepped_low[:, lanes], 1, 1) * decay
    dstep_x = jnp.concatenate(parts, axis=0).T
    dcross_low = dcross.astype(BF16)
    held = state_in_ref[...].astype(BF16)
    dheld = dstate[...]
    dheld_low = dheld.astype(BF16)
    dfactored = (factor * dy).astype(BF16)
    from_state = dot(ssm_b, dheld_low, 1, 1)
    dssm_c = dot(dcross_low, ssm_b) + dot(dfactored, held)
    dssm_b = dot(dcross_low, ssm_c, 0, 0) + dot(tailed, dheld_low)
    dtotals = dy_r * y_pure - stepped_r * dstep_x - tailed.astype(F32) * from_state
    dstep_x = dstep_x + tails * from_state
    end_term = dot(
        jnp.ones((8, STATE), F32), dheld_low.astype(F32) * state_out_ref[...], 1, 1, exact
    )[0:1]
    end_term = jnp.where(turn == 0, jnp.zeros_like(end_term), end_term)
    row, col = iotas(rows, rows)
    upper = jnp.where(col >= row, 1.0, 0.0).astype(F32)
    drate = -(dot(upper, dtotals, precision=exact) + end_term)
    dstate[...] = state_scale(last_row, carry_last, heads) * dheld + dot(dfactored, ssm_c, 0, 0)
    dssm_x = step * dstep_x + skip * dy
    dstep = x_f * dstep_x + jnp.exp(heads_ref[1:2, :inner]) * drate
    draw = dstep * sigmoid(raw)
    none = jnp.zeros((rows, HEAD_DIM), F32)
    dconv = jnp.concatenate([dssm_x, none, dssm_b, dssm_c], axis=1) * dact
    dext[0:rows, :] = dconv
    dpos[0:rows, :] = lane_pos
    u = u_ref[:, :width].astype(F32)
    du = dconv * taps_ref[CONV - 1 : CONV, :]
    stats_ref[CONV - 1 : CONV, :] += jnp.sum(dconv * u, axis=0, keepdims=True)
    for ahead in range(1, CONV):
        reach = dpos[ahead : ahead + rows, 0:1] >= ahead
        shifted = jnp.where(reach, dext[ahead : ahead + rows, :], 0.0)
        tap = CONV - 1 - ahead
        du = du + shifted * taps_ref[tap : tap + 1, :]
        stats_ref[tap : tap + 1, :] += jnp.sum(shifted * u, axis=0, keepdims=True)
    dext[rows : rows + 8, :] = dconv[0:8]
    dpos[rows : rows + 8, :] = lane_pos[0:8]
    stats_ref[4:5, :inner] += jnp.sum(dy * x_f, axis=0, keepdims=True)
    stats_ref[5:6, :inner] += jnp.sum(draw, axis=0, keepdims=True)
    stats_ref[6:7, :inner] += jnp.sum(drate * rate, axis=0, keepdims=True)
    summed = [
        jnp.sum(draw[:, h * SSM_DIM : (h + 1) * SSM_DIM], axis=1, keepdims=True)
        for h in range(heads)
    ]
    lane = lax.broadcasted_iota(jnp.int32, (rows, HEAD_DIM), 1)
    dstep_all = jnp.zeros((rows, HEAD_DIM), F32)
    for h in range(heads):
        dstep_all = jnp.where(lane == h, summed[h], dstep_all)
    du_ref[:, 0:256] = jnp.concatenate([du[:, :inner], dquery], axis=1).astype(BF16)
    du_ref[:, 256:512] = du[:, 256:512].astype(BF16)
    du_ref[:, 512:768] = jnp.concatenate([dgate, dkey], axis=1).astype(BF16)
    du_ref[:, 768:896] = jnp.concatenate([dvalue, dstep_all], axis=1).astype(BF16)


def mixer_forward(u, table, head_rows, taps, slot_of):
    count = u.shape[0]
    blocks = count // HALF
    heads = 3
    inner = heads * SSM_DIM
    width = taps.shape[1]
    at_slot = lambda i, slots: (slots[i], 0)
    in_order = lambda i, slots: (i, 0)
    whole = lambda i, slots: (0, 0)
    return pl.pallas_call(
        mixer_forward_kernel,
        out_shape=(
            jax.ShapeDtypeStruct((count, inner + HEAD_DIM), BF16),
            jax.ShapeDtypeStruct((count, inner + HEAD_DIM), F32),
            jax.ShapeDtypeStruct((count, width), F32),
            jax.ShapeDtypeStruct((blocks * inner, STATE), F32),
            jax.ShapeDtypeStruct((count, 2 * HEAD_DIM), BF16),
        ),
        grid_spec=pltpu.PrefetchScalarGridSpec(
            num_scalar_prefetch=1,
            grid=(blocks,),
            in_specs=[
                pl.BlockSpec((HALF, u.shape[1]), at_slot),
                pl.BlockSpec((HALF, table.shape[1]), in_order),
                pl.BlockSpec(head_rows.shape, whole),
                pl.BlockSpec(taps.shape, whole),
            ],
            out_specs=(
                pl.BlockSpec((HALF, inner + HEAD_DIM), at_slot),
                pl.BlockSpec((HALF, inner + HEAD_DIM), in_order),
                pl.BlockSpec((HALF, width), in_order),
                pl.BlockSpec((inner, STATE), in_order),
                pl.BlockSpec((HALF, 2 * HEAD_DIM), in_order),
            ),
            scratch_shapes=[
                pltpu.VMEM((8 + HALF, width), F32),
                pltpu.VMEM((inner, STATE), F32),
                pltpu.VMEM((count, 2 * HEAD_DIM), BF16),
            ],
        ),
        compiler_params=pltpu.CompilerParams(vmem_limit_bytes=48 << 20),
    )(slot_of, u, table, head_rows, taps)


def mixer_backward(dag, ag, u, table, head_rows, taps, y, conv, states, keyval, slot_of):
    count = u.shape[0]
    blocks = count // HALF
    heads = 3
    inner = heads * SSM_DIM
    width = taps.shape[1]
    last = blocks - 1
    at_slot = lambda i, slots: (slots[last - i], 0)
    in_order = lambda i, slots: (last - i, 0)
    after = lambda i, slots: (jnp.minimum(last - i + 1, last), 0)
    whole = lambda i, slots: (0, 0)
    columns = inner + HEAD_DIM
    return pl.pallas_call(
        mixer_backward_kernel,
        out_shape=(
            jax.ShapeDtypeStruct((count, 896), BF16),
            jax.ShapeDtypeStruct((8, width), F32),
        ),
        grid_spec=pltpu.PrefetchScalarGridSpec(
            num_scalar_prefetch=1,
            grid=(blocks,),
            in_specs=[
                pl.BlockSpec((HALF, columns), at_slot),
                pl.BlockSpec((HALF, columns), at_slot),
                pl.BlockSpec((HALF, u.shape[1]), at_slot),
                pl.BlockSpec((HALF, table.shape[1]), in_order),
                pl.BlockSpec(head_rows.shape, whole),
                pl.BlockSpec(taps.shape, whole),
                pl.BlockSpec((HALF, columns), in_order),
                pl.BlockSpec((HALF, width), in_order),
                pl.BlockSpec((inner, STATE), in_order),
                pl.BlockSpec((inner, STATE), after),
                pl.BlockSpec((count, 2 * HEAD_DIM), whole),
            ],
            out_specs=(
                pl.BlockSpec((HALF, 896), at_slot),
                pl.BlockSpec((8, width), whole),
            ),
            scratch_shapes=[
                pltpu.VMEM((HALF + 8, width), F32),
                pltpu.VMEM((HALF + 8, 128), F32),
                pltpu.VMEM((inner, STATE), F32),
                pltpu.VMEM((HEAD_DIM, count), F32),
                pltpu.VMEM((HEAD_DIM, count), F32),
            ],
        ),
        compiler_params=pltpu.CompilerParams(vmem_limit_bytes=56 << 20),
    )(slot_of, dag, ag, u, table, head_rows, taps, y, conv, states, states, keyval)


MESH = pl.DeviceIdType.MESH


class Place:
    def __init__(self):
        self.c = lax.axis_index("context")
        self.t = lax.axis_index("tensor")
        count = lax.axis_size("context")
        self.chips = [
            self.c,
            self.c + 1 - 2 * (self.c % 2),
            (self.c + count // 2) % count,
            count - 1 - self.c,
        ]

    def slot(self, mask, sibling=False):
        core = 1 - self.t if sibling else self.t
        return self.chips[mask] * 2 + core

    def target(self, mask):
        if mask == 4:
            return {"tensor": 1 - self.t}
        return {"context": self.chips[mask]}

    def greet(self, line=None):
        barrier = pltpu.get_barrier_semaphore()
        targets = [self.target(mask) for mask in (1, 2, 4)]
        if line is not None:
            targets += [line.target(step) for step in range(1, line.count)]
        for target in targets:
            pl.semaphore_signal(barrier, inc=1, device_id=target, device_id_type=MESH)
        pl.semaphore_wait(barrier, len(targets))


class Wire:
    def __init__(self, place, sems):
        self.place = place
        self.sems = sems
        self.sent = []

    def copy(self, source, target, index, mask):
        return pltpu.make_async_remote_copy(
            src_ref=source,
            dst_ref=target,
            send_sem=self.sems.at[0, index],
            recv_sem=self.sems.at[1, index],
            device_id=self.place.target(mask),
            device_id_type=MESH,
        )

    def send(self, source, target, index, mask):
        made = self.copy(source, target, index, mask)
        made.start()
        self.sent.append(made)

    def arrive(self, target, index, mask):
        self.copy(target, target, index, mask).wait_recv()

    def finish(self):
        for made in self.sent:
            made.wait_send()
        self.sent = []


ROWS = HALF
PART = HALF // 2
TOP, END = pl.ds(0, PART), pl.ds(PART, PART)
SCATTER_SEMS = 10
GATHER_SEMS = 14


def scatter_scratch(columns):
    return [
        pltpu.VMEM((4, ROWS, columns), BF16),
        pltpu.VMEM((4, ROWS, columns), BF16),
        pltpu.VMEM((6, PART, columns), BF16),
        pltpu.VMEM((ROWS, columns), F32),
        pltpu.SemaphoreType.DMA((2, SCATTER_SEMS)),
    ]


SCATTER_ORDER = (3, 1, 2, 0)


class Scatter:
    def __init__(self, place, scratch):
        self.place = place
        self.core_in, self.out, self.chip_in, self.kept, sems = scratch
        self.wire = Wire(place, sems)

    def to_core(self, mask, source):
        index = SCATTER_ORDER.index(mask)
        self.wire.send(source, self.core_in.at[index], index, 4)

    def from_core(self, mask):
        index = SCATTER_ORDER.index(mask)
        self.wire.arrive(self.core_in.at[index], index, 4)
        return self.core_in[index].astype(F32)

    def first(self, mine, total, between=None):
        wire, out, kept = self.wire, self.out, self.kept
        both = mine(3) + self.from_core(3)
        out[0] = both.astype(BF16)
        wire.send(out.at[0, TOP], self.chip_in.at[0], 4, 1)
        wire.send(out.at[0, END], self.chip_in.at[1], 5, 2)
        both = mine(1) + self.from_core(1)
        out[1] = both.astype(BF16)
        wire.send(out.at[1, TOP], self.chip_in.at[2], 6, 1)
        kept[END] = both[PART:]
        both = mine(2) + self.from_core(2)
        out[2] = both.astype(BF16)
        wire.send(out.at[2, END], self.chip_in.at[3], 7, 2)
        kept[TOP] = both[:PART]
        total[...] = mine(0) + self.from_core(0)

    def second(self):
        wire, out, kept, came = self.wire, self.out, self.kept, self.chip_in
        wire.arrive(came.at[0], 4, 1)
        out[3, TOP] = (kept[TOP] + came[0].astype(F32)).astype(BF16)
        wire.send(out.at[3, TOP], came.at[4], 8, 2)
        wire.arrive(came.at[1], 5, 2)
        out[3, END] = (kept[END] + came[1].astype(F32)).astype(BF16)
        wire.send(out.at[3, END], came.at[5], 9, 1)

    def last(self, total):
        wire, came = self.wire, self.chip_in
        wire.arrive(came.at[2], 6, 1)
        wire.arrive(came.at[4], 8, 2)
        total[TOP] += came[2].astype(F32) + came[4].astype(F32)
        wire.arrive(came.at[3], 7, 2)
        wire.arrive(came.at[5], 9, 1)
        total[END] += came[3].astype(F32) + came[5].astype(F32)
        wire.finish()


class Gather:
    def __init__(self, place, whole, sems, rows=ROWS, cores=True):
        self.place = place
        self.whole = whole
        self.size = rows
        self.cores = cores
        self.wire = Wire(place, sems)

    def rows(self, mask, sibling=False, half=None):
        place, size = self.place, self.size
        block = place.slot(mask, sibling) if self.cores else place.chips[mask]
        begin = block * size
        if half is None:
            return self.whole.at[pl.ds(pl.multiple_of(begin, size), size)]
        return self.whole.at[pl.ds(pl.multiple_of(begin + half * (size // 2), size // 2), size // 2)]

    def start(self, core=True):
        wire = self.wire
        for half, mask, index in ((0, 1, 0), (1, 2, 1), (1, 1, 2), (0, 2, 3)):
            wire.send(self.rows(0, half=half), self.rows(0, half=half), index, mask)
        if self.cores and core:
            wire.send(self.rows(0), self.rows(0), 6, 4)

    def relay(self):
        wire = self.wire
        wire.arrive(self.rows(1, half=0), 0, 1)
        wire.send(self.rows(1, half=0), self.rows(1, half=0), 4, 2)
        wire.arrive(self.rows(2, half=1), 1, 2)
        wire.send(self.rows(2, half=1), self.rows(2, half=1), 5, 1)

    def near(self):
        wire = self.wire
        wire.arrive(self.rows(1, half=1), 2, 1)
        if self.cores:
            wire.send(self.rows(1), self.rows(1), 7, 4)
        wire.arrive(self.rows(2, half=0), 3, 2)
        if self.cores:
            wire.send(self.rows(2), self.rows(2), 8, 4)

    def far(self):
        wire = self.wire
        wire.arrive(self.rows(3, half=0), 4, 2)
        wire.arrive(self.rows(3, half=1), 5, 1)
        if self.cores:
            wire.send(self.rows(3), self.rows(3), 9, 4)

    def core(self, mask):
        index = (6, 7, 8, 9)[mask]
        self.wire.arrive(self.rows(mask, sibling=True), index, 4)

    def finish(self):
        self.wire.finish()


class Line:
    def __init__(self):
        self.f = lax.axis_index("fsdp")
        self.count = lax.axis_size("fsdp")

    def target(self, step):
        return {"fsdp": (self.f + step) % self.count}

    def copy(self, source, target, sems, step):
        return pltpu.make_async_remote_copy(
            src_ref=source,
            dst_ref=target,
            send_sem=sems.at[0, step],
            recv_sem=sems.at[1, step],
            device_id=self.target(step),
            device_id_type=MESH,
        )


class LineGather:
    def __init__(self, line, whole, sems):
        self.line = line
        self.whole = whole
        self.sems = sems
        self.size = whole.shape[0] // line.count

    def rows(self, block):
        return self.whole.at[pl.ds(pl.multiple_of(block * self.size, self.size), self.size)]

    def copy(self, block, way, step):
        toward = self.line.f + 1 if way == 0 else self.line.f - 1
        return pltpu.make_async_remote_copy(
            src_ref=self.rows(block),
            dst_ref=self.rows(block),
            send_sem=self.sems.at[way, 0, step],
            recv_sem=self.sems.at[way, 1, step],
            device_id={"fsdp": toward},
            device_id_type=MESH,
        )

    def step(self, number, arrive=True):
        f, last = self.line.f, self.line.count - 1
        for way in (0, 1):
            block = f - number if way == 0 else f + number
            there = block >= 0 if way == 0 else block <= last
            goes_on = f < last if way == 0 else f > 0

            @pl.when(there)
            def _():
                if number > 0:
                    self.copy(block, way, number).wait_recv()

                @pl.when(goes_on)
                def _():
                    self.copy(block, way, number + 1).start()

    def finish(self):
        f, last = self.line.f, self.line.count - 1
        for number in range(self.line.count - 1):
            for way in (0, 1):
                block = f - number if way == 0 else f + number
                there = block >= 0 if way == 0 else block <= last
                goes_on = f < last if way == 0 else f > 0

                @pl.when(there & goes_on)
                def _():
                    self.copy(block, way, number + 1).wait_send()


def line_sems(count):
    return pltpu.SemaphoreType.DMA((2, 2, count + 1))


def opening_kernel(
    tokens_ref, cot_ref, in_x_ref, query_ref, bc_ref, gate_ref, keyval_ref, step_ref, ssm_ref, attn_ref,
    gain_ref, segments_ref,
    normed_ref, u_ref, w_ref, wout_ref, cot_all_ref, table_ref,
    x_all, wide, x_sems, cot_sems, w_sems, out_sems,
):
    place = Place()
    line = Line()
    rows_x = Gather(place, x_all, x_sems)
    rows_cot = Gather(place, cot_all_ref, cot_sems)
    weights = LineGather(line, w_ref, w_sems)
    weights_out = LineGather(line, wout_ref, out_sems)
    chips = lax.axis_size("context")
    share = in_x_ref.shape[0]
    heads = step_ref.shape[1] // chips
    inner = heads * SSM_DIM
    chip_rows = pl.ds(pl.multiple_of(place.c * 2 * ROWS, 2 * ROWS), 2 * ROWS)
    place.greet(line)
    x_all[chip_rows, :] = tokens_ref[...]
    rows_x.start(core=False)
    mine = pl.ds(pl.multiple_of(line.f * share, share), share)
    for k in range(chips):

        @pl.when(place.c == k)
        def _():
            inner_part = slice(k * inner, (k + 1) * inner)
            head_part = slice(k * HEAD_DIM, (k + 1) * HEAD_DIM)
            w_ref[mine, 0:256] = jnp.concatenate(
                [in_x_ref[:, inner_part], query_ref[:, head_part]], axis=1
            )
            w_ref[mine, 512:768] = jnp.concatenate(
                [gate_ref[:, inner_part], keyval_ref[:, :HEAD_DIM]], axis=1
            )
            none = jnp.zeros((share, HEAD_DIM - heads), F32)
            steps = step_ref[:, k * heads : (k + 1) * heads].astype(F32)
            w_ref[mine, 768:896] = jnp.concatenate(
                [keyval_ref[:, HEAD_DIM:].astype(F32), steps, none], axis=1
            ).astype(BF16)
            wout_ref[mine, :] = jnp.concatenate(
                [ssm_ref[:, inner_part], attn_ref[:, head_part]], axis=1
            )

    w_ref[mine, 256:512] = bc_ref[...]
    weights.step(0)

    def norm(slot):
        rows = slot_rows(slot)
        x = x_all[rows, :].astype(F32)
        normed_ref[rows, :] = (x * norm_scale(x) * gain_ref[...]).astype(BF16)

    cot_all_ref[chip_rows, :] = cot_ref[...]
    norm(place.slot(0))
    norm(place.slot(0, True))
    rows_x.relay()
    rows_cot.start(core=False)
    weights.step(1)

    numbers = segments_ref[...]
    bounds = [
        jnp.sum(jnp.where(numbers < k, 1.0, 0.0), axis=1, keepdims=True) for k in (1, 2)
    ]
    count = table_ref.shape[0]
    lane = lax.broadcasted_iota(jnp.int32, (8, 128), 1)[0:1]
    power = -(lane % (HEAD_DIM // 2)).astype(F32) / (HEAD_DIM // 2)
    freqs = jnp.exp(power * math.log(10000.0))
    phase = jnp.where(lane < HEAD_DIM, math.pi / 2, 0.0)
    sign = jnp.where((lane >= HEAD_DIM) & (lane < HEAD_DIM + HEAD_DIM // 2), -1.0, 1.0)

    def angles(block, carry):
        row = lax.broadcasted_iota(jnp.int32, (ROWS, 128), 0) + block * ROWS
        row = row.astype(F32)
        start = jnp.where(row >= bounds[0], bounds[0], 0.0)
        start = jnp.where(row >= bounds[1], bounds[1], start)
        pos = row - start
        here = slot_rows(block)
        table_ref[here, 0:128] = jnp.sin(pos * freqs + phase) * sign
        table_ref[here, 128:256] = pos
        return carry

    lax.fori_loop(0, count // ROWS, angles, 0)
    rows_x.near()
    norm(place.slot(1))
    norm(place.slot(2))
    rows_x.far()
    norm(place.slot(3))
    rows_cot.relay()
    for mask in (1, 2, 3):
        rows_x.core(mask)
        norm(place.slot(mask, True))
    for number in range(2, line.count):
        weights.step(number)
    weights_out.step(0)
    rows_cot.near()
    wide[:, 0:768] = w_ref[:, 0:768]
    row, column = iotas(HEAD_DIM, inner)
    copies = jnp.where(column // SSM_DIM == row, 1.0, 0.0).astype(BF16)
    wide[:, 768:1024] = jnp.concatenate(
        [dot(w_ref[:, 896 - HEAD_DIM : 896], copies), w_ref[:, 768 : 768 + HEAD_DIM].astype(F32)],
        axis=1,
    ).astype(BF16)

    def project(slot, carry):
        rows = slot_rows(slot)
        u_ref[rows, :] = dot(normed_ref[rows, :], wide[...])
        return carry

    lax.fori_loop(0, 4, project, 0)
    weights_out.step(1)
    rows_cot.far()
    lax.fori_loop(4, 8, project, 0)
    for number in range(2, line.count):
        weights_out.step(number)
    for mask in (1, 2, 3):
        rows_cot.core(mask)
    rows_x.finish()
    rows_cot.finish()
    weights.finish()
    weights_out.finish()


def opening(tokens, cotangent, weights, gain, segments):
    fsdp = lax.axis_size("fsdp")
    model = tokens.shape[1]
    count = segments.shape[1]
    vmem = pl.BlockSpec(memory_space=pltpu.VMEM)
    shape = jax.ShapeDtypeStruct
    dma = pltpu.SemaphoreType.DMA
    return pl.pallas_call(
        opening_kernel,
        out_shape=(
            shape((count, model), BF16),
            shape((count, 1024), F32),
            shape((model, 896), BF16),
            shape((model, 256), BF16),
            shape((count, model), BF16),
            shape((count, 256), F32),
        ),
        in_specs=[vmem] * 12,
        out_specs=(vmem,) * 6,
        scratch_shapes=[
            pltpu.VMEM((count, model), BF16),
            pltpu.VMEM((model, 1024), BF16),
            dma((2, GATHER_SEMS)),
            dma((2, GATHER_SEMS)),
            line_sems(fsdp),
            line_sems(fsdp),
        ],
        compiler_params=pltpu.CompilerParams(
            collective_id=3, has_side_effects=True, vmem_limit_bytes=60 << 20
        ),
        cost_estimate=pl.CostEstimate(
            flops=2 * count * model * 1024, bytes_accessed=30 << 20, transcendentals=count * 128
        ),
    )(tokens, cotangent, *weights, gain.reshape(1, -1), segments)


def slot_rows(slot):
    return pl.ds(pl.multiple_of(slot * ROWS, ROWS), ROWS)


def norm_scale(values):
    return lax.rsqrt(jnp.mean(values * values, axis=1, keepdims=True) + epsilon)


def middle_kernel(
    ag_ref, wout_ref, gate_ref, up_ref, down_ref, x_ref, cot_ref, cot_all_ref, gain_ref,
    nffn_ref, hidden_ref, dgu_ref, dm_ref, dag_ref, outp_ref, mixed_ref, dmixed_ref, dgain_ref, dw_ref,
    part, wffn_ref, *scratch,
):
    place = Place()
    first = Scatter(place, scratch[0:5])
    back = Scatter(place, scratch[5:10])
    forth = Gather(place, nffn_ref, scratch[10])
    home = Gather(place, dm_ref, scratch[11])
    hid = hidden_ref.shape[1]
    line = Line()
    weights = LineGather(line, wffn_ref, scratch[12])
    share = gate_ref.shape[0]
    place.greet(line)
    mine = pl.ds(pl.multiple_of(line.f * share, share), share)
    lanes = pl.ds(pl.multiple_of(place.c * hid, hid), hid)
    for k, source in enumerate((gate_ref, up_ref, down_ref)):
        wffn_ref[mine, k * hid : (k + 1) * hid] = source[:, lanes]
    weights.step(0)

    def block(mask, sibling=False):
        return dot(ag_ref[slot_rows(place.slot(mask, sibling)), :], wout_ref[...], 1, 1)

    for mask in SCATTER_ORDER:
        rows = slot_rows(place.slot(mask, True))
        part[rows, :] = block(mask, True).astype(BF16)
        first.to_core(mask, part.at[rows])
    first.first(block, mixed_ref)
    weights.step(1)
    first.second()
    mixed_ref[...] += x_ref[...].astype(F32)
    first.last(mixed_ref)
    mixed = mixed_ref[...]
    gain = gain_ref[...]
    scale = norm_scale(mixed)
    own = slot_rows(place.slot(0))
    nffn_ref[own, :] = (mixed * scale * gain).astype(BF16)
    forth.start()
    for number in range(2, line.count):
        weights.step(number)

    def work(slot):
        rows = slot_rows(slot)
        normed = nffn_ref[rows, :]
        gate_up = dot(normed, wffn_ref[:, : 2 * hid])
        dhidden = dot(cot_all_ref[rows, :], wffn_ref[:, 2 * hid :]).astype(BF16).astype(F32)
        gate, up = gate_up[:, :hid], gate_up[:, hid:]
        sig = sigmoid(gate)
        silu = gate * sig
        dgate = dhidden * up * (sig * (1.0 + gate * (1.0 - sig)))
        hidden_ref[rows, :] = (silu * up).astype(BF16)
        dgu_ref[rows, :hid] = dgate.astype(BF16)
        dgu_ref[rows, hid:] = (dhidden * silu).astype(BF16)
        part[rows, :] = dot(dgu_ref[rows, :], wffn_ref[:, : 2 * hid], 1, 1).astype(BF16)

    def hand_over(mask):
        slot = place.slot(mask, True)
        work(slot)
        back.to_core(mask, part.at[slot_rows(slot)])

    work(place.slot(0))
    forth.relay()
    forth.core(0)
    hand_over(0)
    forth.near()
    forth.core(1)
    hand_over(1)
    forth.core(2)
    hand_over(2)
    work(place.slot(1))
    forth.far()
    work(place.slot(2))
    forth.core(3)
    hand_over(3)
    work(place.slot(3))
    forth.finish()

    def ready(mask):
        return part[slot_rows(place.slot(mask)), :].astype(F32)

    back.first(ready, dmixed_ref)

    def out_block(slot, carry):
        rows = slot_rows(slot)
        outp_ref[rows, :] = dot(hidden_ref[rows, :], wffn_ref[:, 2 * hid :], 1, 1).astype(BF16)
        return carry

    lax.fori_loop(0, 8, out_block, 0)
    back.second()
    dw_ref[:, : 2 * hid] = dot(nffn_ref[...], dgu_ref[...], 0, 0).astype(BF16)
    back.last(dmixed_ref)
    dnffn = dmixed_ref[...]
    mixed = mixed_ref[...]
    scale = norm_scale(mixed)
    spread = dnffn * gain
    pull = jnp.mean(spread * mixed, axis=1, keepdims=True)
    dgain_ref[...] = jnp.broadcast_to(
        jnp.sum(dnffn * mixed * scale, axis=0, keepdims=True), dgain_ref.shape
    )
    dmixed = cot_ref[...].astype(F32) + scale * (spread - mixed * (scale * scale * pull))
    dmixed_ref[...] = dmixed
    dm_ref[own, :] = dmixed.astype(BF16)
    home.start()

    def pull_back(slot):
        rows = slot_rows(slot)
        dag_ref[rows, :] = dot(dm_ref[rows, :], wout_ref[...]).astype(BF16)

    pull_back(place.slot(0))
    home.relay()
    dw_ref[:, 2 * hid : 3 * hid] = dot(cot_all_ref[...], hidden_ref[...], 0, 0).astype(BF16)
    home.core(0)
    pull_back(place.slot(0, True))
    home.near()
    pull_back(place.slot(1))
    pull_back(place.slot(2))
    home.far()
    pull_back(place.slot(3))
    for mask in (1, 2, 3):
        home.core(mask)
        pull_back(place.slot(mask, True))
    dw_ref[:, 3 * hid :] = dot(dm_ref[...], ag_ref[...], 0, 0).astype(BF16)
    home.finish()
    weights.finish()


def middle(ag, wout, weights, x_own, cot_own, cot_all, gain):
    count, model = cot_all.shape
    hid = weights[0].shape[1] // lax.axis_size("context")
    columns = ag.shape[1]
    vmem = pl.BlockSpec(memory_space=pltpu.VMEM)
    shape = jax.ShapeDtypeStruct
    return pl.pallas_call(
        middle_kernel,
        out_shape=(
            shape((count, model), BF16),
            shape((count, hid), BF16),
            shape((count, 2 * hid), BF16),
            shape((count, model), BF16),
            shape((count, columns), BF16),
            shape((count, model), BF16),
            shape((ROWS, model), F32),
            shape((ROWS, model), F32),
            shape((8, model), F32),
            shape((model, 3 * hid + columns), BF16),
        ),
        in_specs=[vmem] * 9,
        out_specs=(vmem,) * 10,
        scratch_shapes=[pltpu.VMEM((count, model), BF16), pltpu.VMEM((model, 3 * hid), BF16)]
        + scatter_scratch(model)
        + scatter_scratch(model)
        + [pltpu.SemaphoreType.DMA((2, GATHER_SEMS))] * 2
        + [line_sems(lax.axis_size("fsdp"))],
        compiler_params=pltpu.CompilerParams(
            collective_id=1, has_side_effects=True, vmem_limit_bytes=60 << 20
        ),
        cost_estimate=pl.CostEstimate(
            flops=20 * count * model * hid, bytes_accessed=40 << 20, transcendentals=count * hid
        ),
    )(ag, wout, *weights, x_own, cot_own, cot_all, gain.reshape(1, -1))


def ending_kernel(
    du_ref, w_ref, normed_ref, x_ref, dmixed_ref, gain_ref, mixed_ref, outp_ref, mid_ref, stats_ref,
    dgain_ref,
    grad_ref, out_ref, last_ref, mids_ref, small_ref,
    total, part, dw, arrived, bc_out, bc_in, small_in, *scratch,
):
    place = Place()
    line = Line()
    back = Scatter(place, scratch[0:5])
    final = Scatter(place, scratch[5:10])
    share = mid_ref.shape[0]
    last_all = Gather(place, last_ref, scratch[10], share, False)
    mid_all = Gather(place, mids_ref, scratch[11], share, False)
    small_rows = small_in.shape[1]
    small_all = Gather(place, small_ref, scratch[12], small_rows)
    line_sems, small_sems, pair_sems = scratch[13], scratch[14], scratch[15]
    pair = Wire(place, pair_sems)
    place.greet(line)
    sent = []

    chunk = dw.shape[0] // 4
    for k in range(4):
        dw[k * chunk : (k + 1) * chunk, :] = dot(
            normed_ref[:, k * chunk : (k + 1) * chunk], du_ref[...], 0, 0
        ).astype(BF16)
    for step in range(1, line.count):
        rows = pl.ds(pl.multiple_of((line.f + step) % line.count * share, share), share)
        made = line.copy(dw.at[rows], arrived.at[step], line_sems, step)
        made.start()
        sent.append(made)

    def block(mask, sibling=False):
        return dot(du_ref[slot_rows(place.slot(mask, sibling)), :], w_ref[...], 1, 1)

    for mask in SCATTER_ORDER:
        rows = slot_rows(place.slot(mask, True))
        part[rows, :] = block(mask, True).astype(BF16)
        back.to_core(mask, part.at[rows])
    back.first(block, total)
    mids_ref[pl.ds(pl.multiple_of(place.c * share, share), share), :] = mid_ref[...]
    mid_all.start()
    for mask in SCATTER_ORDER:
        final.to_core(mask, outp_ref.at[slot_rows(place.slot(mask, True))])
    back.second()
    mid_all.relay()
    back.last(total)
    dnormed = total[...]
    x = x_ref[...].astype(F32)
    gain = gain_ref[...]
    scale = norm_scale(x)
    spread = dnormed * gain
    pull = jnp.mean(spread * x, axis=1, keepdims=True)
    grad = dmixed_ref[...] + scale * (spread - x * (scale * scale * pull))
    half = pl.ds(pl.multiple_of(place.t * ROWS, ROWS), ROWS)
    grad_ref[half, :] = grad.astype(BF16)
    pair.send(grad_ref.at[half], grad_ref.at[half], 0, 4)
    small_in[0] = jnp.zeros(small_in.shape[1:], F32)
    small_in[0, 0:1, :] = jnp.sum(dnormed * x * scale, axis=0, keepdims=True)
    small_in[0, 1:2, :] = dgain_ref[0:1, :]
    small_in[0, 8:16, : stats_ref.shape[1]] = stats_ref[...]
    for step in range(1, line.count):
        made = line.copy(small_in.at[0], small_in.at[step], small_sems, step)
        made.start()
        sent.append(made)

    def ready(mask):
        return outp_ref[slot_rows(place.slot(mask)), :].astype(F32)

    final.first(ready, total)
    mid_all.near()
    final.second()
    total[...] += mixed_ref[...]
    mid_all.far()
    final.last(total)
    out_ref[half, :] = total[...].astype(BF16)
    pair.send(out_ref.at[half], out_ref.at[half], 1, 4)

    for step in range(1, line.count):
        line.copy(small_in.at[0], small_in.at[step], small_sems, step).wait_recv()
    summed = small_in[line.f % line.count]
    for other in range(1, line.count):
        summed = summed + small_in[(line.f + line.count - other) % line.count]
    mine = pl.ds(pl.multiple_of(place.slot(0) * small_rows, small_rows), small_rows)
    small_ref[mine, :] = summed
    small_all.start()

    own = pl.ds(pl.multiple_of(line.f * share, share), share)
    for step in range(1, line.count):
        line.copy(arrived.at[step], arrived.at[step], line_sems, step).wait_recv()
    sums = dw[own, :].astype(F32)
    for step in range(1, line.count):
        sums = sums + arrived[step].astype(F32)
    here = pl.ds(pl.multiple_of(place.c * share, share), share)
    bc_out[...] = sums[:, 256:512].astype(BF16)
    pair.send(bc_out, bc_in, 2, 4)
    last_ref[here, 0:256] = sums[:, 0:256].astype(BF16)
    last_ref[here, 512:] = sums[:, 512:].astype(BF16)
    small_all.relay()
    pair.arrive(bc_in, 2, 4)
    last_ref[here, 256:512] = (bc_out[...].astype(F32) + bc_in[...].astype(F32)).astype(BF16)
    last_all.start()
    small_all.near()
    last_all.relay()
    small_all.far()
    last_all.near()
    last_all.far()
    for mask in range(4):
        small_all.core(mask)
    other = pl.ds(pl.multiple_of((1 - place.t) * ROWS, ROWS), ROWS)
    pair.arrive(grad_ref.at[other], 0, 4)
    pair.arrive(out_ref.at[other], 1, 4)
    for made in sent:
        made.wait_send()
    pair.finish()
    mid_all.finish()
    small_all.finish()
    last_all.finish()


def ending(du, w, normed, x_own, dmixed, gain, mixed, outp, mid, stats, dgain, fsdp):
    count, model = normed.shape
    share = mid.shape[0]
    columns = w.shape[1]
    chips = lax.axis_size("context")
    vmem = pl.BlockSpec(memory_space=pltpu.VMEM)
    shape = jax.ShapeDtypeStruct
    dma = pltpu.SemaphoreType.DMA
    return pl.pallas_call(
        ending_kernel,
        out_shape=(
            shape((2 * ROWS, model), BF16),
            shape((2 * ROWS, model), BF16),
            shape((chips * share, columns), BF16),
            shape((chips * share, mid.shape[1]), BF16),
            shape((2 * chips * 16, model), F32),
        ),
        in_specs=[vmem] * 11,
        out_specs=(vmem,) * 5,
        scratch_shapes=[
            pltpu.VMEM((ROWS, model), F32),
            pltpu.VMEM((count, model), BF16),
            pltpu.VMEM((model, columns), BF16),
            pltpu.VMEM((fsdp, share, columns), BF16),
            pltpu.VMEM((share, 256), BF16),
            pltpu.VMEM((share, 256), BF16),
            pltpu.VMEM((fsdp, 16, model), F32),
        ]
        + scatter_scratch(model)
        + scatter_scratch(model)
        + [dma((2, GATHER_SEMS))] * 3
        + [dma((2, fsdp)), dma((2, fsdp)), dma((2, 3))],
        compiler_params=pltpu.CompilerParams(
            collective_id=2, has_side_effects=True, vmem_limit_bytes=60 << 20
        ),
        cost_estimate=pl.CostEstimate(
            flops=4 * count * model * columns, bytes_accessed=30 << 20, transcendentals=0
        ),
    )(du, w, normed, x_own, dmixed, gain.reshape(1, -1), mixed, outp, mid, stats, dgain)


def assemble_kernel(
    last_ref, mid_ref, dx_ref, out_in_ref,
    out_ref, grad_ref, query_ref, keyval_ref, attn_ref, gate_ref, x_ref, bc_ref, step_ref, ssm_ref,
    ffn_gate_ref, ffn_up_ref, ffn_down_ref,
):
    chips = last_ref.shape[0]
    heads = step_ref.shape[1] // chips
    inner = heads * SSM_DIM
    hid = ffn_gate_ref.shape[1] // chips

    def spread(source, begin, width):
        return jnp.concatenate(
            [source[k, :, begin : begin + width].astype(F32) for k in range(chips)], axis=1
        )

    def summed(begin, end):
        total = last_ref[0, :, begin:end].astype(F32)
        for k in range(1, chips):
            total = total + last_ref[k, :, begin:end].astype(F32)
        return total

    out_ref[...] = out_in_ref[...]
    grad_ref[...] = dx_ref[...]
    x_ref[...] = spread(last_ref, 0, inner)
    query_ref[...] = spread(last_ref, inner, HEAD_DIM)
    bc_ref[...] = summed(256, 512)
    gate_ref[...] = spread(last_ref, 512, inner)
    both = summed(640, 896)
    keyval_ref[...] = both[:, HEAD_DIM : 3 * HEAD_DIM]
    step_ref[...] = spread(last_ref, 896 - HEAD_DIM, heads)
    ffn_gate_ref[...] = spread(mid_ref, 0, hid)
    ffn_up_ref[...] = spread(mid_ref, hid, hid)
    ffn_down_ref[...] = spread(mid_ref, 2 * hid, hid)
    ssm_ref[...] = spread(mid_ref, 3 * hid, inner)
    attn_ref[...] = spread(mid_ref, 3 * hid + inner, HEAD_DIM)


def assemble(last, mid, dx, out, widths):
    chips = lax.axis_size("context")
    share = last.shape[0] // chips
    turns = 2
    rows = share // turns
    shape = jax.ShapeDtypeStruct
    block = lambda height, width: pl.BlockSpec((height, width), lambda i: (i, 0))
    slab = lambda width: pl.BlockSpec((chips, rows, width), lambda i: (0, i, 0))
    token_rows = dx.shape[0] // turns
    model = dx.shape[1]
    return pl.pallas_call(
        assemble_kernel,
        grid=(turns,),
        out_shape=(shape(out.shape, BF16), shape(dx.shape, BF16))
        + tuple(shape((share, width), F32) for width in widths),
        in_specs=[
            slab(last.shape[1]), slab(mid.shape[1]), block(token_rows, model),
            block(token_rows, model),
        ],
        out_specs=(block(token_rows, model), block(token_rows, model))
        + tuple(block(rows, width) for width in widths),
        compiler_params=pltpu.CompilerParams(vmem_limit_bytes=40 << 20),
    )(last.reshape(chips, share, -1), mid.reshape(chips, share, -1), dx, out)


def per_device(
    tokens, segments, deal, gain_mix, w_query, w_keyval, w_attn_out, w_gate_z, w_in_x, w_bc, w_step,
    conv_x, conv_bc, step_bias, decay_log, skip, w_ssm_out, gain_ffn, w_ffn_gate, w_ffn_up,
    w_ffn_down, cotangent,
):
    ctx = lax.axis_size("context")
    c = lax.axis_index("context")
    t = lax.axis_index("tensor")
    heads = skip.shape[0] // ctx
    inner = heads * SSM_DIM
    qd = w_query.shape[1] // ctx

    def part(array, width):
        return lax.dynamic_slice_in_dim(array, c * width, width, axis=1)

    order = deal[0]
    ids = jnp.arange(order.shape[0], dtype=jnp.int32)
    slot_of = jnp.sum(jnp.where(order[None, :] == ids[:, None], ids[None, :], 0), axis=1)

    def lanes(values):
        return jnp.repeat(lax.dynamic_slice_in_dim(values, c * heads, heads), SSM_DIM)

    head_rows = jnp.zeros((8, 256), F32)
    head_rows = head_rows.at[0, :inner].set(lanes(step_bias))
    head_rows = head_rows.at[1, :inner].set(lanes(decay_log))
    head_rows = head_rows.at[2, :inner].set(lanes(skip))
    taps = jnp.concatenate(
        [part(conv_x, inner), jnp.zeros((CONV, qd), F32), conv_bc], axis=1
    )

    row_count = tokens.shape[0]
    half = row_count // 2
    x_own = lax.dynamic_slice_in_dim(tokens, t * half, half, axis=0)
    cot_own = lax.dynamic_slice_in_dim(cotangent, t * half, half, axis=0)

    normed, u, w_all, wout_all, cot_all, table = opening(
        tokens,
        cotangent,
        (w_in_x, w_query, w_bc, w_gate_z, w_keyval, w_step, w_ssm_out, w_attn_out),
        gain_mix,
        segments,
    )
    ag, y, conv, states, keyval = mixer_forward(u, table, head_rows, taps, slot_of)

    nffn, hidden, dgu, dm_all, dag, out_part, mixed, dmixed, dgain_rows, dw_mid = middle(
        ag, wout_all, (w_ffn_gate, w_ffn_up, w_ffn_down), x_own, cot_own, cot_all, gain_ffn
    )
    du, stats = mixer_backward(dag, ag, u, table, head_rows, taps, y, conv, states, keyval, slot_of)
    dw_mid = lax.psum_scatter(dw_mid, "fsdp", scatter_dimension=0, tiled=True)
    dx, out, last, mids, small = ending(
        du, w_all, normed, x_own, dmixed, gain_mix, mixed, out_part, dw_mid, stats, dgain_rows,
        lax.axis_size("fsdp"),
    )
    cores = lax.axis_size("tensor")
    weights = (
        w_query, w_keyval, w_attn_out, w_gate_z, w_in_x, w_bc, w_step, w_ssm_out, w_ffn_gate,
        w_ffn_up, w_ffn_down,
    )
    grads = assemble(last, mids, dx, out, [w.shape[1] for w in weights])
    small = small.reshape(ctx, cores, 16, -1)
    everywhere = jnp.sum(small[:, :, 0:2] , axis=(0, 1))
    dconv_bc = jnp.sum(small[:, :, 8 : 8 + CONV, 256:512], axis=(0, 1))
    own = lax.dynamic_index_in_dim(small, t, axis=1, keepdims=False)
    dconv_x = own[:, 8 : 8 + CONV, :inner].transpose(1, 0, 2).reshape(CONV, -1)
    by_head = own[:, 12:15, :inner].reshape(ctx, 3, heads, SSM_DIM)
    dskip = jnp.sum(by_head[:, 0], axis=2).reshape(-1)
    dbias = jnp.sum(by_head[:, 1], axis=2).reshape(-1)
    ddecay = jnp.sum(by_head[:, 2], axis=2).reshape(-1)
    return (
        grads[0],
        grads[1],
        everywhere[0],
        *grads[2:9],
        dconv_x,
        dconv_bc,
        dbias,
        ddecay,
        dskip,
        grads[9],
        everywhere[1],
        *grads[10:13],
    )


def solution(mesh):
    in_specs = (
        P(("fsdp", "context"), None),
        P("fsdp", None),
        P("fsdp", None),
        P(),
        P("fsdp", "tensor"),
        P("fsdp", "tensor"),
        P("fsdp", "tensor"),
        P("fsdp", "tensor"),
        P("fsdp", "tensor"),
        P("fsdp", None),
        P("fsdp", "tensor"),
        P(None, "tensor"),
        P(),
        P("tensor"),
        P("tensor"),
        P("tensor"),
        P("fsdp", "tensor"),
        P(),
        P("fsdp", "tensor"),
        P("fsdp", "tensor"),
        P("fsdp", "tensor"),
        P(("fsdp", "context"), None),
    )
    out_specs = (
        P(("fsdp", "context"), None),
        P(("fsdp", "context"), None),
        P(),
        P("fsdp", "tensor"),
        P("fsdp", "tensor"),
        P("fsdp", "tensor"),
        P("fsdp", "tensor"),
        P("fsdp", "tensor"),
        P("fsdp", None),
        P("fsdp", "tensor"),
        P(None, "tensor"),
        P(),
        P("tensor"),
        P("tensor"),
        P("tensor"),
        P("fsdp", "tensor"),
        P(),
        P("fsdp", "tensor"),
        P("fsdp", "tensor"),
        P("fsdp", "tensor"),
    )
    return jax.shard_map(
        per_device, mesh=mesh, in_specs=in_specs, out_specs=out_specs, check_vma=False
    )
```

```python
import functools
import math

import jax
import jax.numpy as jnp
from jax import lax
from jax.experimental import pallas as pl
from jax.experimental.pallas import tpu as pltpu
from jax.sharding import PartitionSpec as P

HEAD_DIM = 64
SSM_DIM = 64
STATE = 128
CONV = 4
HALF = 256
WINDOW = 4

epsilon = 1e-05
masked = -1e30
F32 = jnp.float32
BF16 = jnp.bfloat16
exact = lax.Precision.HIGHEST


def dot(left, right, left_dim=1, right_dim=0, precision=None):
    return lax.dot_general(
        left,
        right,
        (((left_dim,), (right_dim,)), ((), ())),
        precision=precision,
        preferred_element_type=F32,
    )


def sigmoid(v):
    return 1.0 / (1.0 + jnp.exp(-v))


def softplus(v):
    return jnp.maximum(v, 0.0) + jnp.log1p(jnp.exp(-jnp.abs(v)))


def swap_halves(v):
    half = v.shape[1] // 2
    return jnp.concatenate([v[:, half:], v[:, :half]], axis=1)


def iotas(rows, columns):
    return (
        lax.broadcasted_iota(jnp.int32, (rows, columns), 0),
        lax.broadcasted_iota(jnp.int32, (rows, columns), 1),
    )


def state_scale(last_row, carry_last, heads):
    pieces = [
        jnp.broadcast_to(last_row[:, h * SSM_DIM : h * SSM_DIM + 1], (SSM_DIM, STATE))
        for h in range(heads)
    ]
    return jnp.exp(jnp.concatenate(pieces, axis=0)) * carry_last


def block_decays(step_raw, heads_ref, lane_pos, heads):
    rows = step_raw.shape[0]
    inner = heads * SSM_DIM
    raw = step_raw + heads_ref[0:1, :inner]
    step = softplus(raw)
    rate = step * jnp.exp(heads_ref[1:2, :inner])
    row, col = iotas(rows, rows)
    lower = jnp.where(col <= row, 1.0, 0.0).astype(F32)
    totals = dot(lower, -rate, precision=exact)
    last_row = totals[rows - 1 : rows]
    pos_last = lane_pos[rows - 1 : rows, 0:1]
    local = lax.broadcasted_iota(jnp.int32, (rows, 1), 0).astype(F32)
    carry_on = (lane_pos[:, 0:1] > local).astype(F32)
    keep_last = (local >= (rows - 1) - pos_last).astype(F32)
    carry_last = (pos_last > rows - 1).astype(F32)
    factor = jnp.exp(totals) * carry_on
    tails = jnp.exp(last_row - totals) * keep_last
    return raw, step, rate, totals, last_row, carry_last, factor, tails


def local_mask(lane_pos, rows):
    row, col = iotas(rows, rows)
    gap = (row - col).astype(F32)
    return (gap >= 0) & (gap <= lane_pos[:, 0:1])


def key_window(block):
    start = jnp.maximum(block - WINDOW, 0)
    return start, (block - start) * HALF


def window_mask(lane_pos, offset, rows, keys):
    row, col = iotas(rows, keys)
    gap = (row - col + offset).astype(F32)
    return (gap >= 0) & (gap <= lane_pos[:, 0:1])


def head_decay(totals, totals_t, h, allowed):
    gap = totals[:, h * SSM_DIM : h * SSM_DIM + 1] - totals_t[h * SSM_DIM : h * SSM_DIM + 1, :]
    return jnp.exp(jnp.where(allowed, gap, masked))


def mixer_forward_kernel(
    order_ref, u_ref, normed_ref, table_ref, heads_ref, taps_ref, ag_ref, y_ref, conv_ref, state_in_ref,
    kv_ref, kept_ref, ordered_ref, ext, state, keyval,
):
    block = pl.program_id(0)
    heads = state.shape[0] // SSM_DIM
    inner = heads * SSM_DIM
    width = ext.shape[1]
    rows = u_ref.shape[0]

    @pl.when(block == 0)
    def _():
        ext[0:8, :] = jnp.zeros((8, width), F32)
        state[...] = jnp.zeros(state.shape, F32)
        keyval[...] = jnp.zeros(keyval.shape, BF16)

    lane_pos = table_ref[:, 128:256]
    cosine = table_ref[:, 0:64]
    sine = table_ref[:, 64:128]
    q_at = inner
    u = u_ref[:, :width].astype(F32)
    ext[8 : 8 + rows, :] = u
    conv = u * taps_ref[CONV - 1 : CONV, :]
    for back in range(1, CONV):
        reach = lane_pos[:, 0:1] >= back
        shifted = ext[8 - back : 8 - back + rows, :]
        conv = conv + jnp.where(reach, shifted, 0.0) * taps_ref[CONV - 1 - back : CONV - back, :]
    ext[0:8, :] = u[rows - 8 : rows]
    act = conv * sigmoid(conv)
    ssm_x = act[:, :inner].astype(BF16)
    ssm_b = act[:, 256:384].astype(BF16)
    ssm_c = act[:, 384:512].astype(BF16)
    conv_ref[:, 0:256] = conv[:, 0:256]
    conv_ref[:, 256:512] = conv[:, 256:512]
    query = u[:, q_at : q_at + HEAD_DIM]
    query = (query * cosine + swap_halves(query) * sine).astype(BF16)
    conv_ref[:, q_at : q_at + HEAD_DIM] = query.astype(F32)
    key = u_ref[:, 512 + inner : 512 + inner + HEAD_DIM].astype(F32)
    key = key * cosine + swap_halves(key) * sine
    value = u_ref[:, 768 + inner : 768 + inner + HEAD_DIM].astype(F32)
    pair = jnp.concatenate([key, value], axis=1).astype(BF16)
    kv_ref[...] = pair
    keyval[pl.ds(pl.multiple_of(block * rows, rows), rows), :] = pair
    first, offset = key_window(block)
    span = (WINDOW + 1) * HALF
    window = keyval[pl.ds(pl.multiple_of(first * rows, rows), span), :]
    scores = dot(query * 0.125, window[:, :HEAD_DIM], 1, 1)
    scores = jnp.where(window_mask(lane_pos, offset, rows, span), scores, masked)
    highest = jnp.max(scores, axis=1, keepdims=True)
    weights = jnp.exp(scores - highest)
    total = jnp.sum(weights, axis=1, keepdims=True)
    probs = (weights * (1.0 / total)).astype(BF16)
    attended = dot(probs, window[:, HEAD_DIM:])
    _, step, _, totals, last_row, carry_last, factor, tails = block_decays(
        u_ref[:, 768 : 768 + inner].astype(F32), heads_ref, lane_pos, heads
    )
    totals_t = totals.T
    allowed = local_mask(lane_pos, rows)
    cross = dot(ssm_c, ssm_b, 1, 1)
    x_f = ssm_x.astype(F32)
    stepped = step * x_f
    stepped_low = stepped.astype(BF16)
    parts = []
    for h in range(heads):
        lanes = slice(h * SSM_DIM, (h + 1) * SSM_DIM)
        mix = (head_decay(totals, totals_t, h, allowed) * cross).astype(BF16)
        parts.append(dot(mix, stepped_low[:, lanes]))
    held = state[...]
    state_in_ref[...] = held
    y_pure = jnp.concatenate(parts, axis=1) + factor * dot(ssm_c, held.astype(BF16), 1, 1)
    tailed = (tails * stepped_low.astype(F32)).astype(BF16)
    state[...] = state_scale(last_row, carry_last, heads) * held + dot(tailed, ssm_b, 0, 0)
    y_ref[:, 0:256] = jnp.concatenate(
        [y_pure, jnp.broadcast_to(highest + jnp.log(total), (rows, HEAD_DIM))], axis=1
    )
    y_ref[:, 256:512] = jnp.concatenate([u_ref[:, 768 : 768 + inner], attended], axis=1)
    ordered_ref[...] = normed_ref[...]
    kept_ref[...] = u_ref[:, 0:768].astype(BF16)
    y_full = y_pure + heads_ref[2:3, :inner] * x_f
    gate = u_ref[:, 512 : 512 + inner].astype(F32)
    gated = y_full * (gate * sigmoid(gate))
    ag_ref[...] = jnp.concatenate([gated, attended], axis=1).astype(BF16)


def backward_block(
    block, first_turn, dag, table_ref, heads_ref, taps_ref, y_ref, conv_ref, kept_ref, state_in_ref,
    state_out, kv_ref, stats_ref, dext, dpos, dstate, dkey_t, dvalue_t,
):
    heads = dstate.shape[0] // SSM_DIM
    inner = heads * SSM_DIM
    rows = dag.shape[0]
    lane_pos = table_ref[:, 128:256]
    cosine = table_ref[:, 0:64]
    sine = table_ref[:, 64:128]
    first, offset = key_window(block)
    span = (WINDOW + 1) * HALF
    begin = pl.multiple_of(first * rows, rows)
    window = kv_ref[pl.ds(begin, span), :]
    keys = window[:, :HEAD_DIM]
    values = window[:, HEAD_DIM:]
    query = conv_ref[:, inner : inner + HEAD_DIM] * 0.125
    query_low = query.astype(BF16)
    datt = dag[:, inner : inner + HEAD_DIM]
    datt_f = datt.astype(F32)
    lse = y_ref[:, inner : inner + 1]
    scores = dot(query_low, keys, 1, 1)
    allowed_all = window_mask(lane_pos, offset, rows, span)
    probs = jnp.exp(jnp.where(allowed_all, scores, masked) - lse)
    inward = jnp.sum(datt_f * y_ref[:, 256 + inner : 256 + inner + HEAD_DIM], axis=1, keepdims=True)
    dscores = (probs * (dot(datt, values, 1, 1) - inward)).astype(BF16)
    dquery = dot(dscores, keys) * 0.125
    dkey_t[:, pl.ds(begin, span)] += dot(query.T.astype(BF16), dscores)
    dvalue_t[:, pl.ds(begin, span)] += dot(datt_f.T.astype(BF16), probs.astype(BF16))
    here = pl.ds(pl.multiple_of(block * rows, rows), rows)
    dkey = dkey_t[:, here].T
    dvalue = dvalue_t[:, here].T
    dquery = dquery * cosine - swap_halves(dquery) * sine
    dkey = dkey * cosine - swap_halves(dkey) * sine
    conv = conv_ref[...]
    gate_conv = sigmoid(conv)
    act = conv * gate_conv
    dact = gate_conv * (1.0 + conv * (1.0 - gate_conv))
    ssm_x = act[:, :inner].astype(BF16)
    ssm_b = act[:, 256:384].astype(BF16)
    ssm_c = act[:, 384:512].astype(BF16)
    x_f = ssm_x.astype(F32)
    raw, step, rate, totals, last_row, carry_last, factor, tails = block_decays(
        y_ref[:, 256 : 256 + inner], heads_ref, lane_pos, heads
    )
    totals_t = totals.T
    allowed = local_mask(lane_pos, rows)
    cross = dot(ssm_c, ssm_b, 1, 1)
    gate = kept_ref[:, 512 : 512 + inner].astype(F32)
    sig = sigmoid(gate)
    y_pure = y_ref[:, :inner]
    dgated = dag[:, :inner].astype(F32)
    skip = heads_ref[2:3, :inner]
    dy = dgated * (gate * sig)
    dgate = dgated * (y_pure + skip * x_f) * (sig * (1.0 + gate * (1.0 - sig)))
    dy_low = dy.astype(BF16)
    dy_r = dy_low.astype(F32)
    dy_t = dy.T.astype(BF16)
    stepped_low = (step * x_f).astype(BF16)
    stepped_r = stepped_low.astype(F32)
    tailed = (tails * stepped_r).astype(BF16)
    dcross = jnp.zeros((rows, rows), F32)
    parts = []
    for h in range(heads):
        lanes = slice(h * SSM_DIM, (h + 1) * SSM_DIM)
        decay = head_decay(totals, totals_t, h, allowed)
        mix = (decay * cross).astype(BF16)
        parts.append(dot(dy_t[lanes, :], mix))
        dcross = dcross + dot(dy_low[:, lanes], stepped_low[:, lanes], 1, 1) * decay
    dstep_x = jnp.concatenate(parts, axis=0).T
    dcross_low = dcross.astype(BF16)
    held = state_in_ref[...].astype(BF16)
    dheld = dstate[...]
    dheld_low = dheld.astype(BF16)
    dfactored = (factor * dy).astype(BF16)
    from_state = dot(ssm_b, dheld_low, 1, 1)
    dssm_c = dot(dcross_low, ssm_b) + dot(dfactored, held)
    dssm_b = dot(dcross_low, ssm_c, 0, 0) + dot(tailed, dheld_low)
    dtotals = dy_r * y_pure - stepped_r * dstep_x - tailed.astype(F32) * from_state
    dstep_x = dstep_x + tails * from_state
    end_term = dot(
        jnp.ones((8, STATE), F32), dheld_low.astype(F32) * state_out[...], 1, 1, exact
    )[0:1]
    row, col = iotas(rows, rows)
    upper = jnp.where(col >= row, 1.0, 0.0).astype(F32)
    drate = -(dot(upper, dtotals, precision=exact) + end_term)
    state_out[...] = state_in_ref[...]
    dstate[...] = state_scale(last_row, carry_last, heads) * dheld + dot(dfactored, ssm_c, 0, 0)
    dssm_x = step * dstep_x + skip * dy
    dstep = x_f * dstep_x + jnp.exp(heads_ref[1:2, :inner]) * drate
    draw = dstep * sigmoid(raw)
    none = jnp.zeros((rows, HEAD_DIM), F32)
    dconv = jnp.concatenate([dssm_x, none, dssm_b, dssm_c], axis=1) * dact
    dext[0:rows, :] = dconv
    dpos[0:rows, :] = lane_pos
    u = kept_ref[:, 0:512].astype(F32)
    du = dconv * taps_ref[CONV - 1 : CONV, :]
    stats_ref[CONV - 1 : CONV, :] += jnp.sum(dconv * u, axis=0, keepdims=True)
    for ahead in range(1, CONV):
        reach = dpos[ahead : ahead + rows, 0:1] >= ahead
        shifted = jnp.where(reach, dext[ahead : ahead + rows, :], 0.0)
        tap = CONV - 1 - ahead
        du = du + shifted * taps_ref[tap : tap + 1, :]
        stats_ref[tap : tap + 1, :] += jnp.sum(shifted * u, axis=0, keepdims=True)
    dext[rows : rows + 8, :] = dconv[0:8]
    dpos[rows : rows + 8, :] = lane_pos[0:8]
    stats_ref[4:5, :inner] += jnp.sum(dy * x_f, axis=0, keepdims=True)
    stats_ref[5:6, :inner] += jnp.sum(draw, axis=0, keepdims=True)
    stats_ref[6:7, :inner] += jnp.sum(drate * rate, axis=0, keepdims=True)
    summed = [
        jnp.sum(draw[:, h * SSM_DIM : (h + 1) * SSM_DIM], axis=1, keepdims=True)
        for h in range(heads)
    ]
    lane = lax.broadcasted_iota(jnp.int32, (rows, HEAD_DIM), 1)
    dstep_all = jnp.zeros((rows, HEAD_DIM), F32)
    for h in range(heads):
        dstep_all = jnp.where(lane == h, summed[h], dstep_all)
    return (
        jnp.concatenate([du[:, :inner], dquery], axis=1).astype(BF16),
        du[:, 256:512].astype(BF16),
        jnp.concatenate([dgate, dkey], axis=1).astype(BF16),
        jnp.concatenate([dvalue, dstep_all], axis=1).astype(BF16),
    )


def slot_holding(order, block):
    slot = 0
    for k in range(1, order.shape[0]):
        slot = slot + jnp.where(order[k] == block, k, 0)
    return slot


def mixer_forward(u, normed_t, table, head_rows, taps, slot_of):
    count = u.shape[0]
    blocks = count // HALF
    heads = 3
    inner = heads * SSM_DIM
    width = taps.shape[1]
    at_slot = lambda i, order: (slot_holding(order, i), 0)
    in_order = lambda i, slots: (i, 0)
    whole = lambda i, slots: (0, 0)
    return pl.pallas_call(
        mixer_forward_kernel,
        out_shape=(
            jax.ShapeDtypeStruct((count, inner + HEAD_DIM), BF16),
            jax.ShapeDtypeStruct((count, 512), F32),
            jax.ShapeDtypeStruct((count, width), F32),
            jax.ShapeDtypeStruct((blocks * inner, STATE), F32),
            jax.ShapeDtypeStruct((count, 2 * HEAD_DIM), BF16),
            jax.ShapeDtypeStruct((count, 768), BF16),
            jax.ShapeDtypeStruct(normed_t.shape, BF16),
        ),
        grid_spec=pltpu.PrefetchScalarGridSpec(
            num_scalar_prefetch=1,
            grid=(blocks,),
            in_specs=[
                pl.BlockSpec((HALF, u.shape[1]), at_slot),
                pl.BlockSpec((normed_t.shape[0], HALF), lambda i, order: at_slot(i, order)[::-1]),
                pl.BlockSpec((HALF, table.shape[1]), in_order),
                pl.BlockSpec(head_rows.shape, whole),
                pl.BlockSpec(taps.shape, whole),
            ],
            out_specs=(
                pl.BlockSpec((HALF, inner + HEAD_DIM), at_slot),
                pl.BlockSpec((HALF, 512), in_order),
                pl.BlockSpec((HALF, width), in_order),
                pl.BlockSpec((inner, STATE), in_order),
                pl.BlockSpec((HALF, 2 * HEAD_DIM), in_order),
                pl.BlockSpec((HALF, 768), in_order),
                pl.BlockSpec((normed_t.shape[0], HALF), lambda i, order: (0, i)),
            ),
            scratch_shapes=[
                pltpu.VMEM((8 + HALF, width), F32),
                pltpu.VMEM((inner, STATE), F32),
                pltpu.VMEM((count, 2 * HEAD_DIM), BF16),
            ],
        ),
        compiler_params=pltpu.CompilerParams(vmem_limit_bytes=60 << 20),
    )(slot_of, u, normed_t, table, head_rows, taps)


MESH = pl.DeviceIdType.MESH


class Place:
    def __init__(self):
        self.c = lax.axis_index("context")
        self.t = lax.axis_index("tensor")
        count = lax.axis_size("context")
        self.chips = [
            self.c,
            self.c + 1 - 2 * (self.c % 2),
            (self.c + count // 2) % count,
            count - 1 - self.c,
        ]

    def slot(self, mask, sibling=False):
        core = 1 - self.t if sibling else self.t
        return self.chips[mask] * 2 + core

    def target(self, mask):
        if mask == 4:
            return {"tensor": 1 - self.t}
        return {"context": self.chips[mask]}

    def hello(self, line=None):
        barrier = pltpu.get_barrier_semaphore()
        targets = [self.target(mask) for mask in (1, 2, 4)]
        if line is not None:
            targets += [line.target(step) for step in range(1, line.count)]
        for target in targets:
            pl.semaphore_signal(barrier, inc=1, device_id=target, device_id_type=MESH)
        return len(targets)

    def greet(self, line=None):
        pl.semaphore_wait(pltpu.get_barrier_semaphore(), self.hello(line))


class Wire:
    def __init__(self, place, sems):
        self.place = place
        self.sems = sems
        self.sent = []

    def copy(self, source, target, index, mask):
        return pltpu.make_async_remote_copy(
            src_ref=source,
            dst_ref=target,
            send_sem=self.sems.at[0, index],
            recv_sem=self.sems.at[1, index],
            device_id=self.place.target(mask),
            device_id_type=MESH,
        )

    def send(self, source, target, index, mask):
        def made():
            here = source() if callable(source) else source
            there = target() if callable(target) else target
            return self.copy(here, there, index, mask)

        made().start()
        self.sent.append(made)

    def arrive(self, target, index, mask):
        self.copy(target, target, index, mask).wait_recv()

    def finish(self):
        for made in self.sent:
            made().wait_send()
        self.sent = []


ROWS = HALF
PART = HALF // 2
TOP, END = pl.ds(0, PART), pl.ds(PART, PART)
SCATTER_SEMS = 10
GATHER_SEMS = 14


def scatter_scratch(columns):
    return [
        pltpu.VMEM((4, ROWS, columns), BF16),
        pltpu.VMEM((4, ROWS, columns), BF16),
        pltpu.VMEM((6, PART, columns), BF16),
        pltpu.VMEM((ROWS, columns), F32),
        pltpu.SemaphoreType.DMA((2, SCATTER_SEMS)),
    ]


SCATTER_ORDER = (3, 1, 2, 0)


class Scatter:
    def __init__(self, place, scratch):
        self.place = place
        self.core_in, self.out, self.chip_in, self.kept, sems = scratch
        self.wire = Wire(place, sems)

    def to_core(self, mask, source):
        index = SCATTER_ORDER.index(mask)
        self.wire.send(source, self.core_in.at[index], index, 4)

    def from_core(self, mask):
        index = SCATTER_ORDER.index(mask)
        self.wire.arrive(self.core_in.at[index], index, 4)
        return self.core_in[index].astype(F32)

    def first(self, mine, total, between=None):
        wire, out, kept = self.wire, self.out, self.kept
        both = mine(3) + self.from_core(3)
        out[0] = both.astype(BF16)
        wire.send(lambda: out.at[0, TOP], lambda: self.chip_in.at[0], 4, 1)
        wire.send(lambda: out.at[0, END], lambda: self.chip_in.at[1], 5, 2)
        both = mine(1) + self.from_core(1)
        out[1] = both.astype(BF16)
        wire.send(lambda: out.at[1, TOP], lambda: self.chip_in.at[2], 6, 1)
        kept[END] = both[PART:]
        both = mine(2) + self.from_core(2)
        out[2] = both.astype(BF16)
        wire.send(lambda: out.at[2, END], lambda: self.chip_in.at[3], 7, 2)
        kept[TOP] = both[:PART]
        total[...] = mine(0) + self.from_core(0)

    def second(self):
        wire, out, kept, came = self.wire, self.out, self.kept, self.chip_in
        wire.arrive(came.at[0], 4, 1)
        out[3, TOP] = (kept[TOP] + came[0].astype(F32)).astype(BF16)
        wire.send(lambda: out.at[3, TOP], lambda: came.at[4], 8, 2)
        wire.arrive(came.at[1], 5, 2)
        out[3, END] = (kept[END] + came[1].astype(F32)).astype(BF16)
        wire.send(lambda: out.at[3, END], lambda: came.at[5], 9, 1)

    def last(self, total):
        wire, came = self.wire, self.chip_in
        wire.arrive(came.at[2], 6, 1)
        wire.arrive(came.at[4], 8, 2)
        total[TOP] += came[2].astype(F32) + came[4].astype(F32)
        wire.arrive(came.at[3], 7, 2)
        wire.arrive(came.at[5], 9, 1)
        total[END] += came[3].astype(F32) + came[5].astype(F32)
        wire.finish()


class Gather:
    def __init__(self, place, whole, sems, rows=ROWS, cores=True):
        self.place = place
        self.whole = whole
        self.size = rows
        self.cores = cores
        self.wire = Wire(place, sems)

    def rows(self, mask, sibling=False, half=None):
        place, size = self.place, self.size
        block = place.slot(mask, sibling) if self.cores else place.chips[mask]
        begin = block * size
        if half is None:
            return self.whole.at[pl.ds(pl.multiple_of(begin, size), size)]
        return self.whole.at[pl.ds(pl.multiple_of(begin + half * (size // 2), size // 2), size // 2)]

    def both(self, mask, sibling=False, half=None):
        block = functools.partial(self.rows, mask, sibling, half)
        return block, block

    def start(self, core=True):
        wire = self.wire
        for half, mask, index in ((0, 1, 0), (1, 2, 1), (1, 1, 2), (0, 2, 3)):
            wire.send(*self.both(0, half=half), index, mask)
        if self.cores and core:
            wire.send(*self.both(0), 6, 4)

    def relay(self):
        wire = self.wire
        wire.arrive(self.rows(1, half=0), 0, 1)
        wire.send(*self.both(1, half=0), 4, 2)
        wire.arrive(self.rows(2, half=1), 1, 2)
        wire.send(*self.both(2, half=1), 5, 1)

    def near(self):
        wire = self.wire
        wire.arrive(self.rows(1, half=1), 2, 1)
        if self.cores:
            wire.send(*self.both(1), 7, 4)
        wire.arrive(self.rows(2, half=0), 3, 2)
        if self.cores:
            wire.send(*self.both(2), 8, 4)

    def far(self):
        wire = self.wire
        wire.arrive(self.rows(3, half=0), 4, 2)
        wire.arrive(self.rows(3, half=1), 5, 1)
        if self.cores:
            wire.send(*self.both(3), 9, 4)

    def core(self, mask):
        index = (6, 7, 8, 9)[mask]
        self.wire.arrive(self.rows(mask, sibling=True), index, 4)

    def finish(self):
        self.wire.finish()


class Line:
    def __init__(self):
        self.f = lax.axis_index("fsdp")
        self.count = lax.axis_size("fsdp")

    def target(self, step):
        return {"fsdp": (self.f + step) % self.count}

    def copy(self, source, target, sems, step):
        return pltpu.make_async_remote_copy(
            src_ref=source,
            dst_ref=target,
            send_sem=sems.at[0, step],
            recv_sem=sems.at[1, step],
            device_id=self.target(step),
            device_id_type=MESH,
        )


class LineGather:
    def __init__(self, line, whole, sems):
        self.line = line
        self.whole = whole
        self.sems = sems
        self.size = whole.shape[0] // line.count

    def rows(self, block):
        return self.whole.at[pl.ds(pl.multiple_of(block * self.size, self.size), self.size)]

    def copy(self, block, way, step):
        toward = self.line.f + 1 if way == 0 else self.line.f - 1
        return pltpu.make_async_remote_copy(
            src_ref=self.rows(block),
            dst_ref=self.rows(block),
            send_sem=self.sems.at[way, 0, step],
            recv_sem=self.sems.at[way, 1, step],
            device_id={"fsdp": toward},
            device_id_type=MESH,
        )

    def step(self, number, arrive=True):
        f, last = self.line.f, self.line.count - 1
        for way in (0, 1):
            block = f - number if way == 0 else f + number
            there = block >= 0 if way == 0 else block <= last
            goes_on = f < last if way == 0 else f > 0

            @pl.when(there)
            def _():
                if number > 0:
                    self.copy(block, way, number).wait_recv()

                @pl.when(goes_on)
                def _():
                    self.copy(block, way, number + 1).start()

    def finish(self):
        f, last = self.line.f, self.line.count - 1
        for number in range(self.line.count - 1):
            for way in (0, 1):
                block = f - number if way == 0 else f + number
                there = block >= 0 if way == 0 else block <= last
                goes_on = f < last if way == 0 else f > 0

                @pl.when(there & goes_on)
                def _():
                    self.copy(block, way, number + 1).wait_send()


def line_sems(count):
    return pltpu.SemaphoreType.DMA((2, 2, count + 1))


def opening_kernel(
    tokens_ref, cot_ref, in_x_ref, query_ref, bc_ref, gate_ref, keyval_ref, step_ref, ssm_ref, attn_ref,
    gain_ref, segments_ref, conv_x_ref, conv_bc_ref, bias_ref, decay_ref, skip_ref,
    normed_t_out, u_out, w_out, wout_out, cot_out, table_out, heads_ref, taps_ref,
    x_all, cot_all, normed, normed_t, u, weights_all, wout_all, table, wide,
    x_sems, cot_sems, w_sems, out_sems, local_sems, block_sems,
):
    place = Place()
    line = Line()
    rows_x = Gather(place, x_all, x_sems)
    rows_cot = Gather(place, cot_all, cot_sems)
    weights = LineGather(line, weights_all, w_sems)
    weights_out = LineGather(line, wout_all, out_sems)
    chips = lax.axis_size("context")
    share = in_x_ref.shape[0]
    heads = step_ref.shape[0] // chips
    inner = heads * SSM_DIM
    chip_rows = pl.ds(pl.multiple_of(place.c * 2 * ROWS, 2 * ROWS), 2 * ROWS)
    waiting = []

    def local(source, target, sem):
        made = pltpu.make_async_copy(source, target, sem)
        made.start()
        waiting.append(made)
        return made

    greetings = place.hello(line)
    own_x = pltpu.make_async_copy(tokens_ref, x_all.at[chip_rows], local_sems.at[0])
    own_x.start()
    own_cot = pltpu.make_async_copy(cot_ref, cot_all.at[chip_rows], local_sems.at[1])
    own_cot.start()
    mine = pl.ds(pl.multiple_of(line.f * share, share), share)
    heads_ref[...] = jnp.zeros(heads_ref.shape, F32)
    taps_ref[...] = jnp.zeros(taps_ref.shape, F32)
    for k in range(chips):

        @pl.when(place.c == k)
        def _():
            inner_part = slice(k * inner, (k + 1) * inner)
            head_part = slice(k * HEAD_DIM, (k + 1) * HEAD_DIM)
            weights_all[mine, 0:256] = jnp.concatenate(
                [in_x_ref[:, inner_part], query_ref[:, head_part]], axis=1
            )
            weights_all[mine, 512:768] = jnp.concatenate(
                [gate_ref[:, inner_part], keyval_ref[:, :HEAD_DIM]], axis=1
            )
            wout_all[mine, :] = jnp.concatenate(
                [ssm_ref[:, inner_part], attn_ref[:, head_part]], axis=1
            )
            taps_ref[0:CONV, :inner] = conv_x_ref[:, inner_part]
            for h in range(heads):
                lane = slice(k * heads + h, k * heads + h + 1)
                for row, source in enumerate((bias_ref, decay_ref, skip_ref)):
                    heads_ref[row : row + 1, h * SSM_DIM : (h + 1) * SSM_DIM] = jnp.broadcast_to(
                        source[:, lane], (1, SSM_DIM)
                    )

    taps_ref[0:CONV, 256:512] = conv_bc_ref[...]
    head, column = iotas(step_ref.shape[0], HEAD_DIM)
    chosen = (head == column + place.c * heads) & (column < heads)
    steps = dot(step_ref[...], jnp.where(chosen, 1.0, 0.0).astype(BF16), 0, 0)
    weights_all[mine, 768:896] = jnp.concatenate(
        [keyval_ref[:, HEAD_DIM:].astype(F32), steps], axis=1
    ).astype(BF16)
    weights_all[mine, 256:512] = bc_ref[...]
    own_x.wait()
    own_cot.wait()
    pl.semaphore_wait(pltpu.get_barrier_semaphore(), greetings)
    weights.step(0)
    rows_x.start(core=False)

    def norm(slot):
        rows = slot_rows(slot)
        x = x_all[rows, :].astype(F32)
        normed[rows, :] = (x * norm_scale(x) * gain_ref[...]).astype(BF16)
        columns = pl.ds(pl.multiple_of(slot * ROWS, ROWS), ROWS)
        normed_t[:, columns] = normed[rows, :].T

    norm(place.slot(0))
    norm(place.slot(0, True))

    numbers = segments_ref[...]
    bounds = [
        jnp.sum(jnp.where(numbers < k, 1.0, 0.0), axis=1, keepdims=True) for k in (1, 2)
    ]
    count = table.shape[0]
    lane = lax.broadcasted_iota(jnp.int32, (8, 128), 1)[0:1]
    power = -(lane % (HEAD_DIM // 2)).astype(F32) / (HEAD_DIM // 2)
    freqs = jnp.exp(power * math.log(10000.0))
    phase = jnp.where(lane < HEAD_DIM, math.pi / 2, 0.0)
    sign = jnp.where((lane >= HEAD_DIM) & (lane < HEAD_DIM + HEAD_DIM // 2), -1.0, 1.0)

    def angles(block, carry):
        row = lax.broadcasted_iota(jnp.int32, (ROWS, 128), 0) + block * ROWS
        row = row.astype(F32)
        start = jnp.where(row >= bounds[0], bounds[0], 0.0)
        start = jnp.where(row >= bounds[1], bounds[1], start)
        pos = row - start
        here = slot_rows(block)
        table[here, 0:128] = jnp.sin(pos * freqs + phase) * sign
        table[here, 128:256] = pos
        return carry

    blocks = count // ROWS
    rows_x.relay()
    rows_cot.start(core=False)
    lax.fori_loop(0, blocks // 2, angles, 0)
    weights.step(1)
    lax.fori_loop(blocks // 2, blocks, angles, 0)
    local(table, table_out, local_sems.at[2])
    rows_x.near()
    norm(place.slot(1))
    norm(place.slot(2))
    rows_cot.relay()
    for number in range(2, line.count - 1):
        weights.step(number)
    rows_x.far()
    norm(place.slot(3))
    for mask in (1, 2, 3):
        rows_x.core(mask)
        norm(place.slot(mask, True))
    weights_out.step(0)
    rows_cot.near()
    weights.step(line.count - 1)
    local(weights_all, w_out, local_sems.at[3])
    local(normed_t, normed_t_out, local_sems.at[6])
    wide[:, 0:768] = weights_all[:, 0:768]
    row, column = iotas(HEAD_DIM, inner)
    copies = jnp.where(column // SSM_DIM == row, 1.0, 0.0).astype(BF16)
    wide[:, 768:1024] = jnp.concatenate(
        [
            dot(weights_all[:, 896 - HEAD_DIM : 896], copies),
            weights_all[:, 768 : 768 + HEAD_DIM].astype(F32),
        ],
        axis=1,
    ).astype(BF16)

    def project(slot):
        rows = pl.ds(slot * ROWS, ROWS)
        u[rows, :] = dot(normed[rows, :], wide[...])
        local(u.at[rows], u_out.at[rows], block_sems.at[0, slot])

    for slot in range(blocks // 2):
        project(slot)
    weights_out.step(1)
    rows_cot.far()
    for slot in range(blocks // 2, blocks):
        project(slot)
    for number in range(2, line.count):
        weights_out.step(number)
    local(wout_all, wout_out, local_sems.at[4])
    for mask in (1, 2, 3):
        rows_cot.core(mask)
    local(cot_all, cot_out, local_sems.at[5])
    for made in waiting:
        made.wait()
    rows_x.finish()
    rows_cot.finish()
    weights.finish()
    weights_out.finish()


def opening(tokens, cotangent, weights, gain, segments, taps, by_head):
    fsdp = lax.axis_size("fsdp")
    model = tokens.shape[1]
    count = segments.shape[1]
    blocks = count // ROWS
    vmem = pl.BlockSpec(memory_space=pltpu.VMEM)
    hbm = pl.BlockSpec(memory_space=pl.ANY)
    shape = jax.ShapeDtypeStruct
    dma = pltpu.SemaphoreType.DMA
    buffers = [
        ((model, count), BF16),
        ((count, 1024), F32),
        ((model, 896), BF16),
        ((model, 256), BF16),
        ((count, model), BF16),
        ((count, 256), F32),
    ]
    kept = [buffers[k] for k in (0, 1, 2, 3, 5)]
    return pl.pallas_call(
        opening_kernel,
        out_shape=tuple(shape(*one) for one in buffers) + (shape((8, 256), F32), shape((8, 512), F32)),
        in_specs=[hbm] * 2 + [vmem] * 15,
        out_specs=(hbm,) * 6 + (vmem,) * 2,
        scratch_shapes=[pltpu.VMEM((count, model), BF16)] * 3
        + [pltpu.VMEM(*one) for one in kept]
        + [
            pltpu.VMEM((model, 1024), BF16),
            dma((2, GATHER_SEMS)),
            dma((2, GATHER_SEMS)),
            line_sems(fsdp),
            line_sems(fsdp),
            dma((7,)),
            dma((1, blocks)),
        ],
        compiler_params=pltpu.CompilerParams(
            collective_id=3, has_side_effects=True, vmem_limit_bytes=60 << 20
        ),
        cost_estimate=pl.CostEstimate(
            flops=2 * count * model * 1024, bytes_accessed=30 << 20, transcendentals=count * 128
        ),
    )(
        tokens, cotangent, *weights, gain.reshape(1, -1), segments, *taps,
        *[one.reshape(1, -1) for one in by_head],
    )


def slot_rows(slot):
    return pl.ds(pl.multiple_of(slot * ROWS, ROWS), ROWS)


def norm_scale(values):
    return lax.rsqrt(jnp.mean(values * values, axis=1, keepdims=True) + epsilon)


def middle_kernel(
    ag_ref, wout_ref, gate_ref, up_ref, down_ref, x_ref, cot_ref, cot_all_ref, gain_ref,
    hidden_ref, dag_ref, mixed_ref, dmixed_ref, dgain_ref, down_all_ref, ffn_ref, dout_ref,
    nffn_ref, dgu_ref, dm_ref, dw_ref, arrived, part, wffn_ref, *scratch,
):
    place = Place()
    first = Scatter(place, scratch[0:5])
    back = Scatter(place, scratch[5:10])
    forth = Gather(place, nffn_ref, scratch[10])
    home = Gather(place, dm_ref, scratch[11])
    hid = hidden_ref.shape[1]
    line = Line()
    weights = LineGather(line, wffn_ref, scratch[12])
    share = gate_ref.shape[0]
    place.greet(line)
    mine = pl.ds(pl.multiple_of(line.f * share, share), share)
    lanes = pl.ds(pl.multiple_of(place.c * hid, hid), hid)
    for k, source in enumerate((gate_ref, up_ref, down_ref)):
        wffn_ref[mine, k * hid : (k + 1) * hid] = source[:, lanes]
    weights.step(0)

    def block(mask, sibling=False):
        return dot(ag_ref[slot_rows(place.slot(mask, sibling)), :], wout_ref[...], 1, 1)

    for mask in SCATTER_ORDER:
        rows = slot_rows(place.slot(mask, True))
        part[rows, :] = block(mask, True).astype(BF16)
        first.to_core(mask, part.at[rows])
    first.first(block, mixed_ref)
    weights.step(1)
    first.second()
    half = pl.ds(pl.multiple_of(place.t * ROWS, ROWS), ROWS)
    mixed_ref[...] += x_ref[half, :].astype(F32)
    first.last(mixed_ref)
    mixed = mixed_ref[...]
    gain = gain_ref[...]
    scale = norm_scale(mixed)
    own = slot_rows(place.slot(0))
    nffn_ref[own, :] = (mixed * scale * gain).astype(BF16)
    forth.start()
    for number in range(2, line.count):
        weights.step(number)

    def work(slot):
        rows = slot_rows(slot)
        normed = nffn_ref[rows, :]
        gate_up = dot(normed, wffn_ref[:, : 2 * hid])
        dhidden = dot(cot_all_ref[rows, :], wffn_ref[:, 2 * hid :]).astype(BF16).astype(F32)
        gate, up = gate_up[:, :hid], gate_up[:, hid:]
        sig = sigmoid(gate)
        silu = gate * sig
        dgate = dhidden * up * (sig * (1.0 + gate * (1.0 - sig)))
        hidden_ref[rows, :] = (silu * up).astype(BF16)
        dgu_ref[rows, :hid] = dgate.astype(BF16)
        dgu_ref[rows, hid:] = (dhidden * silu).astype(BF16)
        part[rows, :] = dot(dgu_ref[rows, :], wffn_ref[:, : 2 * hid], 1, 1).astype(BF16)

    def hand_over(mask):
        slot = place.slot(mask, True)
        work(slot)
        back.to_core(mask, part.at[slot_rows(slot)])

    work(place.slot(0))
    forth.relay()
    forth.core(0)
    hand_over(0)
    forth.near()
    forth.core(1)
    hand_over(1)
    forth.core(2)
    hand_over(2)
    work(place.slot(1))
    forth.far()
    work(place.slot(2))
    forth.core(3)
    hand_over(3)
    work(place.slot(3))
    forth.finish()

    def ready(mask):
        return part[slot_rows(place.slot(mask)), :].astype(F32)

    back.first(ready, dmixed_ref)

    back.second()
    chunk = dw_ref.shape[0] // 4
    for k in range(4):
        rows = slice(k * chunk, (k + 1) * chunk)
        dw_ref[rows, : 2 * hid] = dot(nffn_ref[:, rows], dgu_ref[...], 0, 0).astype(BF16)
    back.last(dmixed_ref)
    dnffn = dmixed_ref[...]
    mixed = mixed_ref[...]
    scale = norm_scale(mixed)
    spread = dnffn * gain
    pull = jnp.mean(spread * mixed, axis=1, keepdims=True)
    dgain_ref[...] = jnp.broadcast_to(
        jnp.sum(dnffn * mixed * scale, axis=0, keepdims=True), dgain_ref.shape
    )
    dmixed = cot_ref[half, :].astype(F32) + scale * (spread - mixed * (scale * scale * pull))
    dmixed_ref[...] = dmixed
    dm_ref[own, :] = dmixed.astype(BF16)
    home.start()

    def pull_back(slot):
        rows = slot_rows(slot)
        dag_ref[rows, :] = dot(dm_ref[rows, :], wout_ref[...]).astype(BF16)

    pull_back(place.slot(0))
    home.relay()
    for k in range(4):
        rows = slice(k * chunk, (k + 1) * chunk)
        dw_ref[rows, 2 * hid :] = dot(cot_all_ref[:, rows], hidden_ref[...], 0, 0).astype(BF16)
    line_sent = []
    for step in range(1, line.count):
        rows = pl.ds(pl.multiple_of((line.f + step) % line.count * share, share), share)
        made = line.copy(dw_ref.at[rows], arrived.at[step], scratch[13], step)
        made.start()
        line_sent.append(made)
    home.core(0)
    pull_back(place.slot(0, True))
    home.near()
    pull_back(place.slot(1))
    pull_back(place.slot(2))
    home.far()
    pull_back(place.slot(3))
    for mask in (1, 2, 3):
        home.core(mask)
        pull_back(place.slot(mask, True))
    dout_ref[...] = dot(dm_ref[...], ag_ref[...], 0, 0).astype(BF16)
    down_all_ref[...] = wffn_ref[:, 2 * hid :]
    sums = dw_ref[mine, :].astype(F32)
    for step in range(1, line.count):
        line.copy(arrived.at[step], arrived.at[step], scratch[13], step).wait_recv()
        sums = sums + arrived[step].astype(F32)
    ffn_ref[...] = sums.astype(BF16)
    for made in line_sent:
        made.wait_send()
    home.finish()
    weights.finish()


def middle(ag, wout, weights, x_own, cot_own, cot_all, gain):
    count, model = cot_all.shape
    hid = weights[0].shape[1] // lax.axis_size("context")
    columns = ag.shape[1]
    vmem = pl.BlockSpec(memory_space=pltpu.VMEM)
    shape = jax.ShapeDtypeStruct
    return pl.pallas_call(
        middle_kernel,
        out_shape=(
            shape((count, hid), BF16),
            shape((count, columns), BF16),
            shape((ROWS, model), F32),
            shape((ROWS, model), F32),
            shape((8, model), F32),
            shape((model, hid), BF16),
            shape((weights[0].shape[0], 3 * hid), BF16),
            shape((model, columns), BF16),
        ),
        in_specs=[vmem] * 9,
        out_specs=(vmem,) * 8,
        scratch_shapes=[
            pltpu.VMEM((count, model), BF16),
            pltpu.VMEM((count, 2 * hid), BF16),
            pltpu.VMEM((count, model), BF16),
            pltpu.VMEM((model, 3 * hid), BF16),
            pltpu.VMEM((lax.axis_size("fsdp"), weights[0].shape[0], 3 * hid), BF16),
            pltpu.VMEM((count, model), BF16),
            pltpu.VMEM((model, 3 * hid), BF16),
        ]
        + scatter_scratch(model)
        + scatter_scratch(model)
        + [pltpu.SemaphoreType.DMA((2, GATHER_SEMS))] * 2
        + [line_sems(lax.axis_size("fsdp")), pltpu.SemaphoreType.DMA((2, lax.axis_size("fsdp")))],
        compiler_params=pltpu.CompilerParams(
            collective_id=1, has_side_effects=True, vmem_limit_bytes=60 << 20
        ),
        cost_estimate=pl.CostEstimate(
            flops=20 * count * model * hid, bytes_accessed=40 << 20, transcendentals=count * hid
        ),
    )(ag, wout, *weights, x_own, cot_own, cot_all, gain.reshape(1, -1))


BACK_INPUTS = 5


def closing_kernel(
    pick_ref, dag_ref, kv_ref, heads_ref, taps_ref, dmixed_ref, mixed_ref, tokens_ref, gain_ref, ffn_ref,
    dgain_ref, dout_ref, table_hbm, y_hbm, conv_hbm, kept_hbm, states_hbm, normed_t_hbm, w_hbm,
    hidden_hbm, down_hbm,
    grad_ref, out_ref, last_ref, mids_ref, outs_ref, small_ref,
    table, y, conv, kept, states, normed_t, w, hidden, down,
    du, dw_sum, dw, arrived, arrived_out, total, part, bc_out, bc_in, small_in,
    stats, dext, dpos, dstate, state_out, dkey_t, dvalue_t, *scratch,
):
    place = Place()
    line = Line()
    back = Scatter(place, scratch[0:5])
    final = Scatter(place, scratch[5:10])
    share = ffn_ref.shape[0]
    last_all = Gather(place, last_ref, scratch[10], share, False)
    mid_all = Gather(place, mids_ref, scratch[11], share, False)
    out_all = Gather(place, outs_ref, scratch[12], share, False)
    small_rows = small_in.shape[1]
    small_all = Gather(place, small_ref, scratch[13], small_rows)
    line_sems_, small_sems, out_sems, pair_sems, load_sems, block_sems = scratch[14:20]
    pair = Wire(place, pair_sems)
    greetings = place.hello(line)
    sent = []
    loads = [
        pltpu.make_async_copy(source, target, load_sems.at[k])
        for k, (source, target) in enumerate(
            ((hidden_hbm, hidden), (down_hbm, down), (normed_t_hbm, normed_t), (w_hbm, w))
        )
    ]
    blocks = du.shape[0] // ROWS
    streams = ((table_hbm, table), (y_hbm, y), (conv_hbm, conv), (kept_hbm, kept), (states_hbm, states))

    def fetch(block, buffer):
        copies = []
        for k, (source, target) in enumerate(streams):
            size = target.shape[1]
            begin = pl.multiple_of(block * size, size)
            copies.append(
                pltpu.make_async_copy(
                    source.at[pl.ds(begin, size)], target.at[buffer], block_sems.at[buffer, k]
                )
            )
        return copies

    for made in fetch(blocks - 1, 0) + loads:
        made.start()
    mids_ref[pl.ds(pl.multiple_of(place.c * share, share), share), :] = ffn_ref[...]
    width = dext.shape[1]
    dext[ROWS : ROWS + 8, :] = jnp.zeros((8, width), F32)
    dpos[ROWS : ROWS + 8, :] = jnp.full((8, dpos.shape[1]), -1.0, F32)
    for ref in (dstate, state_out, dkey_t, dvalue_t, stats, dw_sum):
        ref[...] = jnp.zeros(ref.shape, F32)
    pl.semaphore_wait(pltpu.get_barrier_semaphore(), greetings)

    for step in range(1, line.count):
        rows = pl.ds(pl.multiple_of((line.f + step) % line.count * share, share), share)
        made = line.copy(dout_ref.at[rows], arrived_out.at[step], out_sems, step)
        made.start()
        sent.append(made)
    for made in loads:
        made.wait()

    def out_block(mask, sibling=False):
        return dot(hidden[slot_rows(place.slot(mask, sibling)), :], down[...], 1, 1)

    for k, mask in enumerate(SCATTER_ORDER):
        part[k] = out_block(mask, True).astype(BF16)
        final.to_core(mask, part.at[k])
    mid_all.start()
    here = pl.ds(pl.multiple_of(place.c * share, share), share)
    own = pl.ds(pl.multiple_of(line.f * share, share), share)
    half = pl.ds(pl.multiple_of(place.t * ROWS, ROWS), ROWS)

    def my_half(ref):
        return lambda: ref.at[pl.ds(pl.multiple_of(place.t * ROWS, ROWS), ROWS)]

    def collect_out():
        sums = dout_ref[own, :].astype(F32)
        for step in range(1, line.count):
            line.copy(arrived_out.at[step], arrived_out.at[step], out_sems, step).wait_recv()
            sums = sums + arrived_out[step].astype(F32)
        outs_ref[here, :] = sums.astype(BF16)
        out_all.start()

    def finish_out():
        total[...] += mixed_ref[...]
        final.last(total)
        out_ref[half, :] = total[...].astype(BF16)
        pair.send(my_half(out_ref), my_half(out_ref), 1, 4)

    def picked(source, row):
        marks = pick_ref[pl.ds(pl.multiple_of(row * 8, 8), 8), 0:1].astype(BF16)
        found = source[0:ROWS, :] * marks[0:1]
        for k in range(1, blocks):
            found = found + source[k * ROWS : (k + 1) * ROWS, :] * marks[k : k + 1]
        return found

    events = {
        0: (lambda: final.first(out_block, total), mid_all.relay),
        1: (final.second, mid_all.near, collect_out),
        2: (mid_all.far, finish_out, out_all.relay),
        3: (out_all.near,),
        4: (out_all.far,),
    }

    def turn(number, carry):
        block = blocks - 1 - number
        buffer = number % 2
        for made in fetch(block, buffer):
            made.wait()

        @pl.when(number < blocks - 1)
        def _():
            for made in fetch(block - 1, 1 - buffer):
                made.start()

        dag = picked(dag_ref, block)
        pieces = backward_block(
            block, number, dag, table.at[buffer], heads_ref, taps_ref, y.at[buffer],
            conv.at[buffer], kept.at[buffer], states.at[buffer], state_out, kv_ref, stats, dext, dpos,
            dstate, dkey_t, dvalue_t,
        )
        grads = jnp.concatenate(pieces, axis=1)
        du[slot_rows(block), :] = grads
        dw_sum[...] += dot(normed_t[:, slot_rows(block)], grads)
        for when, actions in events.items():

            @pl.when(number == when)
            def _():
                for action in actions:
                    action()

        return carry

    lax.fori_loop(0, blocks, turn, 0)

    dw[...] = dw_sum[...].astype(BF16)
    for step in range(1, line.count):
        rows = pl.ds(pl.multiple_of((line.f + step) % line.count * share, share), share)
        made = line.copy(dw.at[rows], arrived.at[step], line_sems_, step)
        made.start()
        sent.append(made)

    def block_of(mask, sibling=False):
        return dot(picked(du, place.slot(mask, sibling) + blocks), w[...], 1, 1)

    for k, mask in enumerate(SCATTER_ORDER):
        part[k] = block_of(mask, True).astype(BF16)
        back.to_core(mask, part.at[k])
    back.first(block_of, total)
    back.second()
    back.last(total)
    dnormed = total[...]
    x = tokens_ref[half, :].astype(F32)
    gain = gain_ref[...]
    scale = norm_scale(x)
    spread = dnormed * gain
    pull = jnp.mean(spread * x, axis=1, keepdims=True)
    grad = dmixed_ref[...] + scale * (spread - x * (scale * scale * pull))
    grad_ref[half, :] = grad.astype(BF16)
    pair.send(grad_ref.at[half], grad_ref.at[half], 0, 4)
    small_in[0] = jnp.zeros(small_in.shape[1:], F32)
    small_in[0, 0:1, :] = jnp.sum(dnormed * x * scale, axis=0, keepdims=True)
    small_in[0, 1:2, :] = dgain_ref[0:1, :]
    small_in[0, 8:16, :width] = stats[...]
    for step in range(1, line.count):
        made = line.copy(small_in.at[0], small_in.at[step], small_sems, step)
        made.start()
        sent.append(made)
    for step in range(1, line.count):
        line.copy(small_in.at[0], small_in.at[step], small_sems, step).wait_recv()
    summed = small_in[line.f % line.count]
    for other in range(1, line.count):
        summed = summed + small_in[(line.f + line.count - other) % line.count]
    mine = pl.ds(pl.multiple_of(place.slot(0) * small_rows, small_rows), small_rows)
    small_ref[mine, :] = summed
    small_all.start()
    small_all.relay()
    small_all.near()
    small_all.far()

    sums = dw[own, :].astype(F32)
    for step in range(1, line.count):
        line.copy(arrived.at[step], arrived.at[step], line_sems_, step).wait_recv()
        sums = sums + arrived[step].astype(F32)
    bc_out[...] = sums[:, 256:512].astype(BF16)
    pair.send(bc_out, bc_in, 2, 4)
    last_ref[here, 0:256] = sums[:, 0:256].astype(BF16)
    last_ref[here, 512:] = sums[:, 512:].astype(BF16)
    pair.arrive(bc_in, 2, 4)
    last_ref[here, 256:512] = (bc_out[...].astype(F32) + bc_in[...].astype(F32)).astype(BF16)
    last_all.start()
    last_all.relay()
    last_all.near()
    last_all.far()
    for mask in range(4):
        small_all.core(mask)
    other = pl.ds(pl.multiple_of((1 - place.t) * ROWS, ROWS), ROWS)
    pair.arrive(grad_ref.at[other], 0, 4)
    pair.arrive(out_ref.at[other], 1, 4)
    for made in sent:
        made.wait_send()
    pair.finish()
    mid_all.finish()
    out_all.finish()
    small_all.finish()
    last_all.finish()


def closing(small_inputs, streams, loads, fsdp):
    tokens, ffn, dout = small_inputs[7], small_inputs[9], small_inputs[11]
    normed_t, w, hidden, down = loads
    model, count = normed_t.shape
    share = ffn.shape[0]
    columns = w.shape[1]
    chips = lax.axis_size("context")
    blocks = count // ROWS
    vmem = pl.BlockSpec(memory_space=pltpu.VMEM)
    hbm = pl.BlockSpec(memory_space=pl.ANY)
    shape = jax.ShapeDtypeStruct
    dma = pltpu.SemaphoreType.DMA
    space = pltpu.VMEM
    inner = streams[4].shape[0] // blocks
    return pl.pallas_call(
        closing_kernel,
        out_shape=(
            shape((2 * ROWS, model), BF16),
            shape((2 * ROWS, model), BF16),
            shape((chips * share, columns), BF16),
            shape((chips * share, ffn.shape[1]), BF16),
            shape((chips * share, dout.shape[1]), BF16),
            shape((2 * chips * 16, model), F32),
        ),
        in_specs=[vmem] * 12 + [hbm] * 9,
        out_specs=(vmem,) * 6,
        scratch_shapes=[space((2, one.shape[0] // blocks, one.shape[1]), one.dtype) for one in streams]
        + [space(one.shape, one.dtype) for one in loads]
        + [
            space((count, columns), BF16),
            space((model, columns), F32),
            space((model, columns), BF16),
            space((fsdp, share, columns), BF16),
            space((fsdp, share, dout.shape[1]), BF16),
            space((ROWS, model), F32),
            space((4, ROWS, model), BF16),
            space((share, 256), BF16),
            space((share, 256), BF16),
            space((fsdp, 16, model), F32),
            space((8, 512), F32),
            space((ROWS + 8, 512), F32),
            space((ROWS + 8, 128), F32),
            space((inner, STATE), F32),
            space((inner, STATE), F32),
            space((HEAD_DIM, count), F32),
            space((HEAD_DIM, count), F32),
        ]
        + scatter_scratch(model)
        + scatter_scratch(model)
        + [dma((2, GATHER_SEMS))] * 4
        + [dma((2, fsdp)), dma((2, fsdp)), dma((2, fsdp)), dma((2, 3)), dma((4,)), dma((2, BACK_INPUTS))],
        compiler_params=pltpu.CompilerParams(
            collective_id=2, has_side_effects=True, vmem_limit_bytes=61 << 20
        ),
        cost_estimate=pl.CostEstimate(
            flops=4 * count * model * columns, bytes_accessed=30 << 20, transcendentals=0
        ),
    )(*small_inputs, *streams, *loads)


def assemble_kernel(
    last_ref, mid_ref, outs_ref, dx_ref, out_in_ref, small_ref,
    out_ref, grad_ref, query_ref, keyval_ref, attn_ref, gate_ref, x_ref, bc_ref, step_ref, ssm_ref,
    ffn_gate_ref, ffn_up_ref, ffn_down_ref, gain_ref, gain_ffn_ref, conv_x_ref, conv_bc_ref,
    bias_ref, decay_ref, skip_ref,
):
    chips = last_ref.shape[0]
    heads = step_ref.shape[1] // chips
    inner = heads * SSM_DIM
    hid = ffn_gate_ref.shape[1] // chips

    def spread(source, begin, width):
        return jnp.concatenate(
            [source[k, :, begin : begin + width].astype(F32) for k in range(chips)], axis=1
        )

    def summed(begin, end):
        total = last_ref[0, :, begin:end].astype(F32)
        for k in range(1, chips):
            total = total + last_ref[k, :, begin:end].astype(F32)
        return total

    out_ref[...] = out_in_ref[...]
    grad_ref[...] = dx_ref[...]
    x_ref[...] = spread(last_ref, 0, inner)
    query_ref[...] = spread(last_ref, inner, HEAD_DIM)
    bc_ref[...] = summed(256, 512)
    gate_ref[...] = spread(last_ref, 512, inner)
    both = summed(640, 896)
    keyval_ref[...] = both[:, HEAD_DIM : 3 * HEAD_DIM]
    step_ref[...] = spread(last_ref, 896 - HEAD_DIM, heads)
    ffn_gate_ref[...] = spread(mid_ref, 0, hid)
    ffn_up_ref[...] = spread(mid_ref, hid, hid)
    ffn_down_ref[...] = spread(mid_ref, 2 * hid, hid)
    ssm_ref[...] = spread(outs_ref, 0, inner)
    attn_ref[...] = spread(outs_ref, inner, HEAD_DIM)

    @pl.when(pl.program_id(0) == 0)
    def _():
        everywhere = small_ref[0:16, :]
        for k in range(1, small_ref.shape[0] // 16):
            everywhere = everywhere + small_ref[16 * k : 16 * k + 16, :]
        gain_ref[...] = everywhere[0:1]
        gain_ffn_ref[...] = everywhere[1:2]
        conv_bc_ref[...] = everywhere[8 : 8 + CONV, 256:512]
        core = lax.axis_index("tensor")
        own = [
            small_ref[pl.ds(pl.multiple_of((2 * k + core) * 16, 16), 16), :] for k in range(chips)
        ]
        conv_x_ref[...] = jnp.concatenate([one[8 : 8 + CONV, :inner] for one in own], axis=1)
        for row, target in ((12, skip_ref), (13, bias_ref), (14, decay_ref)):
            target[...] = jnp.concatenate(
                [
                    jnp.sum(
                        one[row : row + 1, h * SSM_DIM : (h + 1) * SSM_DIM], axis=1, keepdims=True
                    )
                    for one in own
                    for h in range(heads)
                ],
                axis=1,
            )


def assemble(last, mid, outs, dx, out, small, widths, heads):
    chips = lax.axis_size("context")
    share = last.shape[0] // chips
    turns = 2
    rows = share // turns
    shape = jax.ShapeDtypeStruct
    block = lambda height, width: pl.BlockSpec((height, width), lambda i: (i, 0))
    fixed = lambda height, width: pl.BlockSpec((height, width), lambda i: (0, 0))
    slab = lambda width: pl.BlockSpec((chips, rows, width), lambda i: (0, i, 0))
    token_rows = dx.shape[0] // turns
    model = dx.shape[1]
    tiny = [
        (1, model), (1, model), (CONV, heads * SSM_DIM), (CONV, 2 * STATE), (1, heads), (1, heads),
        (1, heads),
    ]
    return pl.pallas_call(
        assemble_kernel,
        grid=(turns,),
        out_shape=(shape(out.shape, BF16), shape(dx.shape, BF16))
        + tuple(shape((share, width), F32) for width in widths)
        + tuple(shape(one, F32) for one in tiny),
        in_specs=[
            slab(last.shape[1]), slab(mid.shape[1]), slab(outs.shape[1]),
            block(token_rows, model), block(token_rows, model), fixed(*small.shape),
        ],
        out_specs=(block(token_rows, model), block(token_rows, model))
        + tuple(block(rows, width) for width in widths)
        + tuple(fixed(*one) for one in tiny),
        compiler_params=pltpu.CompilerParams(vmem_limit_bytes=60 << 20),
    )(*[one.reshape(chips, share, -1) for one in (last, mid, outs)], dx, out, small)


def per_device(
    tokens, segments, deal, gain_mix, w_query, w_keyval, w_attn_out, w_gate_z, w_in_x, w_bc, w_step,
    conv_x, conv_bc, step_bias, decay_log, skip, w_ssm_out, gain_ffn, w_ffn_gate, w_ffn_up,
    w_ffn_down, cotangent,
):
    ids = jnp.arange(deal.shape[1], dtype=jnp.int32)
    holds = (deal[0][:, None] == ids[None, :]).astype(F32)
    pick = jnp.broadcast_to(jnp.concatenate([holds.T, holds]).reshape(-1, 1), (128, 128))
    normed_t, u, w_all, wout_all, cot_all, table, head_rows, taps = opening(
        tokens,
        cotangent,
        (w_in_x, w_query, w_bc, w_gate_z, w_keyval, w_step.T, w_ssm_out, w_attn_out),
        gain_mix,
        segments,
        (conv_x, conv_bc),
        (step_bias, decay_log, skip),
    )
    ag, y, conv, states, keyval, kept, normed_t = mixer_forward(u, normed_t, table, head_rows, taps, deal[0])
    hidden, dag, mixed, dmixed, dgain, down, dffn, dout = middle(
        ag, wout_all, (w_ffn_gate, w_ffn_up, w_ffn_down), tokens, cotangent, cot_all, gain_ffn
    )
    dx, out, last, mids, outs, small = closing(
        (
            pick, dag, keyval, head_rows, taps, dmixed, mixed, tokens, gain_mix.reshape(1, -1), dffn,
            dgain, dout,
        ),
        (table, y, conv, kept, states),
        (normed_t, w_all, hidden, down),
        lax.axis_size("fsdp"),
    )
    weights = (
        w_query, w_keyval, w_attn_out, w_gate_z, w_in_x, w_bc, w_step, w_ssm_out, w_ffn_gate,
        w_ffn_up, w_ffn_down,
    )
    done = assemble(last, mids, outs, dx, out, small, [w.shape[1] for w in weights], skip.shape[0])
    grads = done[2:13]
    gain, gain_two, taps_x, taps_bc, bias, decay, skips = done[13:]
    return (
        done[0],
        done[1],
        gain.reshape(-1),
        *grads[:7],
        taps_x,
        taps_bc,
        bias.reshape(-1),
        decay.reshape(-1),
        skips.reshape(-1),
        grads[7],
        gain_two.reshape(-1),
        *grads[8:],
    )


def solution(mesh):
    in_specs = (
        P(("fsdp", "context"), None),
        P("fsdp", None),
        P("fsdp", None),
        P(),
        P("fsdp", "tensor"),
        P("fsdp", "tensor"),
        P("fsdp", "tensor"),
        P("fsdp", "tensor"),
        P("fsdp", "tensor"),
        P("fsdp", None),
        P("fsdp", "tensor"),
        P(None, "tensor"),
        P(),
        P("tensor"),
        P("tensor"),
        P("tensor"),
        P("fsdp", "tensor"),
        P(),
        P("fsdp", "tensor"),
        P("fsdp", "tensor"),
        P("fsdp", "tensor"),
        P(("fsdp", "context"), None),
    )
    out_specs = (
        P(("fsdp", "context"), None),
        P(("fsdp", "context"), None),
        P(),
        P("fsdp", "tensor"),
        P("fsdp", "tensor"),
        P("fsdp", "tensor"),
        P("fsdp", "tensor"),
        P("fsdp", "tensor"),
        P("fsdp", None),
        P("fsdp", "tensor"),
        P(None, "tensor"),
        P(),
        P("tensor"),
        P("tensor"),
        P("tensor"),
        P("fsdp", "tensor"),
        P(),
        P("fsdp", "tensor"),
        P("fsdp", "tensor"),
        P("fsdp", "tensor"),
    )
    return jax.shard_map(
        per_device, mesh=mesh, in_specs=in_specs, out_specs=out_specs, check_vma=False
    )
```

```python
import functools
import math

import jax
import jax.numpy as jnp
from jax import lax
from jax.experimental import pallas as pl
from jax.experimental.pallas import tpu as pltpu
from jax.sharding import PartitionSpec as P

HEAD_DIM = 64
SSM_DIM = 64
STATE = 128
CONV = 4
HALF = 256
WINDOW = 4

epsilon = 1e-05
masked = -1e30
F32 = jnp.float32
BF16 = jnp.bfloat16
exact = lax.Precision.HIGHEST


def dot(left, right, left_dim=1, right_dim=0, precision=None):
    return lax.dot_general(
        left,
        right,
        (((left_dim,), (right_dim,)), ((), ())),
        precision=precision,
        preferred_element_type=F32,
    )


def sigmoid(v):
    return 1.0 / (1.0 + jnp.exp(-v))


def softplus(v):
    return jnp.maximum(v, 0.0) + jnp.log1p(jnp.exp(-jnp.abs(v)))


def swap_halves(v):
    half = v.shape[1] // 2
    return jnp.concatenate([v[:, half:], v[:, :half]], axis=1)


def iotas(rows, columns):
    return (
        lax.broadcasted_iota(jnp.int32, (rows, columns), 0),
        lax.broadcasted_iota(jnp.int32, (rows, columns), 1),
    )


def state_scale(last_row, carry_last, heads):
    pieces = [
        jnp.broadcast_to(last_row[:, h * SSM_DIM : h * SSM_DIM + 1], (SSM_DIM, STATE))
        for h in range(heads)
    ]
    return jnp.exp(jnp.concatenate(pieces, axis=0)) * carry_last


def block_decays(step_raw, heads_ref, lane_pos, heads):
    rows = step_raw.shape[0]
    inner = heads * SSM_DIM
    raw = step_raw + heads_ref[0:1, :inner]
    step = softplus(raw)
    rate = step * jnp.exp(heads_ref[1:2, :inner])
    row, col = iotas(rows, rows)
    lower = jnp.where(col <= row, 1.0, 0.0).astype(F32)
    totals = dot(lower, -rate, precision=exact)
    last_row = totals[rows - 1 : rows]
    pos_last = lane_pos[rows - 1 : rows, 0:1]
    local = lax.broadcasted_iota(jnp.int32, (rows, 1), 0).astype(F32)
    carry_on = (lane_pos[:, 0:1] > local).astype(F32)
    keep_last = (local >= (rows - 1) - pos_last).astype(F32)
    carry_last = (pos_last > rows - 1).astype(F32)
    factor = jnp.exp(totals) * carry_on
    tails = jnp.exp(last_row - totals) * keep_last
    return raw, step, rate, totals, last_row, carry_last, factor, tails


def local_mask(lane_pos, rows):
    row, col = iotas(rows, rows)
    gap = (row - col).astype(F32)
    return (gap >= 0) & (gap <= lane_pos[:, 0:1])


def key_window(block):
    start = jnp.maximum(block - WINDOW, 0)
    return start, (block - start) * HALF


def window_mask(lane_pos, offset, rows, keys):
    row, col = iotas(rows, keys)
    gap = (row - col + offset).astype(F32)
    return (gap >= 0) & (gap <= lane_pos[:, 0:1])


def head_decay(totals, totals_t, h, allowed):
    gap = totals[:, h * SSM_DIM : h * SSM_DIM + 1] - totals_t[h * SSM_DIM : h * SSM_DIM + 1, :]
    return jnp.exp(jnp.where(allowed, gap, masked))


def mixer_forward_kernel(
    order_ref, u_ref, normed_ref, table_ref, heads_ref, taps_ref, ag_ref, y_ref, conv_ref, state_in_ref,
    kv_ref, kept_ref, ordered_ref, ext, state, keyval,
):
    block = pl.program_id(0)
    heads = state.shape[0] // SSM_DIM
    inner = heads * SSM_DIM
    width = ext.shape[1]
    rows = u_ref.shape[0]

    @pl.when(block == 0)
    def _():
        ext[0:8, :] = jnp.zeros((8, width), F32)
        state[...] = jnp.zeros(state.shape, F32)
        keyval[...] = jnp.zeros(keyval.shape, BF16)

    lane_pos = table_ref[:, 128:256]
    cosine = table_ref[:, 0:64]
    sine = table_ref[:, 64:128]
    q_at = inner
    u = u_ref[:, :width].astype(F32)
    ext[8 : 8 + rows, :] = u
    conv = u * taps_ref[CONV - 1 : CONV, :]
    for back in range(1, CONV):
        reach = lane_pos[:, 0:1] >= back
        shifted = ext[8 - back : 8 - back + rows, :]
        conv = conv + jnp.where(reach, shifted, 0.0) * taps_ref[CONV - 1 - back : CONV - back, :]
    ext[0:8, :] = u[rows - 8 : rows]
    act = conv * sigmoid(conv)
    ssm_x = act[:, :inner].astype(BF16)
    ssm_b = act[:, 256:384].astype(BF16)
    ssm_c = act[:, 384:512].astype(BF16)
    conv_ref[:, 0:256] = conv[:, 0:256]
    conv_ref[:, 256:512] = conv[:, 256:512]
    query = u[:, q_at : q_at + HEAD_DIM]
    query = (query * cosine + swap_halves(query) * sine).astype(BF16)
    conv_ref[:, q_at : q_at + HEAD_DIM] = query.astype(F32)
    key = u_ref[:, 512 + inner : 512 + inner + HEAD_DIM].astype(F32)
    key = key * cosine + swap_halves(key) * sine
    value = u_ref[:, 768 + inner : 768 + inner + HEAD_DIM].astype(F32)
    pair = jnp.concatenate([key, value], axis=1).astype(BF16)
    kv_ref[...] = pair
    keyval[pl.ds(pl.multiple_of(block * rows, rows), rows), :] = pair
    first, offset = key_window(block)
    span = (WINDOW + 1) * HALF
    window = keyval[pl.ds(pl.multiple_of(first * rows, rows), span), :]
    scores = dot(query * 0.125, window[:, :HEAD_DIM], 1, 1)
    scores = jnp.where(window_mask(lane_pos, offset, rows, span), scores, masked)
    highest = jnp.max(scores, axis=1, keepdims=True)
    weights = jnp.exp(scores - highest)
    total = jnp.sum(weights, axis=1, keepdims=True)
    probs = (weights * (1.0 / total)).astype(BF16)
    attended = dot(probs, window[:, HEAD_DIM:])
    _, step, _, totals, last_row, carry_last, factor, tails = block_decays(
        u_ref[:, 768 : 768 + inner].astype(F32), heads_ref, lane_pos, heads
    )
    totals_t = totals.T
    allowed = local_mask(lane_pos, rows)
    cross = dot(ssm_c, ssm_b, 1, 1)
    x_f = ssm_x.astype(F32)
    stepped = step * x_f
    stepped_low = stepped.astype(BF16)
    parts = []
    for h in range(heads):
        lanes = slice(h * SSM_DIM, (h + 1) * SSM_DIM)
        mix = (head_decay(totals, totals_t, h, allowed) * cross).astype(BF16)
        parts.append(dot(mix, stepped_low[:, lanes]))
    held = state[...]
    state_in_ref[...] = held
    y_pure = jnp.concatenate(parts, axis=1) + factor * dot(ssm_c, held.astype(BF16), 1, 1)
    tailed = (tails * stepped_low.astype(F32)).astype(BF16)
    state[...] = state_scale(last_row, carry_last, heads) * held + dot(tailed, ssm_b, 0, 0)
    y_ref[:, 0:256] = jnp.concatenate(
        [y_pure, jnp.broadcast_to(highest + jnp.log(total), (rows, HEAD_DIM))], axis=1
    )
    y_ref[:, 256:512] = jnp.concatenate([u_ref[:, 768 : 768 + inner], attended], axis=1)
    ordered_ref[...] = normed_ref[...]
    kept_ref[...] = u_ref[:, 0:768].astype(BF16)
    y_full = y_pure + heads_ref[2:3, :inner] * x_f
    gate = u_ref[:, 512 : 512 + inner].astype(F32)
    gated = y_full * (gate * sigmoid(gate))
    ag_ref[...] = jnp.concatenate([gated, attended], axis=1).astype(BF16)


def attention_backward(
    block, dag, table_ref, heads_ref, y_ref, conv_ref, kept_ref, kv_ref, dkey_t, dvalue_t,
):
    inner = dag.shape[1] - HEAD_DIM
    rows = dag.shape[0]
    lane_pos = table_ref[:, 128:256]
    cosine = table_ref[:, 0:64]
    sine = table_ref[:, 64:128]
    first, offset = key_window(block)
    span = (WINDOW + 1) * HALF
    begin = pl.multiple_of(first * rows, rows)
    window = kv_ref[pl.ds(begin, span), :]
    keys = window[:, :HEAD_DIM]
    values = window[:, HEAD_DIM:]
    query = conv_ref[:, inner : inner + HEAD_DIM] * 0.125
    query_low = query.astype(BF16)
    datt = dag[:, inner : inner + HEAD_DIM]
    datt_f = datt.astype(F32)
    lse = y_ref[:, inner : inner + 1]
    scores = dot(query_low, keys, 1, 1)
    allowed_all = window_mask(lane_pos, offset, rows, span)
    probs = jnp.exp(jnp.where(allowed_all, scores, masked) - lse)
    inward = jnp.sum(datt_f * y_ref[:, 256 + inner : 256 + inner + HEAD_DIM], axis=1, keepdims=True)
    dscores = (probs * (dot(datt, values, 1, 1) - inward)).astype(BF16)
    dquery = dot(dscores, keys) * 0.125
    dkey_t[:, pl.ds(begin, span)] += dot(query.T.astype(BF16), dscores)
    dvalue_t[:, pl.ds(begin, span)] += dot(datt_f.T.astype(BF16), probs.astype(BF16))
    here = pl.ds(pl.multiple_of(block * rows, rows), rows)
    dkey = dkey_t[:, here].T
    dvalue = dvalue_t[:, here].T
    dquery = dquery * cosine - swap_halves(dquery) * sine
    dkey = dkey * cosine - swap_halves(dkey) * sine
    conv = conv_ref[:, :inner]
    ssm_x = (conv * sigmoid(conv)).astype(BF16).astype(F32)
    gate = kept_ref[:, 512 : 512 + inner].astype(F32)
    sig = sigmoid(gate)
    dgated = dag[:, :inner].astype(F32)
    y_full = y_ref[:, :inner] + heads_ref[2:3, :inner] * ssm_x
    dgate = dgated * y_full * (sig * (1.0 + gate * (1.0 - sig)))
    return jnp.concatenate([dgate, dquery, dkey, dvalue], axis=1).astype(BF16)


def recurrence_backward(
    dag, table_ref, heads_ref, taps_ref, y_ref, conv_ref, kept_ref, state_in_ref, state_out, stats_ref,
    dext, dpos, dstate,
):
    heads = dstate.shape[0] // SSM_DIM
    inner = heads * SSM_DIM
    rows = dag.shape[0]
    lane_pos = table_ref[:, 128:256]
    conv = conv_ref[...]
    gate_conv = sigmoid(conv)
    act = conv * gate_conv
    dact = gate_conv * (1.0 + conv * (1.0 - gate_conv))
    ssm_x = act[:, :inner].astype(BF16)
    ssm_b = act[:, 256:384].astype(BF16)
    ssm_c = act[:, 384:512].astype(BF16)
    x_f = ssm_x.astype(F32)
    raw, step, rate, totals, last_row, carry_last, factor, tails = block_decays(
        y_ref[:, 256 : 256 + inner], heads_ref, lane_pos, heads
    )
    totals_t = totals.T
    allowed = local_mask(lane_pos, rows)
    cross = dot(ssm_c, ssm_b, 1, 1)
    gate = kept_ref[:, 512 : 512 + inner].astype(F32)
    sig = sigmoid(gate)
    y_pure = y_ref[:, :inner]
    dgated = dag[:, :inner].astype(F32)
    skip = heads_ref[2:3, :inner]
    dy = dgated * (gate * sig)
    dy_low = dy.astype(BF16)
    dy_r = dy_low.astype(F32)
    dy_t = dy.T.astype(BF16)
    stepped_low = (step * x_f).astype(BF16)
    stepped_r = stepped_low.astype(F32)
    tailed = (tails * stepped_r).astype(BF16)
    dcross = jnp.zeros((rows, rows), F32)
    parts = []
    for h in range(heads):
        lanes = slice(h * SSM_DIM, (h + 1) * SSM_DIM)
        decay = head_decay(totals, totals_t, h, allowed)
        mix = (decay * cross).astype(BF16)
        parts.append(dot(dy_t[lanes, :], mix))
        dcross = dcross + dot(dy_low[:, lanes], stepped_low[:, lanes], 1, 1) * decay
    dstep_x = jnp.concatenate(parts, axis=0).T
    dcross_low = dcross.astype(BF16)
    held = state_in_ref[...].astype(BF16)
    dheld = dstate[...]
    dheld_low = dheld.astype(BF16)
    dfactored = (factor * dy).astype(BF16)
    from_state = dot(ssm_b, dheld_low, 1, 1)
    dssm_c = dot(dcross_low, ssm_b) + dot(dfactored, held)
    dssm_b = dot(dcross_low, ssm_c, 0, 0) + dot(tailed, dheld_low)
    dtotals = dy_r * y_pure - stepped_r * dstep_x - tailed.astype(F32) * from_state
    dstep_x = dstep_x + tails * from_state
    end_term = dot(
        jnp.ones((8, STATE), F32), dheld_low.astype(F32) * state_out[...], 1, 1, exact
    )[0:1]
    row, col = iotas(rows, rows)
    upper = jnp.where(col >= row, 1.0, 0.0).astype(F32)
    drate = -(dot(upper, dtotals, precision=exact) + end_term)
    state_out[...] = state_in_ref[...]
    dstate[...] = state_scale(last_row, carry_last, heads) * dheld + dot(dfactored, ssm_c, 0, 0)
    dssm_x = step * dstep_x + skip * dy
    dstep = x_f * dstep_x + jnp.exp(heads_ref[1:2, :inner]) * drate
    draw = dstep * sigmoid(raw)
    none = jnp.zeros((rows, HEAD_DIM), F32)
    dconv = jnp.concatenate([dssm_x, none, dssm_b, dssm_c], axis=1) * dact
    dext[0:rows, :] = dconv
    dpos[0:rows, :] = lane_pos
    u = kept_ref[:, 0:512].astype(F32)
    du = dconv * taps_ref[CONV - 1 : CONV, :]
    stats_ref[CONV - 1 : CONV, :] += jnp.sum(dconv * u, axis=0, keepdims=True)
    for ahead in range(1, CONV):
        reach = dpos[ahead : ahead + rows, 0:1] >= ahead
        shifted = jnp.where(reach, dext[ahead : ahead + rows, :], 0.0)
        tap = CONV - 1 - ahead
        du = du + shifted * taps_ref[tap : tap + 1, :]
        stats_ref[tap : tap + 1, :] += jnp.sum(shifted * u, axis=0, keepdims=True)
    dext[rows : rows + 8, :] = dconv[0:8]
    dpos[rows : rows + 8, :] = lane_pos[0:8]
    stats_ref[4:5, :inner] += jnp.sum(dy * x_f, axis=0, keepdims=True)
    stats_ref[5:6, :inner] += jnp.sum(draw, axis=0, keepdims=True)
    stats_ref[6:7, :inner] += jnp.sum(drate * rate, axis=0, keepdims=True)
    summed = [
        jnp.sum(draw[:, h * SSM_DIM : (h + 1) * SSM_DIM], axis=1, keepdims=True)
        for h in range(heads)
    ]
    lane = lax.broadcasted_iota(jnp.int32, (rows, HEAD_DIM), 1)
    dstep_all = jnp.zeros((rows, HEAD_DIM), F32)
    for h in range(heads):
        dstep_all = jnp.where(lane == h, summed[h], dstep_all)
    return jnp.concatenate([du[:, :inner], dstep_all, du[:, 256:512]], axis=1).astype(BF16)


def slot_holding(order, block):
    slot = 0
    for k in range(1, order.shape[0]):
        slot = slot + jnp.where(order[k] == block, k, 0)
    return slot


def mixer_forward(u, normed_t, table, head_rows, taps, slot_of):
    count = u.shape[0]
    blocks = count // HALF
    heads = 3
    inner = heads * SSM_DIM
    width = taps.shape[1]
    at_slot = lambda i, order: (slot_holding(order, i), 0)
    in_order = lambda i, slots: (i, 0)
    whole = lambda i, slots: (0, 0)
    return pl.pallas_call(
        mixer_forward_kernel,
        out_shape=(
            jax.ShapeDtypeStruct((count, inner + HEAD_DIM), BF16),
            jax.ShapeDtypeStruct((count, 512), F32),
            jax.ShapeDtypeStruct((count, width), F32),
            jax.ShapeDtypeStruct((blocks * inner, STATE), F32),
            jax.ShapeDtypeStruct((count, 2 * HEAD_DIM), BF16),
            jax.ShapeDtypeStruct((count, 768), BF16),
            jax.ShapeDtypeStruct(normed_t.shape, BF16),
        ),
        grid_spec=pltpu.PrefetchScalarGridSpec(
            num_scalar_prefetch=1,
            grid=(blocks,),
            in_specs=[
                pl.BlockSpec((HALF, u.shape[1]), at_slot),
                pl.BlockSpec((normed_t.shape[0], HALF), lambda i, order: at_slot(i, order)[::-1]),
                pl.BlockSpec((HALF, table.shape[1]), in_order),
                pl.BlockSpec(head_rows.shape, whole),
                pl.BlockSpec(taps.shape, whole),
            ],
            out_specs=(
                pl.BlockSpec((HALF, inner + HEAD_DIM), at_slot),
                pl.BlockSpec((HALF, 512), in_order),
                pl.BlockSpec((HALF, width), in_order),
                pl.BlockSpec((inner, STATE), in_order),
                pl.BlockSpec((HALF, 2 * HEAD_DIM), in_order),
                pl.BlockSpec((HALF, 768), in_order),
                pl.BlockSpec((normed_t.shape[0], HALF), lambda i, order: (0, i)),
            ),
            scratch_shapes=[
                pltpu.VMEM((8 + HALF, width), F32),
                pltpu.VMEM((inner, STATE), F32),
                pltpu.VMEM((count, 2 * HEAD_DIM), BF16),
            ],
        ),
        compiler_params=pltpu.CompilerParams(vmem_limit_bytes=60 << 20),
    )(slot_of, u, normed_t, table, head_rows, taps)


MESH = pl.DeviceIdType.MESH


class Place:
    def __init__(self):
        self.c = lax.axis_index("context")
        self.t = lax.axis_index("tensor")
        count = lax.axis_size("context")
        self.chips = [
            self.c,
            self.c + 1 - 2 * (self.c % 2),
            (self.c + count // 2) % count,
            count - 1 - self.c,
        ]

    def slot(self, mask, sibling=False):
        core = 1 - self.t if sibling else self.t
        return self.chips[mask] * 2 + core

    def target(self, mask):
        if mask == 4:
            return {"tensor": 1 - self.t}
        return {"context": self.chips[mask]}

    def hello(self, line=None):
        barrier = pltpu.get_barrier_semaphore()
        targets = [self.target(mask) for mask in (1, 2, 4)]
        if line is not None:
            targets += [line.target(step) for step in range(1, line.count)]
        for target in targets:
            pl.semaphore_signal(barrier, inc=1, device_id=target, device_id_type=MESH)
        return len(targets)

    def greet(self, line=None):
        pl.semaphore_wait(pltpu.get_barrier_semaphore(), self.hello(line))


class Wire:
    def __init__(self, place, sems):
        self.place = place
        self.sems = sems
        self.sent = []

    def copy(self, source, target, index, mask):
        return pltpu.make_async_remote_copy(
            src_ref=source,
            dst_ref=target,
            send_sem=self.sems.at[0, index],
            recv_sem=self.sems.at[1, index],
            device_id=self.place.target(mask),
            device_id_type=MESH,
        )

    def send(self, source, target, index, mask):
        def made():
            here = source() if callable(source) else source
            there = target() if callable(target) else target
            return self.copy(here, there, index, mask)

        made().start()
        self.sent.append(made)

    def arrive(self, target, index, mask):
        self.copy(target, target, index, mask).wait_recv()

    def finish(self):
        for made in self.sent:
            made().wait_send()
        self.sent = []


ROWS = HALF
PART = HALF // 2
TOP, END = pl.ds(0, PART), pl.ds(PART, PART)
SCATTER_SEMS = 10
GATHER_SEMS = 14


def scatter_scratch(columns):
    return [
        pltpu.VMEM((4, ROWS, columns), BF16),
        pltpu.VMEM((4, ROWS, columns), BF16),
        pltpu.VMEM((6, PART, columns), BF16),
        pltpu.VMEM((ROWS, columns), F32),
        pltpu.SemaphoreType.DMA((2, SCATTER_SEMS)),
    ]


SCATTER_ORDER = (3, 1, 2, 0)


class Scatter:
    def __init__(self, place, scratch):
        self.place = place
        self.core_in, self.out, self.chip_in, self.kept, sems = scratch
        self.wire = Wire(place, sems)

    def to_core(self, mask, source):
        index = SCATTER_ORDER.index(mask)
        self.wire.send(source, self.core_in.at[index], index, 4)

    def from_core(self, mask):
        index = SCATTER_ORDER.index(mask)
        self.wire.arrive(self.core_in.at[index], index, 4)
        return self.core_in[index].astype(F32)

    def first(self, mine, total, between=None):
        wire, out, kept = self.wire, self.out, self.kept
        both = mine(3) + self.from_core(3)
        out[0] = both.astype(BF16)
        wire.send(lambda: out.at[0, TOP], lambda: self.chip_in.at[0], 4, 1)
        wire.send(lambda: out.at[0, END], lambda: self.chip_in.at[1], 5, 2)
        both = mine(1) + self.from_core(1)
        out[1] = both.astype(BF16)
        wire.send(lambda: out.at[1, TOP], lambda: self.chip_in.at[2], 6, 1)
        kept[END] = both[PART:]
        both = mine(2) + self.from_core(2)
        out[2] = both.astype(BF16)
        wire.send(lambda: out.at[2, END], lambda: self.chip_in.at[3], 7, 2)
        kept[TOP] = both[:PART]
        total[...] = mine(0) + self.from_core(0)

    def second(self):
        wire, out, kept, came = self.wire, self.out, self.kept, self.chip_in
        wire.arrive(came.at[0], 4, 1)
        out[3, TOP] = (kept[TOP] + came[0].astype(F32)).astype(BF16)
        wire.send(lambda: out.at[3, TOP], lambda: came.at[4], 8, 2)
        wire.arrive(came.at[1], 5, 2)
        out[3, END] = (kept[END] + came[1].astype(F32)).astype(BF16)
        wire.send(lambda: out.at[3, END], lambda: came.at[5], 9, 1)

    def last(self, total):
        wire, came = self.wire, self.chip_in
        wire.arrive(came.at[2], 6, 1)
        wire.arrive(came.at[4], 8, 2)
        total[TOP] += came[2].astype(F32) + came[4].astype(F32)
        wire.arrive(came.at[3], 7, 2)
        wire.arrive(came.at[5], 9, 1)
        total[END] += came[3].astype(F32) + came[5].astype(F32)
        wire.finish()


class Gather:
    def __init__(self, place, whole, sems, rows=ROWS, cores=True):
        self.place = place
        self.whole = whole
        self.size = rows
        self.cores = cores
        self.wire = Wire(place, sems)

    def rows(self, mask, sibling=False, half=None):
        place, size = self.place, self.size
        block = place.slot(mask, sibling) if self.cores else place.chips[mask]
        begin = block * size
        if half is None:
            return self.whole.at[pl.ds(pl.multiple_of(begin, size), size)]
        return self.whole.at[pl.ds(pl.multiple_of(begin + half * (size // 2), size // 2), size // 2)]

    def both(self, mask, sibling=False, half=None):
        block = functools.partial(self.rows, mask, sibling, half)
        return block, block

    def start(self, core=True):
        wire = self.wire
        for half, mask, index in ((0, 1, 0), (1, 2, 1), (1, 1, 2), (0, 2, 3)):
            wire.send(*self.both(0, half=half), index, mask)
        if self.cores and core:
            wire.send(*self.both(0), 6, 4)

    def relay(self):
        wire = self.wire
        wire.arrive(self.rows(1, half=0), 0, 1)
        wire.send(*self.both(1, half=0), 4, 2)
        wire.arrive(self.rows(2, half=1), 1, 2)
        wire.send(*self.both(2, half=1), 5, 1)

    def near(self):
        wire = self.wire
        wire.arrive(self.rows(1, half=1), 2, 1)
        if self.cores:
            wire.send(*self.both(1), 7, 4)
        wire.arrive(self.rows(2, half=0), 3, 2)
        if self.cores:
            wire.send(*self.both(2), 8, 4)

    def far(self):
        wire = self.wire
        wire.arrive(self.rows(3, half=0), 4, 2)
        wire.arrive(self.rows(3, half=1), 5, 1)
        if self.cores:
            wire.send(*self.both(3), 9, 4)

    def core(self, mask):
        index = (6, 7, 8, 9)[mask]
        self.wire.arrive(self.rows(mask, sibling=True), index, 4)

    def finish(self):
        self.wire.finish()


class Line:
    def __init__(self):
        self.f = lax.axis_index("fsdp")
        self.count = lax.axis_size("fsdp")

    def target(self, step):
        return {"fsdp": (self.f + step) % self.count}

    def copy(self, source, target, sems, step):
        return pltpu.make_async_remote_copy(
            src_ref=source,
            dst_ref=target,
            send_sem=sems.at[0, step],
            recv_sem=sems.at[1, step],
            device_id=self.target(step),
            device_id_type=MESH,
        )


class LineGather:
    def __init__(self, line, whole, sems):
        self.line = line
        self.whole = whole
        self.sems = sems
        self.size = whole.shape[0] // line.count

    def rows(self, block):
        return self.whole.at[pl.ds(pl.multiple_of(block * self.size, self.size), self.size)]

    def copy(self, block, way, step):
        toward = self.line.f + 1 if way == 0 else self.line.f - 1
        return pltpu.make_async_remote_copy(
            src_ref=self.rows(block),
            dst_ref=self.rows(block),
            send_sem=self.sems.at[way, 0, step],
            recv_sem=self.sems.at[way, 1, step],
            device_id={"fsdp": toward},
            device_id_type=MESH,
        )

    def step(self, number, arrive=True):
        f, last = self.line.f, self.line.count - 1
        for way in (0, 1):
            block = f - number if way == 0 else f + number
            there = block >= 0 if way == 0 else block <= last
            goes_on = f < last if way == 0 else f > 0

            @pl.when(there)
            def _():
                if number > 0:
                    self.copy(block, way, number).wait_recv()

                @pl.when(goes_on)
                def _():
                    self.copy(block, way, number + 1).start()

    def finish(self):
        f, last = self.line.f, self.line.count - 1
        for number in range(self.line.count - 1):
            for way in (0, 1):
                block = f - number if way == 0 else f + number
                there = block >= 0 if way == 0 else block <= last
                goes_on = f < last if way == 0 else f > 0

                @pl.when(there & goes_on)
                def _():
                    self.copy(block, way, number + 1).wait_send()


def line_sems(count):
    return pltpu.SemaphoreType.DMA((2, 2, count + 1))


def opening_kernel(
    tokens_ref, cot_ref, in_x_ref, query_ref, bc_ref, gate_ref, keyval_ref, step_ref, ssm_ref, attn_ref,
    gain_ref, segments_ref, conv_x_ref, conv_bc_ref, bias_ref, decay_ref, skip_ref,
    normed_t_out, u_out, w_out, wout_out, cot_out, table_out, heads_ref, taps_ref,
    x_all, cot_all, normed, normed_t, u, weights_all, wout_all, table, wide,
    x_sems, cot_sems, w_sems, out_sems, local_sems, block_sems,
):
    place = Place()
    line = Line()
    rows_x = Gather(place, x_all, x_sems)
    rows_cot = Gather(place, cot_all, cot_sems)
    weights = LineGather(line, weights_all, w_sems)
    weights_out = LineGather(line, wout_all, out_sems)
    chips = lax.axis_size("context")
    share = in_x_ref.shape[0]
    heads = step_ref.shape[0] // chips
    inner = heads * SSM_DIM
    chip_rows = pl.ds(pl.multiple_of(place.c * 2 * ROWS, 2 * ROWS), 2 * ROWS)
    waiting = []

    def local(source, target, sem):
        made = pltpu.make_async_copy(source, target, sem)
        made.start()
        waiting.append(made)
        return made

    greetings = place.hello(line)
    own_x = pltpu.make_async_copy(tokens_ref, x_all.at[chip_rows], local_sems.at[0])
    own_x.start()
    own_cot = pltpu.make_async_copy(cot_ref, cot_all.at[chip_rows], local_sems.at[1])
    own_cot.start()
    mine = pl.ds(pl.multiple_of(line.f * share, share), share)
    heads_ref[...] = jnp.zeros(heads_ref.shape, F32)
    taps_ref[...] = jnp.zeros(taps_ref.shape, F32)
    for k in range(chips):

        @pl.when(place.c == k)
        def _():
            inner_part = slice(k * inner, (k + 1) * inner)
            head_part = slice(k * HEAD_DIM, (k + 1) * HEAD_DIM)
            weights_all[mine, 0:256] = jnp.concatenate(
                [gate_ref[:, inner_part], query_ref[:, head_part]], axis=1
            )
            weights_all[mine, 384 : 384 + inner] = in_x_ref[:, inner_part]
            wout_all[mine, :] = jnp.concatenate(
                [ssm_ref[:, inner_part], attn_ref[:, head_part]], axis=1
            )
            taps_ref[0:CONV, :inner] = conv_x_ref[:, inner_part]
            for h in range(heads):
                lane = slice(k * heads + h, k * heads + h + 1)
                for row, source in enumerate((bias_ref, decay_ref, skip_ref)):
                    heads_ref[row : row + 1, h * SSM_DIM : (h + 1) * SSM_DIM] = jnp.broadcast_to(
                        source[:, lane], (1, SSM_DIM)
                    )

    taps_ref[0:CONV, 256:512] = conv_bc_ref[...]
    head, column = iotas(step_ref.shape[0], HEAD_DIM)
    chosen = (head == column + place.c * heads) & (column < heads)
    steps = dot(step_ref[...], jnp.where(chosen, 1.0, 0.0).astype(BF16), 0, 0)
    weights_all[mine, 384 + inner : 640] = steps.astype(BF16)
    weights_all[mine, 256:384] = keyval_ref[...]
    weights_all[mine, 640:896] = bc_ref[...]
    own_x.wait()
    own_cot.wait()
    pl.semaphore_wait(pltpu.get_barrier_semaphore(), greetings)
    weights.step(0)
    rows_x.start(core=False)

    def norm(slot):
        rows = slot_rows(slot)
        x = x_all[rows, :].astype(F32)
        normed[rows, :] = (x * norm_scale(x) * gain_ref[...]).astype(BF16)
        columns = pl.ds(pl.multiple_of(slot * ROWS, ROWS), ROWS)
        normed_t[:, columns] = normed[rows, :].T

    norm(place.slot(0))
    norm(place.slot(0, True))

    numbers = segments_ref[...]
    bounds = [
        jnp.sum(jnp.where(numbers < k, 1.0, 0.0), axis=1, keepdims=True) for k in (1, 2)
    ]
    count = table.shape[0]
    lane = lax.broadcasted_iota(jnp.int32, (8, 128), 1)[0:1]
    power = -(lane % (HEAD_DIM // 2)).astype(F32) / (HEAD_DIM // 2)
    freqs = jnp.exp(power * math.log(10000.0))
    phase = jnp.where(lane < HEAD_DIM, math.pi / 2, 0.0)
    sign = jnp.where((lane >= HEAD_DIM) & (lane < HEAD_DIM + HEAD_DIM // 2), -1.0, 1.0)

    def angles(block, carry):
        row = lax.broadcasted_iota(jnp.int32, (ROWS, 128), 0) + block * ROWS
        row = row.astype(F32)
        start = jnp.where(row >= bounds[0], bounds[0], 0.0)
        start = jnp.where(row >= bounds[1], bounds[1], start)
        pos = row - start
        here = slot_rows(block)
        table[here, 0:128] = jnp.sin(pos * freqs + phase) * sign
        table[here, 128:256] = pos
        return carry

    blocks = count // ROWS
    rows_x.relay()
    rows_cot.start(core=False)
    lax.fori_loop(0, blocks // 2, angles, 0)
    weights.step(1)
    lax.fori_loop(blocks // 2, blocks, angles, 0)
    local(table, table_out, local_sems.at[2])
    rows_x.near()
    norm(place.slot(1))
    norm(place.slot(2))
    rows_cot.relay()
    for number in range(2, line.count - 1):
        weights.step(number)
    rows_x.far()
    norm(place.slot(3))
    for mask in (1, 2, 3):
        rows_x.core(mask)
        norm(place.slot(mask, True))
    weights_out.step(0)
    rows_cot.near()
    weights.step(line.count - 1)
    local(weights_all, w_out, local_sems.at[3])
    local(normed_t, normed_t_out, local_sems.at[6])
    row, column = iotas(HEAD_DIM, inner)
    copies = jnp.where(column // SSM_DIM == row, 1.0, 0.0).astype(BF16)
    wide[:, 0:256] = jnp.concatenate(
        [weights_all[:, 384 : 384 + inner], weights_all[:, inner:256]], axis=1
    )
    wide[:, 256:512] = weights_all[:, 640:896]
    wide[:, 512:768] = jnp.concatenate([weights_all[:, :inner], weights_all[:, 256:320]], axis=1)
    wide[:, 768:1024] = jnp.concatenate(
        [
            dot(weights_all[:, 384 + inner : 640], copies),
            weights_all[:, 320:384].astype(F32),
        ],
        axis=1,
    ).astype(BF16)

    def project(slot):
        rows = pl.ds(slot * ROWS, ROWS)
        u[rows, :] = dot(normed[rows, :], wide[...])
        local(u.at[rows], u_out.at[rows], block_sems.at[0, slot])

    for slot in range(blocks // 2):
        project(slot)
    weights_out.step(1)
    rows_cot.far()
    for slot in range(blocks // 2, blocks):
        project(slot)
    for number in range(2, line.count):
        weights_out.step(number)
    local(wout_all, wout_out, local_sems.at[4])
    for mask in (1, 2, 3):
        rows_cot.core(mask)
    local(cot_all, cot_out, local_sems.at[5])
    for made in waiting:
        made.wait()
    rows_x.finish()
    rows_cot.finish()
    weights.finish()
    weights_out.finish()


def opening(tokens, cotangent, weights, gain, segments, taps, by_head):
    fsdp = lax.axis_size("fsdp")
    model = tokens.shape[1]
    count = segments.shape[1]
    blocks = count // ROWS
    vmem = pl.BlockSpec(memory_space=pltpu.VMEM)
    hbm = pl.BlockSpec(memory_space=pl.ANY)
    shape = jax.ShapeDtypeStruct
    dma = pltpu.SemaphoreType.DMA
    buffers = [
        ((model, count), BF16),
        ((count, 1024), F32),
        ((model, 896), BF16),
        ((model, 256), BF16),
        ((count, model), BF16),
        ((count, 256), F32),
    ]
    kept = [buffers[k] for k in (0, 1, 2, 3, 5)]
    return pl.pallas_call(
        opening_kernel,
        out_shape=tuple(shape(*one) for one in buffers) + (shape((8, 256), F32), shape((8, 512), F32)),
        in_specs=[hbm] * 2 + [vmem] * 15,
        out_specs=(hbm,) * 6 + (vmem,) * 2,
        scratch_shapes=[pltpu.VMEM((count, model), BF16)] * 3
        + [pltpu.VMEM(*one) for one in kept]
        + [
            pltpu.VMEM((model, 1024), BF16),
            dma((2, GATHER_SEMS)),
            dma((2, GATHER_SEMS)),
            line_sems(fsdp),
            line_sems(fsdp),
            dma((7,)),
            dma((1, blocks)),
        ],
        compiler_params=pltpu.CompilerParams(
            collective_id=3, has_side_effects=True, vmem_limit_bytes=60 << 20
        ),
        cost_estimate=pl.CostEstimate(
            flops=2 * count * model * 1024, bytes_accessed=30 << 20, transcendentals=count * 128
        ),
    )(
        tokens, cotangent, *weights, gain.reshape(1, -1), segments, *taps,
        *[one.reshape(1, -1) for one in by_head],
    )


def slot_rows(slot):
    return pl.ds(pl.multiple_of(slot * ROWS, ROWS), ROWS)


def norm_scale(values):
    return lax.rsqrt(jnp.mean(values * values, axis=1, keepdims=True) + epsilon)


def middle_kernel(
    ag_ref, wout_ref, gate_ref, up_ref, down_ref, gain_ref, x_hbm, cot_hbm, cot_all_hbm,
    hidden_ref, dag_ref, mixed_ref, dmixed_ref, dgain_ref, down_all_ref, ffn_ref, dout_ref,
    x_ref, cot_ref, cot_all_ref, nffn_ref, dgu_ref, dm_ref, dw_ref, arrived, part, wffn_ref, *scratch,
):
    place = Place()
    first = Scatter(place, scratch[0:5])
    back = Scatter(place, scratch[5:10])
    forth = Gather(place, nffn_ref, scratch[10])
    home = Gather(place, dm_ref, scratch[11])
    hid = hidden_ref.shape[1]
    line = Line()
    weights = LineGather(line, wffn_ref, scratch[12])
    share = gate_ref.shape[0]
    greetings = place.hello(line)
    half = pl.ds(pl.multiple_of(place.t * ROWS, ROWS), ROWS)
    loads = [
        pltpu.make_async_copy(source, target, scratch[14].at[k])
        for k, (source, target) in enumerate(
            ((x_hbm.at[half], x_ref), (cot_hbm.at[half], cot_ref), (cot_all_hbm, cot_all_ref))
        )
    ]
    for made in loads:
        made.start()
    mine = pl.ds(pl.multiple_of(line.f * share, share), share)
    lanes = pl.ds(pl.multiple_of(place.c * hid, hid), hid)
    for k, source in enumerate((gate_ref, up_ref, down_ref)):
        wffn_ref[mine, k * hid : (k + 1) * hid] = source[:, lanes]

    def block(mask, sibling=False):
        return dot(ag_ref[slot_rows(place.slot(mask, sibling)), :], wout_ref[...], 1, 1)

    for mask in SCATTER_ORDER:
        part[slot_rows(place.slot(mask, True)), :] = block(mask, True).astype(BF16)
    pl.semaphore_wait(pltpu.get_barrier_semaphore(), greetings)
    for mask in SCATTER_ORDER:
        first.to_core(mask, part.at[slot_rows(place.slot(mask, True))])
    weights.step(0)
    first.first(block, mixed_ref)
    weights.step(1)
    first.second()
    for made in loads:
        made.wait()
    mixed_ref[...] += x_ref[...].astype(F32)
    first.last(mixed_ref)
    mixed = mixed_ref[...]
    gain = gain_ref[...]
    scale = norm_scale(mixed)
    own = slot_rows(place.slot(0))
    nffn_ref[own, :] = (mixed * scale * gain).astype(BF16)
    forth.start()
    for number in range(2, line.count):
        weights.step(number)

    def work(slot):
        rows = slot_rows(slot)
        normed = nffn_ref[rows, :]
        gate_up = dot(normed, wffn_ref[:, : 2 * hid])
        dhidden = dot(cot_all_ref[rows, :], wffn_ref[:, 2 * hid :]).astype(BF16).astype(F32)
        gate, up = gate_up[:, :hid], gate_up[:, hid:]
        sig = sigmoid(gate)
        silu = gate * sig
        dgate = dhidden * up * (sig * (1.0 + gate * (1.0 - sig)))
        hidden_ref[rows, :] = (silu * up).astype(BF16)
        dgu_ref[rows, :hid] = dgate.astype(BF16)
        dgu_ref[rows, hid:] = (dhidden * silu).astype(BF16)
        part[rows, :] = dot(dgu_ref[rows, :], wffn_ref[:, : 2 * hid], 1, 1).astype(BF16)

    def hand_over(mask):
        slot = place.slot(mask, True)
        work(slot)
        back.to_core(mask, part.at[slot_rows(slot)])

    work(place.slot(0))
    forth.relay()
    forth.core(0)
    hand_over(0)
    forth.near()
    forth.core(1)
    hand_over(1)
    forth.core(2)
    hand_over(2)
    work(place.slot(1))
    forth.far()
    work(place.slot(2))
    forth.core(3)
    hand_over(3)
    work(place.slot(3))
    forth.finish()

    def ready(mask):
        return part[slot_rows(place.slot(mask)), :].astype(F32)

    back.first(ready, dmixed_ref)

    columns = (pl.ds(0, 2 * hid), pl.ds(2 * hid, hid))
    line_sent = []

    def line_copy(piece, step):
        rows = pl.ds(pl.multiple_of((line.f + step) % line.count * share, share), share)
        return line.copy(
            dw_ref.at[rows, columns[piece]],
            arrived.at[step, :, columns[piece]],
            scratch[13].at[piece],
            step,
        )

    def send_piece(piece, left, right):
        quarter = dw_ref.shape[0] // 4
        for k in range(4):
            rows = slice(k * quarter, (k + 1) * quarter)
            dw_ref[rows, columns[piece]] = dot(left[:, rows], right[...], 0, 0).astype(BF16)
        for step in range(1, line.count):
            made = line_copy(piece, step)
            made.start()
            line_sent.append(made)

    send_piece(1, cot_all_ref, hidden_ref)
    back.second()
    send_piece(0, nffn_ref, dgu_ref)
    back.last(dmixed_ref)
    dnffn = dmixed_ref[...]
    mixed = mixed_ref[...]
    scale = norm_scale(mixed)
    spread = dnffn * gain
    pull = jnp.mean(spread * mixed, axis=1, keepdims=True)
    dgain_ref[...] = jnp.broadcast_to(
        jnp.sum(dnffn * mixed * scale, axis=0, keepdims=True), dgain_ref.shape
    )
    dmixed = cot_ref[...].astype(F32) + scale * (spread - mixed * (scale * scale * pull))
    dmixed_ref[...] = dmixed
    dm_ref[own, :] = dmixed.astype(BF16)
    home.start()

    def pull_back(slot):
        rows = slot_rows(slot)
        dag_ref[rows, :] = dot(dm_ref[rows, :], wout_ref[...]).astype(BF16)

    pull_back(place.slot(0))
    home.relay()
    home.core(0)
    pull_back(place.slot(0, True))
    home.near()
    pull_back(place.slot(1))
    pull_back(place.slot(2))
    home.far()
    pull_back(place.slot(3))
    for mask in (1, 2, 3):
        home.core(mask)
        pull_back(place.slot(mask, True))
    dout_ref[...] = dot(dm_ref[...], ag_ref[...], 0, 0).astype(BF16)
    down_all_ref[...] = wffn_ref[:, 2 * hid :]
    for piece in (1, 0):
        sums = dw_ref[mine, columns[piece]].astype(F32)
        for step in range(1, line.count):
            line_copy(piece, step).wait_recv()
            sums = sums + arrived[step, :, columns[piece]].astype(F32)
        ffn_ref[:, columns[piece]] = sums.astype(BF16)
    for made in line_sent:
        made.wait_send()
    home.finish()
    weights.finish()


def middle(ag, wout, weights, x_own, cot_own, cot_all, gain):
    count, model = cot_all.shape
    hid = weights[0].shape[1] // lax.axis_size("context")
    columns = ag.shape[1]
    vmem = pl.BlockSpec(memory_space=pltpu.VMEM)
    hbm = pl.BlockSpec(memory_space=pl.ANY)
    shape = jax.ShapeDtypeStruct
    return pl.pallas_call(
        middle_kernel,
        out_shape=(
            shape((count, hid), BF16),
            shape((count, columns), BF16),
            shape((ROWS, model), F32),
            shape((ROWS, model), F32),
            shape((8, model), F32),
            shape((model, hid), BF16),
            shape((weights[0].shape[0], 3 * hid), BF16),
            shape((model, columns), BF16),
        ),
        in_specs=[vmem] * 6 + [hbm] * 3,
        out_specs=(vmem,) * 8,
        scratch_shapes=[
            pltpu.VMEM((ROWS, model), BF16),
            pltpu.VMEM((ROWS, model), BF16),
            pltpu.VMEM((count, model), BF16),
            pltpu.VMEM((count, model), BF16),
            pltpu.VMEM((count, 2 * hid), BF16),
            pltpu.VMEM((count, model), BF16),
            pltpu.VMEM((model, 3 * hid), BF16),
            pltpu.VMEM((lax.axis_size("fsdp"), weights[0].shape[0], 3 * hid), BF16),
            pltpu.VMEM((count, model), BF16),
            pltpu.VMEM((model, 3 * hid), BF16),
        ]
        + scatter_scratch(model)
        + scatter_scratch(model)
        + [pltpu.SemaphoreType.DMA((2, GATHER_SEMS))] * 2
        + [line_sems(lax.axis_size("fsdp")), pltpu.SemaphoreType.DMA((2, 2, lax.axis_size("fsdp"))), pltpu.SemaphoreType.DMA((3,))],
        compiler_params=pltpu.CompilerParams(
            collective_id=1, has_side_effects=True, vmem_limit_bytes=60 << 20
        ),
        cost_estimate=pl.CostEstimate(
            flops=20 * count * model * hid, bytes_accessed=40 << 20, transcendentals=count * hid
        ),
    )(ag, wout, *weights, gain.reshape(1, -1), x_own, cot_own, cot_all)


BACK_INPUTS = 5
EARLY = 384


def closing_kernel(
    pick_ref, dag_ref, kv_ref, heads_ref, taps_ref, dmixed_ref, mixed_ref, tokens_ref, gain_ref, ffn_ref,
    dgain_ref, dout_ref, table_hbm, y_hbm, conv_hbm, kept_hbm, states_hbm, normed_t_hbm, w_hbm,
    hidden_hbm, down_hbm,
    grad_ref, out_ref, early_ref, last_ref, mids_ref, outs_ref, small_ref,
    table, y, conv, kept, states, normed_t, w, hidden, down,
    du, dw_sum, dw, arrived, arrived_out, total, part, bc_out, bc_in, small_in,
    stats, dext, dpos, dstate, state_out, dkey_t, dvalue_t, *scratch,
):
    place = Place()
    line = Line()
    back = Scatter(place, scratch[0:5])
    final = Scatter(place, scratch[5:10])
    share = ffn_ref.shape[0]
    last_all = Gather(place, last_ref, scratch[10], share, False)
    early_all = Gather(place, early_ref, scratch[20], share, False)
    mid_all = Gather(place, mids_ref, scratch[11], share, False)
    out_all = Gather(place, outs_ref, scratch[12], share, False)
    small_rows = small_in.shape[1]
    small_all = Gather(place, small_ref, scratch[13], small_rows)
    line_sems_, small_sems, out_sems, pair_sems, load_sems, block_sems = scratch[14:20]
    pair = Wire(place, pair_sems)
    greetings = place.hello(line)
    sent = []
    loads = [
        pltpu.make_async_copy(source, target, load_sems.at[k])
        for k, (source, target) in enumerate(
            ((hidden_hbm, hidden), (down_hbm, down), (normed_t_hbm, normed_t), (w_hbm, w))
        )
    ]
    blocks = du.shape[0] // ROWS
    streams = ((table_hbm, table), (y_hbm, y), (conv_hbm, conv), (kept_hbm, kept), (states_hbm, states))

    def fetch(block, buffer):
        copies = []
        for k, (source, target) in enumerate(streams):
            size = target.shape[1]
            begin = pl.multiple_of(block * size, size)
            copies.append(
                pltpu.make_async_copy(
                    source.at[pl.ds(begin, size)], target.at[buffer], block_sems.at[buffer, k]
                )
            )
        return copies

    for made in fetch(blocks - 1, 0) + loads:
        made.start()
    mids_ref[pl.ds(pl.multiple_of(place.c * share, share), share), :] = ffn_ref[...]
    width = dext.shape[1]
    dext[ROWS : ROWS + 8, :] = jnp.zeros((8, width), F32)
    dpos[ROWS : ROWS + 8, :] = jnp.full((8, dpos.shape[1]), -1.0, F32)
    for ref in (dstate, state_out, dkey_t, dvalue_t, stats, dw_sum):
        ref[...] = jnp.zeros(ref.shape, F32)
    def out_block(mask, sibling=False):
        return dot(hidden[slot_rows(place.slot(mask, sibling)), :], down[...], 1, 1)

    here = pl.ds(pl.multiple_of(place.c * share, share), share)
    own = pl.ds(pl.multiple_of(line.f * share, share), share)
    half = pl.ds(pl.multiple_of(place.t * ROWS, ROWS), ROWS)

    def my_half(ref):
        return lambda: ref.at[pl.ds(pl.multiple_of(place.t * ROWS, ROWS), ROWS)]

    def collect_out():
        sums = dout_ref[own, :].astype(F32)
        for step in range(1, line.count):
            line.copy(arrived_out.at[step], arrived_out.at[step], out_sems, step).wait_recv()
            sums = sums + arrived_out[step].astype(F32)
        outs_ref[here, :] = sums.astype(BF16)
        out_all.start()

    def finish_out():
        total[...] += mixed_ref[...]
        final.last(total)
        out_ref[half, :] = total[...].astype(BF16)
        pair.send(my_half(out_ref), my_half(out_ref), 1, 4)

    def picked(source, row):
        marks = pick_ref[pl.ds(pl.multiple_of(row * 8, 8), 8), 0:1].astype(BF16)
        found = source[0:ROWS, :] * marks[0:1]
        for k in range(1, blocks):
            found = found + source[k * ROWS : (k + 1) * ROWS, :] * marks[k : k + 1]
        return found

    def prefetch(block, buffer):
        for made in fetch(block, buffer):
            made.start()

    def await_block(block, buffer):
        for made in fetch(block, buffer):
            made.wait()

    def happen(number, events):
        for when, actions in events.items():

            @pl.when(number == when)
            def _():
                for action in actions:
                    action()

    def early_turn(number, carry):
        block = blocks - 1 - number
        buffer = number % 2
        await_block(block, buffer)
        prefetch((block + blocks - 1) % blocks, 1 - buffer)
        grads = attention_backward(
            block, picked(dag_ref, block), table.at[buffer], heads_ref, y.at[buffer], conv.at[buffer],
            kept.at[buffer], kv_ref, dkey_t, dvalue_t,
        )
        du[slot_rows(block), :EARLY] = grads
        dw_sum[:, :EARLY] += dot(normed_t[:, slot_rows(block)], grads)
        happen(number, {3: (lambda: final.first(out_block, total), mid_all.relay), 6: (mid_all.near,)})
        return carry

    def late_turn(number, carry):
        block = blocks - 1 - number
        buffer = number % 2
        await_block(block, buffer)

        @pl.when(number < blocks - 1)
        def _():
            prefetch(block - 1, 1 - buffer)

        grads = recurrence_backward(
            picked(dag_ref, block), table.at[buffer], heads_ref, taps_ref, y.at[buffer],
            conv.at[buffer], kept.at[buffer], states.at[buffer], state_out, stats, dext, dpos, dstate,
        )
        du[slot_rows(block), EARLY:] = grads
        dw_sum[:, EARLY:] += dot(normed_t[:, slot_rows(block)], grads)
        happen(
            number,
            {
                0: (final.second,),
                1: (collect_out,),
                3: (mid_all.far, out_all.relay),
                5: (out_all.near,),
            },
        )
        return carry

    columns = (pl.ds(0, EARLY), pl.ds(EARLY + 256, 256), pl.ds(EARLY, 256))

    def line_copy(piece, step):
        rows = pl.ds(pl.multiple_of((line.f + step) % line.count * share, share), share)
        return line.copy(
            dw.at[rows, columns[piece]], arrived.at[step, :, columns[piece]], line_sems_.at[piece], step
        )

    def send_piece(piece):
        dw[:, columns[piece]] = dw_sum[:, columns[piece]].astype(BF16)
        for step in range(1, line.count):
            made = line_copy(piece, step)
            made.start()
            sent.append(made)

    def collected(piece):
        sums = dw[own, columns[piece]].astype(F32)
        for step in range(1, line.count):
            line_copy(piece, step).wait_recv()
            sums = sums + arrived[step, :, columns[piece]].astype(F32)
        return sums.astype(BF16)

    for made in loads:
        made.wait()
    early_turn(0, 0)
    pl.semaphore_wait(pltpu.get_barrier_semaphore(), greetings)
    for step in range(1, line.count):
        rows = pl.ds(pl.multiple_of((line.f + step) % line.count * share, share), share)
        made = line.copy(dout_ref.at[rows], arrived_out.at[step], out_sems, step)
        made.start()
        sent.append(made)
    for k, mask in enumerate(SCATTER_ORDER):
        part[k] = out_block(mask, True).astype(BF16)
        final.to_core(mask, part.at[k])
    mid_all.start()
    lax.fori_loop(1, blocks, early_turn, 0)
    send_piece(0)
    lax.fori_loop(0, blocks, late_turn, 0)
    send_piece(1)
    send_piece(2)

    def block_of(mask, sibling=False):
        return dot(picked(du, place.slot(mask, sibling) + blocks), w[...], 1, 1)

    finish_out()
    for k, mask in enumerate(SCATTER_ORDER):
        part[k] = block_of(mask, True).astype(BF16)
        back.to_core(mask, part.at[k])
    back.first(block_of, total)
    out_all.far()
    early_ref[here, :] = collected(0)
    back.second()
    early_all.start()
    bc_out[...] = collected(1)
    pair.send(bc_out, bc_in, 2, 4)
    back.last(total)
    early_all.relay()
    dnormed = total[...]
    x = tokens_ref[half, :].astype(F32)
    gain = gain_ref[...]
    scale = norm_scale(x)
    spread = dnormed * gain
    pull = jnp.mean(spread * x, axis=1, keepdims=True)
    grad = dmixed_ref[...] + scale * (spread - x * (scale * scale * pull))
    grad_ref[half, :] = grad.astype(BF16)
    pair.send(grad_ref.at[half], grad_ref.at[half], 0, 4)
    small_in[0] = jnp.zeros(small_in.shape[1:], F32)
    small_in[0, 0:1, :] = jnp.sum(dnormed * x * scale, axis=0, keepdims=True)
    small_in[0, 1:2, :] = dgain_ref[0:1, :]
    small_in[0, 8:16, :width] = stats[...]
    for step in range(1, line.count):
        made = line.copy(small_in.at[0], small_in.at[step], small_sems, step)
        made.start()
        sent.append(made)
    early_all.near()
    pair.arrive(bc_in, 2, 4)
    last_ref[here, 256:512] = (bc_out[...].astype(F32) + bc_in[...].astype(F32)).astype(BF16)
    last_ref[here, 0:256] = collected(2)
    last_all.start()
    for step in range(1, line.count):
        line.copy(small_in.at[0], small_in.at[step], small_sems, step).wait_recv()
    summed = small_in[line.f % line.count]
    for other in range(1, line.count):
        summed = summed + small_in[(line.f + line.count - other) % line.count]
    mine = pl.ds(pl.multiple_of(place.slot(0) * small_rows, small_rows), small_rows)
    small_ref[mine, :] = summed
    small_all.start()
    early_all.far()
    last_all.relay()
    small_all.relay()
    small_all.near()
    small_all.far()
    last_all.near()
    last_all.far()
    for mask in range(4):
        small_all.core(mask)
    other = pl.ds(pl.multiple_of((1 - place.t) * ROWS, ROWS), ROWS)
    pair.arrive(grad_ref.at[other], 0, 4)
    pair.arrive(out_ref.at[other], 1, 4)
    for made in sent:
        made.wait_send()
    pair.finish()
    mid_all.finish()
    out_all.finish()
    small_all.finish()
    last_all.finish()
    early_all.finish()


def closing(small_inputs, streams, loads, fsdp):
    tokens, ffn, dout = small_inputs[7], small_inputs[9], small_inputs[11]
    normed_t, w, hidden, down = loads
    model, count = normed_t.shape
    share = ffn.shape[0]
    columns = w.shape[1]
    chips = lax.axis_size("context")
    blocks = count // ROWS
    vmem = pl.BlockSpec(memory_space=pltpu.VMEM)
    hbm = pl.BlockSpec(memory_space=pl.ANY)
    shape = jax.ShapeDtypeStruct
    dma = pltpu.SemaphoreType.DMA
    space = pltpu.VMEM
    inner = streams[4].shape[0] // blocks
    return pl.pallas_call(
        closing_kernel,
        out_shape=(
            shape((2 * ROWS, model), BF16),
            shape((2 * ROWS, model), BF16),
            shape((chips * share, EARLY), BF16),
            shape((chips * share, columns - EARLY), BF16),
            shape((chips * share, ffn.shape[1]), BF16),
            shape((chips * share, dout.shape[1]), BF16),
            shape((2 * chips * 16, model), F32),
        ),
        in_specs=[vmem] * 12 + [hbm] * 9,
        out_specs=(vmem,) * 7,
        scratch_shapes=[space((2, one.shape[0] // blocks, one.shape[1]), one.dtype) for one in streams]
        + [space(one.shape, one.dtype) for one in loads]
        + [
            space((count, columns), BF16),
            space((model, columns), F32),
            space((model, columns), BF16),
            space((fsdp, share, columns), BF16),
            space((fsdp, share, dout.shape[1]), BF16),
            space((ROWS, model), F32),
            space((4, ROWS, model), BF16),
            space((share, 256), BF16),
            space((share, 256), BF16),
            space((fsdp, 16, model), F32),
            space((8, 512), F32),
            space((ROWS + 8, 512), F32),
            space((ROWS + 8, 128), F32),
            space((inner, STATE), F32),
            space((inner, STATE), F32),
            space((HEAD_DIM, count), F32),
            space((HEAD_DIM, count), F32),
        ]
        + scatter_scratch(model)
        + scatter_scratch(model)
        + [dma((2, GATHER_SEMS))] * 4
        + [dma((3, 2, fsdp)), dma((2, fsdp)), dma((2, fsdp)), dma((2, 3)), dma((4,)), dma((2, BACK_INPUTS)), dma((2, GATHER_SEMS))],
        compiler_params=pltpu.CompilerParams(
            collective_id=2, has_side_effects=True, vmem_limit_bytes=61 << 20
        ),
        cost_estimate=pl.CostEstimate(
            flops=4 * count * model * columns, bytes_accessed=30 << 20, transcendentals=0
        ),
    )(*small_inputs, *streams, *loads)


def assemble_kernel(
    early_ref, late_ref, mid_ref, outs_ref, dx_ref, out_in_ref, small_ref,
    out_ref, grad_ref, query_ref, keyval_ref, attn_ref, gate_ref, x_ref, bc_ref, step_ref, ssm_ref,
    ffn_gate_ref, ffn_up_ref, ffn_down_ref, gain_ref, gain_ffn_ref, conv_x_ref, conv_bc_ref,
    bias_ref, decay_ref, skip_ref,
):
    chips = late_ref.shape[0]
    heads = step_ref.shape[1] // chips
    inner = heads * SSM_DIM
    hid = ffn_gate_ref.shape[1] // chips

    def spread(source, begin, width):
        return jnp.concatenate(
            [source[k, :, begin : begin + width].astype(F32) for k in range(chips)], axis=1
        )

    def summed(source, begin, end):
        total = source[0, :, begin:end].astype(F32)
        for k in range(1, chips):
            total = total + source[k, :, begin:end].astype(F32)
        return total

    out_ref[...] = out_in_ref[...]
    grad_ref[...] = dx_ref[...]
    gate_ref[...] = spread(early_ref, 0, inner)
    query_ref[...] = spread(early_ref, inner, HEAD_DIM)
    keyval_ref[...] = summed(early_ref, 256, 384)
    x_ref[...] = spread(late_ref, 0, inner)
    step_ref[...] = spread(late_ref, inner, heads)
    bc_ref[...] = summed(late_ref, 256, 512)
    ffn_gate_ref[...] = spread(mid_ref, 0, hid)
    ffn_up_ref[...] = spread(mid_ref, hid, hid)
    ffn_down_ref[...] = spread(mid_ref, 2 * hid, hid)
    ssm_ref[...] = spread(outs_ref, 0, inner)
    attn_ref[...] = spread(outs_ref, inner, HEAD_DIM)

    @pl.when(pl.program_id(0) == 0)
    def _():
        everywhere = small_ref[0:16, :]
        for k in range(1, small_ref.shape[0] // 16):
            everywhere = everywhere + small_ref[16 * k : 16 * k + 16, :]
        gain_ref[...] = everywhere[0:1]
        gain_ffn_ref[...] = everywhere[1:2]
        conv_bc_ref[...] = everywhere[8 : 8 + CONV, 256:512]
        core = lax.axis_index("tensor")
        own = [
            small_ref[pl.ds(pl.multiple_of((2 * k + core) * 16, 16), 16), :] for k in range(chips)
        ]
        conv_x_ref[...] = jnp.concatenate([one[8 : 8 + CONV, :inner] for one in own], axis=1)
        for row, target in ((12, skip_ref), (13, bias_ref), (14, decay_ref)):
            target[...] = jnp.concatenate(
                [
                    jnp.sum(
                        one[row : row + 1, h * SSM_DIM : (h + 1) * SSM_DIM], axis=1, keepdims=True
                    )
                    for one in own
                    for h in range(heads)
                ],
                axis=1,
            )


def assemble(early, last, mid, outs, dx, out, small, widths, heads):
    chips = lax.axis_size("context")
    share = last.shape[0] // chips
    turns = 2
    rows = share // turns
    shape = jax.ShapeDtypeStruct
    block = lambda height, width: pl.BlockSpec((height, width), lambda i: (i, 0))
    fixed = lambda height, width: pl.BlockSpec((height, width), lambda i: (0, 0))
    slab = lambda width: pl.BlockSpec((chips, rows, width), lambda i: (0, i, 0))
    token_rows = dx.shape[0] // turns
    model = dx.shape[1]
    tiny = [
        (1, model), (1, model), (CONV, heads * SSM_DIM), (CONV, 2 * STATE), (1, heads), (1, heads),
        (1, heads),
    ]
    return pl.pallas_call(
        assemble_kernel,
        grid=(turns,),
        out_shape=(shape(out.shape, BF16), shape(dx.shape, BF16))
        + tuple(shape((share, width), F32) for width in widths)
        + tuple(shape(one, F32) for one in tiny),
        in_specs=[
            slab(early.shape[1]), slab(last.shape[1]), slab(mid.shape[1]), slab(outs.shape[1]),
            block(token_rows, model), block(token_rows, model), fixed(*small.shape),
        ],
        out_specs=(block(token_rows, model), block(token_rows, model))
        + tuple(block(rows, width) for width in widths)
        + tuple(fixed(*one) for one in tiny),
        compiler_params=pltpu.CompilerParams(vmem_limit_bytes=60 << 20),
    )(*[one.reshape(chips, share, -1) for one in (early, last, mid, outs)], dx, out, small)


def per_device(
    tokens, segments, deal, gain_mix, w_query, w_keyval, w_attn_out, w_gate_z, w_in_x, w_bc, w_step,
    conv_x, conv_bc, step_bias, decay_log, skip, w_ssm_out, gain_ffn, w_ffn_gate, w_ffn_up,
    w_ffn_down, cotangent,
):
    ids = jnp.arange(deal.shape[1], dtype=jnp.int32)
    holds = (deal[0][:, None] == ids[None, :]).astype(F32)
    pick = jnp.broadcast_to(jnp.concatenate([holds.T, holds]).reshape(-1, 1), (128, 128))
    normed_t, u, w_all, wout_all, cot_all, table, head_rows, taps = opening(
        tokens,
        cotangent,
        (w_in_x, w_query, w_bc, w_gate_z, w_keyval, w_step.T, w_ssm_out, w_attn_out),
        gain_mix,
        segments,
        (conv_x, conv_bc),
        (step_bias, decay_log, skip),
    )
    ag, y, conv, states, keyval, kept, normed_t = mixer_forward(u, normed_t, table, head_rows, taps, deal[0])
    hidden, dag, mixed, dmixed, dgain, down, dffn, dout = middle(
        ag, wout_all, (w_ffn_gate, w_ffn_up, w_ffn_down), tokens, cotangent, cot_all, gain_ffn
    )
    dx, out, early, last, mids, outs, small = closing(
        (
            pick, dag, keyval, head_rows, taps, dmixed, mixed, tokens, gain_mix.reshape(1, -1), dffn,
            dgain, dout,
        ),
        (table, y, conv, kept, states),
        (normed_t, w_all, hidden, down),
        lax.axis_size("fsdp"),
    )
    weights = (
        w_query, w_keyval, w_attn_out, w_gate_z, w_in_x, w_bc, w_step, w_ssm_out, w_ffn_gate,
        w_ffn_up, w_ffn_down,
    )
    done = assemble(early, last, mids, outs, dx, out, small, [w.shape[1] for w in weights], skip.shape[0])
    grads = done[2:13]
    gain, gain_two, taps_x, taps_bc, bias, decay, skips = done[13:]
    return (
        done[0],
        done[1],
        gain.reshape(-1),
        *grads[:7],
        taps_x,
        taps_bc,
        bias.reshape(-1),
        decay.reshape(-1),
        skips.reshape(-1),
        grads[7],
        gain_two.reshape(-1),
        *grads[8:],
    )


def solution(mesh):
    in_specs = (
        P(("fsdp", "context"), None),
        P("fsdp", None),
        P("fsdp", None),
        P(),
        P("fsdp", "tensor"),
        P("fsdp", "tensor"),
        P("fsdp", "tensor"),
        P("fsdp", "tensor"),
        P("fsdp", "tensor"),
        P("fsdp", None),
        P("fsdp", "tensor"),
        P(None, "tensor"),
        P(),
        P("tensor"),
        P("tensor"),
        P("tensor"),
        P("fsdp", "tensor"),
        P(),
        P("fsdp", "tensor"),
        P("fsdp", "tensor"),
        P("fsdp", "tensor"),
        P(("fsdp", "context"), None),
    )
    out_specs = (
        P(("fsdp", "context"), None),
        P(("fsdp", "context"), None),
        P(),
        P("fsdp", "tensor"),
        P("fsdp", "tensor"),
        P("fsdp", "tensor"),
        P("fsdp", "tensor"),
        P("fsdp", "tensor"),
        P("fsdp", None),
        P("fsdp", "tensor"),
        P(None, "tensor"),
        P(),
        P("tensor"),
        P("tensor"),
        P("tensor"),
        P("fsdp", "tensor"),
        P(),
        P("fsdp", "tensor"),
        P("fsdp", "tensor"),
        P("fsdp", "tensor"),
    )
    return jax.shard_map(
        per_device, mesh=mesh, in_specs=in_specs, out_specs=out_specs, check_vma=False
    )
```

```python
import functools
import math

import jax
import jax.numpy as jnp
from jax import lax
from jax.experimental import pallas as pl
from jax.experimental.pallas import tpu as pltpu
from jax.sharding import PartitionSpec as P

HEAD_DIM = 64
SSM_DIM = 64
STATE = 128
CONV = 4
HALF = 256
WINDOW = 4

epsilon = 1e-05
masked = -1e30
F32 = jnp.float32
BF16 = jnp.bfloat16
exact = lax.Precision.HIGHEST


def dot(left, right, left_dim=1, right_dim=0, precision=None):
    return lax.dot_general(
        left,
        right,
        (((left_dim,), (right_dim,)), ((), ())),
        precision=precision,
        preferred_element_type=F32,
    )


def sigmoid(v):
    return 1.0 / (1.0 + jnp.exp(-v))


def softplus(v):
    return jnp.maximum(v, 0.0) + jnp.log1p(jnp.exp(-jnp.abs(v)))


def swap_halves(v):
    half = v.shape[1] // 2
    return jnp.concatenate([v[:, half:], v[:, :half]], axis=1)


def iotas(rows, columns):
    return (
        lax.broadcasted_iota(jnp.int32, (rows, columns), 0),
        lax.broadcasted_iota(jnp.int32, (rows, columns), 1),
    )


def state_scale(last_row, carry_last, heads):
    pieces = [
        jnp.broadcast_to(last_row[:, h * SSM_DIM : h * SSM_DIM + 1], (SSM_DIM, STATE))
        for h in range(heads)
    ]
    return jnp.exp(jnp.concatenate(pieces, axis=0)) * carry_last


def block_decays(step_raw, heads_ref, lane_pos, heads):
    rows = step_raw.shape[0]
    inner = heads * SSM_DIM
    raw = step_raw + heads_ref[0:1, :inner]
    step = softplus(raw)
    rate = step * jnp.exp(heads_ref[1:2, :inner])
    row, col = iotas(rows, rows)
    lower = jnp.where(col <= row, 1.0, 0.0).astype(F32)
    totals = dot(lower, -rate, precision=exact)
    last_row = totals[rows - 1 : rows]
    pos_last = lane_pos[rows - 1 : rows, 0:1]
    local = lax.broadcasted_iota(jnp.int32, (rows, 1), 0).astype(F32)
    carry_on = (lane_pos[:, 0:1] > local).astype(F32)
    keep_last = (local >= (rows - 1) - pos_last).astype(F32)
    carry_last = (pos_last > rows - 1).astype(F32)
    factor = jnp.exp(totals) * carry_on
    tails = jnp.exp(last_row - totals) * keep_last
    return raw, step, rate, totals, last_row, carry_last, factor, tails


def local_mask(lane_pos, rows):
    row, col = iotas(rows, rows)
    gap = (row - col).astype(F32)
    return (gap >= 0) & (gap <= lane_pos[:, 0:1])


def key_window(block):
    start = jnp.maximum(block - WINDOW, 0)
    return start, (block - start) * HALF


def window_mask(lane_pos, offset, rows, keys):
    last = (lax.broadcasted_iota(jnp.int32, (rows, 1), 0) + offset).astype(F32)
    col = lax.broadcasted_iota(jnp.int32, (8, keys), 1)[0:1].astype(F32)
    return (col <= last) & (col >= last - lane_pos[:, 0:1])


def head_decay(totals, totals_t, h, allowed):
    gap = totals[:, h * SSM_DIM : h * SSM_DIM + 1] - totals_t[h * SSM_DIM : h * SSM_DIM + 1, :]
    return jnp.exp(jnp.where(allowed, gap, masked))


def mixer_forward_kernel(
    order_ref, u_ref, normed_ref, table_ref, heads_ref, taps_ref, ag_ref, y_ref, conv_ref, state_in_ref,
    kv_ref, kept_ref, ordered_ref, ext, state, keyval, found,
):
    block = pl.program_id(0)
    heads = state.shape[0] // SSM_DIM
    inner = heads * SSM_DIM
    width = ext.shape[1]
    rows = u_ref.shape[0]

    @pl.when(block == 0)
    def _():
        ext[0:8, :] = jnp.zeros((8, width), F32)
        state[...] = jnp.zeros(state.shape, F32)
        keyval[...] = jnp.zeros(keyval.shape, BF16)

    lane_pos = table_ref[:, 128:256]
    cosine = table_ref[:, 0:64]
    sine = table_ref[:, 64:128]
    q_at = inner
    u = u_ref[:, :width].astype(F32)
    ext[8 : 8 + rows, :] = u
    conv = u * taps_ref[CONV - 1 : CONV, :]
    for back in range(1, CONV):
        reach = lane_pos[:, 0:1] >= back
        shifted = ext[8 - back : 8 - back + rows, :]
        conv = conv + jnp.where(reach, shifted, 0.0) * taps_ref[CONV - 1 - back : CONV - back, :]
    ext[0:8, :] = u[rows - 8 : rows]
    act = conv * sigmoid(conv)
    ssm_x = act[:, :inner].astype(BF16)
    ssm_b = act[:, 256:384].astype(BF16)
    ssm_c = act[:, 384:512].astype(BF16)
    conv_ref[:, 0:256] = conv[:, 0:256]
    conv_ref[:, 256:512] = conv[:, 256:512]
    query = u[:, q_at : q_at + HEAD_DIM]
    query = (query * cosine + swap_halves(query) * sine).astype(BF16)
    conv_ref[:, q_at : q_at + HEAD_DIM] = query.astype(F32)
    key = u_ref[:, 512 + inner : 512 + inner + HEAD_DIM].astype(F32)
    key = key * cosine + swap_halves(key) * sine
    value = u_ref[:, 768 + inner : 768 + inner + HEAD_DIM].astype(F32)
    pair = jnp.concatenate([key, value], axis=1).astype(BF16)
    kv_ref[...] = pair
    keyval[pl.ds(pl.multiple_of(block * rows, rows), rows), :] = pair
    query_low = query * 0.125

    def attend(first, offset, span):
        window = keyval[pl.ds(pl.multiple_of(first * rows, rows), span), :]
        scores = dot(query_low, window[:, :HEAD_DIM], 1, 1)
        scores = jnp.where(window_mask(lane_pos, offset, rows, span), scores, masked)
        highest = jnp.max(scores, axis=1, keepdims=True)
        weights = jnp.exp(scores - highest)
        total = jnp.sum(weights, axis=1, keepdims=True)
        probs = (weights * (1.0 / total)).astype(BF16)
        found[:, :HEAD_DIM] = dot(probs, window[:, HEAD_DIM:])
        found[:, HEAD_DIM:] = jnp.broadcast_to(highest + jnp.log(total), (rows, HEAD_DIM))

    @pl.when(block < 2)
    def _():
        attend(0, block * rows, 2 * HALF)

    @pl.when((block >= 2) & (block < WINDOW))
    def _():
        attend(0, block * rows, WINDOW * HALF)

    @pl.when(block >= WINDOW)
    def _():
        attend(block - WINDOW, WINDOW * rows, (WINDOW + 1) * HALF)

    attended = found[:, :HEAD_DIM]
    _, step, _, totals, last_row, carry_last, factor, tails = block_decays(
        u_ref[:, 768 : 768 + inner].astype(F32), heads_ref, lane_pos, heads
    )
    totals_t = totals.T
    allowed = local_mask(lane_pos, rows)
    cross = dot(ssm_c, ssm_b, 1, 1)
    x_f = ssm_x.astype(F32)
    stepped = step * x_f
    stepped_low = stepped.astype(BF16)
    parts = []
    for h in range(heads):
        lanes = slice(h * SSM_DIM, (h + 1) * SSM_DIM)
        mix = (head_decay(totals, totals_t, h, allowed) * cross).astype(BF16)
        parts.append(dot(mix, stepped_low[:, lanes]))
    held = state[...]
    state_in_ref[...] = held
    y_pure = jnp.concatenate(parts, axis=1) + factor * dot(ssm_c, held.astype(BF16), 1, 1)
    tailed = (tails * stepped_low.astype(F32)).astype(BF16)
    state[...] = state_scale(last_row, carry_last, heads) * held + dot(tailed, ssm_b, 0, 0)
    y_ref[:, 0:256] = jnp.concatenate(
        [y_pure, found[:, HEAD_DIM:]], axis=1
    )
    y_ref[:, 256:512] = jnp.concatenate([u_ref[:, 768 : 768 + inner], attended], axis=1)
    ordered_ref[...] = normed_ref[...]
    kept_ref[...] = u_ref[:, 0:768].astype(BF16)
    y_full = y_pure + heads_ref[2:3, :inner] * x_f
    gate = u_ref[:, 512 : 512 + inner].astype(F32)
    gated = y_full * (gate * sigmoid(gate))
    ag_ref[...] = jnp.concatenate([gated, attended], axis=1).astype(BF16)


def attention_backward(
    block, dag, table_ref, heads_ref, y_ref, conv_ref, kept_ref, kv_ref, dkey_t, dvalue_t,
):
    inner = dag.shape[1] - HEAD_DIM
    rows = dag.shape[0]
    lane_pos = table_ref[:, 128:256]
    cosine = table_ref[:, 0:64]
    sine = table_ref[:, 64:128]
    first, offset = key_window(block)
    span = (WINDOW + 1) * HALF
    begin = pl.multiple_of(first * rows, rows)
    window = kv_ref[pl.ds(begin, span), :]
    keys = window[:, :HEAD_DIM]
    values = window[:, HEAD_DIM:]
    query = conv_ref[:, inner : inner + HEAD_DIM] * 0.125
    query_low = query.astype(BF16)
    datt = dag[:, inner : inner + HEAD_DIM]
    datt_f = datt.astype(F32)
    lse = y_ref[:, inner : inner + 1]
    scores = dot(query_low, keys, 1, 1)
    allowed_all = window_mask(lane_pos, offset, rows, span)
    probs = jnp.exp(jnp.where(allowed_all, scores, masked) - lse)
    inward = jnp.sum(datt_f * y_ref[:, 256 + inner : 256 + inner + HEAD_DIM], axis=1, keepdims=True)
    dscores = (probs * (dot(datt, values, 1, 1) - inward)).astype(BF16)
    dquery = dot(dscores, keys) * 0.125
    dkey_t[:, pl.ds(begin, span)] += dot(query.T.astype(BF16), dscores)
    dvalue_t[:, pl.ds(begin, span)] += dot(datt_f.T.astype(BF16), probs.astype(BF16))
    here = pl.ds(pl.multiple_of(block * rows, rows), rows)
    dkey = dkey_t[:, here].T
    dvalue = dvalue_t[:, here].T
    dquery = dquery * cosine - swap_halves(dquery) * sine
    dkey = dkey * cosine - swap_halves(dkey) * sine
    conv = conv_ref[:, :inner]
    ssm_x = (conv * sigmoid(conv)).astype(BF16).astype(F32)
    gate = kept_ref[:, 512 : 512 + inner].astype(F32)
    sig = sigmoid(gate)
    dgated = dag[:, :inner].astype(F32)
    y_full = y_ref[:, :inner] + heads_ref[2:3, :inner] * ssm_x
    dgate = dgated * y_full * (sig * (1.0 + gate * (1.0 - sig)))
    return jnp.concatenate([dgate, dquery, dkey, dvalue], axis=1).astype(BF16)


def recurrence_backward(
    dag, table_ref, heads_ref, taps_ref, y_ref, conv_ref, kept_ref, state_in_ref, state_out, stats_ref,
    dext, dpos, dstate,
):
    heads = dstate.shape[0] // SSM_DIM
    inner = heads * SSM_DIM
    rows = dag.shape[0]
    lane_pos = table_ref[:, 128:256]
    conv = conv_ref[...]
    gate_conv = sigmoid(conv)
    act = conv * gate_conv
    dact = gate_conv * (1.0 + conv * (1.0 - gate_conv))
    ssm_x = act[:, :inner].astype(BF16)
    ssm_b = act[:, 256:384].astype(BF16)
    ssm_c = act[:, 384:512].astype(BF16)
    x_f = ssm_x.astype(F32)
    raw, step, rate, totals, last_row, carry_last, factor, tails = block_decays(
        y_ref[:, 256 : 256 + inner], heads_ref, lane_pos, heads
    )
    totals_t = totals.T
    allowed = local_mask(lane_pos, rows)
    cross = dot(ssm_c, ssm_b, 1, 1)
    gate = kept_ref[:, 512 : 512 + inner].astype(F32)
    sig = sigmoid(gate)
    y_pure = y_ref[:, :inner]
    dgated = dag[:, :inner].astype(F32)
    skip = heads_ref[2:3, :inner]
    dy = dgated * (gate * sig)
    dy_low = dy.astype(BF16)
    dy_r = dy_low.astype(F32)
    dy_t = dy.T.astype(BF16)
    stepped_low = (step * x_f).astype(BF16)
    stepped_r = stepped_low.astype(F32)
    tailed = (tails * stepped_r).astype(BF16)
    dcross = jnp.zeros((rows, rows), F32)
    parts = []
    for h in range(heads):
        lanes = slice(h * SSM_DIM, (h + 1) * SSM_DIM)
        decay = head_decay(totals, totals_t, h, allowed)
        mix = (decay * cross).astype(BF16)
        parts.append(dot(dy_t[lanes, :], mix))
        dcross = dcross + dot(dy_low[:, lanes], stepped_low[:, lanes], 1, 1) * decay
    dstep_x = jnp.concatenate(parts, axis=0).T
    dcross_low = dcross.astype(BF16)
    held = state_in_ref[...].astype(BF16)
    dheld = dstate[...]
    dheld_low = dheld.astype(BF16)
    dfactored = (factor * dy).astype(BF16)
    from_state = dot(ssm_b, dheld_low, 1, 1)
    dssm_c = dot(dcross_low, ssm_b) + dot(dfactored, held)
    dssm_b = dot(dcross_low, ssm_c, 0, 0) + dot(tailed, dheld_low)
    dtotals = dy_r * y_pure - stepped_r * dstep_x - tailed.astype(F32) * from_state
    dstep_x = dstep_x + tails * from_state
    end_term = dot(
        jnp.ones((8, STATE), F32), dheld_low.astype(F32) * state_out[...], 1, 1, exact
    )[0:1]
    row, col = iotas(rows, rows)
    upper = jnp.where(col >= row, 1.0, 0.0).astype(F32)
    drate = -(dot(upper, dtotals, precision=exact) + end_term)
    state_out[...] = state_in_ref[...]
    dstate[...] = state_scale(last_row, carry_last, heads) * dheld + dot(dfactored, ssm_c, 0, 0)
    dssm_x = step * dstep_x + skip * dy
    dstep = x_f * dstep_x + jnp.exp(heads_ref[1:2, :inner]) * drate
    draw = dstep * sigmoid(raw)
    none = jnp.zeros((rows, HEAD_DIM), F32)
    dconv = jnp.concatenate([dssm_x, none, dssm_b, dssm_c], axis=1) * dact
    dext[0:rows, :] = dconv
    dpos[0:rows, :] = lane_pos
    u = kept_ref[:, 0:512].astype(F32)
    du = dconv * taps_ref[CONV - 1 : CONV, :]
    stats_ref[CONV - 1 : CONV, :] += jnp.sum(dconv * u, axis=0, keepdims=True)
    for ahead in range(1, CONV):
        reach = dpos[ahead : ahead + rows, 0:1] >= ahead
        shifted = jnp.where(reach, dext[ahead : ahead + rows, :], 0.0)
        tap = CONV - 1 - ahead
        du = du + shifted * taps_ref[tap : tap + 1, :]
        stats_ref[tap : tap + 1, :] += jnp.sum(shifted * u, axis=0, keepdims=True)
    dext[rows : rows + 8, :] = dconv[0:8]
    dpos[rows : rows + 8, :] = lane_pos[0:8]
    stats_ref[4:5, :inner] += jnp.sum(dy * x_f, axis=0, keepdims=True)
    stats_ref[5:6, :inner] += jnp.sum(draw, axis=0, keepdims=True)
    stats_ref[6:7, :inner] += jnp.sum(drate * rate, axis=0, keepdims=True)
    summed = [
        jnp.sum(draw[:, h * SSM_DIM : (h + 1) * SSM_DIM], axis=1, keepdims=True)
        for h in range(heads)
    ]
    lane = lax.broadcasted_iota(jnp.int32, (rows, HEAD_DIM), 1)
    dstep_all = jnp.zeros((rows, HEAD_DIM), F32)
    for h in range(heads):
        dstep_all = jnp.where(lane == h, summed[h], dstep_all)
    return jnp.concatenate([du[:, :inner], dstep_all, du[:, 256:512]], axis=1).astype(BF16)


def slot_holding(order, block):
    slot = 0
    for k in range(1, order.shape[0]):
        slot = slot + jnp.where(order[k] == block, k, 0)
    return slot


def mixer_forward(u, normed_t, table, head_rows, taps, slot_of):
    count = u.shape[0]
    blocks = count // HALF
    heads = 3
    inner = heads * SSM_DIM
    width = taps.shape[1]
    at_slot = lambda i, order: (slot_holding(order, i), 0)
    in_order = lambda i, slots: (i, 0)
    whole = lambda i, slots: (0, 0)
    return pl.pallas_call(
        mixer_forward_kernel,
        out_shape=(
            jax.ShapeDtypeStruct((count, inner + HEAD_DIM), BF16),
            jax.ShapeDtypeStruct((count, 512), F32),
            jax.ShapeDtypeStruct((count, width), F32),
            jax.ShapeDtypeStruct((blocks * inner, STATE), F32),
            jax.ShapeDtypeStruct((count, 2 * HEAD_DIM), BF16),
            jax.ShapeDtypeStruct((count, 768), BF16),
            jax.ShapeDtypeStruct(normed_t.shape, BF16),
        ),
        grid_spec=pltpu.PrefetchScalarGridSpec(
            num_scalar_prefetch=1,
            grid=(blocks,),
            in_specs=[
                pl.BlockSpec((HALF, u.shape[1]), at_slot),
                pl.BlockSpec((normed_t.shape[0], HALF), lambda i, order: at_slot(i, order)[::-1]),
                pl.BlockSpec((HALF, table.shape[1]), in_order),
                pl.BlockSpec(head_rows.shape, whole),
                pl.BlockSpec(taps.shape, whole),
            ],
            out_specs=(
                pl.BlockSpec((HALF, inner + HEAD_DIM), at_slot),
                pl.BlockSpec((HALF, 512), in_order),
                pl.BlockSpec((HALF, width), in_order),
                pl.BlockSpec((inner, STATE), in_order),
                pl.BlockSpec((HALF, 2 * HEAD_DIM), in_order),
                pl.BlockSpec((HALF, 768), in_order),
                pl.BlockSpec((normed_t.shape[0], HALF), lambda i, order: (0, i)),
            ),
            scratch_shapes=[
                pltpu.VMEM((8 + HALF, width), F32),
                pltpu.VMEM((inner, STATE), F32),
                pltpu.VMEM((count, 2 * HEAD_DIM), BF16),
                pltpu.VMEM((HALF, 2 * HEAD_DIM), F32),
            ],
        ),
        compiler_params=pltpu.CompilerParams(vmem_limit_bytes=60 << 20),
    )(slot_of, u, normed_t, table, head_rows, taps)


MESH = pl.DeviceIdType.MESH


class Place:
    def __init__(self):
        self.c = lax.axis_index("context")
        self.t = lax.axis_index("tensor")
        count = lax.axis_size("context")
        self.chips = [
            self.c,
            self.c + 1 - 2 * (self.c % 2),
            (self.c + count // 2) % count,
            count - 1 - self.c,
        ]

    def slot(self, mask, sibling=False):
        core = 1 - self.t if sibling else self.t
        return self.chips[mask] * 2 + core

    def target(self, mask):
        if mask == 4:
            return {"tensor": 1 - self.t}
        return {"context": self.chips[mask]}

    def hello(self, line=None):
        barrier = pltpu.get_barrier_semaphore()
        targets = [self.target(mask) for mask in (1, 2, 4)]
        if line is not None:
            targets += [line.target(step) for step in range(1, line.count)]
        for target in targets:
            pl.semaphore_signal(barrier, inc=1, device_id=target, device_id_type=MESH)
        return len(targets)

    def greet(self, line=None):
        pl.semaphore_wait(pltpu.get_barrier_semaphore(), self.hello(line))


class Wire:
    def __init__(self, place, sems):
        self.place = place
        self.sems = sems
        self.sent = []

    def copy(self, source, target, index, mask):
        return pltpu.make_async_remote_copy(
            src_ref=source,
            dst_ref=target,
            send_sem=self.sems.at[0, index],
            recv_sem=self.sems.at[1, index],
            device_id=self.place.target(mask),
            device_id_type=MESH,
        )

    def send(self, source, target, index, mask):
        def made():
            here = source() if callable(source) else source
            there = target() if callable(target) else target
            return self.copy(here, there, index, mask)

        made().start()
        self.sent.append(made)

    def arrive(self, target, index, mask):
        self.copy(target, target, index, mask).wait_recv()

    def finish(self):
        for made in self.sent:
            made().wait_send()
        self.sent = []


ROWS = HALF
PART = HALF // 2
TOP, END = pl.ds(0, PART), pl.ds(PART, PART)
SCATTER_SEMS = 10
GATHER_SEMS = 14


def scatter_scratch(columns):
    return [
        pltpu.VMEM((4, ROWS, columns), BF16),
        pltpu.VMEM((4, ROWS, columns), BF16),
        pltpu.VMEM((6, PART, columns), BF16),
        pltpu.VMEM((ROWS, columns), BF16),
        pltpu.SemaphoreType.DMA((2, SCATTER_SEMS)),
    ]


SCATTER_ORDER = (3, 1, 2, 0)


class Scatter:
    def __init__(self, place, scratch):
        self.place = place
        self.core_in, self.out, self.chip_in, self.kept, sems = scratch
        self.wire = Wire(place, sems)

    def to_core(self, mask, source):
        index = SCATTER_ORDER.index(mask)
        self.wire.send(source, self.core_in.at[index], index, 4)

    def from_core(self, mask):
        index = SCATTER_ORDER.index(mask)
        self.wire.arrive(self.core_in.at[index], index, 4)
        return self.core_in[index].astype(F32)

    def first(self, mine, total, between=None):
        wire, out, kept = self.wire, self.out, self.kept
        both = mine(3) + self.from_core(3)
        out[0] = both.astype(BF16)
        wire.send(lambda: out.at[0, TOP], lambda: self.chip_in.at[0], 4, 1)
        wire.send(lambda: out.at[0, END], lambda: self.chip_in.at[1], 5, 2)
        both = mine(1) + self.from_core(1)
        out[1] = both.astype(BF16)
        wire.send(lambda: out.at[1, TOP], lambda: self.chip_in.at[2], 6, 1)
        kept[END] = out[1, END]
        both = mine(2) + self.from_core(2)
        out[2] = both.astype(BF16)
        wire.send(lambda: out.at[2, END], lambda: self.chip_in.at[3], 7, 2)
        kept[TOP] = out[2, TOP]
        total[...] = mine(0) + self.from_core(0)

    def second(self):
        wire, out, kept, came = self.wire, self.out, self.kept, self.chip_in
        wire.arrive(came.at[0], 4, 1)
        out[3, TOP] = (kept[TOP].astype(F32) + came[0].astype(F32)).astype(BF16)
        wire.send(lambda: out.at[3, TOP], lambda: came.at[4], 8, 2)
        wire.arrive(came.at[1], 5, 2)
        out[3, END] = (kept[END].astype(F32) + came[1].astype(F32)).astype(BF16)
        wire.send(lambda: out.at[3, END], lambda: came.at[5], 9, 1)

    def last(self, total):
        wire, came = self.wire, self.chip_in
        wire.arrive(came.at[2], 6, 1)
        wire.arrive(came.at[4], 8, 2)
        total[TOP] += came[2].astype(F32) + came[4].astype(F32)
        wire.arrive(came.at[3], 7, 2)
        wire.arrive(came.at[5], 9, 1)
        total[END] += came[3].astype(F32) + came[5].astype(F32)
        wire.finish()


class Gather:
    def __init__(self, place, whole, sems, rows=ROWS, cores=True):
        self.place = place
        self.whole = whole
        self.size = rows
        self.cores = cores
        self.wire = Wire(place, sems)

    def rows(self, mask, sibling=False, half=None):
        place, size = self.place, self.size
        block = place.slot(mask, sibling) if self.cores else place.chips[mask]
        begin = block * size
        if half is None:
            return self.whole.at[pl.ds(pl.multiple_of(begin, size), size)]
        return self.whole.at[pl.ds(pl.multiple_of(begin + half * (size // 2), size // 2), size // 2)]

    def both(self, mask, sibling=False, half=None):
        block = functools.partial(self.rows, mask, sibling, half)
        return block, block

    def start(self, core=True):
        wire = self.wire
        for half, mask, index in ((0, 1, 0), (1, 2, 1), (1, 1, 2), (0, 2, 3)):
            wire.send(*self.both(0, half=half), index, mask)
        if self.cores and core:
            wire.send(*self.both(0), 6, 4)

    def relay(self):
        wire = self.wire
        wire.arrive(self.rows(1, half=0), 0, 1)
        wire.send(*self.both(1, half=0), 4, 2)
        wire.arrive(self.rows(2, half=1), 1, 2)
        wire.send(*self.both(2, half=1), 5, 1)

    def near(self):
        wire = self.wire
        wire.arrive(self.rows(1, half=1), 2, 1)
        if self.cores:
            wire.send(*self.both(1), 7, 4)
        wire.arrive(self.rows(2, half=0), 3, 2)
        if self.cores:
            wire.send(*self.both(2), 8, 4)

    def far(self):
        wire = self.wire
        wire.arrive(self.rows(3, half=0), 4, 2)
        wire.arrive(self.rows(3, half=1), 5, 1)
        if self.cores:
            wire.send(*self.both(3), 9, 4)

    def core(self, mask):
        index = (6, 7, 8, 9)[mask]
        self.wire.arrive(self.rows(mask, sibling=True), index, 4)

    def finish(self):
        self.wire.finish()


class Line:
    def __init__(self):
        self.f = lax.axis_index("fsdp")
        self.count = lax.axis_size("fsdp")

    def target(self, step):
        return {"fsdp": (self.f + step) % self.count}

    def copy(self, source, target, sems, step):
        return pltpu.make_async_remote_copy(
            src_ref=source,
            dst_ref=target,
            send_sem=sems.at[0, step],
            recv_sem=sems.at[1, step],
            device_id=self.target(step),
            device_id_type=MESH,
        )


class LineGather:
    def __init__(self, line, whole, sems):
        self.line = line
        self.whole = whole
        self.sems = sems
        self.size = whole.shape[0] // line.count

    def rows(self, block):
        return self.whole.at[pl.ds(pl.multiple_of(block * self.size, self.size), self.size)]

    def copy(self, block, way, step):
        toward = self.line.f + 1 if way == 0 else self.line.f - 1
        return pltpu.make_async_remote_copy(
            src_ref=self.rows(block),
            dst_ref=self.rows(block),
            send_sem=self.sems.at[way, 0, step],
            recv_sem=self.sems.at[way, 1, step],
            device_id={"fsdp": toward},
            device_id_type=MESH,
        )

    def step(self, number, arrive=True):
        f, last = self.line.f, self.line.count - 1
        for way in (0, 1):
            block = f - number if way == 0 else f + number
            there = block >= 0 if way == 0 else block <= last
            goes_on = f < last if way == 0 else f > 0

            @pl.when(there)
            def _():
                if number > 0:
                    self.copy(block, way, number).wait_recv()

                @pl.when(goes_on)
                def _():
                    self.copy(block, way, number + 1).start()

    def finish(self):
        f, last = self.line.f, self.line.count - 1
        for number in range(self.line.count - 1):
            for way in (0, 1):
                block = f - number if way == 0 else f + number
                there = block >= 0 if way == 0 else block <= last
                goes_on = f < last if way == 0 else f > 0

                @pl.when(there & goes_on)
                def _():
                    self.copy(block, way, number + 1).wait_send()


def line_sems(count):
    return pltpu.SemaphoreType.DMA((2, 2, count + 1))


def opening_kernel(
    tokens_ref, cot_ref, in_x_ref, query_ref, bc_ref, gate_ref, keyval_ref, step_ref, ssm_ref, attn_ref,
    gain_ref, segments_ref, conv_x_ref, conv_bc_ref, bias_ref, decay_ref, skip_ref,
    normed_t_out, u_out, w_out, wout_out, cot_out, table_out, heads_ref, taps_ref,
    x_all, cot_all, normed, normed_t, u, weights_all, wout_all, table, wide,
    x_sems, cot_sems, w_sems, out_sems, local_sems, block_sems,
):
    place = Place()
    line = Line()
    rows_x = Gather(place, x_all, x_sems)
    rows_cot = Gather(place, cot_all, cot_sems)
    weights = LineGather(line, weights_all, w_sems)
    weights_out = LineGather(line, wout_all, out_sems)
    chips = lax.axis_size("context")
    share = in_x_ref.shape[0]
    heads = step_ref.shape[0] // chips
    inner = heads * SSM_DIM
    chip_rows = pl.ds(pl.multiple_of(place.c * 2 * ROWS, 2 * ROWS), 2 * ROWS)
    waiting = []

    def local(source, target, sem):
        made = pltpu.make_async_copy(source, target, sem)
        made.start()
        waiting.append(made)
        return made

    greetings = place.hello(line)
    own_x = pltpu.make_async_copy(tokens_ref, x_all.at[chip_rows], local_sems.at[0])
    own_x.start()
    own_cot = pltpu.make_async_copy(cot_ref, cot_all.at[chip_rows], local_sems.at[1])
    own_cot.start()
    mine = pl.ds(pl.multiple_of(line.f * share, share), share)
    heads_ref[...] = jnp.zeros(heads_ref.shape, F32)
    taps_ref[...] = jnp.zeros(taps_ref.shape, F32)
    for k in range(chips):

        @pl.when(place.c == k)
        def _():
            inner_part = slice(k * inner, (k + 1) * inner)
            head_part = slice(k * HEAD_DIM, (k + 1) * HEAD_DIM)
            weights_all[mine, 0:256] = jnp.concatenate(
                [gate_ref[:, inner_part], query_ref[:, head_part]], axis=1
            )
            weights_all[mine, 384 : 384 + inner] = in_x_ref[:, inner_part]
            wout_all[mine, :] = jnp.concatenate(
                [ssm_ref[:, inner_part], attn_ref[:, head_part]], axis=1
            )
            taps_ref[0:CONV, :inner] = conv_x_ref[:, inner_part]
            for h in range(heads):
                lane = slice(k * heads + h, k * heads + h + 1)
                for row, source in enumerate((bias_ref, decay_ref, skip_ref)):
                    heads_ref[row : row + 1, h * SSM_DIM : (h + 1) * SSM_DIM] = jnp.broadcast_to(
                        source[:, lane], (1, SSM_DIM)
                    )

    taps_ref[0:CONV, 256:512] = conv_bc_ref[...]
    head, column = iotas(step_ref.shape[0], HEAD_DIM)
    chosen = (head == column + place.c * heads) & (column < heads)
    steps = dot(step_ref[...], jnp.where(chosen, 1.0, 0.0).astype(BF16), 0, 0)
    weights_all[mine, 384 + inner : 640] = steps.astype(BF16)
    weights_all[mine, 256:384] = keyval_ref[...]
    weights_all[mine, 640:896] = bc_ref[...]
    own_x.wait()
    own_cot.wait()
    pl.semaphore_wait(pltpu.get_barrier_semaphore(), greetings)
    weights.step(0)
    rows_x.start(core=False)

    def norm(slot):
        rows = slot_rows(slot)
        x = x_all[rows, :].astype(F32)
        normed[rows, :] = (x * norm_scale(x) * gain_ref[...]).astype(BF16)
        columns = pl.ds(pl.multiple_of(slot * ROWS, ROWS), ROWS)
        normed_t[:, columns] = normed[rows, :].T

    norm(place.slot(0))
    norm(place.slot(0, True))

    numbers = segments_ref[...]
    bounds = [
        jnp.sum(jnp.where(numbers < k, 1.0, 0.0), axis=1, keepdims=True) for k in (1, 2)
    ]
    count = table.shape[0]
    lane = lax.broadcasted_iota(jnp.int32, (8, 128), 1)[0:1]
    power = -(lane % (HEAD_DIM // 2)).astype(F32) / (HEAD_DIM // 2)
    freqs = jnp.exp(power * math.log(10000.0))
    phase = jnp.where(lane < HEAD_DIM, math.pi / 2, 0.0)
    sign = jnp.where((lane >= HEAD_DIM) & (lane < HEAD_DIM + HEAD_DIM // 2), -1.0, 1.0)

    def angles(block, carry):
        row = lax.broadcasted_iota(jnp.int32, (ROWS, 128), 0) + block * ROWS
        row = row.astype(F32)
        start = jnp.where(row >= bounds[0], bounds[0], 0.0)
        start = jnp.where(row >= bounds[1], bounds[1], start)
        pos = row - start
        here = slot_rows(block)
        table[here, 0:128] = jnp.sin(pos * freqs + phase) * sign
        table[here, 128:256] = pos
        return carry

    blocks = count // ROWS
    rows_x.relay()
    rows_cot.start(core=False)
    lax.fori_loop(0, blocks // 2, angles, 0)
    weights.step(1)
    lax.fori_loop(blocks // 2, blocks, angles, 0)
    local(table, table_out, local_sems.at[2])
    rows_x.near()
    norm(place.slot(1))
    norm(place.slot(2))
    rows_cot.relay()
    for number in range(2, line.count - 1):
        weights.step(number)
    rows_x.far()
    norm(place.slot(3))
    for mask in (1, 2, 3):
        rows_x.core(mask)
        norm(place.slot(mask, True))
    weights_out.step(0)
    rows_cot.near()
    weights.step(line.count - 1)
    local(weights_all, w_out, local_sems.at[3])
    local(normed_t, normed_t_out, local_sems.at[6])
    row, column = iotas(HEAD_DIM, inner)
    copies = jnp.where(column // SSM_DIM == row, 1.0, 0.0).astype(BF16)
    wide[:, 0:256] = jnp.concatenate(
        [weights_all[:, 384 : 384 + inner], weights_all[:, inner:256]], axis=1
    )
    wide[:, 256:512] = weights_all[:, 640:896]
    wide[:, 512:768] = jnp.concatenate([weights_all[:, :inner], weights_all[:, 256:320]], axis=1)
    wide[:, 768:1024] = jnp.concatenate(
        [
            dot(weights_all[:, 384 + inner : 640], copies),
            weights_all[:, 320:384].astype(F32),
        ],
        axis=1,
    ).astype(BF16)

    def project(slot):
        rows = pl.ds(slot * ROWS, ROWS)
        u[rows, :] = dot(normed[rows, :], wide[...])
        local(u.at[rows], u_out.at[rows], block_sems.at[0, slot])

    for slot in range(blocks // 2):
        project(slot)
    weights_out.step(1)
    rows_cot.far()
    for slot in range(blocks // 2, blocks):
        project(slot)
    for number in range(2, line.count):
        weights_out.step(number)
    local(wout_all, wout_out, local_sems.at[4])
    for mask in (1, 2, 3):
        rows_cot.core(mask)
    local(cot_all, cot_out, local_sems.at[5])
    for made in waiting:
        made.wait()
    rows_x.finish()
    rows_cot.finish()
    weights.finish()
    weights_out.finish()


def opening(tokens, cotangent, weights, gain, segments, taps, by_head):
    fsdp = lax.axis_size("fsdp")
    model = tokens.shape[1]
    count = segments.shape[1]
    blocks = count // ROWS
    vmem = pl.BlockSpec(memory_space=pltpu.VMEM)
    hbm = pl.BlockSpec(memory_space=pl.ANY)
    shape = jax.ShapeDtypeStruct
    dma = pltpu.SemaphoreType.DMA
    buffers = [
        ((model, count), BF16),
        ((count, 1024), F32),
        ((model, 896), BF16),
        ((model, 256), BF16),
        ((count, model), BF16),
        ((count, 256), F32),
    ]
    kept = [buffers[k] for k in (0, 1, 2, 3, 5)]
    return pl.pallas_call(
        opening_kernel,
        out_shape=tuple(shape(*one) for one in buffers) + (shape((8, 256), F32), shape((8, 512), F32)),
        in_specs=[hbm] * 2 + [vmem] * 15,
        out_specs=(hbm,) * 6 + (vmem,) * 2,
        scratch_shapes=[pltpu.VMEM((count, model), BF16)] * 3
        + [pltpu.VMEM(*one) for one in kept]
        + [
            pltpu.VMEM((model, 1024), BF16),
            dma((2, GATHER_SEMS)),
            dma((2, GATHER_SEMS)),
            line_sems(fsdp),
            line_sems(fsdp),
            dma((7,)),
            dma((1, blocks)),
        ],
        compiler_params=pltpu.CompilerParams(
            collective_id=3, has_side_effects=True, vmem_limit_bytes=60 << 20
        ),
        cost_estimate=pl.CostEstimate(
            flops=2 * count * model * 1024, bytes_accessed=30 << 20, transcendentals=count * 128
        ),
    )(
        tokens, cotangent, *weights, gain.reshape(1, -1), segments, *taps,
        *[one.reshape(1, -1) for one in by_head],
    )


def slot_rows(slot):
    return pl.ds(pl.multiple_of(slot * ROWS, ROWS), ROWS)


def norm_scale(values):
    return lax.rsqrt(jnp.mean(values * values, axis=1, keepdims=True) + epsilon)


def middle_kernel(
    ag_ref, wout_ref, gate_ref, up_ref, down_ref, gain_ref, x_hbm, cot_hbm, cot_all_hbm,
    hidden_ref, dag_ref, mixed_ref, dmixed_ref, dgain_ref, down_all_ref, ffn_ref, dout_ref,
    x_ref, cot_ref, cot_all_ref, nffn_ref, dgu_ref, dm_ref, dw_ref, arrived, part, wffn_ref, *scratch,
):
    place = Place()
    first = Scatter(place, scratch[0:5])
    back = Scatter(place, scratch[5:10])
    forth = Gather(place, nffn_ref, scratch[10])
    home = Gather(place, dm_ref, scratch[11])
    hid = hidden_ref.shape[1]
    line = Line()
    weights = LineGather(line, wffn_ref, scratch[12])
    share = gate_ref.shape[0]
    greetings = place.hello(line)
    half = pl.ds(pl.multiple_of(place.t * ROWS, ROWS), ROWS)
    loads = [
        pltpu.make_async_copy(source, target, scratch[14].at[k])
        for k, (source, target) in enumerate(
            ((x_hbm.at[half], x_ref), (cot_hbm.at[half], cot_ref), (cot_all_hbm, cot_all_ref))
        )
    ]
    for made in loads:
        made.start()
    mine = pl.ds(pl.multiple_of(line.f * share, share), share)
    lanes = pl.ds(pl.multiple_of(place.c * hid, hid), hid)
    for k, source in enumerate((gate_ref, up_ref, down_ref)):
        wffn_ref[mine, k * hid : (k + 1) * hid] = source[:, lanes]

    def block(mask, sibling=False):
        return dot(ag_ref[slot_rows(place.slot(mask, sibling)), :], wout_ref[...], 1, 1)

    for mask in SCATTER_ORDER:
        part[slot_rows(place.slot(mask, True)), :] = block(mask, True).astype(BF16)
    pl.semaphore_wait(pltpu.get_barrier_semaphore(), greetings)
    for mask in SCATTER_ORDER:
        first.to_core(mask, part.at[slot_rows(place.slot(mask, True))])
    weights.step(0)
    first.first(block, mixed_ref)
    weights.step(1)
    first.second()
    for made in loads:
        made.wait()
    mixed_ref[...] += x_ref[...].astype(F32)
    first.last(mixed_ref)
    mixed = mixed_ref[...]
    gain = gain_ref[...]
    scale = norm_scale(mixed)
    own = slot_rows(place.slot(0))
    nffn_ref[own, :] = (mixed * scale * gain).astype(BF16)
    forth.start()
    for number in range(2, line.count):
        weights.step(number)

    def work(slot):
        rows = slot_rows(slot)
        normed = nffn_ref[rows, :]
        gate_up = dot(normed, wffn_ref[:, : 2 * hid])
        dhidden = dot(cot_all_ref[rows, :], wffn_ref[:, 2 * hid :]).astype(BF16).astype(F32)
        gate, up = gate_up[:, :hid], gate_up[:, hid:]
        sig = sigmoid(gate)
        silu = gate * sig
        dgate = dhidden * up * (sig * (1.0 + gate * (1.0 - sig)))
        hidden_ref[rows, :] = (silu * up).astype(BF16)
        dgu_ref[rows, :hid] = dgate.astype(BF16)
        dgu_ref[rows, hid:] = (dhidden * silu).astype(BF16)
        part[rows, :] = dot(dgu_ref[rows, :], wffn_ref[:, : 2 * hid], 1, 1).astype(BF16)

    def hand_over(mask):
        slot = place.slot(mask, True)
        work(slot)
        back.to_core(mask, part.at[slot_rows(slot)])

    work(place.slot(0))
    forth.relay()
    forth.core(0)
    hand_over(0)
    forth.near()
    forth.core(1)
    hand_over(1)
    forth.core(2)
    hand_over(2)
    work(place.slot(1))
    forth.far()
    work(place.slot(2))
    forth.core(3)
    hand_over(3)
    work(place.slot(3))
    forth.finish()

    def ready(mask):
        return part[slot_rows(place.slot(mask)), :].astype(F32)

    back.first(ready, dmixed_ref)

    columns = (pl.ds(0, 2 * hid), pl.ds(2 * hid, hid))
    line_sent = []

    def line_copy(piece, step):
        rows = pl.ds(pl.multiple_of((line.f + step) % line.count * share, share), share)
        return line.copy(
            dw_ref.at[rows, columns[piece]],
            arrived.at[step, :, columns[piece]],
            scratch[13].at[piece],
            step,
        )

    def send_piece(piece, left, right):
        quarter = dw_ref.shape[0] // 4
        for k in range(4):
            rows = slice(k * quarter, (k + 1) * quarter)
            dw_ref[rows, columns[piece]] = dot(left[:, rows], right[...], 0, 0).astype(BF16)
        for step in range(1, line.count):
            made = line_copy(piece, step)
            made.start()
            line_sent.append(made)

    send_piece(1, cot_all_ref, hidden_ref)
    back.second()
    send_piece(0, nffn_ref, dgu_ref)
    back.last(dmixed_ref)
    dnffn = dmixed_ref[...]
    mixed = mixed_ref[...]
    scale = norm_scale(mixed)
    spread = dnffn * gain
    pull = jnp.mean(spread * mixed, axis=1, keepdims=True)
    dgain_ref[...] = jnp.broadcast_to(
        jnp.sum(dnffn * mixed * scale, axis=0, keepdims=True), dgain_ref.shape
    )
    dmixed = cot_ref[...].astype(F32) + scale * (spread - mixed * (scale * scale * pull))
    dmixed_ref[...] = dmixed
    dm_ref[own, :] = dmixed.astype(BF16)
    home.start()

    def pull_back(slot):
        rows = slot_rows(slot)
        dag_ref[rows, :] = dot(dm_ref[rows, :], wout_ref[...]).astype(BF16)

    pull_back(place.slot(0))
    home.relay()
    home.core(0)
    pull_back(place.slot(0, True))
    home.near()
    pull_back(place.slot(1))
    pull_back(place.slot(2))
    home.far()
    pull_back(place.slot(3))
    for mask in (1, 2, 3):
        home.core(mask)
        pull_back(place.slot(mask, True))
    dout_ref[...] = dot(dm_ref[...], ag_ref[...], 0, 0).astype(BF16)
    down_all_ref[...] = wffn_ref[:, 2 * hid :]
    for piece in (1, 0):
        sums = dw_ref[mine, columns[piece]].astype(F32)
        for step in range(1, line.count):
            line_copy(piece, step).wait_recv()
            sums = sums + arrived[step, :, columns[piece]].astype(F32)
        ffn_ref[:, columns[piece]] = sums.astype(BF16)
    for made in line_sent:
        made.wait_send()
    home.finish()
    weights.finish()


def middle(ag, wout, weights, x_own, cot_own, cot_all, gain):
    count, model = cot_all.shape
    hid = weights[0].shape[1] // lax.axis_size("context")
    columns = ag.shape[1]
    vmem = pl.BlockSpec(memory_space=pltpu.VMEM)
    hbm = pl.BlockSpec(memory_space=pl.ANY)
    shape = jax.ShapeDtypeStruct
    return pl.pallas_call(
        middle_kernel,
        out_shape=(
            shape((count, hid), BF16),
            shape((count, columns), BF16),
            shape((ROWS, model), F32),
            shape((ROWS, model), F32),
            shape((8, model), F32),
            shape((model, hid), BF16),
            shape((weights[0].shape[0], 3 * hid), BF16),
            shape((model, columns), BF16),
        ),
        in_specs=[vmem] * 6 + [hbm] * 3,
        out_specs=(vmem,) * 8,
        scratch_shapes=[
            pltpu.VMEM((ROWS, model), BF16),
            pltpu.VMEM((ROWS, model), BF16),
            pltpu.VMEM((count, model), BF16),
            pltpu.VMEM((count, model), BF16),
            pltpu.VMEM((count, 2 * hid), BF16),
            pltpu.VMEM((count, model), BF16),
            pltpu.VMEM((model, 3 * hid), BF16),
            pltpu.VMEM((lax.axis_size("fsdp"), weights[0].shape[0], 3 * hid), BF16),
            pltpu.VMEM((count, model), BF16),
            pltpu.VMEM((model, 3 * hid), BF16),
        ]
        + scatter_scratch(model)
        + scatter_scratch(model)
        + [pltpu.SemaphoreType.DMA((2, GATHER_SEMS))] * 2
        + [line_sems(lax.axis_size("fsdp")), pltpu.SemaphoreType.DMA((2, 2, lax.axis_size("fsdp"))), pltpu.SemaphoreType.DMA((3,))],
        compiler_params=pltpu.CompilerParams(
            collective_id=1, has_side_effects=True, vmem_limit_bytes=60 << 20
        ),
        cost_estimate=pl.CostEstimate(
            flops=20 * count * model * hid, bytes_accessed=40 << 20, transcendentals=count * hid
        ),
    )(ag, wout, *weights, gain.reshape(1, -1), x_own, cot_own, cot_all)


BACK_INPUTS = 5
EARLY = 384


def closing_kernel(
    pick_ref, dag_ref, kv_ref, heads_ref, taps_ref, dmixed_ref, gain_ref, ffn_ref,
    dgain_ref, dout_ref, table_hbm, y_hbm, conv_hbm, kept_hbm, states_hbm, normed_t_hbm, w_hbm,
    hidden_hbm, down_hbm, mixed_hbm, tokens_hbm,
    grad_ref, out_ref, early_ref, bc_ref, last_ref, mids_ref, outs_ref, small_ref,
    table, y, conv, kept, states, normed_t, w, hidden, down, x_ref,
    dnorm, early_du, dw_sum, dw, arrived, arrived_out, total, out_total, part, out_part, bc_out, bc_in, small_in,
    stats, dext, dpos, dstate, state_out, dkey_t, dvalue_t, *scratch,
):
    place = Place()
    line = Line()
    back = Scatter(place, scratch[0:5])
    final = Scatter(place, scratch[5:10])
    share = ffn_ref.shape[0]
    last_all = Gather(place, last_ref, scratch[10], share, False)
    early_all = Gather(place, early_ref, scratch[20], share, False)
    bc_all = Gather(place, bc_ref, scratch[21], share, False)
    mid_all = Gather(place, mids_ref, scratch[11], share, False)
    out_all = Gather(place, outs_ref, scratch[12], share, False)
    small_rows = small_in.shape[1]
    small_all = Gather(place, small_ref, scratch[13], small_rows)
    line_sems_, small_sems, out_sems, pair_sems, load_sems, block_sems = scratch[14:20]
    pair = Wire(place, pair_sems)
    greetings = place.hello(line)
    sent = []
    loads = [
        pltpu.make_async_copy(source, target, load_sems.at[k])
        for k, (source, target) in enumerate(
            (
                (hidden_hbm, hidden), (down_hbm, down), (normed_t_hbm, normed_t), (w_hbm, w),
                (mixed_hbm, out_total),
                (tokens_hbm.at[pl.ds(pl.multiple_of(place.t * ROWS, ROWS), ROWS)], x_ref),
            )
        )
    ]
    blocks = dnorm.shape[0] // ROWS
    streams = ((table_hbm, table), (y_hbm, y), (conv_hbm, conv), (kept_hbm, kept), (states_hbm, states))

    early_lanes = (pl.ds(0, 256), pl.ds(0, 512), pl.ds(0, 256), pl.ds(512, 256), None)
    late_lanes = (pl.ds(128, 128), pl.ds(0, 512), pl.ds(0, 512), pl.ds(0, 768), pl.ds(0, STATE))

    def fetch(block, buffer, late):
        copies = []
        for k, (source, target) in enumerate(streams):
            lanes = late_lanes[k] if late else early_lanes[k]
            if lanes is None:
                continue
            size = target.shape[1]
            begin = pl.multiple_of(block * size, size)
            copies.append(
                pltpu.make_async_copy(
                    source.at[pl.ds(begin, size), lanes],
                    target.at[buffer, :, lanes],
                    block_sems.at[buffer, k],
                )
            )
        return copies

    for made in fetch(blocks - 1, 0, False) + loads:
        made.start()
    mids_ref[pl.ds(pl.multiple_of(place.c * share, share), share), :] = ffn_ref[...]
    width = dext.shape[1]
    dext[ROWS : ROWS + 8, :] = jnp.zeros((8, width), F32)
    dpos[ROWS : ROWS + 8, :] = jnp.full((8, dpos.shape[1]), -1.0, F32)
    for ref in (dstate, state_out, dkey_t, dvalue_t, stats, dw_sum):
        ref[...] = jnp.zeros(ref.shape, F32)
    def out_block(mask, sibling=False):
        return dot(hidden[slot_rows(place.slot(mask, sibling)), :], down[...], 1, 1)

    def out_rows(mask):
        return out_block(mask) + out_total[...] if mask == 0 else out_block(mask)

    here = pl.ds(pl.multiple_of(place.c * share, share), share)
    own = pl.ds(pl.multiple_of(line.f * share, share), share)
    half = pl.ds(pl.multiple_of(place.t * ROWS, ROWS), ROWS)

    def my_half(ref):
        return lambda: ref.at[pl.ds(pl.multiple_of(place.t * ROWS, ROWS), ROWS)]

    def collect_out():
        sums = dout_ref[own, :].astype(F32)
        for step in range(1, line.count):
            line.copy(arrived_out.at[step - 1], arrived_out.at[step - 1], out_sems, step).wait_recv()
            sums = sums + arrived_out[step - 1].astype(F32)
        outs_ref[here, :] = sums.astype(BF16)
        out_all.start()

    def finish_out():
        final.last(out_total)
        out_ref[half, :] = out_total[...].astype(BF16)
        pair.send(my_half(out_ref), my_half(out_ref), 1, 4)

    def picked(source, row):
        marks = pick_ref[pl.ds(pl.multiple_of(row * 8, 8), 8), 0:1].astype(BF16)
        found = source[0:ROWS, :] * marks[0:1]
        for k in range(1, blocks):
            found = found + source[k * ROWS : (k + 1) * ROWS, :] * marks[k : k + 1]
        return found

    def prefetch(block, buffer, late):
        for made in fetch(block, buffer, late):
            made.start()

    def await_block(block, buffer, late):
        for made in fetch(block, buffer, late):
            made.wait()

    def happen(number, events):
        for when, actions in events.items():

            @pl.when(number == when)
            def _():
                for action in actions:
                    action()

    def early_turn(number, carry):
        block = blocks - 1 - number
        buffer = number % 2
        await_block(block, buffer, False)

        @pl.when(number < blocks - 1)
        def _():
            prefetch(block - 1, 1 - buffer, False)

        @pl.when(number == blocks - 1)
        def _():
            prefetch(blocks - 1, 1 - buffer, True)

        grads = attention_backward(
            block, picked(dag_ref, block), table.at[buffer], heads_ref, y.at[buffer], conv.at[buffer],
            kept.at[buffer], kv_ref, dkey_t, dvalue_t,
        )
        early_du[slot_rows(block), :] = grads
        dw_sum[:, :EARLY] += dot(normed_t[:, slot_rows(block)], grads)
        happen(number, {3: (lambda: final.first(out_rows, out_total),), 6: (mid_all.relay,)})
        return carry

    def late_turn(number, carry):
        block = blocks - 1 - number
        buffer = number % 2
        await_block(block, buffer, True)

        @pl.when(number < blocks - 1)
        def _():
            prefetch(block - 1, 1 - buffer, True)

        grads = recurrence_backward(
            picked(dag_ref, block), table.at[buffer], heads_ref, taps_ref, y.at[buffer],
            conv.at[buffer], kept.at[buffer], states.at[buffer], state_out, stats, dext, dpos, dstate,
        )
        whole = jnp.concatenate([early_du[slot_rows(block), :], grads], axis=1)
        dnorm[slot_rows(block), :] = dot(whole, w[...], 1, 1).astype(BF16)
        dw_sum[:, EARLY:] += dot(normed_t[:, slot_rows(block)], grads)
        happen(
            number,
            {
                1: (mid_all.near,),
                3: (collect_out, mid_all.far),
                5: (final.second,),
                6: (out_all.relay,),
            },
        )
        return carry

    columns = (pl.ds(0, EARLY), pl.ds(EARLY + 256, 256), pl.ds(EARLY, 256))

    def line_copy(piece, step):
        rows = pl.ds(pl.multiple_of((line.f + step) % line.count * share, share), share)
        return line.copy(
            dw.at[rows, columns[piece]], arrived.at[step - 1, :, columns[piece]], line_sems_.at[piece], step
        )

    def send_piece(piece):
        dw[:, columns[piece]] = dw_sum[:, columns[piece]].astype(BF16)
        for step in range(1, line.count):
            made = line_copy(piece, step)
            made.start()
            sent.append(made)

    def collected(piece):
        sums = dw[own, columns[piece]].astype(F32)
        for step in range(1, line.count):
            line_copy(piece, step).wait_recv()
            sums = sums + arrived[step - 1, :, columns[piece]].astype(F32)
        return sums.astype(BF16)

    for made in loads:
        made.wait()
    early_turn(0, 0)
    pl.semaphore_wait(pltpu.get_barrier_semaphore(), greetings)
    for step in range(1, line.count):
        rows = pl.ds(pl.multiple_of((line.f + step) % line.count * share, share), share)
        made = line.copy(dout_ref.at[rows], arrived_out.at[step - 1], out_sems, step)
        made.start()
        sent.append(made)
    for k, mask in enumerate(SCATTER_ORDER):
        out_part[k] = out_block(mask, True).astype(BF16)
        final.to_core(mask, out_part.at[k])
    mid_all.start()
    lax.fori_loop(1, blocks, early_turn, 0)
    send_piece(0)
    lax.fori_loop(0, blocks, late_turn, 0)
    send_piece(1)
    send_piece(2)

    def block_of(mask, sibling=False):
        return picked(dnorm, place.slot(mask, sibling) + blocks)

    for k, mask in enumerate(SCATTER_ORDER):
        part[k] = block_of(mask, True)
        back.to_core(mask, part.at[k])
    back.first(lambda mask: block_of(mask).astype(F32), total)
    out_all.near()
    finish_out()
    out_all.far()
    early_ref[here, :] = collected(0)
    back.second()
    early_all.start()
    bc_out[...] = collected(1)
    pair.send(bc_out, bc_in, 2, 4)
    back.last(total)
    early_all.relay()
    dnormed = total[...]
    x = x_ref[...].astype(F32)
    gain = gain_ref[...]
    scale = norm_scale(x)
    spread = dnormed * gain
    pull = jnp.mean(spread * x, axis=1, keepdims=True)
    grad = dmixed_ref[...] + scale * (spread - x * (scale * scale * pull))
    grad_ref[half, :] = grad.astype(BF16)
    pair.send(grad_ref.at[half], grad_ref.at[half], 0, 4)
    small_in[0] = jnp.zeros(small_in.shape[1:], F32)
    small_in[0, 0:1, :] = jnp.sum(dnormed * x * scale, axis=0, keepdims=True)
    small_in[0, 1:2, :] = dgain_ref[0:1, :]
    small_in[0, 8:16, :width] = stats[...]
    for step in range(1, line.count):
        made = line.copy(small_in.at[0], small_in.at[step], small_sems, step)
        made.start()
        sent.append(made)
    pair.arrive(bc_in, 2, 4)
    bc_ref[here, :] = (bc_out[...].astype(F32) + bc_in[...].astype(F32)).astype(BF16)
    bc_all.start()
    early_all.near()
    last_ref[here, :] = collected(2)
    last_all.start()
    bc_all.relay()
    for step in range(1, line.count):
        line.copy(small_in.at[0], small_in.at[step], small_sems, step).wait_recv()
    summed = small_in[line.f % line.count]
    for other in range(1, line.count):
        summed = summed + small_in[(line.f + line.count - other) % line.count]
    mine = pl.ds(pl.multiple_of(place.slot(0) * small_rows, small_rows), small_rows)
    small_ref[mine, :] = summed
    small_all.start()
    early_all.far()
    last_all.relay()
    small_all.relay()
    small_all.near()
    small_all.far()
    bc_all.near()
    bc_all.far()
    last_all.near()
    last_all.far()
    for mask in range(4):
        small_all.core(mask)
    other = pl.ds(pl.multiple_of((1 - place.t) * ROWS, ROWS), ROWS)
    pair.arrive(grad_ref.at[other], 0, 4)
    pair.arrive(out_ref.at[other], 1, 4)
    for made in sent:
        made.wait_send()
    pair.finish()
    mid_all.finish()
    out_all.finish()
    small_all.finish()
    last_all.finish()
    early_all.finish()
    bc_all.finish()


def closing(small_inputs, streams, loads, fsdp):
    ffn, dout = small_inputs[7], small_inputs[9]
    normed_t, w, hidden, down, _, _ = loads
    model, count = normed_t.shape
    share = ffn.shape[0]
    columns = w.shape[1]
    chips = lax.axis_size("context")
    blocks = count // ROWS
    vmem = pl.BlockSpec(memory_space=pltpu.VMEM)
    hbm = pl.BlockSpec(memory_space=pl.ANY)
    shape = jax.ShapeDtypeStruct
    dma = pltpu.SemaphoreType.DMA
    space = pltpu.VMEM
    inner = streams[4].shape[0] // blocks
    return pl.pallas_call(
        closing_kernel,
        out_shape=(
            shape((2 * ROWS, model), BF16),
            shape((2 * ROWS, model), BF16),
            shape((chips * share, EARLY), BF16),
            shape((chips * share, 256), BF16),
            shape((chips * share, 256), BF16),
            shape((chips * share, ffn.shape[1]), BF16),
            shape((chips * share, dout.shape[1]), BF16),
            shape((2 * chips * 16, model), F32),
        ),
        in_specs=[vmem] * 10 + [hbm] * 11,
        out_specs=(vmem,) * 8,
        scratch_shapes=[space((2, one.shape[0] // blocks, one.shape[1]), one.dtype) for one in streams]
        + [space(one.shape, one.dtype) for one in loads[:4]]
        + [space((ROWS, model), BF16)]
        + [
            space((count, model), BF16),
            space((count, EARLY), BF16),
            space((model, columns), F32),
            space((model, columns), BF16),
            space((fsdp - 1, share, columns), BF16),
            space((fsdp - 1, share, dout.shape[1]), BF16),
            space((ROWS, model), F32),
            space((ROWS, model), F32),
            space((4, ROWS, model), BF16),
            space((4, ROWS, model), BF16),
            space((share, 256), BF16),
            space((share, 256), BF16),
            space((fsdp, 16, model), F32),
            space((8, 512), F32),
            space((ROWS + 8, 512), F32),
            space((ROWS + 8, 128), F32),
            space((inner, STATE), F32),
            space((inner, STATE), F32),
            space((HEAD_DIM, count), F32),
            space((HEAD_DIM, count), F32),
        ]
        + scatter_scratch(model)
        + scatter_scratch(model)
        + [dma((2, GATHER_SEMS))] * 4
        + [dma((3, 2, fsdp)), dma((2, fsdp)), dma((2, fsdp)), dma((2, 3)), dma((6,)), dma((2, BACK_INPUTS)), dma((2, GATHER_SEMS)), dma((2, GATHER_SEMS))],
        compiler_params=pltpu.CompilerParams(
            collective_id=2, has_side_effects=True, vmem_limit_bytes=61 << 20
        ),
        cost_estimate=pl.CostEstimate(
            flops=4 * count * model * columns, bytes_accessed=30 << 20, transcendentals=0
        ),
    )(*small_inputs, *streams, *loads)


def assemble_kernel(
    early_ref, bcs_ref, late_ref, mid_ref, outs_ref, dx_ref, out_in_ref, small_ref, steps_ref,
    out_ref, grad_ref, query_ref, keyval_ref, attn_ref, gate_ref, x_ref, bc_ref, step_ref, ssm_ref,
    ffn_gate_ref, ffn_up_ref, ffn_down_ref, gain_ref, gain_ffn_ref, conv_x_ref, conv_bc_ref,
    bias_ref, decay_ref, skip_ref,
):
    chips = late_ref.shape[0]
    heads = step_ref.shape[0] // chips
    inner = heads * SSM_DIM
    hid = ffn_gate_ref.shape[1] // chips

    def spread(source, begin, width):
        return jnp.concatenate(
            [source[k, :, begin : begin + width].astype(F32) for k in range(chips)], axis=1
        )

    def summed(source, begin, end):
        total = source[0, :, begin:end].astype(F32)
        for k in range(1, chips):
            total = total + source[k, :, begin:end].astype(F32)
        return total

    out_ref[...] = out_in_ref[...]
    grad_ref[...] = dx_ref[...]
    gate_ref[...] = spread(early_ref, 0, inner)
    query_ref[...] = spread(early_ref, inner, HEAD_DIM)
    keyval_ref[...] = summed(early_ref, 256, 384)
    x_ref[...] = spread(late_ref, 0, inner)
    bc_ref[...] = summed(bcs_ref, 0, 256)
    ffn_gate_ref[...] = spread(mid_ref, 0, hid)
    ffn_up_ref[...] = spread(mid_ref, hid, hid)
    ffn_down_ref[...] = spread(mid_ref, 2 * hid, hid)
    ssm_ref[...] = spread(outs_ref, 0, inner)
    attn_ref[...] = spread(outs_ref, inner, HEAD_DIM)

    @pl.when(pl.program_id(0) == 0)
    def _():
        step_ref[...] = spread(steps_ref, inner, heads).T
        everywhere = small_ref[0:16, :]
        for k in range(1, small_ref.shape[0] // 16):
            everywhere = everywhere + small_ref[16 * k : 16 * k + 16, :]
        gain_ref[...] = everywhere[0:1]
        gain_ffn_ref[...] = everywhere[1:2]
        conv_bc_ref[...] = everywhere[8 : 8 + CONV, 256:512]
        core = lax.axis_index("tensor")
        own = [
            small_ref[pl.ds(pl.multiple_of((2 * k + core) * 16, 16), 16), :] for k in range(chips)
        ]
        conv_x_ref[...] = jnp.concatenate([one[8 : 8 + CONV, :inner] for one in own], axis=1)
        for row, target in ((12, skip_ref), (13, bias_ref), (14, decay_ref)):
            target[...] = jnp.concatenate(
                [
                    jnp.sum(
                        one[row : row + 1, h * SSM_DIM : (h + 1) * SSM_DIM], axis=1, keepdims=True
                    )
                    for one in own
                    for h in range(heads)
                ],
                axis=1,
            )


def assemble(early, bcs, last, mid, outs, dx, out, small, widths, heads):
    chips = lax.axis_size("context")
    share = last.shape[0] // chips
    turns = 2
    rows = share // turns
    shape = jax.ShapeDtypeStruct
    block = lambda height, width: pl.BlockSpec((height, width), lambda i: (i, 0))
    fixed = lambda height, width: pl.BlockSpec((height, width), lambda i: (0, 0))
    slab = lambda width: pl.BlockSpec((chips, rows, width), lambda i: (0, i, 0))
    token_rows = dx.shape[0] // turns
    model = dx.shape[1]
    tiny = [
        (1, model), (1, model), (CONV, heads * SSM_DIM), (CONV, 2 * STATE), (1, heads), (1, heads),
        (1, heads),
    ]
    return pl.pallas_call(
        assemble_kernel,
        grid=(turns,),
        out_shape=(shape(out.shape, BF16), shape(dx.shape, BF16))
        + tuple(shape((share, w) if w > heads else (w, share), F32) for w in widths)
        + tuple(shape(one, F32) for one in tiny),
        in_specs=[
            slab(early.shape[1]), slab(bcs.shape[1]), slab(last.shape[1]), slab(mid.shape[1]), slab(outs.shape[1]),
            block(token_rows, model), block(token_rows, model), fixed(*small.shape),
            pl.BlockSpec((chips, share, last.shape[1]), lambda i: (0, 0, 0)),
        ],
        out_specs=(block(token_rows, model), block(token_rows, model))
        + tuple(block(rows, w) if w > heads else fixed(w, share) for w in widths)
        + tuple(fixed(*one) for one in tiny),
        compiler_params=pltpu.CompilerParams(vmem_limit_bytes=60 << 20),
    )(*[one.reshape(chips, share, -1) for one in (early, bcs, last, mid, outs)], dx, out, small,
      last.reshape(chips, share, -1))


def per_device(
    tokens, segments, deal, gain_mix, w_query, w_keyval, w_attn_out, w_gate_z, w_in_x, w_bc, w_step,
    conv_x, conv_bc, step_bias, decay_log, skip, w_ssm_out, gain_ffn, w_ffn_gate, w_ffn_up,
    w_ffn_down, cotangent,
):
    ids = jnp.arange(deal.shape[1], dtype=jnp.int32)
    holds = (deal[0][:, None] == ids[None, :]).astype(F32)
    pick = jnp.broadcast_to(jnp.concatenate([holds.T, holds]).reshape(-1, 1), (128, 128))
    normed_t, u, w_all, wout_all, cot_all, table, head_rows, taps = opening(
        tokens,
        cotangent,
        (w_in_x, w_query, w_bc, w_gate_z, w_keyval, w_step.T, w_ssm_out, w_attn_out),
        gain_mix,
        segments,
        (conv_x, conv_bc),
        (step_bias, decay_log, skip),
    )
    ag, y, conv, states, keyval, kept, normed_t = mixer_forward(u, normed_t, table, head_rows, taps, deal[0])
    hidden, dag, mixed, dmixed, dgain, down, dffn, dout = middle(
        ag, wout_all, (w_ffn_gate, w_ffn_up, w_ffn_down), tokens, cotangent, cot_all, gain_ffn
    )
    dx, out, early, bcs, last, mids, outs, small = closing(
        (
            pick, dag, keyval, head_rows, taps, dmixed, gain_mix.reshape(1, -1), dffn,
            dgain, dout,
        ),
        (table, y, conv, kept, states),
        (normed_t, w_all, hidden, down, mixed, tokens),
        lax.axis_size("fsdp"),
    )
    weights = (
        w_query, w_keyval, w_attn_out, w_gate_z, w_in_x, w_bc, w_step, w_ssm_out, w_ffn_gate,
        w_ffn_up, w_ffn_down,
    )
    done = assemble(early, bcs, last, mids, outs, dx, out, small, [w.shape[1] for w in weights], skip.shape[0])
    grads = done[2:13]
    gain, gain_two, taps_x, taps_bc, bias, decay, skips = done[13:]
    return (
        done[0],
        done[1],
        gain.reshape(-1),
        *grads[:6],
        grads[6].T,
        taps_x,
        taps_bc,
        bias.reshape(-1),
        decay.reshape(-1),
        skips.reshape(-1),
        grads[7],
        gain_two.reshape(-1),
        *grads[8:],
    )


def solution(mesh):
    in_specs = (
        P(("fsdp", "context"), None),
        P("fsdp", None),
        P("fsdp", None),
        P(),
        P("fsdp", "tensor"),
        P("fsdp", "tensor"),
        P("fsdp", "tensor"),
        P("fsdp", "tensor"),
        P("fsdp", "tensor"),
        P("fsdp", None),
        P("fsdp", "tensor"),
        P(None, "tensor"),
        P(),
        P("tensor"),
        P("tensor"),
        P("tensor"),
        P("fsdp", "tensor"),
        P(),
        P("fsdp", "tensor"),
        P("fsdp", "tensor"),
        P("fsdp", "tensor"),
        P(("fsdp", "context"), None),
    )
    out_specs = (
        P(("fsdp", "context"), None),
        P(("fsdp", "context"), None),
        P(),
        P("fsdp", "tensor"),
        P("fsdp", "tensor"),
        P("fsdp", "tensor"),
        P("fsdp", "tensor"),
        P("fsdp", "tensor"),
        P("fsdp", None),
        P("fsdp", "tensor"),
        P(None, "tensor"),
        P(),
        P("tensor"),
        P("tensor"),
        P("tensor"),
        P("fsdp", "tensor"),
        P(),
        P("fsdp", "tensor"),
        P("fsdp", "tensor"),
        P("fsdp", "tensor"),
    )
    return jax.shard_map(
        per_device, mesh=mesh, in_specs=in_specs, out_specs=out_specs, check_vma=False
    )
```

```python
import functools
import math

import jax
import jax.numpy as jnp
from jax import lax
from jax.experimental import pallas as pl
from jax.experimental.pallas import tpu as pltpu
from jax.sharding import PartitionSpec as P

HEAD_DIM = 64
SSM_DIM = 64
STATE = 128
CONV = 4
HALF = 256
WINDOW = 4

epsilon = 1e-05
masked = -1e30
F32 = jnp.float32
BF16 = jnp.bfloat16
exact = lax.Precision.HIGHEST


def dot(left, right, left_dim=1, right_dim=0, precision=None):
    return lax.dot_general(
        left,
        right,
        (((left_dim,), (right_dim,)), ((), ())),
        precision=precision,
        preferred_element_type=F32,
    )


def exact_sums(ones, values, right_dim=0):
    high = values.astype(BF16)
    rest = values - high.astype(F32)
    middle = rest.astype(BF16)
    low = (rest - middle.astype(F32)).astype(BF16)
    return sum(dot(ones, one, 1, right_dim) for one in (low, middle, high))


def sigmoid(v):
    return 1.0 / (1.0 + jnp.exp(-v))


def softplus(v):
    return jnp.maximum(v, 0.0) + jnp.log1p(jnp.exp(-jnp.abs(v)))


def swap_halves(v):
    half = v.shape[1] // 2
    return jnp.concatenate([v[:, half:], v[:, :half]], axis=1)


def iotas(rows, columns):
    return (
        lax.broadcasted_iota(jnp.int32, (rows, columns), 0),
        lax.broadcasted_iota(jnp.int32, (rows, columns), 1),
    )


def state_scale(last_row, carry_last, heads):
    pieces = [
        jnp.broadcast_to(last_row[:, h * SSM_DIM : h * SSM_DIM + 1], (SSM_DIM, STATE))
        for h in range(heads)
    ]
    return jnp.exp(jnp.concatenate(pieces, axis=0)) * carry_last


def block_decays(step_raw, heads_ref, lane_pos, heads):
    rows = step_raw.shape[0]
    inner = heads * SSM_DIM
    raw = step_raw + heads_ref[0:1, :inner]
    step = softplus(raw)
    rate = step * jnp.exp(heads_ref[1:2, :inner])
    row, col = iotas(rows, rows)
    lower = jnp.where(col <= row, 1.0, 0.0).astype(BF16)
    totals = exact_sums(lower, -rate)
    last_row = totals[rows - 1 : rows]
    pos_last = lane_pos[rows - 1 : rows, 0:1]
    local = lax.broadcasted_iota(jnp.int32, (rows, 1), 0).astype(F32)
    carry_on = (lane_pos[:, 0:1] > local).astype(F32)
    keep_last = (local >= (rows - 1) - pos_last).astype(F32)
    carry_last = (pos_last > rows - 1).astype(F32)
    factor = jnp.exp(totals) * carry_on
    tails = jnp.exp(last_row - totals) * keep_last
    return raw, step, rate, totals, last_row, carry_last, factor, tails


def local_mask(lane_pos, rows):
    row, col = iotas(rows, rows)
    gap = (row - col).astype(F32)
    return (gap >= 0) & (gap <= lane_pos[:, 0:1])


def key_window(block):
    start = jnp.maximum(block - WINDOW, 0)
    return start, (block - start) * HALF


def window_mask(lane_pos, offset, rows, keys):
    last = (lax.broadcasted_iota(jnp.int32, (rows, 1), 0) + offset).astype(F32)
    col = lax.broadcasted_iota(jnp.int32, (8, keys), 1)[0:1].astype(F32)
    return (col <= last) & (col >= last - lane_pos[:, 0:1])


def head_decay(totals, totals_t, h, allowed):
    gap = totals[:, h * SSM_DIM : h * SSM_DIM + 1] - totals_t[h * SSM_DIM : h * SSM_DIM + 1, :]
    return jnp.exp(jnp.where(allowed, gap, masked))


def mixer_forward_kernel(
    order_ref, u_ref, normed_ref, table_ref, heads_ref, taps_ref, ag_ref, y_ref, conv_ref, state_in_ref,
    kv_ref, kept_ref, ordered_ref, kv_t_ref, ext, state, keys_t, values, found,
):
    block = pl.program_id(0)
    heads = state.shape[0] // SSM_DIM
    inner = heads * SSM_DIM
    width = ext.shape[1]
    rows = u_ref.shape[0]

    @pl.when(block == 0)
    def _():
        ext[0:8, :] = jnp.zeros((8, width), F32)
        state[...] = jnp.zeros(state.shape, F32)
        keys_t[...] = jnp.zeros(keys_t.shape, BF16)
        values[...] = jnp.zeros(values.shape, BF16)

    lane_pos = table_ref[:, 128:256]
    cosine = table_ref[:, 0:64]
    sine = table_ref[:, 64:128]
    q_at = inner
    u = u_ref[:, :width].astype(F32)
    ext[8 : 8 + rows, :] = u
    conv = u * taps_ref[CONV - 1 : CONV, :]
    for back in range(1, CONV):
        reach = lane_pos[:, 0:1] >= back
        shifted = ext[8 - back : 8 - back + rows, :]
        conv = conv + jnp.where(reach, shifted, 0.0) * taps_ref[CONV - 1 - back : CONV - back, :]
    ext[0:8, :] = u[rows - 8 : rows]
    act = conv * sigmoid(conv)
    ssm_x = act[:, :inner].astype(BF16)
    ssm_b = act[:, 256:384].astype(BF16)
    ssm_c = act[:, 384:512].astype(BF16)
    conv_ref[:, 0:256] = conv[:, 0:256]
    conv_ref[:, 256:512] = conv[:, 256:512]
    query = u[:, q_at : q_at + HEAD_DIM]
    query = (query * cosine + swap_halves(query) * sine).astype(BF16)
    conv_ref[:, q_at : q_at + HEAD_DIM] = query.astype(F32)
    key = u_ref[:, 512 + inner : 512 + inner + HEAD_DIM].astype(F32)
    key = key * cosine + swap_halves(key) * sine
    value = u_ref[:, 768 + inner : 768 + inner + HEAD_DIM].astype(F32)
    pair = jnp.concatenate([key, value], axis=1).astype(BF16)
    pair_t = jnp.concatenate([key, value], axis=1).T.astype(BF16)
    kv_ref[...] = pair
    kv_t_ref[...] = pair_t
    here = pl.ds(pl.multiple_of(block * rows, rows), rows)
    values[here, :] = value.astype(BF16)
    keys_t[:, here] = pair_t[:HEAD_DIM]
    query_low = query * 0.125

    def attend(first, offset, span):
        begin = pl.multiple_of(first * rows, rows)
        scores = dot(query_low, keys_t[:, pl.ds(begin, span)])
        scores = jnp.where(window_mask(lane_pos, offset, rows, span), scores, masked)
        highest = jnp.max(scores, axis=1, keepdims=True)
        weights = jnp.exp(scores - highest)
        total = jnp.sum(weights, axis=1, keepdims=True)
        probs = (weights * (1.0 / total)).astype(BF16)
        found[:, :HEAD_DIM] = dot(probs, values[pl.ds(begin, span), :])
        found[:, HEAD_DIM:] = jnp.broadcast_to(highest + jnp.log(total), (rows, HEAD_DIM))

    @pl.when(block < 2)
    def _():
        attend(0, block * rows, 2 * HALF)

    @pl.when((block >= 2) & (block < WINDOW))
    def _():
        attend(0, block * rows, WINDOW * HALF)

    @pl.when(block >= WINDOW)
    def _():
        attend(block - WINDOW, WINDOW * rows, (WINDOW + 1) * HALF)

    attended = found[:, :HEAD_DIM]
    _, step, _, totals, last_row, carry_last, factor, tails = block_decays(
        u_ref[:, 768 : 768 + inner].astype(F32), heads_ref, lane_pos, heads
    )
    totals_t = totals.T
    allowed = local_mask(lane_pos, rows)
    cross = dot(ssm_c, ssm_b, 1, 1)
    x_f = ssm_x.astype(F32)
    stepped = step * x_f
    stepped_low = stepped.astype(BF16)
    parts = []
    for h in range(heads):
        lanes = slice(h * SSM_DIM, (h + 1) * SSM_DIM)
        mix = (head_decay(totals, totals_t, h, allowed) * cross).astype(BF16)
        parts.append(dot(mix, stepped_low[:, lanes]))
    held = state[...]
    state_in_ref[...] = held
    y_pure = jnp.concatenate(parts, axis=1) + factor * dot(ssm_c, held.astype(BF16), 1, 1)
    tailed = (tails * stepped_low.astype(F32)).astype(BF16)
    state[...] = state_scale(last_row, carry_last, heads) * held + dot(tailed, ssm_b, 0, 0)
    y_ref[:, 0:256] = jnp.concatenate(
        [y_pure, found[:, HEAD_DIM:]], axis=1
    )
    y_ref[:, 256:512] = jnp.concatenate([u_ref[:, 768 : 768 + inner], attended], axis=1)
    ordered_ref[...] = normed_ref[...]
    kept_ref[...] = u_ref[:, 0:768].astype(BF16)
    y_full = y_pure + heads_ref[2:3, :inner] * x_f
    gate = u_ref[:, 512 : 512 + inner].astype(F32)
    gated = y_full * (gate * sigmoid(gate))
    ag_ref[...] = jnp.concatenate([gated, attended], axis=1).astype(BF16)


def attention_backward(
    block, dag, table_ref, heads_ref, y_ref, conv_ref, kept_ref, kv_ref, kv_t_ref, dkey_t, dvalue_t,
):
    inner = dag.shape[1] - HEAD_DIM
    rows = dag.shape[0]
    lane_pos = table_ref[:, 128:256]
    cosine = table_ref[:, 0:64]
    sine = table_ref[:, 64:128]
    first, offset = key_window(block)
    span = (WINDOW + 1) * HALF
    begin = pl.multiple_of(first * rows, rows)
    keys = kv_ref[pl.ds(begin, span), :HEAD_DIM]
    keys_t = kv_t_ref[:HEAD_DIM, pl.ds(begin, span)]
    values_t = kv_t_ref[HEAD_DIM:, pl.ds(begin, span)]
    query = conv_ref[:, inner : inner + HEAD_DIM] * 0.125
    query_low = query.astype(BF16)
    datt = dag[:, inner : inner + HEAD_DIM]
    datt_f = datt.astype(F32)
    lse = y_ref[:, inner : inner + 1]
    scores = dot(query_low, keys_t)
    allowed_all = window_mask(lane_pos, offset, rows, span)
    probs = jnp.exp(jnp.where(allowed_all, scores, masked) - lse)
    inward = jnp.sum(datt_f * y_ref[:, 256 + inner : 256 + inner + HEAD_DIM], axis=1, keepdims=True)
    dscores = (probs * (dot(datt, values_t) - inward)).astype(BF16)
    dquery = dot(dscores, keys) * 0.125
    dkey_t[:, pl.ds(begin, span)] += dot(query.T.astype(BF16), dscores)
    dvalue_t[:, pl.ds(begin, span)] += dot(datt_f.T.astype(BF16), probs.astype(BF16))
    here = pl.ds(pl.multiple_of(block * rows, rows), rows)
    dkey = dkey_t[:, here].T
    dvalue = dvalue_t[:, here].T
    dquery = dquery * cosine - swap_halves(dquery) * sine
    dkey = dkey * cosine - swap_halves(dkey) * sine
    conv = conv_ref[:, :inner]
    ssm_x = (conv * sigmoid(conv)).astype(BF16).astype(F32)
    gate = kept_ref[:, 512 : 512 + inner].astype(F32)
    sig = sigmoid(gate)
    dgated = dag[:, :inner].astype(F32)
    y_full = y_ref[:, :inner] + heads_ref[2:3, :inner] * ssm_x
    dgate = dgated * y_full * (sig * (1.0 + gate * (1.0 - sig)))
    return jnp.concatenate([dgate, dquery, dkey, dvalue], axis=1).astype(BF16)


def recurrence_backward(
    dag, table_ref, heads_ref, taps_ref, y_ref, conv_ref, kept_ref, state_in_ref, state_out, stats_ref,
    dext, dpos, dstate,
):
    heads = dstate.shape[0] // SSM_DIM
    inner = heads * SSM_DIM
    rows = dag.shape[0]
    lane_pos = table_ref[:, 128:256]
    conv = conv_ref[...]
    gate_conv = sigmoid(conv)
    act = conv * gate_conv
    dact = gate_conv * (1.0 + conv * (1.0 - gate_conv))
    ssm_x = act[:, :inner].astype(BF16)
    ssm_b = act[:, 256:384].astype(BF16)
    ssm_c = act[:, 384:512].astype(BF16)
    x_f = ssm_x.astype(F32)
    raw, step, rate, totals, last_row, carry_last, factor, tails = block_decays(
        y_ref[:, 256 : 256 + inner], heads_ref, lane_pos, heads
    )
    totals_t = totals.T
    allowed = local_mask(lane_pos, rows)
    cross = dot(ssm_c, ssm_b, 1, 1)
    gate = kept_ref[:, 512 : 512 + inner].astype(F32)
    sig = sigmoid(gate)
    y_pure = y_ref[:, :inner]
    dgated = dag[:, :inner].astype(F32)
    skip = heads_ref[2:3, :inner]
    dy = dgated * (gate * sig)
    dy_low = dy.astype(BF16)
    dy_r = dy_low.astype(F32)
    dy_t = dy.T.astype(BF16)
    stepped_low = (step * x_f).astype(BF16)
    stepped_r = stepped_low.astype(F32)
    tailed = (tails * stepped_r).astype(BF16)
    dcross = jnp.zeros((rows, rows), F32)
    parts = []
    for h in range(heads):
        lanes = slice(h * SSM_DIM, (h + 1) * SSM_DIM)
        decay = head_decay(totals, totals_t, h, allowed)
        mix = (decay * cross).astype(BF16)
        parts.append(dot(dy_t[lanes, :], mix))
        dcross = dcross + dot(dy_low[:, lanes], stepped_low[:, lanes], 1, 1) * decay
    dstep_x = jnp.concatenate(parts, axis=0).T
    dcross_low = dcross.astype(BF16)
    held = state_in_ref[...].astype(BF16)
    dheld = dstate[...]
    dheld_low = dheld.astype(BF16)
    dfactored = (factor * dy).astype(BF16)
    from_state = dot(ssm_b, dheld_low, 1, 1)
    dssm_c = dot(dcross_low, ssm_b) + dot(dfactored, held)
    dssm_b = dot(dcross_low, ssm_c, 0, 0) + dot(tailed, dheld_low)
    dtotals = dy_r * y_pure - stepped_r * dstep_x - tailed.astype(F32) * from_state
    dstep_x = dstep_x + tails * from_state
    end_term = exact_sums(
        jnp.ones((16, STATE), BF16), dheld_low.astype(F32) * state_out[...], 1
    )[0:1]
    row, col = iotas(rows, rows)
    upper = jnp.where(col >= row, 1.0, 0.0).astype(BF16)
    drate = -(exact_sums(upper, dtotals) + end_term)
    state_out[...] = state_in_ref[...]
    dstate[...] = state_scale(last_row, carry_last, heads) * dheld + dot(dfactored, ssm_c, 0, 0)
    dssm_x = step * dstep_x + skip * dy
    dstep = x_f * dstep_x + jnp.exp(heads_ref[1:2, :inner]) * drate
    draw = dstep * sigmoid(raw)
    none = jnp.zeros((rows, HEAD_DIM), F32)
    dconv = jnp.concatenate([dssm_x, none, dssm_b, dssm_c], axis=1) * dact
    dext[0:rows, :] = dconv
    dpos[0:rows, :] = lane_pos
    u = kept_ref[:, 0:512].astype(F32)
    du = dconv * taps_ref[CONV - 1 : CONV, :]
    stats_ref[CONV - 1 : CONV, :] += jnp.sum(dconv * u, axis=0, keepdims=True)
    for ahead in range(1, CONV):
        reach = dpos[ahead : ahead + rows, 0:1] >= ahead
        shifted = jnp.where(reach, dext[ahead : ahead + rows, :], 0.0)
        tap = CONV - 1 - ahead
        du = du + shifted * taps_ref[tap : tap + 1, :]
        stats_ref[tap : tap + 1, :] += jnp.sum(shifted * u, axis=0, keepdims=True)
    dext[rows : rows + 8, :] = dconv[0:8]
    dpos[rows : rows + 8, :] = lane_pos[0:8]
    stats_ref[4:5, :inner] += jnp.sum(dy * x_f, axis=0, keepdims=True)
    stats_ref[5:6, :inner] += jnp.sum(draw, axis=0, keepdims=True)
    stats_ref[6:7, :inner] += jnp.sum(drate * rate, axis=0, keepdims=True)
    summed = [
        jnp.sum(draw[:, h * SSM_DIM : (h + 1) * SSM_DIM], axis=1, keepdims=True)
        for h in range(heads)
    ]
    lane = lax.broadcasted_iota(jnp.int32, (rows, HEAD_DIM), 1)
    dstep_all = jnp.zeros((rows, HEAD_DIM), F32)
    for h in range(heads):
        dstep_all = jnp.where(lane == h, summed[h], dstep_all)
    return jnp.concatenate([du[:, :inner], dstep_all, du[:, 256:512]], axis=1).astype(BF16)


def slot_holding(order, block):
    slot = 0
    for k in range(1, order.shape[0]):
        slot = slot + jnp.where(order[k] == block, k, 0)
    return slot


def mixer_forward(u, normed_t, table, head_rows, taps, slot_of):
    count = u.shape[0]
    blocks = count // HALF
    heads = 3
    inner = heads * SSM_DIM
    width = taps.shape[1]
    at_slot = lambda i, order: (slot_holding(order, i), 0)
    in_order = lambda i, slots: (i, 0)
    whole = lambda i, slots: (0, 0)
    return pl.pallas_call(
        mixer_forward_kernel,
        out_shape=(
            jax.ShapeDtypeStruct((count, inner + HEAD_DIM), BF16),
            jax.ShapeDtypeStruct((count, 512), F32),
            jax.ShapeDtypeStruct((count, width), F32),
            jax.ShapeDtypeStruct((blocks * inner, STATE), F32),
            jax.ShapeDtypeStruct((count, 2 * HEAD_DIM), BF16),
            jax.ShapeDtypeStruct((count, 768), BF16),
            jax.ShapeDtypeStruct(normed_t.shape, BF16),
            jax.ShapeDtypeStruct((2 * HEAD_DIM, count), BF16),
        ),
        grid_spec=pltpu.PrefetchScalarGridSpec(
            num_scalar_prefetch=1,
            grid=(blocks,),
            in_specs=[
                pl.BlockSpec((HALF, u.shape[1]), at_slot),
                pl.BlockSpec((normed_t.shape[0], HALF), lambda i, order: at_slot(i, order)[::-1]),
                pl.BlockSpec((HALF, table.shape[1]), in_order),
                pl.BlockSpec(head_rows.shape, whole),
                pl.BlockSpec(taps.shape, whole),
            ],
            out_specs=(
                pl.BlockSpec((HALF, inner + HEAD_DIM), at_slot),
                pl.BlockSpec((HALF, 512), in_order),
                pl.BlockSpec((HALF, width), in_order),
                pl.BlockSpec((inner, STATE), in_order),
                pl.BlockSpec((HALF, 2 * HEAD_DIM), in_order),
                pl.BlockSpec((HALF, 768), in_order),
                pl.BlockSpec((normed_t.shape[0], HALF), lambda i, order: (0, i)),
                pl.BlockSpec((2 * HEAD_DIM, HALF), lambda i, order: (0, i)),
            ),
            scratch_shapes=[
                pltpu.VMEM((8 + HALF, width), F32),
                pltpu.VMEM((inner, STATE), F32),
                pltpu.VMEM((HEAD_DIM, count), BF16),
                pltpu.VMEM((count, HEAD_DIM), BF16),
                pltpu.VMEM((HALF, 2 * HEAD_DIM), F32),
            ],
        ),
        compiler_params=pltpu.CompilerParams(vmem_limit_bytes=60 << 20),
    )(slot_of, u, normed_t, table, head_rows, taps)


MESH = pl.DeviceIdType.MESH


class Place:
    def __init__(self):
        self.c = lax.axis_index("context")
        self.t = lax.axis_index("tensor")
        count = lax.axis_size("context")
        self.chips = [
            self.c,
            self.c + 1 - 2 * (self.c % 2),
            (self.c + count // 2) % count,
            count - 1 - self.c,
        ]

    def slot(self, mask, sibling=False):
        core = 1 - self.t if sibling else self.t
        return self.chips[mask] * 2 + core

    def target(self, mask):
        if mask == 4:
            return {"tensor": 1 - self.t}
        return {"context": self.chips[mask]}

    def hello(self, line=None):
        barrier = pltpu.get_barrier_semaphore()
        targets = [self.target(mask) for mask in (1, 2, 4)]
        if line is not None:
            targets += [line.target(step) for step in range(1, line.count)]
        for target in targets:
            pl.semaphore_signal(barrier, inc=1, device_id=target, device_id_type=MESH)
        return len(targets)

    def greet(self, line=None):
        pl.semaphore_wait(pltpu.get_barrier_semaphore(), self.hello(line))


class Wire:
    def __init__(self, place, sems):
        self.place = place
        self.sems = sems
        self.sent = []

    def copy(self, source, target, index, mask):
        return pltpu.make_async_remote_copy(
            src_ref=source,
            dst_ref=target,
            send_sem=self.sems.at[0, index],
            recv_sem=self.sems.at[1, index],
            device_id=self.place.target(mask),
            device_id_type=MESH,
        )

    def send(self, source, target, index, mask):
        def made():
            here = source() if callable(source) else source
            there = target() if callable(target) else target
            return self.copy(here, there, index, mask)

        made().start()
        self.sent.append(made)

    def arrive(self, target, index, mask):
        self.copy(target, target, index, mask).wait_recv()

    def finish(self):
        for made in self.sent:
            made().wait_send()
        self.sent = []


ROWS = HALF
PART = HALF // 2
TOP, END = pl.ds(0, PART), pl.ds(PART, PART)
SCATTER_SEMS = 10
GATHER_SEMS = 14


def scatter_scratch(columns):
    return [
        pltpu.VMEM((4, ROWS, columns), BF16),
        pltpu.VMEM((4, ROWS, columns), BF16),
        pltpu.VMEM((6, PART, columns), BF16),
        pltpu.VMEM((ROWS, columns), BF16),
        pltpu.SemaphoreType.DMA((2, SCATTER_SEMS)),
    ]


SCATTER_ORDER = (3, 1, 2, 0)


class Scatter:
    def __init__(self, place, scratch):
        self.place = place
        self.core_in, self.out, self.chip_in, self.kept, sems = scratch
        self.wire = Wire(place, sems)

    def to_core(self, mask, source):
        index = SCATTER_ORDER.index(mask)
        self.wire.send(source, self.core_in.at[index], index, 4)

    def from_core(self, mask):
        index = SCATTER_ORDER.index(mask)
        self.wire.arrive(self.core_in.at[index], index, 4)
        return self.core_in[index].astype(F32)

    def first(self, mine, total, between=None):
        wire, out, kept = self.wire, self.out, self.kept
        both = mine(3) + self.from_core(3)
        out[0] = both.astype(BF16)
        wire.send(lambda: out.at[0, TOP], lambda: self.chip_in.at[0], 4, 1)
        wire.send(lambda: out.at[0, END], lambda: self.chip_in.at[1], 5, 2)
        both = mine(1) + self.from_core(1)
        out[1] = both.astype(BF16)
        wire.send(lambda: out.at[1, TOP], lambda: self.chip_in.at[2], 6, 1)
        kept[END] = out[1, END]
        both = mine(2) + self.from_core(2)
        out[2] = both.astype(BF16)
        wire.send(lambda: out.at[2, END], lambda: self.chip_in.at[3], 7, 2)
        kept[TOP] = out[2, TOP]
        total[...] = mine(0) + self.from_core(0)

    def second(self):
        wire, out, kept, came = self.wire, self.out, self.kept, self.chip_in
        wire.arrive(came.at[0], 4, 1)
        out[3, TOP] = (kept[TOP].astype(F32) + came[0].astype(F32)).astype(BF16)
        wire.send(lambda: out.at[3, TOP], lambda: came.at[4], 8, 2)
        wire.arrive(came.at[1], 5, 2)
        out[3, END] = (kept[END].astype(F32) + came[1].astype(F32)).astype(BF16)
        wire.send(lambda: out.at[3, END], lambda: came.at[5], 9, 1)

    def last(self, total):
        wire, came = self.wire, self.chip_in
        wire.arrive(came.at[2], 6, 1)
        wire.arrive(came.at[4], 8, 2)
        total[TOP] += came[2].astype(F32) + came[4].astype(F32)
        wire.arrive(came.at[3], 7, 2)
        wire.arrive(came.at[5], 9, 1)
        total[END] += came[3].astype(F32) + came[5].astype(F32)
        wire.finish()


class Gather:
    def __init__(self, place, whole, sems, rows=ROWS, cores=True):
        self.place = place
        self.whole = whole
        self.size = rows
        self.cores = cores
        self.wire = Wire(place, sems)

    def rows(self, mask, sibling=False, half=None):
        place, size = self.place, self.size
        block = place.slot(mask, sibling) if self.cores else place.chips[mask]
        begin = block * size
        if half is None:
            return self.whole.at[pl.ds(pl.multiple_of(begin, size), size)]
        return self.whole.at[pl.ds(pl.multiple_of(begin + half * (size // 2), size // 2), size // 2)]

    def both(self, mask, sibling=False, half=None):
        block = functools.partial(self.rows, mask, sibling, half)
        return block, block

    def start(self, core=True):
        wire = self.wire
        for half, mask, index in ((0, 1, 0), (1, 2, 1), (1, 1, 2), (0, 2, 3)):
            wire.send(*self.both(0, half=half), index, mask)
        if self.cores and core:
            wire.send(*self.both(0), 6, 4)

    def relay(self):
        wire = self.wire
        wire.arrive(self.rows(1, half=0), 0, 1)
        wire.send(*self.both(1, half=0), 4, 2)
        wire.arrive(self.rows(2, half=1), 1, 2)
        wire.send(*self.both(2, half=1), 5, 1)

    def near(self):
        wire = self.wire
        wire.arrive(self.rows(1, half=1), 2, 1)
        if self.cores:
            wire.send(*self.both(1), 7, 4)
        wire.arrive(self.rows(2, half=0), 3, 2)
        if self.cores:
            wire.send(*self.both(2), 8, 4)

    def far(self):
        wire = self.wire
        wire.arrive(self.rows(3, half=0), 4, 2)
        wire.arrive(self.rows(3, half=1), 5, 1)
        if self.cores:
            wire.send(*self.both(3), 9, 4)

    def core(self, mask):
        index = (6, 7, 8, 9)[mask]
        self.wire.arrive(self.rows(mask, sibling=True), index, 4)

    def finish(self):
        self.wire.finish()


class Line:
    def __init__(self):
        self.f = lax.axis_index("fsdp")
        self.count = lax.axis_size("fsdp")

    def target(self, step):
        return {"fsdp": (self.f + step) % self.count}

    def copy(self, source, target, sems, step):
        return pltpu.make_async_remote_copy(
            src_ref=source,
            dst_ref=target,
            send_sem=sems.at[0, step],
            recv_sem=sems.at[1, step],
            device_id=self.target(step),
            device_id_type=MESH,
        )


class LineGather:
    def __init__(self, line, whole, sems):
        self.line = line
        self.whole = whole
        self.sems = sems
        self.size = whole.shape[0] // line.count

    def rows(self, block):
        return self.whole.at[pl.ds(pl.multiple_of(block * self.size, self.size), self.size)]

    def copy(self, block, way, step):
        toward = self.line.f + 1 if way == 0 else self.line.f - 1
        return pltpu.make_async_remote_copy(
            src_ref=self.rows(block),
            dst_ref=self.rows(block),
            send_sem=self.sems.at[way, 0, step],
            recv_sem=self.sems.at[way, 1, step],
            device_id={"fsdp": toward},
            device_id_type=MESH,
        )

    def step(self, number, arrive=True):
        f, last = self.line.f, self.line.count - 1
        for way in (0, 1):
            block = f - number if way == 0 else f + number
            there = block >= 0 if way == 0 else block <= last
            goes_on = f < last if way == 0 else f > 0

            @pl.when(there)
            def _():
                if number > 0:
                    self.copy(block, way, number).wait_recv()

                @pl.when(goes_on)
                def _():
                    self.copy(block, way, number + 1).start()

    def finish(self):
        f, last = self.line.f, self.line.count - 1
        for number in range(self.line.count - 1):
            for way in (0, 1):
                block = f - number if way == 0 else f + number
                there = block >= 0 if way == 0 else block <= last
                goes_on = f < last if way == 0 else f > 0

                @pl.when(there & goes_on)
                def _():
                    self.copy(block, way, number + 1).wait_send()


def line_sems(count):
    return pltpu.SemaphoreType.DMA((2, 2, count + 1))


def opening_kernel(
    tokens_ref, cot_ref, in_x_ref, query_ref, bc_ref, gate_ref, keyval_ref, step_ref, ssm_ref, attn_ref,
    gain_ref, segments_ref, conv_x_ref, conv_bc_ref, bias_ref, decay_ref, skip_ref,
    normed_t_out, u_out, w_out, wout_out, cot_out, table_out, heads_ref, taps_ref,
    x_all, cot_all, normed, normed_t, u, weights_all, wout_all, table, wide,
    x_sems, cot_sems, w_sems, out_sems, local_sems, block_sems,
):
    place = Place()
    line = Line()
    rows_x = Gather(place, x_all, x_sems)
    rows_cot = Gather(place, cot_all, cot_sems)
    weights = LineGather(line, weights_all, w_sems)
    weights_out = LineGather(line, wout_all, out_sems)
    chips = lax.axis_size("context")
    share = in_x_ref.shape[0]
    heads = step_ref.shape[0] // chips
    inner = heads * SSM_DIM
    chip_rows = pl.ds(pl.multiple_of(place.c * 2 * ROWS, 2 * ROWS), 2 * ROWS)
    waiting = []

    def local(source, target, sem):
        made = pltpu.make_async_copy(source, target, sem)
        made.start()
        waiting.append(made)
        return made

    greetings = place.hello(line)
    own_x = pltpu.make_async_copy(tokens_ref, x_all.at[chip_rows], local_sems.at[0])
    own_x.start()
    own_cot = pltpu.make_async_copy(cot_ref, cot_all.at[chip_rows], local_sems.at[1])
    own_cot.start()
    mine = pl.ds(pl.multiple_of(line.f * share, share), share)
    heads_ref[...] = jnp.zeros(heads_ref.shape, F32)
    taps_ref[...] = jnp.zeros(taps_ref.shape, F32)
    for k in range(chips):

        @pl.when(place.c == k)
        def _():
            inner_part = slice(k * inner, (k + 1) * inner)
            head_part = slice(k * HEAD_DIM, (k + 1) * HEAD_DIM)
            weights_all[mine, 0:256] = jnp.concatenate(
                [gate_ref[:, inner_part], query_ref[:, head_part]], axis=1
            )
            weights_all[mine, 384 : 384 + inner] = in_x_ref[:, inner_part]
            wout_all[mine, :] = jnp.concatenate(
                [ssm_ref[:, inner_part], attn_ref[:, head_part]], axis=1
            )
            taps_ref[0:CONV, :inner] = conv_x_ref[:, inner_part]
            for h in range(heads):
                lane = slice(k * heads + h, k * heads + h + 1)
                for row, source in enumerate((bias_ref, decay_ref, skip_ref)):
                    heads_ref[row : row + 1, h * SSM_DIM : (h + 1) * SSM_DIM] = jnp.broadcast_to(
                        source[:, lane], (1, SSM_DIM)
                    )

    taps_ref[0:CONV, 256:512] = conv_bc_ref[...]
    head, column = iotas(step_ref.shape[0], HEAD_DIM)
    chosen = (head == column + place.c * heads) & (column < heads)
    steps = dot(step_ref[...], jnp.where(chosen, 1.0, 0.0).astype(BF16), 0, 0)
    weights_all[mine, 384 + inner : 640] = steps.astype(BF16)
    weights_all[mine, 256:384] = keyval_ref[...]
    weights_all[mine, 640:896] = bc_ref[...]
    own_x.wait()
    own_cot.wait()
    pl.semaphore_wait(pltpu.get_barrier_semaphore(), greetings)
    weights.step(0)
    rows_x.start(core=False)

    def norm(slot):
        rows = slot_rows(slot)
        x = x_all[rows, :].astype(F32)
        normed[rows, :] = (x * norm_scale(x) * gain_ref[...]).astype(BF16)
        columns = pl.ds(pl.multiple_of(slot * ROWS, ROWS), ROWS)
        normed_t[:, columns] = normed[rows, :].T

    norm(place.slot(0))
    norm(place.slot(0, True))

    numbers = segments_ref[...]
    bounds = [
        jnp.sum(jnp.where(numbers < k, 1.0, 0.0), axis=1, keepdims=True) for k in (1, 2)
    ]
    count = table.shape[0]
    lane = lax.broadcasted_iota(jnp.int32, (8, 128), 1)[0:1]
    power = -(lane % (HEAD_DIM // 2)).astype(F32) / (HEAD_DIM // 2)
    freqs = jnp.exp(power * math.log(10000.0))
    phase = jnp.where(lane < HEAD_DIM, math.pi / 2, 0.0)
    sign = jnp.where((lane >= HEAD_DIM) & (lane < HEAD_DIM + HEAD_DIM // 2), -1.0, 1.0)

    def angles(block, carry):
        row = lax.broadcasted_iota(jnp.int32, (ROWS, 128), 0) + block * ROWS
        row = row.astype(F32)
        start = jnp.where(row >= bounds[0], bounds[0], 0.0)
        start = jnp.where(row >= bounds[1], bounds[1], start)
        pos = row - start
        here = slot_rows(block)
        table[here, 0:128] = jnp.sin(pos * freqs + phase) * sign
        table[here, 128:256] = pos
        return carry

    blocks = count // ROWS
    rows_x.relay()
    rows_cot.start(core=False)
    lax.fori_loop(0, blocks // 2, angles, 0)
    weights.step(1)
    lax.fori_loop(blocks // 2, blocks, angles, 0)
    local(table, table_out, local_sems.at[2])
    rows_x.near()
    norm(place.slot(1))
    norm(place.slot(2))
    rows_cot.relay()
    for number in range(2, line.count - 1):
        weights.step(number)
    rows_x.far()
    norm(place.slot(3))
    for mask in (1, 2, 3):
        rows_x.core(mask)
        norm(place.slot(mask, True))
    weights_out.step(0)
    rows_cot.near()
    weights.step(line.count - 1)
    local(weights_all, w_out, local_sems.at[3])
    local(normed_t, normed_t_out, local_sems.at[6])
    row, column = iotas(HEAD_DIM, inner)
    copies = jnp.where(column // SSM_DIM == row, 1.0, 0.0).astype(BF16)
    wide[:, 0:256] = jnp.concatenate(
        [weights_all[:, 384 : 384 + inner], weights_all[:, inner:256]], axis=1
    )
    wide[:, 256:512] = weights_all[:, 640:896]
    wide[:, 512:768] = jnp.concatenate([weights_all[:, :inner], weights_all[:, 256:320]], axis=1)
    wide[:, 768:1024] = jnp.concatenate(
        [
            dot(weights_all[:, 384 + inner : 640], copies),
            weights_all[:, 320:384].astype(F32),
        ],
        axis=1,
    ).astype(BF16)

    def project(slot):
        rows = pl.ds(slot * ROWS, ROWS)
        u[rows, :] = dot(normed[rows, :], wide[...])
        local(u.at[rows], u_out.at[rows], block_sems.at[0, slot])

    for slot in range(blocks // 2):
        project(slot)
    weights_out.step(1)
    rows_cot.far()
    for slot in range(blocks // 2, blocks):
        project(slot)
    for number in range(2, line.count):
        weights_out.step(number)
    local(wout_all, wout_out, local_sems.at[4])
    for mask in (1, 2, 3):
        rows_cot.core(mask)
    local(cot_all, cot_out, local_sems.at[5])
    for made in waiting:
        made.wait()
    rows_x.finish()
    rows_cot.finish()
    weights.finish()
    weights_out.finish()


def opening(tokens, cotangent, weights, gain, segments, taps, by_head):
    fsdp = lax.axis_size("fsdp")
    model = tokens.shape[1]
    count = segments.shape[1]
    blocks = count // ROWS
    vmem = pl.BlockSpec(memory_space=pltpu.VMEM)
    hbm = pl.BlockSpec(memory_space=pl.ANY)
    shape = jax.ShapeDtypeStruct
    dma = pltpu.SemaphoreType.DMA
    buffers = [
        ((model, count), BF16),
        ((count, 1024), F32),
        ((model, 896), BF16),
        ((model, 256), BF16),
        ((count, model), BF16),
        ((count, 256), F32),
    ]
    kept = [buffers[k] for k in (0, 1, 2, 3, 5)]
    return pl.pallas_call(
        opening_kernel,
        out_shape=tuple(shape(*one) for one in buffers) + (shape((8, 256), F32), shape((8, 512), F32)),
        in_specs=[hbm] * 2 + [vmem] * 15,
        out_specs=(hbm,) * 6 + (vmem,) * 2,
        scratch_shapes=[pltpu.VMEM((count, model), BF16)] * 3
        + [pltpu.VMEM(*one) for one in kept]
        + [
            pltpu.VMEM((model, 1024), BF16),
            dma((2, GATHER_SEMS)),
            dma((2, GATHER_SEMS)),
            line_sems(fsdp),
            line_sems(fsdp),
            dma((7,)),
            dma((1, blocks)),
        ],
        compiler_params=pltpu.CompilerParams(
            collective_id=3, has_side_effects=True, vmem_limit_bytes=60 << 20
        ),
        cost_estimate=pl.CostEstimate(
            flops=2 * count * model * 1024, bytes_accessed=30 << 20, transcendentals=count * 128
        ),
    )(
        tokens, cotangent, *weights, gain.reshape(1, -1), segments, *taps,
        *[one.reshape(1, -1) for one in by_head],
    )


def slot_rows(slot):
    return pl.ds(pl.multiple_of(slot * ROWS, ROWS), ROWS)


def norm_scale(values):
    return lax.rsqrt(jnp.mean(values * values, axis=1, keepdims=True) + epsilon)


def middle_kernel(
    ag_ref, wout_ref, gate_ref, up_ref, down_ref, gain_ref, x_hbm, cot_hbm, cot_all_hbm,
    hidden_ref, dag_ref, mixed_ref, dmixed_ref, dgain_ref, down_all_ref, ffn_ref, dout_ref,
    x_ref, cot_ref, cot_all_ref, nffn_ref, dgu_ref, dm_ref, dw_ref, arrived, part, wffn_ref, *scratch,
):
    place = Place()
    first = Scatter(place, scratch[0:5])
    back = Scatter(place, scratch[5:10])
    forth = Gather(place, nffn_ref, scratch[10])
    home = Gather(place, dm_ref, scratch[11])
    hid = hidden_ref.shape[1]
    line = Line()
    weights = LineGather(line, wffn_ref, scratch[12])
    share = gate_ref.shape[0]
    greetings = place.hello(line)
    half = pl.ds(pl.multiple_of(place.t * ROWS, ROWS), ROWS)
    loads = [
        pltpu.make_async_copy(source, target, scratch[14].at[k])
        for k, (source, target) in enumerate(
            ((x_hbm.at[half], x_ref), (cot_hbm.at[half], cot_ref), (cot_all_hbm, cot_all_ref))
        )
    ]
    for made in loads:
        made.start()
    mine = pl.ds(pl.multiple_of(line.f * share, share), share)
    lanes = pl.ds(pl.multiple_of(place.c * hid, hid), hid)
    for k, source in enumerate((gate_ref, up_ref, down_ref)):
        wffn_ref[mine, k * hid : (k + 1) * hid] = source[:, lanes]

    def block(mask, sibling=False):
        return dot(ag_ref[slot_rows(place.slot(mask, sibling)), :], wout_ref[...], 1, 1)

    for mask in SCATTER_ORDER:
        part[slot_rows(place.slot(mask, True)), :] = block(mask, True).astype(BF16)
    pl.semaphore_wait(pltpu.get_barrier_semaphore(), greetings)
    for mask in SCATTER_ORDER:
        first.to_core(mask, part.at[slot_rows(place.slot(mask, True))])
    weights.step(0)
    first.first(block, mixed_ref)
    weights.step(1)
    first.second()
    for made in loads:
        made.wait()
    mixed_ref[...] += x_ref[...].astype(F32)
    first.last(mixed_ref)
    mixed = mixed_ref[...]
    gain = gain_ref[...]
    scale = norm_scale(mixed)
    own = slot_rows(place.slot(0))
    nffn_ref[own, :] = (mixed * scale * gain).astype(BF16)
    forth.start()
    for number in range(2, line.count):
        weights.step(number)

    def work(slot):
        rows = slot_rows(slot)
        normed = nffn_ref[rows, :]
        gate_up = dot(normed, wffn_ref[:, : 2 * hid])
        dhidden = dot(cot_all_ref[rows, :], wffn_ref[:, 2 * hid :]).astype(BF16).astype(F32)
        gate, up = gate_up[:, :hid], gate_up[:, hid:]
        sig = sigmoid(gate)
        silu = gate * sig
        dgate = dhidden * up * (sig * (1.0 + gate * (1.0 - sig)))
        hidden_ref[rows, :] = (silu * up).astype(BF16)
        dgu_ref[rows, :hid] = dgate.astype(BF16)
        dgu_ref[rows, hid:] = (dhidden * silu).astype(BF16)
        part[rows, :] = dot(dgu_ref[rows, :], wffn_ref[:, : 2 * hid], 1, 1).astype(BF16)

    def hand_over(mask):
        slot = place.slot(mask, True)
        work(slot)
        back.to_core(mask, part.at[slot_rows(slot)])

    work(place.slot(0))
    forth.relay()
    forth.core(0)
    hand_over(0)
    forth.near()
    forth.core(1)
    hand_over(1)
    forth.core(2)
    hand_over(2)
    work(place.slot(1))
    forth.far()
    work(place.slot(2))
    forth.core(3)
    hand_over(3)
    work(place.slot(3))
    forth.finish()

    def ready(mask):
        return part[slot_rows(place.slot(mask)), :].astype(F32)

    back.first(ready, dmixed_ref)

    columns = (pl.ds(0, 2 * hid), pl.ds(2 * hid, hid))
    line_sent = []

    def line_copy(piece, step):
        rows = pl.ds(pl.multiple_of((line.f + step) % line.count * share, share), share)
        return line.copy(
            dw_ref.at[rows, columns[piece]],
            arrived.at[step, :, columns[piece]],
            scratch[13].at[piece],
            step,
        )

    def send_piece(piece, left, right):
        quarter = dw_ref.shape[0] // 4
        for k in range(4):
            rows = slice(k * quarter, (k + 1) * quarter)
            dw_ref[rows, columns[piece]] = dot(left[:, rows], right[...], 0, 0).astype(BF16)
        for step in range(1, line.count):
            made = line_copy(piece, step)
            made.start()
            line_sent.append(made)

    send_piece(1, cot_all_ref, hidden_ref)
    back.second()
    send_piece(0, nffn_ref, dgu_ref)
    back.last(dmixed_ref)
    dnffn = dmixed_ref[...]
    mixed = mixed_ref[...]
    scale = norm_scale(mixed)
    spread = dnffn * gain
    pull = jnp.mean(spread * mixed, axis=1, keepdims=True)
    dgain_ref[...] = jnp.broadcast_to(
        jnp.sum(dnffn * mixed * scale, axis=0, keepdims=True), dgain_ref.shape
    )
    dmixed = cot_ref[...].astype(F32) + scale * (spread - mixed * (scale * scale * pull))
    dmixed_ref[...] = dmixed
    dm_ref[own, :] = dmixed.astype(BF16)
    home.start()

    def pull_back(slot):
        rows = slot_rows(slot)
        dag_ref[rows, :] = dot(dm_ref[rows, :], wout_ref[...]).astype(BF16)

    pull_back(place.slot(0))
    home.relay()
    home.core(0)
    pull_back(place.slot(0, True))
    home.near()
    pull_back(place.slot(1))
    pull_back(place.slot(2))
    home.far()
    pull_back(place.slot(3))
    for mask in (1, 2, 3):
        home.core(mask)
        pull_back(place.slot(mask, True))
    dout_ref[...] = dot(dm_ref[...], ag_ref[...], 0, 0).astype(BF16)
    down_all_ref[...] = wffn_ref[:, 2 * hid :]
    for piece in (1, 0):
        sums = dw_ref[mine, columns[piece]].astype(F32)
        for step in range(1, line.count):
            line_copy(piece, step).wait_recv()
            sums = sums + arrived[step, :, columns[piece]].astype(F32)
        ffn_ref[:, columns[piece]] = sums.astype(BF16)
    for made in line_sent:
        made.wait_send()
    home.finish()
    weights.finish()


def middle(ag, wout, weights, x_own, cot_own, cot_all, gain):
    count, model = cot_all.shape
    hid = weights[0].shape[1] // lax.axis_size("context")
    columns = ag.shape[1]
    vmem = pl.BlockSpec(memory_space=pltpu.VMEM)
    hbm = pl.BlockSpec(memory_space=pl.ANY)
    shape = jax.ShapeDtypeStruct
    return pl.pallas_call(
        middle_kernel,
        out_shape=(
            shape((count, hid), BF16),
            shape((count, columns), BF16),
            shape((ROWS, model), F32),
            shape((ROWS, model), F32),
            shape((8, model), F32),
            shape((model, hid), BF16),
            shape((weights[0].shape[0], 3 * hid), BF16),
            shape((model, columns), BF16),
        ),
        in_specs=[vmem] * 6 + [hbm] * 3,
        out_specs=(vmem,) * 8,
        scratch_shapes=[
            pltpu.VMEM((ROWS, model), BF16),
            pltpu.VMEM((ROWS, model), BF16),
            pltpu.VMEM((count, model), BF16),
            pltpu.VMEM((count, model), BF16),
            pltpu.VMEM((count, 2 * hid), BF16),
            pltpu.VMEM((count, model), BF16),
            pltpu.VMEM((model, 3 * hid), BF16),
            pltpu.VMEM((lax.axis_size("fsdp"), weights[0].shape[0], 3 * hid), BF16),
            pltpu.VMEM((count, model), BF16),
            pltpu.VMEM((model, 3 * hid), BF16),
        ]
        + scatter_scratch(model)
        + scatter_scratch(model)
        + [pltpu.SemaphoreType.DMA((2, GATHER_SEMS))] * 2
        + [line_sems(lax.axis_size("fsdp")), pltpu.SemaphoreType.DMA((2, 2, lax.axis_size("fsdp"))), pltpu.SemaphoreType.DMA((3,))],
        compiler_params=pltpu.CompilerParams(
            collective_id=1, has_side_effects=True, vmem_limit_bytes=60 << 20
        ),
        cost_estimate=pl.CostEstimate(
            flops=20 * count * model * hid, bytes_accessed=40 << 20, transcendentals=count * hid
        ),
    )(ag, wout, *weights, gain.reshape(1, -1), x_own, cot_own, cot_all)


BACK_INPUTS = 5
EARLY = 384


def closing_kernel(
    order_ref, dag_ref, kv_ref, kv_t_ref, heads_ref, taps_ref, dmixed_ref, gain_ref, ffn_ref,
    dgain_ref, dout_ref, table_hbm, y_hbm, conv_hbm, kept_hbm, states_hbm, normed_t_hbm, w_hbm,
    hidden_hbm, down_hbm, mixed_hbm, tokens_hbm,
    grad_ref, out_ref, early_ref, bc_ref, last_ref, mids_ref, outs_ref, small_ref,
    table, y, conv, kept, states, normed_t, w, hidden, down, x_ref,
    dnorm, early_du, dw_sum, dw, arrived, arrived_out, total, out_total, part, out_part, bc_out, bc_in, small_in,
    stats, dext, dpos, dstate, state_out, dkey_t, dvalue_t, *scratch,
):
    place = Place()
    line = Line()
    back = Scatter(place, scratch[0:5])
    final = Scatter(place, scratch[5:10])
    share = ffn_ref.shape[0]
    last_all = Gather(place, last_ref, scratch[10], share, False)
    early_all = Gather(place, early_ref, scratch[20], share, False)
    bc_all = Gather(place, bc_ref, scratch[21], share, False)
    mid_all = Gather(place, mids_ref, scratch[11], share, False)
    out_all = Gather(place, outs_ref, scratch[12], share, False)
    small_rows = small_in.shape[1]
    small_all = Gather(place, small_ref, scratch[13], small_rows)
    line_sems_, small_sems, out_sems, pair_sems, load_sems, block_sems = scratch[14:20]
    pair = Wire(place, pair_sems)
    greetings = place.hello(line)
    sent = []
    loads = [
        pltpu.make_async_copy(source, target, load_sems.at[k])
        for k, (source, target) in enumerate(
            (
                (hidden_hbm, hidden), (down_hbm, down), (normed_t_hbm, normed_t), (w_hbm, w),
                (mixed_hbm, out_total),
                (tokens_hbm.at[pl.ds(pl.multiple_of(place.t * ROWS, ROWS), ROWS)], x_ref),
            )
        )
    ]
    blocks = dnorm.shape[0] // ROWS
    streams = ((table_hbm, table), (y_hbm, y), (conv_hbm, conv), (kept_hbm, kept), (states_hbm, states))

    early_lanes = (pl.ds(0, 256), pl.ds(0, 512), pl.ds(0, 256), pl.ds(512, 256), None)
    late_lanes = (pl.ds(128, 128), pl.ds(0, 512), pl.ds(0, 512), pl.ds(0, 768), pl.ds(0, STATE))

    def fetch(block, buffer, late):
        copies = []
        for k, (source, target) in enumerate(streams):
            lanes = late_lanes[k] if late else early_lanes[k]
            if lanes is None:
                continue
            size = target.shape[1]
            begin = pl.multiple_of(block * size, size)
            copies.append(
                pltpu.make_async_copy(
                    source.at[pl.ds(begin, size), lanes],
                    target.at[buffer, :, lanes],
                    block_sems.at[buffer, k],
                )
            )
        return copies

    for made in fetch(blocks - 1, 0, False) + loads:
        made.start()
    mids_ref[pl.ds(pl.multiple_of(place.c * share, share), share), :] = ffn_ref[...]
    width = dext.shape[1]
    dext[ROWS : ROWS + 8, :] = jnp.zeros((8, width), F32)
    dpos[ROWS : ROWS + 8, :] = jnp.full((8, dpos.shape[1]), -1.0, F32)
    for ref in (dstate, state_out, dkey_t, dvalue_t, stats, dw_sum):
        ref[...] = jnp.zeros(ref.shape, F32)
    def out_block(mask, sibling=False):
        return dot(hidden[slot_rows(place.slot(mask, sibling)), :], down[...], 1, 1)

    def out_rows(mask):
        return out_block(mask) + out_total[...] if mask == 0 else out_block(mask)

    here = pl.ds(pl.multiple_of(place.c * share, share), share)
    own = pl.ds(pl.multiple_of(line.f * share, share), share)
    half = pl.ds(pl.multiple_of(place.t * ROWS, ROWS), ROWS)

    def my_half(ref):
        return lambda: ref.at[pl.ds(pl.multiple_of(place.t * ROWS, ROWS), ROWS)]

    def collect_out():
        sums = dout_ref[own, :].astype(F32)
        for step in range(1, line.count):
            line.copy(arrived_out.at[step - 1], arrived_out.at[step - 1], out_sems, step).wait_recv()
            sums = sums + arrived_out[step - 1].astype(F32)
        outs_ref[here, :] = sums.astype(BF16)
        out_all.start()

    def finish_out():
        final.last(out_total)
        out_ref[half, :] = out_total[...].astype(BF16)
        pair.send(my_half(out_ref), my_half(out_ref), 1, 4)

    lane = lax.broadcasted_iota(jnp.int32, (8, blocks), 1)[0:1]
    order = order_ref[...]

    def blend(source, marks):
        marks = [jnp.where(one, 1.0, 0.0).astype(BF16) for one in marks]
        found = source[0:ROWS, :] * marks[0]
        for k in range(1, blocks):
            found = found + source[k * ROWS : (k + 1) * ROWS, :] * marks[k]
        return found

    def from_slots(source, block):
        return blend(source, [order[:, k : k + 1] == block for k in range(blocks)])

    def from_stream(source, slot):
        dealt = jnp.sum(jnp.where(lane == slot, order, 0), axis=1, keepdims=True)
        return blend(source, [dealt == k for k in range(blocks)])

    def prefetch(block, buffer, late):
        for made in fetch(block, buffer, late):
            made.start()

    def await_block(block, buffer, late):
        for made in fetch(block, buffer, late):
            made.wait()

    def happen(number, events):
        for when, actions in events.items():

            @pl.when(number == when)
            def _():
                for action in actions:
                    action()

    def early_turn(number, carry):
        block = blocks - 1 - number
        buffer = number % 2
        await_block(block, buffer, False)

        @pl.when(number < blocks - 1)
        def _():
            prefetch(block - 1, 1 - buffer, False)

        @pl.when(number == blocks - 1)
        def _():
            prefetch(blocks - 1, 1 - buffer, True)

        grads = attention_backward(
            block, from_slots(dag_ref, block), table.at[buffer], heads_ref, y.at[buffer], conv.at[buffer],
            kept.at[buffer], kv_ref, kv_t_ref, dkey_t, dvalue_t,
        )
        early_du[slot_rows(block), :] = grads
        dw_sum[:, :EARLY] += dot(normed_t[:, slot_rows(block)], grads)
        happen(number, {3: (lambda: final.first(out_rows, out_total),), 6: (mid_all.relay,)})
        return carry

    def late_turn(number, carry):
        block = blocks - 1 - number
        buffer = number % 2
        await_block(block, buffer, True)

        @pl.when(number < blocks - 1)
        def _():
            prefetch(block - 1, 1 - buffer, True)

        grads = recurrence_backward(
            from_slots(dag_ref, block), table.at[buffer], heads_ref, taps_ref, y.at[buffer],
            conv.at[buffer], kept.at[buffer], states.at[buffer], state_out, stats, dext, dpos, dstate,
        )
        whole = jnp.concatenate([early_du[slot_rows(block), :], grads], axis=1)
        dnorm[slot_rows(block), :] = dot(whole, w[...], 1, 1).astype(BF16)
        dw_sum[:, EARLY:] += dot(normed_t[:, slot_rows(block)], grads)
        happen(
            number,
            {
                1: (mid_all.near,),
                3: (collect_out, mid_all.far),
                5: (final.second,),
                6: (out_all.relay,),
            },
        )
        return carry

    columns = (pl.ds(0, EARLY), pl.ds(EARLY + 256, 256), pl.ds(EARLY, 256))

    def line_copy(piece, step):
        rows = pl.ds(pl.multiple_of((line.f + step) % line.count * share, share), share)
        return line.copy(
            dw.at[rows, columns[piece]], arrived.at[step - 1, :, columns[piece]], line_sems_.at[piece], step
        )

    def send_piece(piece):
        dw[:, columns[piece]] = dw_sum[:, columns[piece]].astype(BF16)
        for step in range(1, line.count):
            made = line_copy(piece, step)
            made.start()
            sent.append(made)

    def collected(piece):
        sums = dw[own, columns[piece]].astype(F32)
        for step in range(1, line.count):
            line_copy(piece, step).wait_recv()
            sums = sums + arrived[step - 1, :, columns[piece]].astype(F32)
        return sums.astype(BF16)

    for made in loads:
        made.wait()
    early_turn(0, 0)
    pl.semaphore_wait(pltpu.get_barrier_semaphore(), greetings)
    for step in range(1, line.count):
        rows = pl.ds(pl.multiple_of((line.f + step) % line.count * share, share), share)
        made = line.copy(dout_ref.at[rows], arrived_out.at[step - 1], out_sems, step)
        made.start()
        sent.append(made)
    for k, mask in enumerate(SCATTER_ORDER):
        out_part[k] = out_block(mask, True).astype(BF16)
        final.to_core(mask, out_part.at[k])
    mid_all.start()
    lax.fori_loop(1, blocks, early_turn, 0)
    send_piece(0)
    lax.fori_loop(0, blocks, late_turn, 0)
    send_piece(1)
    send_piece(2)

    def block_of(mask, sibling=False):
        return from_stream(dnorm, place.slot(mask, sibling))

    for k, mask in enumerate(SCATTER_ORDER):
        part[k] = block_of(mask, True)
        back.to_core(mask, part.at[k])
    back.first(lambda mask: block_of(mask).astype(F32), total)
    out_all.near()
    finish_out()
    out_all.far()
    early_ref[here, :] = collected(0)
    back.second()
    early_all.start()
    bc_out[...] = collected(1)
    pair.send(bc_out, bc_in, 2, 4)
    back.last(total)
    early_all.relay()
    dnormed = total[...]
    x = x_ref[...].astype(F32)
    gain = gain_ref[...]
    scale = norm_scale(x)
    spread = dnormed * gain
    pull = jnp.mean(spread * x, axis=1, keepdims=True)
    grad = dmixed_ref[...] + scale * (spread - x * (scale * scale * pull))
    grad_ref[half, :] = grad.astype(BF16)
    pair.send(grad_ref.at[half], grad_ref.at[half], 0, 4)
    small_in[0] = jnp.zeros(small_in.shape[1:], F32)
    small_in[0, 0:1, :] = jnp.sum(dnormed * x * scale, axis=0, keepdims=True)
    small_in[0, 1:2, :] = dgain_ref[0:1, :]
    small_in[0, 8:16, :width] = stats[...]
    for step in range(1, line.count):
        made = line.copy(small_in.at[0], small_in.at[step], small_sems, step)
        made.start()
        sent.append(made)
    pair.arrive(bc_in, 2, 4)
    bc_ref[here, :] = (bc_out[...].astype(F32) + bc_in[...].astype(F32)).astype(BF16)
    bc_all.start()
    early_all.near()
    last_ref[here, :] = collected(2)
    last_all.start()
    bc_all.relay()
    for step in range(1, line.count):
        line.copy(small_in.at[0], small_in.at[step], small_sems, step).wait_recv()
    summed = small_in[line.f % line.count]
    for other in range(1, line.count):
        summed = summed + small_in[(line.f + line.count - other) % line.count]
    mine = pl.ds(pl.multiple_of(place.slot(0) * small_rows, small_rows), small_rows)
    small_ref[mine, :] = summed
    small_all.start()
    early_all.far()
    last_all.relay()
    small_all.relay()
    small_all.near()
    small_all.far()
    bc_all.near()
    bc_all.far()
    last_all.near()
    last_all.far()
    for mask in range(4):
        small_all.core(mask)
    other = pl.ds(pl.multiple_of((1 - place.t) * ROWS, ROWS), ROWS)
    pair.arrive(grad_ref.at[other], 0, 4)
    pair.arrive(out_ref.at[other], 1, 4)
    for made in sent:
        made.wait_send()
    pair.finish()
    mid_all.finish()
    out_all.finish()
    small_all.finish()
    last_all.finish()
    early_all.finish()
    bc_all.finish()


def closing(small_inputs, streams, loads, fsdp):
    ffn, dout = small_inputs[8], small_inputs[10]
    normed_t, w, hidden, down, _, _ = loads
    model, count = normed_t.shape
    share = ffn.shape[0]
    columns = w.shape[1]
    chips = lax.axis_size("context")
    blocks = count // ROWS
    vmem = pl.BlockSpec(memory_space=pltpu.VMEM)
    hbm = pl.BlockSpec(memory_space=pl.ANY)
    shape = jax.ShapeDtypeStruct
    dma = pltpu.SemaphoreType.DMA
    space = pltpu.VMEM
    inner = streams[4].shape[0] // blocks
    return pl.pallas_call(
        closing_kernel,
        out_shape=(
            shape((2 * ROWS, model), BF16),
            shape((2 * ROWS, model), BF16),
            shape((chips * share, EARLY), BF16),
            shape((chips * share, 256), BF16),
            shape((chips * share, 256), BF16),
            shape((chips * share, ffn.shape[1]), BF16),
            shape((chips * share, dout.shape[1]), BF16),
            shape((2 * chips * 16, model), F32),
        ),
        in_specs=[vmem] * 11 + [hbm] * 11,
        out_specs=(vmem,) * 8,
        scratch_shapes=[space((2, one.shape[0] // blocks, one.shape[1]), one.dtype) for one in streams]
        + [space(one.shape, one.dtype) for one in loads[:4]]
        + [space((ROWS, model), BF16)]
        + [
            space((count, model), BF16),
            space((count, EARLY), BF16),
            space((model, columns), F32),
            space((model, columns), BF16),
            space((fsdp - 1, share, columns), BF16),
            space((fsdp - 1, share, dout.shape[1]), BF16),
            space((ROWS, model), F32),
            space((ROWS, model), F32),
            space((4, ROWS, model), BF16),
            space((4, ROWS, model), BF16),
            space((share, 256), BF16),
            space((share, 256), BF16),
            space((fsdp, 16, model), F32),
            space((8, 512), F32),
            space((ROWS + 8, 512), F32),
            space((ROWS + 8, 128), F32),
            space((inner, STATE), F32),
            space((inner, STATE), F32),
            space((HEAD_DIM, count), F32),
            space((HEAD_DIM, count), F32),
        ]
        + scatter_scratch(model)
        + scatter_scratch(model)
        + [dma((2, GATHER_SEMS))] * 4
        + [dma((3, 2, fsdp)), dma((2, fsdp)), dma((2, fsdp)), dma((2, 3)), dma((6,)), dma((2, BACK_INPUTS)), dma((2, GATHER_SEMS)), dma((2, GATHER_SEMS))],
        compiler_params=pltpu.CompilerParams(
            collective_id=2, has_side_effects=True, vmem_limit_bytes=61 << 20
        ),
        cost_estimate=pl.CostEstimate(
            flops=4 * count * model * columns, bytes_accessed=30 << 20, transcendentals=0
        ),
    )(*small_inputs, *streams, *loads)


def assemble_kernel(
    early_ref, bcs_ref, late_ref, mid_ref, outs_ref, dx_ref, out_in_ref, small_ref, steps_ref,
    out_ref, grad_ref, query_ref, keyval_ref, attn_ref, gate_ref, x_ref, bc_ref, step_ref, ssm_ref,
    ffn_gate_ref, ffn_up_ref, ffn_down_ref, gain_ref, gain_ffn_ref, conv_x_ref, conv_bc_ref,
    bias_ref, decay_ref, skip_ref,
):
    chips = late_ref.shape[0]
    heads = step_ref.shape[0] // chips
    inner = heads * SSM_DIM
    hid = ffn_gate_ref.shape[1] // chips

    def spread(source, begin, width):
        return jnp.concatenate(
            [source[k, :, begin : begin + width].astype(F32) for k in range(chips)], axis=1
        )

    def summed(source, begin, end):
        total = source[0, :, begin:end].astype(F32)
        for k in range(1, chips):
            total = total + source[k, :, begin:end].astype(F32)
        return total

    out_ref[...] = out_in_ref[...]
    grad_ref[...] = dx_ref[...]
    gate_ref[...] = spread(early_ref, 0, inner)
    query_ref[...] = spread(early_ref, inner, HEAD_DIM)
    keyval_ref[...] = summed(early_ref, 256, 384)
    x_ref[...] = spread(late_ref, 0, inner)
    bc_ref[...] = summed(bcs_ref, 0, 256)
    ffn_gate_ref[...] = spread(mid_ref, 0, hid)
    ffn_up_ref[...] = spread(mid_ref, hid, hid)
    ffn_down_ref[...] = spread(mid_ref, 2 * hid, hid)
    ssm_ref[...] = spread(outs_ref, 0, inner)
    attn_ref[...] = spread(outs_ref, inner, HEAD_DIM)

    @pl.when(pl.program_id(0) == 0)
    def _():
        step_ref[...] = spread(steps_ref, inner, heads).T
        everywhere = small_ref[0:16, :]
        for k in range(1, small_ref.shape[0] // 16):
            everywhere = everywhere + small_ref[16 * k : 16 * k + 16, :]
        gain_ref[...] = everywhere[0:1]
        gain_ffn_ref[...] = everywhere[1:2]
        conv_bc_ref[...] = everywhere[8 : 8 + CONV, 256:512]
        core = lax.axis_index("tensor")
        own = [
            small_ref[pl.ds(pl.multiple_of((2 * k + core) * 16, 16), 16), :] for k in range(chips)
        ]
        conv_x_ref[...] = jnp.concatenate([one[8 : 8 + CONV, :inner] for one in own], axis=1)
        for row, target in ((12, skip_ref), (13, bias_ref), (14, decay_ref)):
            target[...] = jnp.concatenate(
                [
                    jnp.sum(
                        one[row : row + 1, h * SSM_DIM : (h + 1) * SSM_DIM], axis=1, keepdims=True
                    )
                    for one in own
                    for h in range(heads)
                ],
                axis=1,
            )


def assemble(early, bcs, last, mid, outs, dx, out, small, widths, heads):
    chips = lax.axis_size("context")
    share = last.shape[0] // chips
    turns = 2
    rows = share // turns
    shape = jax.ShapeDtypeStruct
    block = lambda height, width: pl.BlockSpec((height, width), lambda i: (i, 0))
    fixed = lambda height, width: pl.BlockSpec((height, width), lambda i: (0, 0))
    slab = lambda width: pl.BlockSpec((chips, rows, width), lambda i: (0, i, 0))
    token_rows = dx.shape[0] // turns
    model = dx.shape[1]
    tiny = [
        (1, model), (1, model), (CONV, heads * SSM_DIM), (CONV, 2 * STATE), (1, heads), (1, heads),
        (1, heads),
    ]
    return pl.pallas_call(
        assemble_kernel,
        grid=(turns,),
        out_shape=(shape(out.shape, BF16), shape(dx.shape, BF16))
        + tuple(shape((share, w) if w > heads else (w, share), F32) for w in widths)
        + tuple(shape(one, F32) for one in tiny),
        in_specs=[
            slab(early.shape[1]), slab(bcs.shape[1]), slab(last.shape[1]), slab(mid.shape[1]), slab(outs.shape[1]),
            block(token_rows, model), block(token_rows, model), fixed(*small.shape),
            pl.BlockSpec((chips, share, last.shape[1]), lambda i: (0, 0, 0)),
        ],
        out_specs=(block(token_rows, model), block(token_rows, model))
        + tuple(block(rows, w) if w > heads else fixed(w, share) for w in widths)
        + tuple(fixed(*one) for one in tiny),
        compiler_params=pltpu.CompilerParams(vmem_limit_bytes=60 << 20),
    )(*[one.reshape(chips, share, -1) for one in (early, bcs, last, mid, outs)], dx, out, small,
      last.reshape(chips, share, -1))


def per_device(
    tokens, segments, deal, gain_mix, w_query, w_keyval, w_attn_out, w_gate_z, w_in_x, w_bc, w_step,
    conv_x, conv_bc, step_bias, decay_log, skip, w_ssm_out, gain_ffn, w_ffn_gate, w_ffn_up,
    w_ffn_down, cotangent,
):
    normed_t, u, w_all, wout_all, cot_all, table, head_rows, taps = opening(
        tokens,
        cotangent,
        (w_in_x, w_query, w_bc, w_gate_z, w_keyval, w_step.T, w_ssm_out, w_attn_out),
        gain_mix,
        segments,
        (conv_x, conv_bc),
        (step_bias, decay_log, skip),
    )
    ag, y, conv, states, keyval, kept, normed_t, keyval_t = mixer_forward(u, normed_t, table, head_rows, taps, deal[0])
    hidden, dag, mixed, dmixed, dgain, down, dffn, dout = middle(
        ag, wout_all, (w_ffn_gate, w_ffn_up, w_ffn_down), tokens, cotangent, cot_all, gain_ffn
    )
    dx, out, early, bcs, last, mids, outs, small = closing(
        (
            deal, dag, keyval, keyval_t, head_rows, taps, dmixed, gain_mix.reshape(1, -1), dffn,
            dgain, dout,
        ),
        (table, y, conv, kept, states),
        (normed_t, w_all, hidden, down, mixed, tokens),
        lax.axis_size("fsdp"),
    )
    weights = (
        w_query, w_keyval, w_attn_out, w_gate_z, w_in_x, w_bc, w_step, w_ssm_out, w_ffn_gate,
        w_ffn_up, w_ffn_down,
    )
    done = assemble(early, bcs, last, mids, outs, dx, out, small, [w.shape[1] for w in weights], skip.shape[0])
    grads = done[2:13]
    gain, gain_two, taps_x, taps_bc, bias, decay, skips = done[13:]
    return (
        done[0],
        done[1],
        gain.reshape(-1),
        *grads[:6],
        grads[6].T,
        taps_x,
        taps_bc,
        bias.reshape(-1),
        decay.reshape(-1),
        skips.reshape(-1),
        grads[7],
        gain_two.reshape(-1),
        *grads[8:],
    )


def solution(mesh):
    in_specs = (
        P(("fsdp", "context"), None),
        P("fsdp", None),
        P("fsdp", None),
        P(),
        P("fsdp", "tensor"),
        P("fsdp", "tensor"),
        P("fsdp", "tensor"),
        P("fsdp", "tensor"),
        P("fsdp", "tensor"),
        P("fsdp", None),
        P("fsdp", "tensor"),
        P(None, "tensor"),
        P(),
        P("tensor"),
        P("tensor"),
        P("tensor"),
        P("fsdp", "tensor"),
        P(),
        P("fsdp", "tensor"),
        P("fsdp", "tensor"),
        P("fsdp", "tensor"),
        P(("fsdp", "context"), None),
    )
    out_specs = (
        P(("fsdp", "context"), None),
        P(("fsdp", "context"), None),
        P(),
        P("fsdp", "tensor"),
        P("fsdp", "tensor"),
        P("fsdp", "tensor"),
        P("fsdp", "tensor"),
        P("fsdp", "tensor"),
        P("fsdp", None),
        P("fsdp", "tensor"),
        P(None, "tensor"),
        P(),
        P("tensor"),
        P("tensor"),
        P("tensor"),
        P("fsdp", "tensor"),
        P(),
        P("fsdp", "tensor"),
        P("fsdp", "tensor"),
        P("fsdp", "tensor"),
    )
    return jax.shard_map(
        per_device, mesh=mesh, in_specs=in_specs, out_specs=out_specs, check_vma=False
    )
```

```python
import functools
import math

import jax
import jax.numpy as jnp
from jax import lax
from jax.experimental import pallas as pl
from jax.experimental.pallas import tpu as pltpu
from jax.sharding import PartitionSpec as P

HEAD_DIM = 64
SSM_DIM = 64
STATE = 128
CONV = 4
HALF = 256
WINDOW = 4

epsilon = 1e-05
masked = -1e30
F32 = jnp.float32
BF16 = jnp.bfloat16
exact = lax.Precision.HIGHEST


def dot(left, right, left_dim=1, right_dim=0, precision=None):
    return lax.dot_general(
        left,
        right,
        (((left_dim,), (right_dim,)), ((), ())),
        precision=precision,
        preferred_element_type=F32,
    )


def exact_sums(ones, values, right_dim=0):
    high = values.astype(BF16)
    rest = values - high.astype(F32)
    middle = rest.astype(BF16)
    low = (rest - middle.astype(F32)).astype(BF16)
    return sum(dot(ones, one, 1, right_dim) for one in (low, middle, high))


def sigmoid(v):
    return 1.0 / (1.0 + jnp.exp(-v))


def softplus(v):
    return jnp.maximum(v, 0.0) + jnp.log1p(jnp.exp(-jnp.abs(v)))


def swap_halves(v):
    half = v.shape[1] // 2
    return jnp.concatenate([v[:, half:], v[:, :half]], axis=1)


def iotas(rows, columns):
    return (
        lax.broadcasted_iota(jnp.int32, (rows, columns), 0),
        lax.broadcasted_iota(jnp.int32, (rows, columns), 1),
    )


def state_scale(last_row, carry_last, heads):
    pieces = [
        jnp.broadcast_to(last_row[:, h * SSM_DIM : h * SSM_DIM + 1], (SSM_DIM, STATE))
        for h in range(heads)
    ]
    return jnp.exp(jnp.concatenate(pieces, axis=0)) * carry_last


def block_decays(step_raw, heads_ref, lane_pos, heads):
    rows = step_raw.shape[0]
    inner = heads * SSM_DIM
    raw = step_raw + heads_ref[0:1, :inner]
    step = softplus(raw)
    rate = step * jnp.exp(heads_ref[1:2, :inner])
    row, col = iotas(rows, rows)
    lower = jnp.where(col <= row, 1.0, 0.0).astype(BF16)
    totals = exact_sums(lower, -rate)
    last_row = totals[rows - 1 : rows]
    pos_last = lane_pos[rows - 1 : rows, 0:1]
    local = lax.broadcasted_iota(jnp.int32, (rows, 1), 0).astype(F32)
    carry_on = (lane_pos[:, 0:1] > local).astype(F32)
    keep_last = (local >= (rows - 1) - pos_last).astype(F32)
    carry_last = (pos_last > rows - 1).astype(F32)
    factor = jnp.exp(totals) * carry_on
    tails = jnp.exp(last_row - totals) * keep_last
    return raw, step, rate, totals, last_row, carry_last, factor, tails


def local_mask(lane_pos, rows):
    row, col = iotas(rows, rows)
    gap = (row - col).astype(F32)
    return (gap >= 0) & (gap <= lane_pos[:, 0:1])


def key_window(block):
    start = jnp.maximum(block - WINDOW, 0)
    return start, (block - start) * HALF


def window_mask(lane_pos, offset, rows, keys):
    last = (lax.broadcasted_iota(jnp.int32, (rows, 1), 0) + offset).astype(F32)
    col = lax.broadcasted_iota(jnp.int32, (8, keys), 1)[0:1].astype(F32)
    return (col <= last) & (col >= last - lane_pos[:, 0:1])


def head_decay(totals, totals_t, h, allowed):
    gap = totals[:, h * SSM_DIM : h * SSM_DIM + 1] - totals_t[h * SSM_DIM : h * SSM_DIM + 1, :]
    return jnp.exp(jnp.where(allowed, gap, masked))


def mixer_forward_kernel(
    order_ref, u_ref, normed_ref, table_ref, heads_ref, taps_ref, ag_ref, y_ref, conv_ref, state_in_ref,
    kv_ref, kept_ref, ordered_ref, kv_t_ref, ext, state, keys_t, values, found,
):
    block = pl.program_id(0)
    heads = state.shape[0] // SSM_DIM
    inner = heads * SSM_DIM
    width = ext.shape[1]
    rows = u_ref.shape[0]

    @pl.when(block == 0)
    def _():
        ext[0:8, :] = jnp.zeros((8, width), F32)
        state[...] = jnp.zeros(state.shape, F32)
        keys_t[...] = jnp.zeros(keys_t.shape, BF16)
        values[...] = jnp.zeros(values.shape, BF16)

    lane_pos = table_ref[:, 128:256]
    cosine = table_ref[:, 0:64]
    sine = table_ref[:, 64:128]
    q_at = inner
    u = u_ref[:, :width].astype(F32)
    ext[8 : 8 + rows, :] = u
    conv = u * taps_ref[CONV - 1 : CONV, :]
    for back in range(1, CONV):
        reach = lane_pos[:, 0:1] >= back
        shifted = ext[8 - back : 8 - back + rows, :]
        conv = conv + jnp.where(reach, shifted, 0.0) * taps_ref[CONV - 1 - back : CONV - back, :]
    ext[0:8, :] = u[rows - 8 : rows]
    act = conv * sigmoid(conv)
    ssm_x = act[:, :inner].astype(BF16)
    ssm_b = act[:, 256:384].astype(BF16)
    ssm_c = act[:, 384:512].astype(BF16)
    conv_ref[:, 0:256] = conv[:, 0:256]
    conv_ref[:, 256:512] = conv[:, 256:512]
    query = u[:, q_at : q_at + HEAD_DIM]
    query = (query * cosine + swap_halves(query) * sine).astype(BF16)
    conv_ref[:, q_at : q_at + HEAD_DIM] = query.astype(F32)
    key = u_ref[:, 512 + inner : 512 + inner + HEAD_DIM].astype(F32)
    key = key * cosine + swap_halves(key) * sine
    value = u_ref[:, 768 + inner : 768 + inner + HEAD_DIM].astype(F32)
    pair = jnp.concatenate([key, value], axis=1).astype(BF16)
    pair_t = jnp.concatenate([key, value], axis=1).T.astype(BF16)
    kv_ref[...] = pair
    kv_t_ref[...] = pair_t
    here = pl.ds(pl.multiple_of(block * rows, rows), rows)
    values[here, :] = value.astype(BF16)
    keys_t[:, here] = pair_t[:HEAD_DIM]
    query_low = query * 0.125

    def attend(first, offset, span):
        begin = pl.multiple_of(first * rows, rows)
        scores = dot(query_low, keys_t[:, pl.ds(begin, span)])
        scores = jnp.where(window_mask(lane_pos, offset, rows, span), scores, masked)
        highest = jnp.max(scores, axis=1, keepdims=True)
        weights = jnp.exp(scores - highest)
        total = jnp.sum(weights, axis=1, keepdims=True)
        probs = (weights * (1.0 / total)).astype(BF16)
        found[:, :HEAD_DIM] = dot(probs, values[pl.ds(begin, span), :])
        found[:, HEAD_DIM:] = jnp.broadcast_to(highest + jnp.log(total), (rows, HEAD_DIM))

    @pl.when(block < 2)
    def _():
        attend(0, block * rows, 2 * HALF)

    @pl.when((block >= 2) & (block < WINDOW))
    def _():
        attend(0, block * rows, WINDOW * HALF)

    @pl.when(block >= WINDOW)
    def _():
        attend(block - WINDOW, WINDOW * rows, (WINDOW + 1) * HALF)

    attended = found[:, :HEAD_DIM]
    _, step, _, totals, last_row, carry_last, factor, tails = block_decays(
        u_ref[:, 768 : 768 + inner].astype(F32), heads_ref, lane_pos, heads
    )
    totals_t = totals.T
    allowed = local_mask(lane_pos, rows)
    cross = dot(ssm_c, ssm_b, 1, 1)
    x_f = ssm_x.astype(F32)
    stepped = step * x_f
    stepped_low = stepped.astype(BF16)
    parts = []
    for h in range(heads):
        lanes = slice(h * SSM_DIM, (h + 1) * SSM_DIM)
        mix = (head_decay(totals, totals_t, h, allowed) * cross).astype(BF16)
        parts.append(dot(mix, stepped_low[:, lanes]))
    held = state[...]
    state_in_ref[...] = held
    y_pure = jnp.concatenate(parts, axis=1) + factor * dot(ssm_c, held.astype(BF16), 1, 1)
    tailed = (tails * stepped_low.astype(F32)).astype(BF16)
    state[...] = state_scale(last_row, carry_last, heads) * held + dot(tailed, ssm_b, 0, 0)
    y_ref[:, 0:256] = jnp.concatenate(
        [y_pure, found[:, HEAD_DIM:]], axis=1
    )
    y_ref[:, 256:512] = jnp.concatenate([u_ref[:, 768 : 768 + inner], attended], axis=1)
    ordered_ref[...] = normed_ref[...]
    kept_ref[...] = u_ref[:, 0:768].astype(BF16)
    y_full = y_pure + heads_ref[2:3, :inner] * x_f
    gate = u_ref[:, 512 : 512 + inner].astype(F32)
    gated = y_full * (gate * sigmoid(gate))
    ag_ref[...] = jnp.concatenate([gated, attended], axis=1).astype(BF16)


def attention_backward(
    block, dag, table_ref, heads_ref, y_ref, conv_ref, kept_ref, kv_ref, kv_t_ref, dkey_t, dvalue_t,
):
    inner = dag.shape[1] - HEAD_DIM
    rows = dag.shape[0]
    lane_pos = table_ref[:, 128:256]
    cosine = table_ref[:, 0:64]
    sine = table_ref[:, 64:128]
    first, offset = key_window(block)
    span = (WINDOW + 1) * HALF
    begin = pl.multiple_of(first * rows, rows)
    keys = kv_ref[pl.ds(begin, span), :HEAD_DIM]
    keys_t = kv_t_ref[:HEAD_DIM, pl.ds(begin, span)]
    values_t = kv_t_ref[HEAD_DIM:, pl.ds(begin, span)]
    query = conv_ref[:, inner : inner + HEAD_DIM] * 0.125
    query_low = query.astype(BF16)
    datt = dag[:, inner : inner + HEAD_DIM]
    datt_f = datt.astype(F32)
    lse = y_ref[:, inner : inner + 1]
    scores = dot(query_low, keys_t)
    allowed_all = window_mask(lane_pos, offset, rows, span)
    probs = jnp.exp(jnp.where(allowed_all, scores, masked) - lse)
    inward = jnp.sum(datt_f * y_ref[:, 256 + inner : 256 + inner + HEAD_DIM], axis=1, keepdims=True)
    dscores = (probs * (dot(datt, values_t) - inward)).astype(BF16)
    dquery = dot(dscores, keys) * 0.125
    dkey_t[:, pl.ds(begin, span)] += dot(query.T.astype(BF16), dscores)
    dvalue_t[:, pl.ds(begin, span)] += dot(datt_f.T.astype(BF16), probs.astype(BF16))
    here = pl.ds(pl.multiple_of(block * rows, rows), rows)
    dkey = dkey_t[:, here].T
    dvalue = dvalue_t[:, here].T
    dquery = dquery * cosine - swap_halves(dquery) * sine
    dkey = dkey * cosine - swap_halves(dkey) * sine
    conv = conv_ref[:, :inner]
    ssm_x = (conv * sigmoid(conv)).astype(BF16).astype(F32)
    gate = kept_ref[:, 512 : 512 + inner].astype(F32)
    sig = sigmoid(gate)
    dgated = dag[:, :inner].astype(F32)
    y_full = y_ref[:, :inner] + heads_ref[2:3, :inner] * ssm_x
    dgate = dgated * y_full * (sig * (1.0 + gate * (1.0 - sig)))
    return jnp.concatenate([dgate, dquery, dkey, dvalue], axis=1).astype(BF16)


def recurrence_backward(
    dag, table_ref, heads_ref, taps_ref, y_ref, conv_ref, kept_ref, state_in_ref, state_out, stats_ref,
    dext, dpos, dstate,
):
    heads = dstate.shape[0] // SSM_DIM
    inner = heads * SSM_DIM
    rows = dag.shape[0]
    lane_pos = table_ref[:, 128:256]
    conv = conv_ref[...]
    gate_conv = sigmoid(conv)
    act = conv * gate_conv
    dact = gate_conv * (1.0 + conv * (1.0 - gate_conv))
    ssm_x = act[:, :inner].astype(BF16)
    ssm_b = act[:, 256:384].astype(BF16)
    ssm_c = act[:, 384:512].astype(BF16)
    x_f = ssm_x.astype(F32)
    raw, step, rate, totals, last_row, carry_last, factor, tails = block_decays(
        y_ref[:, 256 : 256 + inner], heads_ref, lane_pos, heads
    )
    totals_t = totals.T
    allowed = local_mask(lane_pos, rows)
    cross = dot(ssm_c, ssm_b, 1, 1)
    gate = kept_ref[:, 512 : 512 + inner].astype(F32)
    sig = sigmoid(gate)
    y_pure = y_ref[:, :inner]
    dgated = dag[:, :inner].astype(F32)
    skip = heads_ref[2:3, :inner]
    dy = dgated * (gate * sig)
    dy_low = dy.astype(BF16)
    dy_r = dy_low.astype(F32)
    dy_t = dy.T.astype(BF16)
    stepped_low = (step * x_f).astype(BF16)
    stepped_r = stepped_low.astype(F32)
    tailed = (tails * stepped_r).astype(BF16)
    dcross = jnp.zeros((rows, rows), F32)
    parts = []
    for h in range(heads):
        lanes = slice(h * SSM_DIM, (h + 1) * SSM_DIM)
        decay = head_decay(totals, totals_t, h, allowed)
        mix = (decay * cross).astype(BF16)
        parts.append(dot(dy_t[lanes, :], mix))
        dcross = dcross + dot(dy_low[:, lanes], stepped_low[:, lanes], 1, 1) * decay
    dstep_x = jnp.concatenate(parts, axis=0).T
    dcross_low = dcross.astype(BF16)
    held = state_in_ref[...].astype(BF16)
    dheld = dstate[...]
    dheld_low = dheld.astype(BF16)
    dfactored = (factor * dy).astype(BF16)
    from_state = dot(ssm_b, dheld_low, 1, 1)
    dssm_c = dot(dcross_low, ssm_b) + dot(dfactored, held)
    dssm_b = dot(dcross_low, ssm_c, 0, 0) + dot(tailed, dheld_low)
    dtotals = dy_r * y_pure - stepped_r * dstep_x - tailed.astype(F32) * from_state
    dstep_x = dstep_x + tails * from_state
    end_term = exact_sums(
        jnp.ones((16, STATE), BF16), dheld_low.astype(F32) * state_out[...], 1
    )[0:1]
    row, col = iotas(rows, rows)
    upper = jnp.where(col >= row, 1.0, 0.0).astype(BF16)
    drate = -(exact_sums(upper, dtotals) + end_term)
    state_out[...] = state_in_ref[...]
    dstate[...] = state_scale(last_row, carry_last, heads) * dheld + dot(dfactored, ssm_c, 0, 0)
    dssm_x = step * dstep_x + skip * dy
    dstep = x_f * dstep_x + jnp.exp(heads_ref[1:2, :inner]) * drate
    draw = dstep * sigmoid(raw)
    none = jnp.zeros((rows, HEAD_DIM), F32)
    dconv = jnp.concatenate([dssm_x, none, dssm_b, dssm_c], axis=1) * dact
    dext[0:rows, :] = dconv
    dpos[0:rows, :] = lane_pos
    u = kept_ref[:, 0:512].astype(F32)
    du = dconv * taps_ref[CONV - 1 : CONV, :]
    stats_ref[CONV - 1 : CONV, :] += jnp.sum(dconv * u, axis=0, keepdims=True)
    for ahead in range(1, CONV):
        reach = dpos[ahead : ahead + rows, 0:1] >= ahead
        shifted = jnp.where(reach, dext[ahead : ahead + rows, :], 0.0)
        tap = CONV - 1 - ahead
        du = du + shifted * taps_ref[tap : tap + 1, :]
        stats_ref[tap : tap + 1, :] += jnp.sum(shifted * u, axis=0, keepdims=True)
    dext[rows : rows + 8, :] = dconv[0:8]
    dpos[rows : rows + 8, :] = lane_pos[0:8]
    stats_ref[4:5, :inner] += jnp.sum(dy * x_f, axis=0, keepdims=True)
    stats_ref[5:6, :inner] += jnp.sum(draw, axis=0, keepdims=True)
    stats_ref[6:7, :inner] += jnp.sum(drate * rate, axis=0, keepdims=True)
    summed = [
        jnp.sum(draw[:, h * SSM_DIM : (h + 1) * SSM_DIM], axis=1, keepdims=True)
        for h in range(heads)
    ]
    lane = lax.broadcasted_iota(jnp.int32, (rows, HEAD_DIM), 1)
    dstep_all = jnp.zeros((rows, HEAD_DIM), F32)
    for h in range(heads):
        dstep_all = jnp.where(lane == h, summed[h], dstep_all)
    return jnp.concatenate([du[:, :inner], dstep_all, du[:, 256:512]], axis=1).astype(BF16)


def slot_holding(order, block):
    slot = 0
    for k in range(1, order.shape[0]):
        slot = slot + jnp.where(order[k] == block, k, 0)
    return slot


def mixer_forward(u, normed_t, table, head_rows, taps, slot_of):
    count = u.shape[0]
    blocks = count // HALF
    heads = 3
    inner = heads * SSM_DIM
    width = taps.shape[1]
    at_slot = lambda i, order: (slot_holding(order, i), 0)
    in_order = lambda i, slots: (i, 0)
    whole = lambda i, slots: (0, 0)
    return pl.pallas_call(
        mixer_forward_kernel,
        out_shape=(
            jax.ShapeDtypeStruct((count, inner + HEAD_DIM), BF16),
            jax.ShapeDtypeStruct((count, 512), F32),
            jax.ShapeDtypeStruct((count, width), F32),
            jax.ShapeDtypeStruct((blocks * inner, STATE), F32),
            jax.ShapeDtypeStruct((count, 2 * HEAD_DIM), BF16),
            jax.ShapeDtypeStruct((count, 768), BF16),
            jax.ShapeDtypeStruct(normed_t.shape, BF16),
            jax.ShapeDtypeStruct((2 * HEAD_DIM, count), BF16),
        ),
        grid_spec=pltpu.PrefetchScalarGridSpec(
            num_scalar_prefetch=1,
            grid=(blocks,),
            in_specs=[
                pl.BlockSpec((HALF, u.shape[1]), at_slot),
                pl.BlockSpec((normed_t.shape[0], HALF), lambda i, order: at_slot(i, order)[::-1]),
                pl.BlockSpec((HALF, table.shape[1]), in_order),
                pl.BlockSpec(head_rows.shape, whole),
                pl.BlockSpec(taps.shape, whole),
            ],
            out_specs=(
                pl.BlockSpec((HALF, inner + HEAD_DIM), at_slot),
                pl.BlockSpec((HALF, 512), in_order),
                pl.BlockSpec((HALF, width), in_order),
                pl.BlockSpec((inner, STATE), in_order),
                pl.BlockSpec((HALF, 2 * HEAD_DIM), in_order),
                pl.BlockSpec((HALF, 768), in_order),
                pl.BlockSpec((normed_t.shape[0], HALF), lambda i, order: (0, i)),
                pl.BlockSpec((2 * HEAD_DIM, HALF), lambda i, order: (0, i)),
            ),
            scratch_shapes=[
                pltpu.VMEM((8 + HALF, width), F32),
                pltpu.VMEM((inner, STATE), F32),
                pltpu.VMEM((HEAD_DIM, count), BF16),
                pltpu.VMEM((count, HEAD_DIM), BF16),
                pltpu.VMEM((HALF, 2 * HEAD_DIM), F32),
            ],
        ),
        compiler_params=pltpu.CompilerParams(vmem_limit_bytes=60 << 20),
    )(slot_of, u, normed_t, table, head_rows, taps)


MESH = pl.DeviceIdType.MESH


class Place:
    def __init__(self):
        self.c = lax.axis_index("context")
        self.t = lax.axis_index("tensor")
        count = lax.axis_size("context")
        self.chips = [
            self.c,
            self.c + 1 - 2 * (self.c % 2),
            (self.c + count // 2) % count,
            count - 1 - self.c,
        ]

    def slot(self, mask, sibling=False):
        core = 1 - self.t if sibling else self.t
        return self.chips[mask] * 2 + core

    def target(self, mask):
        if mask == 4:
            return {"tensor": 1 - self.t}
        return {"context": self.chips[mask]}

    def hello(self, line=None):
        barrier = pltpu.get_barrier_semaphore()
        targets = [self.target(mask) for mask in (1, 2, 4)]
        if line is not None:
            targets += [line.target(step) for step in range(1, line.count)]
        for target in targets:
            pl.semaphore_signal(barrier, inc=1, device_id=target, device_id_type=MESH)
        return len(targets)

    def greet(self, line=None):
        pl.semaphore_wait(pltpu.get_barrier_semaphore(), self.hello(line))


class Wire:
    def __init__(self, place, sems):
        self.place = place
        self.sems = sems
        self.sent = []

    def copy(self, source, target, index, mask):
        return pltpu.make_async_remote_copy(
            src_ref=source,
            dst_ref=target,
            send_sem=self.sems.at[0, index],
            recv_sem=self.sems.at[1, index],
            device_id=self.place.target(mask),
            device_id_type=MESH,
        )

    def send(self, source, target, index, mask):
        def made():
            here = source() if callable(source) else source
            there = target() if callable(target) else target
            return self.copy(here, there, index, mask)

        made().start()
        self.sent.append(made)

    def arrive(self, target, index, mask):
        self.copy(target, target, index, mask).wait_recv()

    def finish(self):
        for made in self.sent:
            made().wait_send()
        self.sent = []


ROWS = HALF
PART = HALF // 2
TOP, END = pl.ds(0, PART), pl.ds(PART, PART)
SCATTER_SEMS = 10
GATHER_SEMS = 14


def scatter_scratch(columns, kept=BF16):
    return [
        pltpu.VMEM((4, ROWS, columns), BF16),
        pltpu.VMEM((4, ROWS, columns), BF16),
        pltpu.VMEM((6, PART, columns), BF16),
        pltpu.VMEM((ROWS, columns), kept),
        pltpu.SemaphoreType.DMA((2, SCATTER_SEMS)),
    ]


SCATTER_ORDER = (3, 1, 2, 0)


class Scatter:
    def __init__(self, place, scratch):
        self.place = place
        self.core_in, self.out, self.chip_in, self.kept, sems = scratch
        self.wire = Wire(place, sems)

    def to_core(self, mask, source):
        index = SCATTER_ORDER.index(mask)
        self.wire.send(source, self.core_in.at[index], index, 4)

    def from_core(self, mask):
        index = SCATTER_ORDER.index(mask)
        self.wire.arrive(self.core_in.at[index], index, 4)
        return self.core_in[index].astype(F32)

    def first(self, mine, total, between=None):
        wire, out, kept = self.wire, self.out, self.kept
        both = mine(3) + self.from_core(3)
        out[0] = both.astype(BF16)
        wire.send(lambda: out.at[0, TOP], lambda: self.chip_in.at[0], 4, 1)
        wire.send(lambda: out.at[0, END], lambda: self.chip_in.at[1], 5, 2)
        both = mine(1) + self.from_core(1)
        out[1] = both.astype(BF16)
        wire.send(lambda: out.at[1, TOP], lambda: self.chip_in.at[2], 6, 1)
        kept[END] = both[PART:].astype(kept.dtype)
        both = mine(2) + self.from_core(2)
        out[2] = both.astype(BF16)
        wire.send(lambda: out.at[2, END], lambda: self.chip_in.at[3], 7, 2)
        kept[TOP] = both[:PART].astype(kept.dtype)
        total[...] = mine(0) + self.from_core(0)

    def second(self):
        wire, out, kept, came = self.wire, self.out, self.kept, self.chip_in
        wire.arrive(came.at[0], 4, 1)
        out[3, TOP] = (kept[TOP].astype(F32) + came[0].astype(F32)).astype(BF16)
        wire.send(lambda: out.at[3, TOP], lambda: came.at[4], 8, 2)
        wire.arrive(came.at[1], 5, 2)
        out[3, END] = (kept[END].astype(F32) + came[1].astype(F32)).astype(BF16)
        wire.send(lambda: out.at[3, END], lambda: came.at[5], 9, 1)

    def last(self, total):
        wire, came = self.wire, self.chip_in
        wire.arrive(came.at[2], 6, 1)
        wire.arrive(came.at[4], 8, 2)
        total[TOP] += came[2].astype(F32) + came[4].astype(F32)
        wire.arrive(came.at[3], 7, 2)
        wire.arrive(came.at[5], 9, 1)
        total[END] += came[3].astype(F32) + came[5].astype(F32)
        wire.finish()


class Gather:
    def __init__(self, place, whole, sems, rows=ROWS, cores=True):
        self.place = place
        self.whole = whole
        self.size = rows
        self.cores = cores
        self.wire = Wire(place, sems)

    def rows(self, mask, sibling=False, half=None):
        place, size = self.place, self.size
        block = place.slot(mask, sibling) if self.cores else place.chips[mask]
        begin = block * size
        if half is None:
            return self.whole.at[pl.ds(pl.multiple_of(begin, size), size)]
        return self.whole.at[pl.ds(pl.multiple_of(begin + half * (size // 2), size // 2), size // 2)]

    def both(self, mask, sibling=False, half=None):
        block = functools.partial(self.rows, mask, sibling, half)
        return block, block

    def start(self, core=True):
        wire = self.wire
        for half, mask, index in ((0, 1, 0), (1, 2, 1), (1, 1, 2), (0, 2, 3)):
            wire.send(*self.both(0, half=half), index, mask)
        if self.cores and core:
            wire.send(*self.both(0), 6, 4)

    def relay(self):
        wire = self.wire
        wire.arrive(self.rows(1, half=0), 0, 1)
        wire.send(*self.both(1, half=0), 4, 2)
        wire.arrive(self.rows(2, half=1), 1, 2)
        wire.send(*self.both(2, half=1), 5, 1)

    def near(self):
        wire = self.wire
        wire.arrive(self.rows(1, half=1), 2, 1)
        if self.cores:
            wire.send(*self.both(1), 7, 4)
        wire.arrive(self.rows(2, half=0), 3, 2)
        if self.cores:
            wire.send(*self.both(2), 8, 4)

    def far(self):
        wire = self.wire
        wire.arrive(self.rows(3, half=0), 4, 2)
        wire.arrive(self.rows(3, half=1), 5, 1)
        if self.cores:
            wire.send(*self.both(3), 9, 4)

    def core(self, mask):
        index = (6, 7, 8, 9)[mask]
        self.wire.arrive(self.rows(mask, sibling=True), index, 4)

    def finish(self):
        self.wire.finish()


class Line:
    def __init__(self):
        self.f = lax.axis_index("fsdp")
        self.count = lax.axis_size("fsdp")

    def target(self, step):
        return {"fsdp": (self.f + step) % self.count}

    def copy(self, source, target, sems, step):
        return pltpu.make_async_remote_copy(
            src_ref=source,
            dst_ref=target,
            send_sem=sems.at[0, step],
            recv_sem=sems.at[1, step],
            device_id=self.target(step),
            device_id_type=MESH,
        )


class LineGather:
    def __init__(self, line, whole, sems):
        self.line = line
        self.whole = whole
        self.sems = sems
        self.size = whole.shape[0] // line.count

    def rows(self, block):
        return self.whole.at[pl.ds(pl.multiple_of(block * self.size, self.size), self.size)]

    def copy(self, block, way, step):
        toward = self.line.f + 1 if way == 0 else self.line.f - 1
        return pltpu.make_async_remote_copy(
            src_ref=self.rows(block),
            dst_ref=self.rows(block),
            send_sem=self.sems.at[way, 0, step],
            recv_sem=self.sems.at[way, 1, step],
            device_id={"fsdp": toward},
            device_id_type=MESH,
        )

    def step(self, number, arrive=True):
        f, last = self.line.f, self.line.count - 1
        for way in (0, 1):
            block = f - number if way == 0 else f + number
            there = block >= 0 if way == 0 else block <= last
            goes_on = f < last if way == 0 else f > 0

            @pl.when(there)
            def _():
                if number > 0:
                    self.copy(block, way, number).wait_recv()

                @pl.when(goes_on)
                def _():
                    self.copy(block, way, number + 1).start()

    def finish(self):
        f, last = self.line.f, self.line.count - 1
        for number in range(self.line.count - 1):
            for way in (0, 1):
                block = f - number if way == 0 else f + number
                there = block >= 0 if way == 0 else block <= last
                goes_on = f < last if way == 0 else f > 0

                @pl.when(there & goes_on)
                def _():
                    self.copy(block, way, number + 1).wait_send()


def line_sems(count):
    return pltpu.SemaphoreType.DMA((2, 2, count + 1))


def opening_kernel(
    tokens_ref, cot_ref, in_x_ref, query_ref, bc_ref, gate_ref, keyval_ref, step_ref, ssm_ref, attn_ref,
    gain_ref, segments_ref, conv_x_ref, conv_bc_ref, bias_ref, decay_ref, skip_ref,
    normed_t_out, u_out, w_out, wout_out, cot_out, table_out, heads_ref, taps_ref,
    x_all, cot_all, normed, normed_t, u, weights_all, wout_all, table, wide,
    x_sems, cot_sems, w_sems, out_sems, local_sems, block_sems,
):
    place = Place()
    line = Line()
    rows_x = Gather(place, x_all, x_sems)
    rows_cot = Gather(place, cot_all, cot_sems)
    weights = LineGather(line, weights_all, w_sems)
    weights_out = LineGather(line, wout_all, out_sems)
    chips = lax.axis_size("context")
    share = in_x_ref.shape[0]
    heads = step_ref.shape[0] // chips
    inner = heads * SSM_DIM
    chip_rows = pl.ds(pl.multiple_of(place.c * 2 * ROWS, 2 * ROWS), 2 * ROWS)
    waiting = []

    def local(source, target, sem):
        made = pltpu.make_async_copy(source, target, sem)
        made.start()
        waiting.append(made)
        return made

    greetings = place.hello(line)
    own_x = pltpu.make_async_copy(tokens_ref, x_all.at[chip_rows], local_sems.at[0])
    own_x.start()
    own_cot = pltpu.make_async_copy(cot_ref, cot_all.at[chip_rows], local_sems.at[1])
    own_cot.start()
    mine = pl.ds(pl.multiple_of(line.f * share, share), share)
    heads_ref[...] = jnp.zeros(heads_ref.shape, F32)
    taps_ref[...] = jnp.zeros(taps_ref.shape, F32)
    for k in range(chips):

        @pl.when(place.c == k)
        def _():
            inner_part = slice(k * inner, (k + 1) * inner)
            head_part = slice(k * HEAD_DIM, (k + 1) * HEAD_DIM)
            weights_all[mine, 0:256] = jnp.concatenate(
                [gate_ref[:, inner_part], query_ref[:, head_part]], axis=1
            )
            weights_all[mine, 384 : 384 + inner] = in_x_ref[:, inner_part]
            wout_all[mine, :] = jnp.concatenate(
                [ssm_ref[:, inner_part], attn_ref[:, head_part]], axis=1
            )
            taps_ref[0:CONV, :inner] = conv_x_ref[:, inner_part]
            for h in range(heads):
                lane = slice(k * heads + h, k * heads + h + 1)
                for row, source in enumerate((bias_ref, decay_ref, skip_ref)):
                    heads_ref[row : row + 1, h * SSM_DIM : (h + 1) * SSM_DIM] = jnp.broadcast_to(
                        source[:, lane], (1, SSM_DIM)
                    )

    taps_ref[0:CONV, 256:512] = conv_bc_ref[...]
    head, column = iotas(step_ref.shape[0], HEAD_DIM)
    chosen = (head == column + place.c * heads) & (column < heads)
    steps = dot(step_ref[...], jnp.where(chosen, 1.0, 0.0).astype(BF16), 0, 0)
    weights_all[mine, 384 + inner : 640] = steps.astype(BF16)
    weights_all[mine, 256:384] = keyval_ref[...]
    weights_all[mine, 640:896] = bc_ref[...]
    own_x.wait()
    own_cot.wait()
    pl.semaphore_wait(pltpu.get_barrier_semaphore(), greetings)
    weights.step(0)
    rows_x.start(core=False)

    def norm(slot):
        rows = slot_rows(slot)
        x = x_all[rows, :].astype(F32)
        normed[rows, :] = (x * norm_scale(x) * gain_ref[...]).astype(BF16)
        columns = pl.ds(pl.multiple_of(slot * ROWS, ROWS), ROWS)
        normed_t[:, columns] = normed[rows, :].T

    norm(place.slot(0))
    norm(place.slot(0, True))

    numbers = segments_ref[...]
    bounds = [
        jnp.sum(jnp.where(numbers < k, 1.0, 0.0), axis=1, keepdims=True) for k in (1, 2)
    ]
    count = table.shape[0]
    lane = lax.broadcasted_iota(jnp.int32, (8, 128), 1)[0:1]
    power = -(lane % (HEAD_DIM // 2)).astype(F32) / (HEAD_DIM // 2)
    freqs = jnp.exp(power * math.log(10000.0))
    phase = jnp.where(lane < HEAD_DIM, math.pi / 2, 0.0)
    sign = jnp.where((lane >= HEAD_DIM) & (lane < HEAD_DIM + HEAD_DIM // 2), -1.0, 1.0)

    def angles(block, carry):
        row = lax.broadcasted_iota(jnp.int32, (ROWS, 128), 0) + block * ROWS
        row = row.astype(F32)
        start = jnp.where(row >= bounds[0], bounds[0], 0.0)
        start = jnp.where(row >= bounds[1], bounds[1], start)
        pos = row - start
        here = slot_rows(block)
        table[here, 0:128] = jnp.sin(pos * freqs + phase) * sign
        table[here, 128:256] = pos
        return carry

    blocks = count // ROWS
    rows_x.relay()
    rows_cot.start(core=False)
    lax.fori_loop(0, blocks // 2, angles, 0)
    weights.step(1)
    lax.fori_loop(blocks // 2, blocks, angles, 0)
    local(table, table_out, local_sems.at[2])
    rows_x.near()
    norm(place.slot(1))
    norm(place.slot(2))
    rows_cot.relay()
    for number in range(2, line.count - 1):
        weights.step(number)
    rows_x.far()
    norm(place.slot(3))
    for mask in (1, 2, 3):
        rows_x.core(mask)
        norm(place.slot(mask, True))
    weights_out.step(0)
    rows_cot.near()
    weights.step(line.count - 1)
    local(weights_all, w_out, local_sems.at[3])
    local(normed_t, normed_t_out, local_sems.at[6])
    row, column = iotas(HEAD_DIM, inner)
    copies = jnp.where(column // SSM_DIM == row, 1.0, 0.0).astype(BF16)
    wide[:, 0:256] = jnp.concatenate(
        [weights_all[:, 384 : 384 + inner], weights_all[:, inner:256]], axis=1
    )
    wide[:, 256:512] = weights_all[:, 640:896]
    wide[:, 512:768] = jnp.concatenate([weights_all[:, :inner], weights_all[:, 256:320]], axis=1)
    wide[:, 768:1024] = jnp.concatenate(
        [
            dot(weights_all[:, 384 + inner : 640], copies),
            weights_all[:, 320:384].astype(F32),
        ],
        axis=1,
    ).astype(BF16)

    def project(slot):
        rows = pl.ds(slot * ROWS, ROWS)
        u[rows, :] = dot(normed[rows, :], wide[...])
        local(u.at[rows], u_out.at[rows], block_sems.at[0, slot])

    for slot in range(blocks // 2):
        project(slot)
    weights_out.step(1)
    rows_cot.far()
    for slot in range(blocks // 2, blocks):
        project(slot)
    for number in range(2, line.count):
        weights_out.step(number)
    local(wout_all, wout_out, local_sems.at[4])
    for mask in (1, 2, 3):
        rows_cot.core(mask)
    local(cot_all, cot_out, local_sems.at[5])
    for made in waiting:
        made.wait()
    rows_x.finish()
    rows_cot.finish()
    weights.finish()
    weights_out.finish()


def opening(tokens, cotangent, weights, gain, segments, taps, by_head):
    fsdp = lax.axis_size("fsdp")
    model = tokens.shape[1]
    count = segments.shape[1]
    blocks = count // ROWS
    vmem = pl.BlockSpec(memory_space=pltpu.VMEM)
    hbm = pl.BlockSpec(memory_space=pl.ANY)
    shape = jax.ShapeDtypeStruct
    dma = pltpu.SemaphoreType.DMA
    buffers = [
        ((model, count), BF16),
        ((count, 1024), F32),
        ((model, 896), BF16),
        ((model, 256), BF16),
        ((count, model), BF16),
        ((count, 256), F32),
    ]
    kept = [buffers[k] for k in (0, 1, 2, 3, 5)]
    return pl.pallas_call(
        opening_kernel,
        out_shape=tuple(shape(*one) for one in buffers) + (shape((8, 256), F32), shape((8, 512), F32)),
        in_specs=[hbm] * 2 + [vmem] * 15,
        out_specs=(hbm,) * 6 + (vmem,) * 2,
        scratch_shapes=[pltpu.VMEM((count, model), BF16)] * 3
        + [pltpu.VMEM(*one) for one in kept]
        + [
            pltpu.VMEM((model, 1024), BF16),
            dma((2, GATHER_SEMS)),
            dma((2, GATHER_SEMS)),
            line_sems(fsdp),
            line_sems(fsdp),
            dma((7,)),
            dma((1, blocks)),
        ],
        compiler_params=pltpu.CompilerParams(
            collective_id=3, has_side_effects=True, vmem_limit_bytes=60 << 20
        ),
        cost_estimate=pl.CostEstimate(
            flops=2 * count * model * 1024, bytes_accessed=30 << 20, transcendentals=count * 128
        ),
    )(
        tokens, cotangent, *weights, gain.reshape(1, -1), segments, *taps,
        *[one.reshape(1, -1) for one in by_head],
    )


def slot_rows(slot):
    return pl.ds(pl.multiple_of(slot * ROWS, ROWS), ROWS)


def norm_scale(values):
    return lax.rsqrt(jnp.mean(values * values, axis=1, keepdims=True) + epsilon)


def middle_kernel(
    ag_ref, wout_ref, gate_ref, up_ref, down_ref, gain_ref, x_hbm, cot_hbm, cot_all_hbm,
    hidden_ref, dag_ref, mixed_ref, dmixed_ref, dgain_ref, down_all_ref, ffn_ref, dout_ref,
    x_ref, cot_ref, cot_all_ref, nffn_ref, dgu_ref, dm_ref, dw_ref, arrived, part, wffn_ref, *scratch,
):
    place = Place()
    first = Scatter(place, scratch[0:5])
    back = Scatter(place, scratch[5:10])
    forth = Gather(place, nffn_ref, scratch[10])
    home = Gather(place, dm_ref, scratch[11])
    hid = hidden_ref.shape[1]
    line = Line()
    weights = LineGather(line, wffn_ref, scratch[12])
    share = gate_ref.shape[0]
    greetings = place.hello(line)
    half = pl.ds(pl.multiple_of(place.t * ROWS, ROWS), ROWS)
    loads = [
        pltpu.make_async_copy(source, target, scratch[14].at[k])
        for k, (source, target) in enumerate(
            ((x_hbm.at[half], x_ref), (cot_hbm.at[half], cot_ref), (cot_all_hbm, cot_all_ref))
        )
    ]
    for made in loads:
        made.start()
    mine = pl.ds(pl.multiple_of(line.f * share, share), share)
    lanes = pl.ds(pl.multiple_of(place.c * hid, hid), hid)
    for k, source in enumerate((gate_ref, up_ref, down_ref)):
        wffn_ref[mine, k * hid : (k + 1) * hid] = source[:, lanes]

    def block(mask, sibling=False):
        return dot(ag_ref[slot_rows(place.slot(mask, sibling)), :], wout_ref[...], 1, 1)

    for mask in SCATTER_ORDER:
        part[slot_rows(place.slot(mask, True)), :] = block(mask, True).astype(BF16)
    pl.semaphore_wait(pltpu.get_barrier_semaphore(), greetings)
    for mask in SCATTER_ORDER:
        first.to_core(mask, part.at[slot_rows(place.slot(mask, True))])
    weights.step(0)
    first.first(block, mixed_ref)
    weights.step(1)
    first.second()
    for made in loads:
        made.wait()
    mixed_ref[...] += x_ref[...].astype(F32)
    first.last(mixed_ref)
    mixed = mixed_ref[...]
    gain = gain_ref[...]
    scale = norm_scale(mixed)
    own = slot_rows(place.slot(0))
    nffn_ref[own, :] = (mixed * scale * gain).astype(BF16)
    forth.start()
    for number in range(2, line.count):
        weights.step(number)

    def work(slot):
        rows = slot_rows(slot)
        normed = nffn_ref[rows, :]
        gate_up = dot(normed, wffn_ref[:, : 2 * hid])
        dhidden = dot(cot_all_ref[rows, :], wffn_ref[:, 2 * hid :]).astype(BF16).astype(F32)
        gate, up = gate_up[:, :hid], gate_up[:, hid:]
        sig = sigmoid(gate)
        silu = gate * sig
        dgate = dhidden * up * (sig * (1.0 + gate * (1.0 - sig)))
        hidden_ref[rows, :] = (silu * up).astype(BF16)
        dgu_ref[rows, :hid] = dgate.astype(BF16)
        dgu_ref[rows, hid:] = (dhidden * silu).astype(BF16)
        part[rows, :] = dot(dgu_ref[rows, :], wffn_ref[:, : 2 * hid], 1, 1).astype(BF16)

    def hand_over(mask):
        slot = place.slot(mask, True)
        work(slot)
        back.to_core(mask, part.at[slot_rows(slot)])

    work(place.slot(0))
    forth.relay()
    forth.core(0)
    hand_over(0)
    forth.near()
    forth.core(1)
    hand_over(1)
    forth.core(2)
    hand_over(2)
    work(place.slot(1))
    forth.far()
    work(place.slot(2))
    forth.core(3)
    hand_over(3)
    work(place.slot(3))
    forth.finish()

    def ready(mask):
        return part[slot_rows(place.slot(mask)), :].astype(F32)

    back.first(ready, dmixed_ref)

    columns = (pl.ds(0, 2 * hid), pl.ds(2 * hid, hid))
    line_sent = []

    def line_copy(piece, step):
        rows = pl.ds(pl.multiple_of((line.f + step) % line.count * share, share), share)
        return line.copy(
            dw_ref.at[rows, columns[piece]],
            arrived.at[step, :, columns[piece]],
            scratch[13].at[piece],
            step,
        )

    def send_piece(piece, left, right):
        quarter = dw_ref.shape[0] // 4
        for k in range(4):
            rows = slice(k * quarter, (k + 1) * quarter)
            dw_ref[rows, columns[piece]] = dot(left[:, rows], right[...], 0, 0).astype(BF16)
        for step in range(1, line.count):
            made = line_copy(piece, step)
            made.start()
            line_sent.append(made)

    send_piece(1, cot_all_ref, hidden_ref)
    back.second()
    send_piece(0, nffn_ref, dgu_ref)
    back.last(dmixed_ref)
    dnffn = dmixed_ref[...]
    mixed = mixed_ref[...]
    scale = norm_scale(mixed)
    spread = dnffn * gain
    pull = jnp.mean(spread * mixed, axis=1, keepdims=True)
    dgain_ref[...] = jnp.broadcast_to(
        jnp.sum(dnffn * mixed * scale, axis=0, keepdims=True), dgain_ref.shape
    )
    dmixed = cot_ref[...].astype(F32) + scale * (spread - mixed * (scale * scale * pull))
    dmixed_ref[...] = dmixed
    dm_ref[own, :] = dmixed.astype(BF16)
    home.start()

    def pull_back(slot):
        rows = slot_rows(slot)
        dag_ref[rows, :] = dot(dm_ref[rows, :], wout_ref[...]).astype(BF16)

    pull_back(place.slot(0))
    home.relay()
    home.core(0)
    pull_back(place.slot(0, True))
    home.near()
    pull_back(place.slot(1))
    pull_back(place.slot(2))
    home.far()
    pull_back(place.slot(3))
    for mask in (1, 2, 3):
        home.core(mask)
        pull_back(place.slot(mask, True))
    dout_ref[...] = dot(dm_ref[...], ag_ref[...], 0, 0).astype(BF16)
    down_all_ref[...] = wffn_ref[:, 2 * hid :]
    for piece in (1, 0):
        sums = dw_ref[mine, columns[piece]].astype(F32)
        for step in range(1, line.count):
            line_copy(piece, step).wait_recv()
            sums = sums + arrived[step, :, columns[piece]].astype(F32)
        ffn_ref[:, columns[piece]] = sums.astype(BF16)
    for made in line_sent:
        made.wait_send()
    home.finish()
    weights.finish()


def middle(ag, wout, weights, x_own, cot_own, cot_all, gain):
    count, model = cot_all.shape
    hid = weights[0].shape[1] // lax.axis_size("context")
    columns = ag.shape[1]
    vmem = pl.BlockSpec(memory_space=pltpu.VMEM)
    hbm = pl.BlockSpec(memory_space=pl.ANY)
    shape = jax.ShapeDtypeStruct
    return pl.pallas_call(
        middle_kernel,
        out_shape=(
            shape((count, hid), BF16),
            shape((count, columns), BF16),
            shape((ROWS, model), F32),
            shape((ROWS, model), F32),
            shape((8, model), F32),
            shape((model, hid), BF16),
            shape((weights[0].shape[0], 3 * hid), BF16),
            shape((model, columns), BF16),
        ),
        in_specs=[vmem] * 6 + [hbm] * 3,
        out_specs=(vmem,) * 8,
        scratch_shapes=[
            pltpu.VMEM((ROWS, model), BF16),
            pltpu.VMEM((ROWS, model), BF16),
            pltpu.VMEM((count, model), BF16),
            pltpu.VMEM((count, model), BF16),
            pltpu.VMEM((count, 2 * hid), BF16),
            pltpu.VMEM((count, model), BF16),
            pltpu.VMEM((model, 3 * hid), BF16),
            pltpu.VMEM((lax.axis_size("fsdp"), weights[0].shape[0], 3 * hid), BF16),
            pltpu.VMEM((count, model), BF16),
            pltpu.VMEM((model, 3 * hid), BF16),
        ]
        + scatter_scratch(model, F32)
        + scatter_scratch(model, F32)
        + [pltpu.SemaphoreType.DMA((2, GATHER_SEMS))] * 2
        + [line_sems(lax.axis_size("fsdp")), pltpu.SemaphoreType.DMA((2, 2, lax.axis_size("fsdp"))), pltpu.SemaphoreType.DMA((3,))],
        compiler_params=pltpu.CompilerParams(
            collective_id=1, has_side_effects=True, vmem_limit_bytes=60 << 20
        ),
        cost_estimate=pl.CostEstimate(
            flops=20 * count * model * hid, bytes_accessed=40 << 20, transcendentals=count * hid
        ),
    )(ag, wout, *weights, gain.reshape(1, -1), x_own, cot_own, cot_all)


BACK_INPUTS = 5
EARLY = 384


def closing_kernel(
    order_ref, dag_ref, kv_ref, kv_t_ref, heads_ref, taps_ref, dmixed_ref, gain_ref, ffn_ref,
    dgain_ref, dout_ref, table_hbm, y_hbm, conv_hbm, kept_hbm, states_hbm, normed_t_hbm, w_hbm,
    hidden_hbm, down_hbm, mixed_hbm, tokens_hbm,
    grad_ref, out_ref, early_ref, bc_ref, last_ref, mids_ref, outs_ref, small_ref,
    table, y, conv, kept, states, normed_t, w, hidden, down, x_ref,
    dnorm, early_du, dw_sum, dw, arrived, arrived_out, total, out_total, part, out_part, bc_out, bc_in, small_in,
    stats, dext, dpos, dstate, state_out, dkey_t, dvalue_t, *scratch,
):
    place = Place()
    line = Line()
    back = Scatter(place, scratch[0:5])
    final = Scatter(place, scratch[5:10])
    share = ffn_ref.shape[0]
    last_all = Gather(place, last_ref, scratch[10], share, False)
    early_all = Gather(place, early_ref, scratch[20], share, False)
    bc_all = Gather(place, bc_ref, scratch[21], share, False)
    mid_all = Gather(place, mids_ref, scratch[11], share, False)
    out_all = Gather(place, outs_ref, scratch[12], share, False)
    small_rows = small_in.shape[1]
    small_all = Gather(place, small_ref, scratch[13], small_rows)
    line_sems_, small_sems, out_sems, pair_sems, load_sems, block_sems = scratch[14:20]
    pair = Wire(place, pair_sems)
    greetings = place.hello(line)
    sent = []
    loads = [
        pltpu.make_async_copy(source, target, load_sems.at[k])
        for k, (source, target) in enumerate(
            (
                (hidden_hbm, hidden), (down_hbm, down), (normed_t_hbm, normed_t), (w_hbm, w),
                (mixed_hbm, out_total),
                (tokens_hbm.at[pl.ds(pl.multiple_of(place.t * ROWS, ROWS), ROWS)], x_ref),
            )
        )
    ]
    blocks = dnorm.shape[0] // ROWS
    streams = ((table_hbm, table), (y_hbm, y), (conv_hbm, conv), (kept_hbm, kept), (states_hbm, states))

    early_lanes = (pl.ds(0, 256), pl.ds(0, 512), pl.ds(0, 256), pl.ds(512, 256), None)
    late_lanes = (pl.ds(128, 128), pl.ds(0, 512), pl.ds(0, 512), pl.ds(0, 768), pl.ds(0, STATE))

    def fetch(block, buffer, late):
        copies = []
        for k, (source, target) in enumerate(streams):
            lanes = late_lanes[k] if late else early_lanes[k]
            if lanes is None:
                continue
            size = target.shape[1]
            begin = pl.multiple_of(block * size, size)
            copies.append(
                pltpu.make_async_copy(
                    source.at[pl.ds(begin, size), lanes],
                    target.at[buffer, :, lanes],
                    block_sems.at[buffer, k],
                )
            )
        return copies

    for made in fetch(blocks - 1, 0, False) + loads:
        made.start()
    mids_ref[pl.ds(pl.multiple_of(place.c * share, share), share), :] = ffn_ref[...]
    width = dext.shape[1]
    dext[ROWS : ROWS + 8, :] = jnp.zeros((8, width), F32)
    dpos[ROWS : ROWS + 8, :] = jnp.full((8, dpos.shape[1]), -1.0, F32)
    for ref in (dstate, state_out, dkey_t, dvalue_t, stats, dw_sum):
        ref[...] = jnp.zeros(ref.shape, F32)
    def out_block(mask, sibling=False):
        return dot(hidden[slot_rows(place.slot(mask, sibling)), :], down[...], 1, 1)

    def out_rows(mask):
        return out_block(mask) + out_total[...] if mask == 0 else out_block(mask)

    here = pl.ds(pl.multiple_of(place.c * share, share), share)
    own = pl.ds(pl.multiple_of(line.f * share, share), share)
    half = pl.ds(pl.multiple_of(place.t * ROWS, ROWS), ROWS)

    def my_half(ref):
        return lambda: ref.at[pl.ds(pl.multiple_of(place.t * ROWS, ROWS), ROWS)]

    def collect_out():
        sums = dout_ref[own, :].astype(F32)
        for step in range(1, line.count):
            line.copy(arrived_out.at[step - 1], arrived_out.at[step - 1], out_sems, step).wait_recv()
            sums = sums + arrived_out[step - 1].astype(F32)
        outs_ref[here, :] = sums.astype(BF16)
        out_all.start()

    def finish_out():
        final.last(out_total)
        out_ref[half, :] = out_total[...].astype(BF16)
        pair.send(my_half(out_ref), my_half(out_ref), 1, 4)

    lane = lax.broadcasted_iota(jnp.int32, (8, blocks), 1)[0:1]
    order = order_ref[...]

    def blend(source, marks):
        marks = [jnp.where(one, 1.0, 0.0).astype(BF16) for one in marks]
        found = source[0:ROWS, :] * marks[0]
        for k in range(1, blocks):
            found = found + source[k * ROWS : (k + 1) * ROWS, :] * marks[k]
        return found

    def from_slots(source, block):
        return blend(source, [order[:, k : k + 1] == block for k in range(blocks)])

    def from_stream(source, slot):
        dealt = jnp.sum(jnp.where(lane == slot, order, 0), axis=1, keepdims=True)
        return blend(source, [dealt == k for k in range(blocks)])

    def prefetch(block, buffer, late):
        for made in fetch(block, buffer, late):
            made.start()

    def await_block(block, buffer, late):
        for made in fetch(block, buffer, late):
            made.wait()

    def happen(number, events):
        for when, actions in events.items():

            @pl.when(number == when)
            def _():
                for action in actions:
                    action()

    def early_turn(number, carry):
        block = blocks - 1 - number
        buffer = number % 2
        await_block(block, buffer, False)

        @pl.when(number < blocks - 1)
        def _():
            prefetch(block - 1, 1 - buffer, False)

        @pl.when(number == blocks - 1)
        def _():
            prefetch(blocks - 1, 1 - buffer, True)

        grads = attention_backward(
            block, from_slots(dag_ref, block), table.at[buffer], heads_ref, y.at[buffer], conv.at[buffer],
            kept.at[buffer], kv_ref, kv_t_ref, dkey_t, dvalue_t,
        )
        early_du[slot_rows(block), :] = grads
        dw_sum[:, :EARLY] += dot(normed_t[:, slot_rows(block)], grads)
        happen(number, {3: (lambda: final.first(out_rows, out_total),), 6: (mid_all.relay,)})
        return carry

    def late_turn(number, carry):
        block = blocks - 1 - number
        buffer = number % 2
        await_block(block, buffer, True)

        @pl.when(number < blocks - 1)
        def _():
            prefetch(block - 1, 1 - buffer, True)

        grads = recurrence_backward(
            from_slots(dag_ref, block), table.at[buffer], heads_ref, taps_ref, y.at[buffer],
            conv.at[buffer], kept.at[buffer], states.at[buffer], state_out, stats, dext, dpos, dstate,
        )
        whole = jnp.concatenate([early_du[slot_rows(block), :], grads], axis=1)
        dnorm[slot_rows(block), :] = dot(whole, w[...], 1, 1).astype(BF16)
        dw_sum[:, EARLY:] += dot(normed_t[:, slot_rows(block)], grads)
        happen(
            number,
            {
                1: (mid_all.near,),
                3: (collect_out, mid_all.far),
                5: (final.second,),
                6: (out_all.relay,),
            },
        )
        return carry

    columns = (pl.ds(0, EARLY), pl.ds(EARLY + 256, 256), pl.ds(EARLY, 256))

    def line_copy(piece, step):
        rows = pl.ds(pl.multiple_of((line.f + step) % line.count * share, share), share)
        return line.copy(
            dw.at[rows, columns[piece]], arrived.at[step - 1, :, columns[piece]], line_sems_.at[piece], step
        )

    def send_piece(piece):
        dw[:, columns[piece]] = dw_sum[:, columns[piece]].astype(BF16)
        for step in range(1, line.count):
            made = line_copy(piece, step)
            made.start()
            sent.append(made)

    def collected(piece):
        sums = dw[own, columns[piece]].astype(F32)
        for step in range(1, line.count):
            line_copy(piece, step).wait_recv()
            sums = sums + arrived[step - 1, :, columns[piece]].astype(F32)
        return sums.astype(BF16)

    for made in loads:
        made.wait()
    early_turn(0, 0)
    pl.semaphore_wait(pltpu.get_barrier_semaphore(), greetings)
    for step in range(1, line.count):
        rows = pl.ds(pl.multiple_of((line.f + step) % line.count * share, share), share)
        made = line.copy(dout_ref.at[rows], arrived_out.at[step - 1], out_sems, step)
        made.start()
        sent.append(made)
    for k, mask in enumerate(SCATTER_ORDER):
        out_part[k] = out_block(mask, True).astype(BF16)
        final.to_core(mask, out_part.at[k])
    mid_all.start()
    lax.fori_loop(1, blocks, early_turn, 0)
    send_piece(0)
    lax.fori_loop(0, blocks, late_turn, 0)
    send_piece(1)
    send_piece(2)

    def block_of(mask, sibling=False):
        return from_stream(dnorm, place.slot(mask, sibling))

    for k, mask in enumerate(SCATTER_ORDER):
        part[k] = block_of(mask, True)
        back.to_core(mask, part.at[k])
    back.first(lambda mask: block_of(mask).astype(F32), total)
    out_all.near()
    finish_out()
    out_all.far()
    early_ref[here, :] = collected(0)
    back.second()
    early_all.start()
    bc_out[...] = collected(1)
    pair.send(bc_out, bc_in, 2, 4)
    back.last(total)
    early_all.relay()
    dnormed = total[...]
    x = x_ref[...].astype(F32)
    gain = gain_ref[...]
    scale = norm_scale(x)
    spread = dnormed * gain
    pull = jnp.mean(spread * x, axis=1, keepdims=True)
    grad = dmixed_ref[...] + scale * (spread - x * (scale * scale * pull))
    grad_ref[half, :] = grad.astype(BF16)
    pair.send(grad_ref.at[half], grad_ref.at[half], 0, 4)
    small_in[0] = jnp.zeros(small_in.shape[1:], F32)
    small_in[0, 0:1, :] = jnp.sum(dnormed * x * scale, axis=0, keepdims=True)
    small_in[0, 1:2, :] = dgain_ref[0:1, :]
    small_in[0, 8:16, :width] = stats[...]
    for step in range(1, line.count):
        made = line.copy(small_in.at[0], small_in.at[step], small_sems, step)
        made.start()
        sent.append(made)
    pair.arrive(bc_in, 2, 4)
    bc_ref[here, :] = (bc_out[...].astype(F32) + bc_in[...].astype(F32)).astype(BF16)
    bc_all.start()
    early_all.near()
    last_ref[here, :] = collected(2)
    last_all.start()
    bc_all.relay()
    for step in range(1, line.count):
        line.copy(small_in.at[0], small_in.at[step], small_sems, step).wait_recv()
    summed = small_in[line.f % line.count]
    for other in range(1, line.count):
        summed = summed + small_in[(line.f + line.count - other) % line.count]
    mine = pl.ds(pl.multiple_of(place.slot(0) * small_rows, small_rows), small_rows)
    small_ref[mine, :] = summed
    small_all.start()
    early_all.far()
    last_all.relay()
    small_all.relay()
    small_all.near()
    small_all.far()
    bc_all.near()
    bc_all.far()
    last_all.near()
    last_all.far()
    for mask in range(4):
        small_all.core(mask)
    other = pl.ds(pl.multiple_of((1 - place.t) * ROWS, ROWS), ROWS)
    pair.arrive(grad_ref.at[other], 0, 4)
    pair.arrive(out_ref.at[other], 1, 4)
    for made in sent:
        made.wait_send()
    pair.finish()
    mid_all.finish()
    out_all.finish()
    small_all.finish()
    last_all.finish()
    early_all.finish()
    bc_all.finish()


def closing(small_inputs, streams, loads, fsdp):
    ffn, dout = small_inputs[8], small_inputs[10]
    normed_t, w, hidden, down, _, _ = loads
    model, count = normed_t.shape
    share = ffn.shape[0]
    columns = w.shape[1]
    chips = lax.axis_size("context")
    blocks = count // ROWS
    vmem = pl.BlockSpec(memory_space=pltpu.VMEM)
    hbm = pl.BlockSpec(memory_space=pl.ANY)
    shape = jax.ShapeDtypeStruct
    dma = pltpu.SemaphoreType.DMA
    space = pltpu.VMEM
    inner = streams[4].shape[0] // blocks
    return pl.pallas_call(
        closing_kernel,
        out_shape=(
            shape((2 * ROWS, model), BF16),
            shape((2 * ROWS, model), BF16),
            shape((chips * share, EARLY), BF16),
            shape((chips * share, 256), BF16),
            shape((chips * share, 256), BF16),
            shape((chips * share, ffn.shape[1]), BF16),
            shape((chips * share, dout.shape[1]), BF16),
            shape((2 * chips * 16, model), F32),
        ),
        in_specs=[vmem] * 11 + [hbm] * 11,
        out_specs=(vmem,) * 8,
        scratch_shapes=[space((2, one.shape[0] // blocks, one.shape[1]), one.dtype) for one in streams]
        + [space(one.shape, one.dtype) for one in loads[:4]]
        + [space((ROWS, model), BF16)]
        + [
            space((count, model), BF16),
            space((count, EARLY), BF16),
            space((model, columns), F32),
            space((model, columns), BF16),
            space((fsdp - 1, share, columns), BF16),
            space((fsdp - 1, share, dout.shape[1]), BF16),
            space((ROWS, model), F32),
            space((ROWS, model), F32),
            space((4, ROWS, model), BF16),
            space((4, ROWS, model), BF16),
            space((share, 256), BF16),
            space((share, 256), BF16),
            space((fsdp, 16, model), F32),
            space((8, 512), F32),
            space((ROWS + 8, 512), F32),
            space((ROWS + 8, 128), F32),
            space((inner, STATE), F32),
            space((inner, STATE), F32),
            space((HEAD_DIM, count), F32),
            space((HEAD_DIM, count), F32),
        ]
        + scatter_scratch(model)
        + scatter_scratch(model)
        + [dma((2, GATHER_SEMS))] * 4
        + [dma((3, 2, fsdp)), dma((2, fsdp)), dma((2, fsdp)), dma((2, 3)), dma((6,)), dma((2, BACK_INPUTS)), dma((2, GATHER_SEMS)), dma((2, GATHER_SEMS))],
        compiler_params=pltpu.CompilerParams(
            collective_id=2, has_side_effects=True, vmem_limit_bytes=61 << 20
        ),
        cost_estimate=pl.CostEstimate(
            flops=4 * count * model * columns, bytes_accessed=30 << 20, transcendentals=0
        ),
    )(*small_inputs, *streams, *loads)


def assemble_kernel(
    early_ref, bcs_ref, late_ref, mid_ref, outs_ref, dx_ref, out_in_ref, small_ref, steps_ref,
    out_ref, grad_ref, query_ref, keyval_ref, attn_ref, gate_ref, x_ref, bc_ref, step_ref, ssm_ref,
    ffn_gate_ref, ffn_up_ref, ffn_down_ref, gain_ref, gain_ffn_ref, conv_x_ref, conv_bc_ref,
    bias_ref, decay_ref, skip_ref,
):
    chips = late_ref.shape[0]
    heads = step_ref.shape[0] // chips
    inner = heads * SSM_DIM
    hid = ffn_gate_ref.shape[1] // chips

    def spread(source, begin, width):
        return jnp.concatenate(
            [source[k, :, begin : begin + width].astype(F32) for k in range(chips)], axis=1
        )

    def summed(source, begin, end):
        total = source[0, :, begin:end].astype(F32)
        for k in range(1, chips):
            total = total + source[k, :, begin:end].astype(F32)
        return total

    out_ref[...] = out_in_ref[...]
    grad_ref[...] = dx_ref[...]
    gate_ref[...] = spread(early_ref, 0, inner)
    query_ref[...] = spread(early_ref, inner, HEAD_DIM)
    keyval_ref[...] = summed(early_ref, 256, 384)
    x_ref[...] = spread(late_ref, 0, inner)
    bc_ref[...] = summed(bcs_ref, 0, 256)
    ffn_gate_ref[...] = spread(mid_ref, 0, hid)
    ffn_up_ref[...] = spread(mid_ref, hid, hid)
    ffn_down_ref[...] = spread(mid_ref, 2 * hid, hid)
    ssm_ref[...] = spread(outs_ref, 0, inner)
    attn_ref[...] = spread(outs_ref, inner, HEAD_DIM)

    @pl.when(pl.program_id(0) == 0)
    def _():
        step_ref[...] = spread(steps_ref, inner, heads).T
        everywhere = small_ref[0:16, :]
        for k in range(1, small_ref.shape[0] // 16):
            everywhere = everywhere + small_ref[16 * k : 16 * k + 16, :]
        gain_ref[...] = everywhere[0:1]
        gain_ffn_ref[...] = everywhere[1:2]
        conv_bc_ref[...] = everywhere[8 : 8 + CONV, 256:512]
        core = lax.axis_index("tensor")
        own = [
            small_ref[pl.ds(pl.multiple_of((2 * k + core) * 16, 16), 16), :] for k in range(chips)
        ]
        conv_x_ref[...] = jnp.concatenate([one[8 : 8 + CONV, :inner] for one in own], axis=1)
        for row, target in ((12, skip_ref), (13, bias_ref), (14, decay_ref)):
            target[...] = jnp.concatenate(
                [
                    jnp.sum(
                        one[row : row + 1, h * SSM_DIM : (h + 1) * SSM_DIM], axis=1, keepdims=True
                    )
                    for one in own
                    for h in range(heads)
                ],
                axis=1,
            )


def assemble(early, bcs, last, mid, outs, dx, out, small, widths, heads):
    chips = lax.axis_size("context")
    share = last.shape[0] // chips
    turns = 2
    rows = share // turns
    shape = jax.ShapeDtypeStruct
    block = lambda height, width: pl.BlockSpec((height, width), lambda i: (i, 0))
    fixed = lambda height, width: pl.BlockSpec((height, width), lambda i: (0, 0))
    slab = lambda width: pl.BlockSpec((chips, rows, width), lambda i: (0, i, 0))
    token_rows = dx.shape[0] // turns
    model = dx.shape[1]
    tiny = [
        (1, model), (1, model), (CONV, heads * SSM_DIM), (CONV, 2 * STATE), (1, heads), (1, heads),
        (1, heads),
    ]
    return pl.pallas_call(
        assemble_kernel,
        grid=(turns,),
        out_shape=(shape(out.shape, BF16), shape(dx.shape, BF16))
        + tuple(shape((share, w) if w > heads else (w, share), F32) for w in widths)
        + tuple(shape(one, F32) for one in tiny),
        in_specs=[
            slab(early.shape[1]), slab(bcs.shape[1]), slab(last.shape[1]), slab(mid.shape[1]), slab(outs.shape[1]),
            block(token_rows, model), block(token_rows, model), fixed(*small.shape),
            pl.BlockSpec((chips, share, last.shape[1]), lambda i: (0, 0, 0)),
        ],
        out_specs=(block(token_rows, model), block(token_rows, model))
        + tuple(block(rows, w) if w > heads else fixed(w, share) for w in widths)
        + tuple(fixed(*one) for one in tiny),
        compiler_params=pltpu.CompilerParams(vmem_limit_bytes=60 << 20),
    )(*[one.reshape(chips, share, -1) for one in (early, bcs, last, mid, outs)], dx, out, small,
      last.reshape(chips, share, -1))


def per_device(
    tokens, segments, deal, gain_mix, w_query, w_keyval, w_attn_out, w_gate_z, w_in_x, w_bc, w_step,
    conv_x, conv_bc, step_bias, decay_log, skip, w_ssm_out, gain_ffn, w_ffn_gate, w_ffn_up,
    w_ffn_down, cotangent,
):
    normed_t, u, w_all, wout_all, cot_all, table, head_rows, taps = opening(
        tokens,
        cotangent,
        (w_in_x, w_query, w_bc, w_gate_z, w_keyval, w_step.T, w_ssm_out, w_attn_out),
        gain_mix,
        segments,
        (conv_x, conv_bc),
        (step_bias, decay_log, skip),
    )
    ag, y, conv, states, keyval, kept, normed_t, keyval_t = mixer_forward(u, normed_t, table, head_rows, taps, deal[0])
    hidden, dag, mixed, dmixed, dgain, down, dffn, dout = middle(
        ag, wout_all, (w_ffn_gate, w_ffn_up, w_ffn_down), tokens, cotangent, cot_all, gain_ffn
    )
    dx, out, early, bcs, last, mids, outs, small = closing(
        (
            deal, dag, keyval, keyval_t, head_rows, taps, dmixed, gain_mix.reshape(1, -1), dffn,
            dgain, dout,
        ),
        (table, y, conv, kept, states),
        (normed_t, w_all, hidden, down, mixed, tokens),
        lax.axis_size("fsdp"),
    )
    weights = (
        w_query, w_keyval, w_attn_out, w_gate_z, w_in_x, w_bc, w_step, w_ssm_out, w_ffn_gate,
        w_ffn_up, w_ffn_down,
    )
    done = assemble(early, bcs, last, mids, outs, dx, out, small, [w.shape[1] for w in weights], skip.shape[0])
    grads = done[2:13]
    gain, gain_two, taps_x, taps_bc, bias, decay, skips = done[13:]
    return (
        done[0],
        done[1],
        gain.reshape(-1),
        *grads[:6],
        grads[6].T,
        taps_x,
        taps_bc,
        bias.reshape(-1),
        decay.reshape(-1),
        skips.reshape(-1),
        grads[7],
        gain_two.reshape(-1),
        *grads[8:],
    )


def solution(mesh):
    in_specs = (
        P(("fsdp", "context"), None),
        P("fsdp", None),
        P("fsdp", None),
        P(),
        P("fsdp", "tensor"),
        P("fsdp", "tensor"),
        P("fsdp", "tensor"),
        P("fsdp", "tensor"),
        P("fsdp", "tensor"),
        P("fsdp", None),
        P("fsdp", "tensor"),
        P(None, "tensor"),
        P(),
        P("tensor"),
        P("tensor"),
        P("tensor"),
        P("fsdp", "tensor"),
        P(),
        P("fsdp", "tensor"),
        P("fsdp", "tensor"),
        P("fsdp", "tensor"),
        P(("fsdp", "context"), None),
    )
    out_specs = (
        P(("fsdp", "context"), None),
        P(("fsdp", "context"), None),
        P(),
        P("fsdp", "tensor"),
        P("fsdp", "tensor"),
        P("fsdp", "tensor"),
        P("fsdp", "tensor"),
        P("fsdp", "tensor"),
        P("fsdp", None),
        P("fsdp", "tensor"),
        P(None, "tensor"),
        P(),
        P("tensor"),
        P("tensor"),
        P("tensor"),
        P("fsdp", "tensor"),
        P(),
        P("fsdp", "tensor"),
        P("fsdp", "tensor"),
        P("fsdp", "tensor"),
    )
    return jax.shard_map(
        per_device, mesh=mesh, in_specs=in_specs, out_specs=out_specs, check_vma=False
    )
```

```python
import functools
import math

import jax
import jax.numpy as jnp
from jax import lax
from jax.experimental import pallas as pl
from jax.experimental.pallas import tpu as pltpu
from jax.sharding import PartitionSpec as P

HEAD_DIM = 64
SSM_DIM = 64
STATE = 128
CONV = 4
HALF = 256
WINDOW = 4

epsilon = 1e-05
masked = -1e30
F32 = jnp.float32
BF16 = jnp.bfloat16
exact = lax.Precision.HIGHEST


def dot(left, right, left_dim=1, right_dim=0, precision=None):
    return lax.dot_general(
        left,
        right,
        (((left_dim,), (right_dim,)), ((), ())),
        precision=precision,
        preferred_element_type=F32,
    )


def exact_sums(ones, values, right_dim=0):
    high = values.astype(BF16)
    rest = values - high.astype(F32)
    middle = rest.astype(BF16)
    low = (rest - middle.astype(F32)).astype(BF16)
    return sum(dot(ones, one, 1, right_dim) for one in (low, middle, high))


def sigmoid(v):
    return 1.0 / (1.0 + jnp.exp(-v))


def softplus(v):
    return jnp.maximum(v, 0.0) + jnp.log1p(jnp.exp(-jnp.abs(v)))


def swap_halves(v):
    half = v.shape[1] // 2
    return jnp.concatenate([v[:, half:], v[:, :half]], axis=1)


def iotas(rows, columns):
    return (
        lax.broadcasted_iota(jnp.int32, (rows, columns), 0),
        lax.broadcasted_iota(jnp.int32, (rows, columns), 1),
    )


def state_scale(last_row, carry_last, heads):
    pieces = [
        jnp.broadcast_to(last_row[:, h * SSM_DIM : h * SSM_DIM + 1], (SSM_DIM, STATE))
        for h in range(heads)
    ]
    return jnp.exp(jnp.concatenate(pieces, axis=0)) * carry_last


def block_decays(step_raw, heads_ref, lane_pos, heads):
    rows = step_raw.shape[0]
    inner = heads * SSM_DIM
    raw = step_raw + heads_ref[0:1, :inner]
    step = softplus(raw)
    rate = step * jnp.exp(heads_ref[1:2, :inner])
    row, col = iotas(rows, rows)
    lower = jnp.where(col <= row, 1.0, 0.0).astype(BF16)
    totals = exact_sums(lower, -rate)
    last_row = totals[rows - 1 : rows]
    pos_last = lane_pos[rows - 1 : rows, 0:1]
    local = lax.broadcasted_iota(jnp.int32, (rows, 1), 0).astype(F32)
    carry_on = (lane_pos[:, 0:1] > local).astype(F32)
    keep_last = (local >= (rows - 1) - pos_last).astype(F32)
    carry_last = (pos_last > rows - 1).astype(F32)
    factor = jnp.exp(totals) * carry_on
    tails = jnp.exp(last_row - totals) * keep_last
    return raw, step, rate, totals, last_row, carry_last, factor, tails


def local_mask(lane_pos, rows):
    row, col = iotas(rows, rows)
    gap = (row - col).astype(F32)
    return (gap >= 0) & (gap <= lane_pos[:, 0:1])


def key_window(block):
    start = jnp.maximum(block - WINDOW, 0)
    return start, (block - start) * HALF


def window_mask(lane_pos, offset, rows, keys):
    last = (lax.broadcasted_iota(jnp.int32, (rows, 1), 0) + offset).astype(F32)
    col = lax.broadcasted_iota(jnp.int32, (8, keys), 1)[0:1].astype(F32)
    return (col <= last) & (col >= last - lane_pos[:, 0:1])


def head_decay(totals, totals_t, h, allowed):
    gap = totals[:, h * SSM_DIM : h * SSM_DIM + 1] - totals_t[h * SSM_DIM : h * SSM_DIM + 1, :]
    return jnp.exp(jnp.where(allowed, gap, masked))


def mixer_forward_kernel(
    order_ref, u_ref, normed_ref, table_ref, heads_ref, taps_ref, ag_ref, y_ref, conv_ref, state_in_ref,
    kv_ref, kept_ref, ordered_ref, kv_t_ref, ext, state, keys_t, values, found,
):
    block = pl.program_id(0)
    heads = state.shape[0] // SSM_DIM
    inner = heads * SSM_DIM
    width = ext.shape[1]
    rows = u_ref.shape[0]

    @pl.when(block == 0)
    def _():
        ext[0:8, :] = jnp.zeros((8, width), F32)
        state[...] = jnp.zeros(state.shape, F32)
        keys_t[...] = jnp.zeros(keys_t.shape, BF16)
        values[...] = jnp.zeros(values.shape, BF16)

    lane_pos = table_ref[:, 128:256]
    cosine = table_ref[:, 0:64]
    sine = table_ref[:, 64:128]
    q_at = inner
    u = u_ref[:, :width].astype(F32)
    ext[8 : 8 + rows, :] = u
    conv = u * taps_ref[CONV - 1 : CONV, :]
    for back in range(1, CONV):
        reach = lane_pos[:, 0:1] >= back
        shifted = ext[8 - back : 8 - back + rows, :]
        conv = conv + jnp.where(reach, shifted, 0.0) * taps_ref[CONV - 1 - back : CONV - back, :]
    ext[0:8, :] = u[rows - 8 : rows]
    act = conv * sigmoid(conv)
    ssm_x = act[:, :inner].astype(BF16)
    ssm_b = act[:, 256:384].astype(BF16)
    ssm_c = act[:, 384:512].astype(BF16)
    conv_ref[:, 0:256] = conv[:, 0:256]
    conv_ref[:, 256:512] = conv[:, 256:512]
    query = u[:, q_at : q_at + HEAD_DIM]
    query = (query * cosine + swap_halves(query) * sine).astype(BF16)
    conv_ref[:, q_at : q_at + HEAD_DIM] = query.astype(F32)
    key = u_ref[:, 512 + inner : 512 + inner + HEAD_DIM].astype(F32)
    key = key * cosine + swap_halves(key) * sine
    value = u_ref[:, 768 + inner : 768 + inner + HEAD_DIM].astype(F32)
    pair = jnp.concatenate([key, value], axis=1).astype(BF16)
    pair_t = jnp.concatenate([key, value], axis=1).T.astype(BF16)
    kv_ref[...] = pair
    kv_t_ref[...] = pair_t
    here = pl.ds(pl.multiple_of(block * rows, rows), rows)
    values[here, :] = value.astype(BF16)
    keys_t[:, here] = pair_t[:HEAD_DIM]
    query_low = query * 0.125

    def attend(first, offset, span):
        begin = pl.multiple_of(first * rows, rows)
        scores = dot(query_low, keys_t[:, pl.ds(begin, span)])
        scores = jnp.where(window_mask(lane_pos, offset, rows, span), scores, masked)
        highest = jnp.max(scores, axis=1, keepdims=True)
        weights = jnp.exp(scores - highest)
        total = jnp.sum(weights, axis=1, keepdims=True)
        probs = (weights * (1.0 / total)).astype(BF16)
        found[:, :HEAD_DIM] = dot(probs, values[pl.ds(begin, span), :])
        found[:, HEAD_DIM:] = jnp.broadcast_to(highest + jnp.log(total), (rows, HEAD_DIM))

    @pl.when(block < 2)
    def _():
        attend(0, block * rows, 2 * HALF)

    @pl.when((block >= 2) & (block < WINDOW))
    def _():
        attend(0, block * rows, WINDOW * HALF)

    @pl.when(block >= WINDOW)
    def _():
        attend(block - WINDOW, WINDOW * rows, (WINDOW + 1) * HALF)

    attended = found[:, :HEAD_DIM]
    _, step, _, totals, last_row, carry_last, factor, tails = block_decays(
        u_ref[:, 768 : 768 + inner].astype(F32), heads_ref, lane_pos, heads
    )
    totals_t = totals.T
    allowed = local_mask(lane_pos, rows)
    cross = dot(ssm_c, ssm_b, 1, 1)
    x_f = ssm_x.astype(F32)
    stepped = step * x_f
    stepped_low = stepped.astype(BF16)
    parts = []
    for h in range(heads):
        lanes = slice(h * SSM_DIM, (h + 1) * SSM_DIM)
        mix = (head_decay(totals, totals_t, h, allowed) * cross).astype(BF16)
        parts.append(dot(mix, stepped_low[:, lanes]))
    held = state[...]
    state_in_ref[...] = held
    y_pure = jnp.concatenate(parts, axis=1) + factor * dot(ssm_c, held.astype(BF16), 1, 1)
    tailed = (tails * stepped_low.astype(F32)).astype(BF16)
    state[...] = state_scale(last_row, carry_last, heads) * held + dot(tailed, ssm_b, 0, 0)
    y_ref[:, 0:256] = jnp.concatenate(
        [y_pure, found[:, HEAD_DIM:]], axis=1
    )
    y_ref[:, 256:512] = jnp.concatenate([u_ref[:, 768 : 768 + inner], attended], axis=1)
    ordered_ref[...] = normed_ref[...]
    kept_ref[...] = u_ref[:, 0:768].astype(BF16)
    y_full = y_pure + heads_ref[2:3, :inner] * x_f
    gate = u_ref[:, 512 : 512 + inner].astype(F32)
    gated = y_full * (gate * sigmoid(gate))
    ag_ref[...] = jnp.concatenate([gated, attended], axis=1).astype(BF16)


def attention_backward(
    block, dag, table_ref, heads_ref, y_ref, conv_ref, kept_ref, kv_ref, kv_t_ref, dkey_t, dvalue_t,
):
    inner = dag.shape[1] - HEAD_DIM
    rows = dag.shape[0]
    lane_pos = table_ref[:, 128:256]
    cosine = table_ref[:, 0:64]
    sine = table_ref[:, 64:128]
    first, offset = key_window(block)
    span = (WINDOW + 1) * HALF
    begin = pl.multiple_of(first * rows, rows)
    keys = kv_ref[pl.ds(begin, span), :HEAD_DIM]
    keys_t = kv_t_ref[:HEAD_DIM, pl.ds(begin, span)]
    values_t = kv_t_ref[HEAD_DIM:, pl.ds(begin, span)]
    query = conv_ref[:, inner : inner + HEAD_DIM] * 0.125
    query_low = query.astype(BF16)
    datt = dag[:, inner : inner + HEAD_DIM]
    datt_f = datt.astype(F32)
    lse = y_ref[:, inner : inner + 1]
    scores = dot(query_low, keys_t)
    allowed_all = window_mask(lane_pos, offset, rows, span)
    probs = jnp.exp(jnp.where(allowed_all, scores, masked) - lse)
    inward = jnp.sum(datt_f * y_ref[:, 256 + inner : 256 + inner + HEAD_DIM], axis=1, keepdims=True)
    dscores = (probs * (dot(datt, values_t) - inward)).astype(BF16)
    dquery = dot(dscores, keys) * 0.125
    dkey_t[:, pl.ds(begin, span)] += dot(query.T.astype(BF16), dscores)
    dvalue_t[:, pl.ds(begin, span)] += dot(datt_f.T.astype(BF16), probs.astype(BF16))
    here = pl.ds(pl.multiple_of(block * rows, rows), rows)
    dkey = dkey_t[:, here].T
    dvalue = dvalue_t[:, here].T
    dquery = dquery * cosine - swap_halves(dquery) * sine
    dkey = dkey * cosine - swap_halves(dkey) * sine
    conv = conv_ref[:, :inner]
    ssm_x = (conv * sigmoid(conv)).astype(BF16).astype(F32)
    gate = kept_ref[:, 512 : 512 + inner].astype(F32)
    sig = sigmoid(gate)
    dgated = dag[:, :inner].astype(F32)
    y_full = y_ref[:, :inner] + heads_ref[2:3, :inner] * ssm_x
    dgate = dgated * y_full * (sig * (1.0 + gate * (1.0 - sig)))
    return jnp.concatenate([dgate, dquery, dkey, dvalue], axis=1).astype(BF16)


def recurrence_backward(
    dag, table_ref, heads_ref, taps_ref, y_ref, conv_ref, kept_ref, state_in_ref, state_out, stats_ref,
    dext, dpos, dstate,
):
    heads = dstate.shape[0] // SSM_DIM
    inner = heads * SSM_DIM
    rows = dag.shape[0]
    lane_pos = table_ref[:, 128:256]
    conv = conv_ref[...]
    gate_conv = sigmoid(conv)
    act = conv * gate_conv
    dact = gate_conv * (1.0 + conv * (1.0 - gate_conv))
    ssm_x = act[:, :inner].astype(BF16)
    ssm_b = act[:, 256:384].astype(BF16)
    ssm_c = act[:, 384:512].astype(BF16)
    x_f = ssm_x.astype(F32)
    raw, step, rate, totals, last_row, carry_last, factor, tails = block_decays(
        y_ref[:, 256 : 256 + inner], heads_ref, lane_pos, heads
    )
    totals_t = totals.T
    allowed = local_mask(lane_pos, rows)
    cross = dot(ssm_c, ssm_b, 1, 1)
    gate = kept_ref[:, 512 : 512 + inner].astype(F32)
    sig = sigmoid(gate)
    y_pure = y_ref[:, :inner]
    dgated = dag[:, :inner].astype(F32)
    skip = heads_ref[2:3, :inner]
    dy = dgated * (gate * sig)
    dy_low = dy.astype(BF16)
    dy_r = dy_low.astype(F32)
    dy_t = dy.T.astype(BF16)
    stepped_low = (step * x_f).astype(BF16)
    stepped_r = stepped_low.astype(F32)
    tailed = (tails * stepped_r).astype(BF16)
    dcross = jnp.zeros((rows, rows), F32)
    parts = []
    for h in range(heads):
        lanes = slice(h * SSM_DIM, (h + 1) * SSM_DIM)
        decay = head_decay(totals, totals_t, h, allowed)
        mix = (decay * cross).astype(BF16)
        parts.append(dot(dy_t[lanes, :], mix))
        dcross = dcross + dot(dy_low[:, lanes], stepped_low[:, lanes], 1, 1) * decay
    dstep_x = jnp.concatenate(parts, axis=0).T
    dcross_low = dcross.astype(BF16)
    held = state_in_ref[...].astype(BF16)
    dheld = dstate[...]
    dheld_low = dheld.astype(BF16)
    dfactored = (factor * dy).astype(BF16)
    from_state = dot(ssm_b, dheld_low, 1, 1)
    dssm_c = dot(dcross_low, ssm_b) + dot(dfactored, held)
    dssm_b = dot(dcross_low, ssm_c, 0, 0) + dot(tailed, dheld_low)
    dtotals = dy_r * y_pure - stepped_r * dstep_x - tailed.astype(F32) * from_state
    dstep_x = dstep_x + tails * from_state
    end_term = exact_sums(
        jnp.ones((16, STATE), BF16), dheld_low.astype(F32) * state_out[...], 1
    )[0:1]
    row, col = iotas(rows, rows)
    upper = jnp.where(col >= row, 1.0, 0.0).astype(BF16)
    drate = -(exact_sums(upper, dtotals) + end_term)
    state_out[...] = state_in_ref[...]
    dstate[...] = state_scale(last_row, carry_last, heads) * dheld + dot(dfactored, ssm_c, 0, 0)
    dssm_x = step * dstep_x + skip * dy
    dstep = x_f * dstep_x + jnp.exp(heads_ref[1:2, :inner]) * drate
    draw = dstep * sigmoid(raw)
    none = jnp.zeros((rows, HEAD_DIM), F32)
    dconv = jnp.concatenate([dssm_x, none, dssm_b, dssm_c], axis=1) * dact
    dext[0:rows, :] = dconv
    dpos[0:rows, :] = lane_pos
    u = kept_ref[:, 0:512].astype(F32)
    du = dconv * taps_ref[CONV - 1 : CONV, :]
    stats_ref[CONV - 1 : CONV, :] += jnp.sum(dconv * u, axis=0, keepdims=True)
    for ahead in range(1, CONV):
        reach = dpos[ahead : ahead + rows, 0:1] >= ahead
        shifted = jnp.where(reach, dext[ahead : ahead + rows, :], 0.0)
        tap = CONV - 1 - ahead
        du = du + shifted * taps_ref[tap : tap + 1, :]
        stats_ref[tap : tap + 1, :] += jnp.sum(shifted * u, axis=0, keepdims=True)
    dext[rows : rows + 8, :] = dconv[0:8]
    dpos[rows : rows + 8, :] = lane_pos[0:8]
    stats_ref[4:5, :inner] += jnp.sum(dy * x_f, axis=0, keepdims=True)
    stats_ref[5:6, :inner] += jnp.sum(draw, axis=0, keepdims=True)
    stats_ref[6:7, :inner] += jnp.sum(drate * rate, axis=0, keepdims=True)
    summed = [
        jnp.sum(draw[:, h * SSM_DIM : (h + 1) * SSM_DIM], axis=1, keepdims=True)
        for h in range(heads)
    ]
    lane = lax.broadcasted_iota(jnp.int32, (rows, HEAD_DIM), 1)
    dstep_all = jnp.zeros((rows, HEAD_DIM), F32)
    for h in range(heads):
        dstep_all = jnp.where(lane == h, summed[h], dstep_all)
    return jnp.concatenate([du[:, :inner], dstep_all, du[:, 256:512]], axis=1).astype(BF16)


def slot_holding(order, block):
    slot = 0
    for k in range(1, order.shape[0]):
        slot = slot + jnp.where(order[k] == block, k, 0)
    return slot


def mixer_forward(u, normed_t, table, head_rows, taps, slot_of):
    count = u.shape[0]
    blocks = count // HALF
    heads = 3
    inner = heads * SSM_DIM
    width = taps.shape[1]
    at_slot = lambda i, order: (slot_holding(order, i), 0)
    in_order = lambda i, slots: (i, 0)
    whole = lambda i, slots: (0, 0)
    return pl.pallas_call(
        mixer_forward_kernel,
        out_shape=(
            jax.ShapeDtypeStruct((count, inner + HEAD_DIM), BF16),
            jax.ShapeDtypeStruct((count, 512), F32),
            jax.ShapeDtypeStruct((count, width), F32),
            jax.ShapeDtypeStruct((blocks * inner, STATE), F32),
            jax.ShapeDtypeStruct((count, 2 * HEAD_DIM), BF16),
            jax.ShapeDtypeStruct((count, 768), BF16),
            jax.ShapeDtypeStruct(normed_t.shape, BF16),
            jax.ShapeDtypeStruct((2 * HEAD_DIM, count), BF16),
        ),
        grid_spec=pltpu.PrefetchScalarGridSpec(
            num_scalar_prefetch=1,
            grid=(blocks,),
            in_specs=[
                pl.BlockSpec((HALF, u.shape[1]), at_slot),
                pl.BlockSpec((normed_t.shape[0], HALF), lambda i, order: at_slot(i, order)[::-1]),
                pl.BlockSpec((HALF, table.shape[1]), in_order),
                pl.BlockSpec(head_rows.shape, whole),
                pl.BlockSpec(taps.shape, whole),
            ],
            out_specs=(
                pl.BlockSpec((HALF, inner + HEAD_DIM), at_slot),
                pl.BlockSpec((HALF, 512), in_order),
                pl.BlockSpec((HALF, width), in_order),
                pl.BlockSpec((inner, STATE), in_order),
                pl.BlockSpec((HALF, 2 * HEAD_DIM), in_order),
                pl.BlockSpec((HALF, 768), in_order),
                pl.BlockSpec((normed_t.shape[0], HALF), lambda i, order: (0, i)),
                pl.BlockSpec((2 * HEAD_DIM, HALF), lambda i, order: (0, i)),
            ),
            scratch_shapes=[
                pltpu.VMEM((8 + HALF, width), F32),
                pltpu.VMEM((inner, STATE), F32),
                pltpu.VMEM((HEAD_DIM, count), BF16),
                pltpu.VMEM((count, HEAD_DIM), BF16),
                pltpu.VMEM((HALF, 2 * HEAD_DIM), F32),
            ],
        ),
        compiler_params=pltpu.CompilerParams(vmem_limit_bytes=60 << 20),
    )(slot_of, u, normed_t, table, head_rows, taps)


MESH = pl.DeviceIdType.MESH


class Place:
    def __init__(self):
        self.c = lax.axis_index("context")
        self.t = lax.axis_index("tensor")
        count = lax.axis_size("context")
        self.chips = [
            self.c,
            self.c + 1 - 2 * (self.c % 2),
            (self.c + count // 2) % count,
            count - 1 - self.c,
        ]

    def slot(self, mask, sibling=False):
        core = 1 - self.t if sibling else self.t
        return self.chips[mask] * 2 + core

    def target(self, mask):
        if mask == 4:
            return {"tensor": 1 - self.t}
        return {"context": self.chips[mask]}

    def hello(self, line=None):
        barrier = pltpu.get_barrier_semaphore()
        targets = [self.target(mask) for mask in (1, 2, 4)]
        if line is not None:
            targets += [line.target(step) for step in range(1, line.count)]
        for target in targets:
            pl.semaphore_signal(barrier, inc=1, device_id=target, device_id_type=MESH)
        return len(targets)

    def greet(self, line=None):
        pl.semaphore_wait(pltpu.get_barrier_semaphore(), self.hello(line))


class Wire:
    def __init__(self, place, sems):
        self.place = place
        self.sems = sems
        self.sent = []

    def copy(self, source, target, index, mask):
        return pltpu.make_async_remote_copy(
            src_ref=source,
            dst_ref=target,
            send_sem=self.sems.at[0, index],
            recv_sem=self.sems.at[1, index],
            device_id=self.place.target(mask),
            device_id_type=MESH,
        )

    def send(self, source, target, index, mask):
        def made():
            here = source() if callable(source) else source
            there = target() if callable(target) else target
            return self.copy(here, there, index, mask)

        made().start()
        self.sent.append(made)

    def arrive(self, target, index, mask):
        self.copy(target, target, index, mask).wait_recv()

    def finish(self):
        for made in self.sent:
            made().wait_send()
        self.sent = []


ROWS = HALF
PART = HALF // 2
TOP, END = pl.ds(0, PART), pl.ds(PART, PART)
SCATTER_SEMS = 10
GATHER_SEMS = 14


def scatter_scratch(columns, kept=BF16):
    return [
        pltpu.VMEM((4, ROWS, columns), BF16),
        pltpu.VMEM((4, ROWS, columns), BF16),
        pltpu.VMEM((6, PART, columns), BF16),
        pltpu.VMEM((ROWS, columns), kept),
        pltpu.SemaphoreType.DMA((2, SCATTER_SEMS)),
    ]


SCATTER_ORDER = (3, 1, 2, 0)


class Scatter:
    def __init__(self, place, scratch):
        self.place = place
        self.core_in, self.out, self.chip_in, self.kept, sems = scratch
        self.wire = Wire(place, sems)

    def to_core(self, mask, source):
        index = SCATTER_ORDER.index(mask)
        self.wire.send(source, self.core_in.at[index], index, 4)

    def from_core(self, mask):
        index = SCATTER_ORDER.index(mask)
        self.wire.arrive(self.core_in.at[index], index, 4)
        return self.core_in[index].astype(F32)

    def first(self, mine, total, between=None):
        wire, out, kept = self.wire, self.out, self.kept
        both = mine(3) + self.from_core(3)
        out[0] = both.astype(BF16)
        wire.send(lambda: out.at[0, TOP], lambda: self.chip_in.at[0], 4, 1)
        wire.send(lambda: out.at[0, END], lambda: self.chip_in.at[1], 5, 2)
        both = mine(1) + self.from_core(1)
        out[1] = both.astype(BF16)
        wire.send(lambda: out.at[1, TOP], lambda: self.chip_in.at[2], 6, 1)
        kept[END] = both[PART:].astype(kept.dtype)
        both = mine(2) + self.from_core(2)
        out[2] = both.astype(BF16)
        wire.send(lambda: out.at[2, END], lambda: self.chip_in.at[3], 7, 2)
        kept[TOP] = both[:PART].astype(kept.dtype)
        total[...] = mine(0) + self.from_core(0)

    def second(self):
        wire, out, kept, came = self.wire, self.out, self.kept, self.chip_in
        wire.arrive(came.at[0], 4, 1)
        out[3, TOP] = (kept[TOP].astype(F32) + came[0].astype(F32)).astype(BF16)
        wire.send(lambda: out.at[3, TOP], lambda: came.at[4], 8, 2)
        wire.arrive(came.at[1], 5, 2)
        out[3, END] = (kept[END].astype(F32) + came[1].astype(F32)).astype(BF16)
        wire.send(lambda: out.at[3, END], lambda: came.at[5], 9, 1)

    def last(self, total):
        wire, came = self.wire, self.chip_in
        wire.arrive(came.at[2], 6, 1)
        wire.arrive(came.at[4], 8, 2)
        total[TOP] += came[2].astype(F32) + came[4].astype(F32)
        wire.arrive(came.at[3], 7, 2)
        wire.arrive(came.at[5], 9, 1)
        total[END] += came[3].astype(F32) + came[5].astype(F32)
        wire.finish()


class Gather:
    def __init__(self, place, whole, sems, rows=ROWS, cores=True):
        self.place = place
        self.whole = whole
        self.size = rows
        self.cores = cores
        self.wire = Wire(place, sems)

    def rows(self, mask, sibling=False, half=None):
        place, size = self.place, self.size
        block = place.slot(mask, sibling) if self.cores else place.chips[mask]
        begin = block * size
        if half is None:
            return self.whole.at[pl.ds(pl.multiple_of(begin, size), size)]
        return self.whole.at[pl.ds(pl.multiple_of(begin + half * (size // 2), size // 2), size // 2)]

    def both(self, mask, sibling=False, half=None):
        block = functools.partial(self.rows, mask, sibling, half)
        return block, block

    def start(self, core=True):
        wire = self.wire
        for half, mask, index in ((0, 1, 0), (1, 2, 1), (1, 1, 2), (0, 2, 3)):
            wire.send(*self.both(0, half=half), index, mask)
        if self.cores and core:
            wire.send(*self.both(0), 6, 4)

    def relay(self):
        wire = self.wire
        wire.arrive(self.rows(1, half=0), 0, 1)
        wire.send(*self.both(1, half=0), 4, 2)
        wire.arrive(self.rows(2, half=1), 1, 2)
        wire.send(*self.both(2, half=1), 5, 1)

    def near(self):
        wire = self.wire
        wire.arrive(self.rows(1, half=1), 2, 1)
        if self.cores:
            wire.send(*self.both(1), 7, 4)
        wire.arrive(self.rows(2, half=0), 3, 2)
        if self.cores:
            wire.send(*self.both(2), 8, 4)

    def far(self):
        wire = self.wire
        wire.arrive(self.rows(3, half=0), 4, 2)
        wire.arrive(self.rows(3, half=1), 5, 1)
        if self.cores:
            wire.send(*self.both(3), 9, 4)

    def core(self, mask):
        index = (6, 7, 8, 9)[mask]
        self.wire.arrive(self.rows(mask, sibling=True), index, 4)

    def finish(self):
        self.wire.finish()


class Line:
    def __init__(self):
        self.f = lax.axis_index("fsdp")
        self.count = lax.axis_size("fsdp")

    def target(self, step):
        return {"fsdp": (self.f + step) % self.count}

    def copy(self, source, target, sems, step):
        return pltpu.make_async_remote_copy(
            src_ref=source,
            dst_ref=target,
            send_sem=sems.at[0, step],
            recv_sem=sems.at[1, step],
            device_id=self.target(step),
            device_id_type=MESH,
        )


class LineGather:
    def __init__(self, line, whole, sems):
        self.line = line
        self.whole = whole
        self.sems = sems
        self.size = whole.shape[0] // line.count

    def rows(self, block):
        return self.whole.at[pl.ds(pl.multiple_of(block * self.size, self.size), self.size)]

    def copy(self, block, way, step):
        toward = self.line.f + 1 if way == 0 else self.line.f - 1
        return pltpu.make_async_remote_copy(
            src_ref=self.rows(block),
            dst_ref=self.rows(block),
            send_sem=self.sems.at[way, 0, step],
            recv_sem=self.sems.at[way, 1, step],
            device_id={"fsdp": toward},
            device_id_type=MESH,
        )

    def step(self, number, arrive=True):
        f, last = self.line.f, self.line.count - 1
        for way in (0, 1):
            block = f - number if way == 0 else f + number
            there = block >= 0 if way == 0 else block <= last
            goes_on = f < last if way == 0 else f > 0

            @pl.when(there)
            def _():
                if number > 0:
                    self.copy(block, way, number).wait_recv()

                @pl.when(goes_on)
                def _():
                    self.copy(block, way, number + 1).start()

    def finish(self):
        f, last = self.line.f, self.line.count - 1
        for number in range(self.line.count - 1):
            for way in (0, 1):
                block = f - number if way == 0 else f + number
                there = block >= 0 if way == 0 else block <= last
                goes_on = f < last if way == 0 else f > 0

                @pl.when(there & goes_on)
                def _():
                    self.copy(block, way, number + 1).wait_send()


def line_sems(count):
    return pltpu.SemaphoreType.DMA((2, 2, count + 1))


def opening_kernel(
    tokens_ref, cot_ref, in_x_ref, query_ref, bc_ref, gate_ref, keyval_ref, step_ref, ssm_ref, attn_ref,
    gain_ref, segments_ref, conv_x_ref, conv_bc_ref, bias_ref, decay_ref, skip_ref,
    normed_t_out, u_out, w_out, wout_out, cot_out, table_out, heads_ref, taps_ref,
    x_all, cot_all, normed, normed_t, u, weights_all, wout_all, table, wide,
    x_sems, cot_sems, w_sems, out_sems, local_sems, block_sems,
):
    place = Place()
    line = Line()
    rows_x = Gather(place, x_all, x_sems)
    rows_cot = Gather(place, cot_all, cot_sems)
    weights = LineGather(line, weights_all, w_sems)
    weights_out = LineGather(line, wout_all, out_sems)
    chips = lax.axis_size("context")
    share = in_x_ref.shape[0]
    heads = step_ref.shape[0] // chips
    inner = heads * SSM_DIM
    chip_rows = pl.ds(pl.multiple_of(place.c * 2 * ROWS, 2 * ROWS), 2 * ROWS)
    waiting = []

    def local(source, target, sem):
        made = pltpu.make_async_copy(source, target, sem)
        made.start()
        waiting.append(made)
        return made

    greetings = place.hello(line)
    own_x = pltpu.make_async_copy(tokens_ref, x_all.at[chip_rows], local_sems.at[0])
    own_x.start()
    own_cot = pltpu.make_async_copy(cot_ref, cot_all.at[chip_rows], local_sems.at[1])
    own_cot.start()
    mine = pl.ds(pl.multiple_of(line.f * share, share), share)
    heads_ref[...] = jnp.zeros(heads_ref.shape, F32)
    taps_ref[...] = jnp.zeros(taps_ref.shape, F32)
    for k in range(chips):

        @pl.when(place.c == k)
        def _():
            inner_part = slice(k * inner, (k + 1) * inner)
            head_part = slice(k * HEAD_DIM, (k + 1) * HEAD_DIM)
            weights_all[mine, 0:256] = jnp.concatenate(
                [gate_ref[:, inner_part], query_ref[:, head_part]], axis=1
            )
            weights_all[mine, 384 : 384 + inner] = in_x_ref[:, inner_part]
            wout_all[mine, :] = jnp.concatenate(
                [ssm_ref[:, inner_part], attn_ref[:, head_part]], axis=1
            )
            taps_ref[0:CONV, :inner] = conv_x_ref[:, inner_part]
            for h in range(heads):
                lane = slice(k * heads + h, k * heads + h + 1)
                for row, source in enumerate((bias_ref, decay_ref, skip_ref)):
                    heads_ref[row : row + 1, h * SSM_DIM : (h + 1) * SSM_DIM] = jnp.broadcast_to(
                        source[:, lane], (1, SSM_DIM)
                    )

    taps_ref[0:CONV, 256:512] = conv_bc_ref[...]
    head, column = iotas(step_ref.shape[0], HEAD_DIM)
    chosen = (head == column + place.c * heads) & (column < heads)
    steps = dot(step_ref[...], jnp.where(chosen, 1.0, 0.0).astype(BF16), 0, 0)
    weights_all[mine, 384 + inner : 640] = steps.astype(BF16)
    weights_all[mine, 256:384] = keyval_ref[...]
    weights_all[mine, 640:896] = bc_ref[...]
    own_x.wait()
    own_cot.wait()
    pl.semaphore_wait(pltpu.get_barrier_semaphore(), greetings)
    weights.step(0)
    rows_x.start(core=False)

    def norm(slot):
        rows = slot_rows(slot)
        x = x_all[rows, :].astype(F32)
        normed[rows, :] = (x * norm_scale(x) * gain_ref[...]).astype(BF16)
        columns = pl.ds(pl.multiple_of(slot * ROWS, ROWS), ROWS)
        normed_t[:, columns] = normed[rows, :].T

    norm(place.slot(0))
    norm(place.slot(0, True))

    numbers = segments_ref[...]
    bounds = [
        jnp.sum(jnp.where(numbers < k, 1.0, 0.0), axis=1, keepdims=True) for k in (1, 2)
    ]
    count = table.shape[0]
    lane = lax.broadcasted_iota(jnp.int32, (8, 128), 1)[0:1]
    power = -(lane % (HEAD_DIM // 2)).astype(F32) / (HEAD_DIM // 2)
    freqs = jnp.exp(power * math.log(10000.0))
    phase = jnp.where(lane < HEAD_DIM, math.pi / 2, 0.0)
    sign = jnp.where((lane >= HEAD_DIM) & (lane < HEAD_DIM + HEAD_DIM // 2), -1.0, 1.0)

    def angles(block, carry):
        row = lax.broadcasted_iota(jnp.int32, (ROWS, 128), 0) + block * ROWS
        row = row.astype(F32)
        start = jnp.where(row >= bounds[0], bounds[0], 0.0)
        start = jnp.where(row >= bounds[1], bounds[1], start)
        pos = row - start
        here = slot_rows(block)
        table[here, 0:128] = jnp.sin(pos * freqs + phase) * sign
        table[here, 128:256] = pos
        return carry

    blocks = count // ROWS
    rows_x.relay()
    rows_cot.start(core=False)
    lax.fori_loop(0, blocks // 2, angles, 0)
    weights.step(1)
    lax.fori_loop(blocks // 2, blocks, angles, 0)
    local(table, table_out, local_sems.at[2])
    rows_x.near()
    norm(place.slot(1))
    norm(place.slot(2))
    rows_cot.relay()
    for number in range(2, line.count - 1):
        weights.step(number)
    rows_x.far()
    norm(place.slot(3))
    for mask in (1, 2, 3):
        rows_x.core(mask)
        norm(place.slot(mask, True))
    weights_out.step(0)
    rows_cot.near()
    weights.step(line.count - 1)
    local(weights_all, w_out, local_sems.at[3])
    local(normed_t, normed_t_out, local_sems.at[6])
    row, column = iotas(HEAD_DIM, inner)
    copies = jnp.where(column // SSM_DIM == row, 1.0, 0.0).astype(BF16)
    wide[:, 0:256] = jnp.concatenate(
        [weights_all[:, 384 : 384 + inner], weights_all[:, inner:256]], axis=1
    )
    wide[:, 256:512] = weights_all[:, 640:896]
    wide[:, 512:768] = jnp.concatenate([weights_all[:, :inner], weights_all[:, 256:320]], axis=1)
    wide[:, 768:1024] = jnp.concatenate(
        [
            dot(weights_all[:, 384 + inner : 640], copies),
            weights_all[:, 320:384].astype(F32),
        ],
        axis=1,
    ).astype(BF16)

    def project(slot):
        rows = pl.ds(slot * ROWS, ROWS)
        u[rows, :] = dot(normed[rows, :], wide[...])
        local(u.at[rows], u_out.at[rows], block_sems.at[0, slot])

    for slot in range(blocks // 2):
        project(slot)
    weights_out.step(1)
    rows_cot.far()
    for slot in range(blocks // 2, blocks):
        project(slot)
    for number in range(2, line.count):
        weights_out.step(number)
    local(wout_all, wout_out, local_sems.at[4])
    for mask in (1, 2, 3):
        rows_cot.core(mask)
    local(cot_all, cot_out, local_sems.at[5])
    for made in waiting:
        made.wait()
    rows_x.finish()
    rows_cot.finish()
    weights.finish()
    weights_out.finish()


def opening(tokens, cotangent, weights, gain, segments, taps, by_head):
    fsdp = lax.axis_size("fsdp")
    model = tokens.shape[1]
    count = segments.shape[1]
    blocks = count // ROWS
    vmem = pl.BlockSpec(memory_space=pltpu.VMEM)
    hbm = pl.BlockSpec(memory_space=pl.ANY)
    shape = jax.ShapeDtypeStruct
    dma = pltpu.SemaphoreType.DMA
    buffers = [
        ((model, count), BF16),
        ((count, 1024), F32),
        ((model, 896), BF16),
        ((model, 256), BF16),
        ((count, model), BF16),
        ((count, 256), F32),
    ]
    kept = [buffers[k] for k in (0, 1, 2, 3, 5)]
    return pl.pallas_call(
        opening_kernel,
        out_shape=tuple(shape(*one) for one in buffers) + (shape((8, 256), F32), shape((8, 512), F32)),
        in_specs=[hbm] * 2 + [vmem] * 15,
        out_specs=(hbm,) * 6 + (vmem,) * 2,
        scratch_shapes=[pltpu.VMEM((count, model), BF16)] * 3
        + [pltpu.VMEM(*one) for one in kept]
        + [
            pltpu.VMEM((model, 1024), BF16),
            dma((2, GATHER_SEMS)),
            dma((2, GATHER_SEMS)),
            line_sems(fsdp),
            line_sems(fsdp),
            dma((7,)),
            dma((1, blocks)),
        ],
        compiler_params=pltpu.CompilerParams(
            collective_id=3, has_side_effects=True, vmem_limit_bytes=60 << 20
        ),
        cost_estimate=pl.CostEstimate(
            flops=2 * count * model * 1024, bytes_accessed=30 << 20, transcendentals=count * 128
        ),
    )(
        tokens, cotangent, *weights, gain.reshape(1, -1), segments, *taps,
        *[one.reshape(1, -1) for one in by_head],
    )


def slot_rows(slot):
    return pl.ds(pl.multiple_of(slot * ROWS, ROWS), ROWS)


def norm_scale(values):
    return lax.rsqrt(jnp.mean(values * values, axis=1, keepdims=True) + epsilon)


def middle_kernel(
    ag_ref, wout_ref, gate_ref, up_ref, down_ref, gain_ref, x_hbm, cot_hbm, cot_all_hbm,
    hidden_ref, dag_ref, mixed_ref, dmixed_ref, dgain_ref, down_all_ref, ffn_ref, dout_ref,
    x_ref, cot_ref, cot_all_ref, nffn_ref, dgu_ref, dm_ref, dw_ref, arrived, part, wffn_ref, *scratch,
):
    place = Place()
    first = Scatter(place, scratch[0:5])
    back = Scatter(place, scratch[5:10])
    forth = Gather(place, nffn_ref, scratch[10])
    home = Gather(place, dm_ref, scratch[11])
    hid = hidden_ref.shape[1]
    line = Line()
    weights = LineGather(line, wffn_ref, scratch[12])
    share = gate_ref.shape[0]
    greetings = place.hello(line)
    half = pl.ds(pl.multiple_of(place.t * ROWS, ROWS), ROWS)
    loads = [
        pltpu.make_async_copy(source, target, scratch[14].at[k])
        for k, (source, target) in enumerate(
            ((x_hbm.at[half], x_ref), (cot_hbm.at[half], cot_ref), (cot_all_hbm, cot_all_ref))
        )
    ]
    for made in loads:
        made.start()
    mine = pl.ds(pl.multiple_of(line.f * share, share), share)
    lanes = pl.ds(pl.multiple_of(place.c * hid, hid), hid)
    for k, source in enumerate((gate_ref, up_ref, down_ref)):
        wffn_ref[mine, k * hid : (k + 1) * hid] = source[:, lanes]

    def block(mask, sibling=False):
        return dot(ag_ref[slot_rows(place.slot(mask, sibling)), :], wout_ref[...], 1, 1)

    for mask in SCATTER_ORDER:
        part[slot_rows(place.slot(mask, True)), :] = block(mask, True).astype(BF16)
    pl.semaphore_wait(pltpu.get_barrier_semaphore(), greetings)
    for mask in SCATTER_ORDER:
        first.to_core(mask, part.at[slot_rows(place.slot(mask, True))])
    weights.step(0)
    first.first(block, mixed_ref)
    weights.step(1)
    first.second()
    for made in loads:
        made.wait()
    mixed_ref[...] += x_ref[...].astype(F32)
    first.last(mixed_ref)
    mixed = mixed_ref[...]
    gain = gain_ref[...]
    scale = norm_scale(mixed)
    own = slot_rows(place.slot(0))
    nffn_ref[own, :] = (mixed * scale * gain).astype(BF16)
    forth.start()
    for number in range(2, line.count):
        weights.step(number)

    def work(slot):
        rows = slot_rows(slot)
        normed = nffn_ref[rows, :]
        gate_up = dot(normed, wffn_ref[:, : 2 * hid])
        dhidden = dot(cot_all_ref[rows, :], wffn_ref[:, 2 * hid :]).astype(BF16).astype(F32)
        gate, up = gate_up[:, :hid], gate_up[:, hid:]
        sig = sigmoid(gate)
        silu = gate * sig
        dgate = dhidden * up * (sig * (1.0 + gate * (1.0 - sig)))
        hidden_ref[rows, :] = (silu * up).astype(BF16)
        dgu_ref[rows, :hid] = dgate.astype(BF16)
        dgu_ref[rows, hid:] = (dhidden * silu).astype(BF16)
        part[rows, :] = dot(dgu_ref[rows, :], wffn_ref[:, : 2 * hid], 1, 1).astype(BF16)

    def hand_over(mask):
        slot = place.slot(mask, True)
        work(slot)
        back.to_core(mask, part.at[slot_rows(slot)])

    work(place.slot(0))
    forth.relay()
    forth.core(0)
    hand_over(0)
    forth.near()
    forth.core(1)
    hand_over(1)
    forth.core(2)
    hand_over(2)
    work(place.slot(1))
    forth.far()
    work(place.slot(2))
    forth.core(3)
    hand_over(3)
    work(place.slot(3))
    forth.finish()

    def ready(mask):
        return part[slot_rows(place.slot(mask)), :].astype(F32)

    back.first(ready, dmixed_ref)

    columns = (pl.ds(0, 2 * hid), pl.ds(2 * hid, hid))
    line_sent = []

    def line_copy(piece, step):
        rows = pl.ds(pl.multiple_of((line.f + step) % line.count * share, share), share)
        return line.copy(
            dw_ref.at[rows, columns[piece]],
            arrived.at[step, :, columns[piece]],
            scratch[13].at[piece],
            step,
        )

    def send_piece(piece, left, right):
        quarter = dw_ref.shape[0] // 4
        for k in range(4):
            rows = slice(k * quarter, (k + 1) * quarter)
            dw_ref[rows, columns[piece]] = dot(left[:, rows], right[...], 0, 0).astype(BF16)
        for step in range(1, line.count):
            made = line_copy(piece, step)
            made.start()
            line_sent.append(made)

    send_piece(1, cot_all_ref, hidden_ref)
    back.second()
    send_piece(0, nffn_ref, dgu_ref)
    back.last(dmixed_ref)
    dnffn = dmixed_ref[...]
    mixed = mixed_ref[...]
    scale = norm_scale(mixed)
    spread = dnffn * gain
    pull = jnp.mean(spread * mixed, axis=1, keepdims=True)
    dgain_ref[...] = jnp.broadcast_to(
        jnp.sum(dnffn * mixed * scale, axis=0, keepdims=True), dgain_ref.shape
    )
    dmixed = cot_ref[...].astype(F32) + scale * (spread - mixed * (scale * scale * pull))
    dmixed_ref[...] = dmixed
    dm_ref[own, :] = dmixed.astype(BF16)
    home.start()

    def pull_back(slot):
        rows = slot_rows(slot)
        dag_ref[rows, :] = dot(dm_ref[rows, :], wout_ref[...]).astype(BF16)

    pull_back(place.slot(0))
    home.relay()
    home.core(0)
    pull_back(place.slot(0, True))
    home.near()
    pull_back(place.slot(1))
    pull_back(place.slot(2))
    home.far()
    pull_back(place.slot(3))
    for mask in (1, 2, 3):
        home.core(mask)
        pull_back(place.slot(mask, True))
    dout_ref[...] = dot(dm_ref[...], ag_ref[...], 0, 0).astype(BF16)
    down_all_ref[...] = wffn_ref[:, 2 * hid :]
    for piece in (1, 0):
        sums = dw_ref[mine, columns[piece]].astype(F32)
        for step in range(1, line.count):
            line_copy(piece, step).wait_recv()
            sums = sums + arrived[step, :, columns[piece]].astype(F32)
        ffn_ref[:, columns[piece]] = sums.astype(BF16)
    for made in line_sent:
        made.wait_send()
    home.finish()
    weights.finish()


def middle(ag, wout, weights, x_own, cot_own, cot_all, gain):
    count, model = cot_all.shape
    hid = weights[0].shape[1] // lax.axis_size("context")
    columns = ag.shape[1]
    vmem = pl.BlockSpec(memory_space=pltpu.VMEM)
    hbm = pl.BlockSpec(memory_space=pl.ANY)
    shape = jax.ShapeDtypeStruct
    return pl.pallas_call(
        middle_kernel,
        out_shape=(
            shape((count, hid), BF16),
            shape((count, columns), BF16),
            shape((ROWS, model), F32),
            shape((ROWS, model), F32),
            shape((8, model), F32),
            shape((model, hid), BF16),
            shape((weights[0].shape[0], 3 * hid), BF16),
            shape((model, columns), BF16),
        ),
        in_specs=[vmem] * 6 + [hbm] * 3,
        out_specs=(vmem,) * 8,
        scratch_shapes=[
            pltpu.VMEM((ROWS, model), BF16),
            pltpu.VMEM((ROWS, model), BF16),
            pltpu.VMEM((count, model), BF16),
            pltpu.VMEM((count, model), BF16),
            pltpu.VMEM((count, 2 * hid), BF16),
            pltpu.VMEM((count, model), BF16),
            pltpu.VMEM((model, 3 * hid), BF16),
            pltpu.VMEM((lax.axis_size("fsdp"), weights[0].shape[0], 3 * hid), BF16),
            pltpu.VMEM((count, model), BF16),
            pltpu.VMEM((model, 3 * hid), BF16),
        ]
        + scatter_scratch(model, F32)
        + scatter_scratch(model, F32)
        + [pltpu.SemaphoreType.DMA((2, GATHER_SEMS))] * 2
        + [line_sems(lax.axis_size("fsdp")), pltpu.SemaphoreType.DMA((2, 2, lax.axis_size("fsdp"))), pltpu.SemaphoreType.DMA((3,))],
        compiler_params=pltpu.CompilerParams(
            collective_id=1, has_side_effects=True, vmem_limit_bytes=60 << 20
        ),
        cost_estimate=pl.CostEstimate(
            flops=20 * count * model * hid, bytes_accessed=40 << 20, transcendentals=count * hid
        ),
    )(ag, wout, *weights, gain.reshape(1, -1), x_own, cot_own, cot_all)


BACK_INPUTS = 5
EARLY = 384


def closing_kernel(
    order_ref, dag_ref, kv_ref, kv_t_ref, heads_ref, taps_ref, dmixed_ref, gain_ref, ffn_ref,
    dgain_ref, dout_ref, table_hbm, y_hbm, conv_hbm, kept_hbm, states_hbm, normed_t_hbm, w_hbm,
    hidden_hbm, down_hbm, mixed_hbm, tokens_hbm,
    grad_ref, out_ref, early_ref, bc_ref, last_ref, mids_ref, outs_ref, small_ref,
    table, y, conv, kept, states, normed_t, w, hidden, down, x_ref,
    dnorm, early_du, dw_sum, dw, arrived, arrived_out, total, out_total, part, out_part, bc_out, bc_in, small_in,
    stats, dext, dpos, dstate, state_out, dkey_t, dvalue_t, *scratch,
):
    place = Place()
    line = Line()
    back = Scatter(place, scratch[0:5])
    final = Scatter(place, scratch[5:10])
    share = ffn_ref.shape[0]
    last_all = Gather(place, last_ref, scratch[10], share, False)
    early_all = Gather(place, early_ref, scratch[20], share, False)
    bc_all = Gather(place, bc_ref, scratch[21], share, False)
    mid_all = Gather(place, mids_ref, scratch[11], share, False)
    out_all = Gather(place, outs_ref, scratch[12], share, False)
    small_rows = small_in.shape[1]
    small_all = Gather(place, small_ref, scratch[13], small_rows)
    line_sems_, small_sems, out_sems, pair_sems, load_sems, block_sems = scratch[14:20]
    pair = Wire(place, pair_sems)
    greetings = place.hello(line)
    sent = []
    loads = [
        pltpu.make_async_copy(source, target, load_sems.at[k])
        for k, (source, target) in enumerate(
            (
                (hidden_hbm, hidden), (down_hbm, down), (normed_t_hbm, normed_t), (w_hbm, w),
                (mixed_hbm, out_total),
                (tokens_hbm.at[pl.ds(pl.multiple_of(place.t * ROWS, ROWS), ROWS)], x_ref),
            )
        )
    ]
    blocks = dnorm.shape[0] // ROWS
    streams = ((table_hbm, table), (y_hbm, y), (conv_hbm, conv), (kept_hbm, kept), (states_hbm, states))

    early_lanes = (pl.ds(0, 256), pl.ds(0, 512), pl.ds(0, 256), pl.ds(512, 256), None)
    late_lanes = (pl.ds(128, 128), pl.ds(0, 512), pl.ds(0, 512), pl.ds(0, 768), pl.ds(0, STATE))

    def fetch(block, buffer, late):
        copies = []
        for k, (source, target) in enumerate(streams):
            lanes = late_lanes[k] if late else early_lanes[k]
            if lanes is None:
                continue
            size = target.shape[1]
            begin = pl.multiple_of(block * size, size)
            copies.append(
                pltpu.make_async_copy(
                    source.at[pl.ds(begin, size), lanes],
                    target.at[buffer, :, lanes],
                    block_sems.at[buffer, k],
                )
            )
        return copies

    for made in fetch(blocks - 1, 0, False) + loads:
        made.start()
    mids_ref[pl.ds(pl.multiple_of(place.c * share, share), share), :] = ffn_ref[...]
    width = dext.shape[1]
    dext[ROWS : ROWS + 8, :] = jnp.zeros((8, width), F32)
    dpos[ROWS : ROWS + 8, :] = jnp.full((8, dpos.shape[1]), -1.0, F32)
    for ref in (dstate, state_out, dkey_t, dvalue_t, stats, dw_sum):
        ref[...] = jnp.zeros(ref.shape, F32)
    def out_block(mask, sibling=False):
        return dot(hidden[slot_rows(place.slot(mask, sibling)), :], down[...], 1, 1)

    def out_rows(mask):
        return out_block(mask) + out_total[...] if mask == 0 else out_block(mask)

    here = pl.ds(pl.multiple_of(place.c * share, share), share)
    own = pl.ds(pl.multiple_of(line.f * share, share), share)
    half = pl.ds(pl.multiple_of(place.t * ROWS, ROWS), ROWS)

    def my_half(ref):
        return lambda: ref.at[pl.ds(pl.multiple_of(place.t * ROWS, ROWS), ROWS)]

    def collect_out():
        sums = dout_ref[own, :].astype(F32)
        for step in range(1, line.count):
            line.copy(arrived_out.at[step - 1], arrived_out.at[step - 1], out_sems, step).wait_recv()
            sums = sums + arrived_out[step - 1].astype(F32)
        outs_ref[here, :] = sums.astype(BF16)
        out_all.start()

    def finish_out():
        final.last(out_total)
        out_ref[half, :] = out_total[...].astype(BF16)
        pair.send(my_half(out_ref), my_half(out_ref), 1, 4)

    lane = lax.broadcasted_iota(jnp.int32, (8, blocks), 1)[0:1]
    order = order_ref[...]

    def blend(source, marks):
        marks = [jnp.where(one, 1.0, 0.0).astype(BF16) for one in marks]
        found = source[0:ROWS, :] * marks[0]
        for k in range(1, blocks):
            found = found + source[k * ROWS : (k + 1) * ROWS, :] * marks[k]
        return found

    def from_slots(source, block):
        return blend(source, [order[:, k : k + 1] == block for k in range(blocks)])

    def from_stream(source, slot):
        dealt = jnp.sum(jnp.where(lane == slot, order, 0), axis=1, keepdims=True)
        return blend(source, [dealt == k for k in range(blocks)])

    def prefetch(block, buffer, late):
        for made in fetch(block, buffer, late):
            made.start()

    def await_block(block, buffer, late):
        for made in fetch(block, buffer, late):
            made.wait()

    def happen(number, events):
        for when, actions in events.items():

            @pl.when(number == when)
            def _():
                for action in actions:
                    action()

    def early_turn(number, carry):
        block = blocks - 1 - number
        buffer = number % 2
        await_block(block, buffer, False)

        @pl.when(number < blocks - 1)
        def _():
            prefetch(block - 1, 1 - buffer, False)

        @pl.when(number == blocks - 1)
        def _():
            prefetch(blocks - 1, 1 - buffer, True)

        grads = attention_backward(
            block, from_slots(dag_ref, block), table.at[buffer], heads_ref, y.at[buffer], conv.at[buffer],
            kept.at[buffer], kv_ref, kv_t_ref, dkey_t, dvalue_t,
        )
        early_du[slot_rows(block), :] = grads
        dw_sum[:, :EARLY] += dot(normed_t[:, slot_rows(block)], grads)
        happen(number, {3: (lambda: final.first(out_rows, out_total),), 6: (mid_all.relay,)})
        return carry

    def late_turn(number, carry):
        block = blocks - 1 - number
        buffer = number % 2
        await_block(block, buffer, True)

        @pl.when(number < blocks - 1)
        def _():
            prefetch(block - 1, 1 - buffer, True)

        grads = recurrence_backward(
            from_slots(dag_ref, block), table.at[buffer], heads_ref, taps_ref, y.at[buffer],
            conv.at[buffer], kept.at[buffer], states.at[buffer], state_out, stats, dext, dpos, dstate,
        )
        whole = jnp.concatenate([early_du[slot_rows(block), :], grads], axis=1)
        dnorm[slot_rows(block), :] = dot(whole, w[...], 1, 1).astype(BF16)
        dw_sum[:, EARLY:] += dot(normed_t[:, slot_rows(block)], grads)
        happen(
            number,
            {
                1: (mid_all.near,),
                3: (collect_out, mid_all.far),
                5: (final.second,),
                6: (out_all.relay,),
            },
        )
        return carry

    columns = (pl.ds(0, EARLY), pl.ds(EARLY + 256, 256), pl.ds(EARLY, 256))

    def line_copy(piece, step):
        rows = pl.ds(pl.multiple_of((line.f + step) % line.count * share, share), share)
        return line.copy(
            dw.at[rows, columns[piece]], arrived.at[step - 1, :, columns[piece]], line_sems_.at[piece], step
        )

    def send_piece(piece):
        dw[:, columns[piece]] = dw_sum[:, columns[piece]].astype(BF16)
        for step in range(1, line.count):
            made = line_copy(piece, step)
            made.start()
            sent.append(made)

    def collected(piece):
        sums = dw[own, columns[piece]].astype(F32)
        for step in range(1, line.count):
            line_copy(piece, step).wait_recv()
            sums = sums + arrived[step - 1, :, columns[piece]].astype(F32)
        return sums.astype(BF16)

    for made in loads:
        made.wait()
    early_turn(0, 0)
    pl.semaphore_wait(pltpu.get_barrier_semaphore(), greetings)
    for step in range(1, line.count):
        rows = pl.ds(pl.multiple_of((line.f + step) % line.count * share, share), share)
        made = line.copy(dout_ref.at[rows], arrived_out.at[step - 1], out_sems, step)
        made.start()
        sent.append(made)
    for k, mask in enumerate(SCATTER_ORDER):
        out_part[k] = out_block(mask, True).astype(BF16)
        final.to_core(mask, out_part.at[k])
    mid_all.start()
    lax.fori_loop(1, blocks, early_turn, 0)
    send_piece(0)
    lax.fori_loop(0, blocks, late_turn, 0)
    send_piece(1)
    send_piece(2)

    def block_of(mask, sibling=False):
        return from_stream(dnorm, place.slot(mask, sibling))

    for k, mask in enumerate(SCATTER_ORDER):
        part[k] = block_of(mask, True)
        back.to_core(mask, part.at[k])
    back.first(lambda mask: block_of(mask).astype(F32), total)
    out_all.near()
    finish_out()
    back.second()
    out_all.far()
    early_ref[here, :] = collected(0)
    early_all.start()
    bc_out[...] = collected(1)
    pair.send(bc_out, bc_in, 2, 4)
    back.last(total)
    early_all.relay()
    dnormed = total[...]
    x = x_ref[...].astype(F32)
    gain = gain_ref[...]
    scale = norm_scale(x)
    spread = dnormed * gain
    pull = jnp.mean(spread * x, axis=1, keepdims=True)
    grad = dmixed_ref[...] + scale * (spread - x * (scale * scale * pull))
    grad_ref[half, :] = grad.astype(BF16)
    pair.send(grad_ref.at[half], grad_ref.at[half], 0, 4)
    small_in[0] = jnp.zeros(small_in.shape[1:], F32)
    small_in[0, 0:1, :] = jnp.sum(dnormed * x * scale, axis=0, keepdims=True)
    small_in[0, 1:2, :] = dgain_ref[0:1, :]
    small_in[0, 8:16, :width] = stats[...]
    for step in range(1, line.count):
        made = line.copy(small_in.at[0], small_in.at[step], small_sems, step)
        made.start()
        sent.append(made)
    pair.arrive(bc_in, 2, 4)
    bc_ref[here, :] = (bc_out[...].astype(F32) + bc_in[...].astype(F32)).astype(BF16)
    bc_all.start()
    early_all.near()
    last_ref[here, :] = collected(2)
    last_all.start()
    bc_all.relay()
    for step in range(1, line.count):
        line.copy(small_in.at[0], small_in.at[step], small_sems, step).wait_recv()
    summed = small_in[line.f % line.count]
    for other in range(1, line.count):
        summed = summed + small_in[(line.f + line.count - other) % line.count]
    mine = pl.ds(pl.multiple_of(place.slot(0) * small_rows, small_rows), small_rows)
    small_ref[mine, :] = summed
    small_all.start()
    early_all.far()
    last_all.relay()
    small_all.relay()
    small_all.near()
    small_all.far()
    bc_all.near()
    bc_all.far()
    last_all.near()
    last_all.far()
    for mask in range(4):
        small_all.core(mask)
    other = pl.ds(pl.multiple_of((1 - place.t) * ROWS, ROWS), ROWS)
    pair.arrive(grad_ref.at[other], 0, 4)
    pair.arrive(out_ref.at[other], 1, 4)
    for made in sent:
        made.wait_send()
    pair.finish()
    mid_all.finish()
    out_all.finish()
    small_all.finish()
    last_all.finish()
    early_all.finish()
    bc_all.finish()


def closing(small_inputs, streams, loads, fsdp):
    ffn, dout = small_inputs[8], small_inputs[10]
    normed_t, w, hidden, down, _, _ = loads
    model, count = normed_t.shape
    share = ffn.shape[0]
    columns = w.shape[1]
    chips = lax.axis_size("context")
    blocks = count // ROWS
    vmem = pl.BlockSpec(memory_space=pltpu.VMEM)
    hbm = pl.BlockSpec(memory_space=pl.ANY)
    shape = jax.ShapeDtypeStruct
    dma = pltpu.SemaphoreType.DMA
    space = pltpu.VMEM
    inner = streams[4].shape[0] // blocks
    return pl.pallas_call(
        closing_kernel,
        out_shape=(
            shape((2 * ROWS, model), BF16),
            shape((2 * ROWS, model), BF16),
            shape((chips * share, EARLY), BF16),
            shape((chips * share, 256), BF16),
            shape((chips * share, 256), BF16),
            shape((chips * share, ffn.shape[1]), BF16),
            shape((chips * share, dout.shape[1]), BF16),
            shape((2 * chips * 16, model), F32),
        ),
        in_specs=[vmem] * 11 + [hbm] * 11,
        out_specs=(vmem,) * 8,
        scratch_shapes=[space((2, one.shape[0] // blocks, one.shape[1]), one.dtype) for one in streams]
        + [space(one.shape, one.dtype) for one in loads[:4]]
        + [space((ROWS, model), BF16)]
        + [
            space((count, model), BF16),
            space((count, EARLY), BF16),
            space((model, columns), F32),
            space((model, columns), BF16),
            space((fsdp - 1, share, columns), BF16),
            space((fsdp - 1, share, dout.shape[1]), BF16),
            space((ROWS, model), F32),
            space((ROWS, model), F32),
            space((4, ROWS, model), BF16),
            space((4, ROWS, model), BF16),
            space((share, 256), BF16),
            space((share, 256), BF16),
            space((fsdp, 16, model), F32),
            space((8, 512), F32),
            space((ROWS + 8, 512), F32),
            space((ROWS + 8, 128), F32),
            space((inner, STATE), F32),
            space((inner, STATE), F32),
            space((HEAD_DIM, count), F32),
            space((HEAD_DIM, count), F32),
        ]
        + scatter_scratch(model)
        + scatter_scratch(model)
        + [dma((2, GATHER_SEMS))] * 4
        + [dma((3, 2, fsdp)), dma((2, fsdp)), dma((2, fsdp)), dma((2, 3)), dma((6,)), dma((2, BACK_INPUTS)), dma((2, GATHER_SEMS)), dma((2, GATHER_SEMS))],
        compiler_params=pltpu.CompilerParams(
            collective_id=2, has_side_effects=True, vmem_limit_bytes=61 << 20
        ),
        cost_estimate=pl.CostEstimate(
            flops=4 * count * model * columns, bytes_accessed=30 << 20, transcendentals=0
        ),
    )(*small_inputs, *streams, *loads)


def assemble_kernel(
    early_ref, bcs_ref, late_ref, mid_ref, outs_ref, dx_ref, out_in_ref, small_ref, steps_ref,
    out_ref, grad_ref, query_ref, keyval_ref, attn_ref, gate_ref, x_ref, bc_ref, step_ref, ssm_ref,
    ffn_gate_ref, ffn_up_ref, ffn_down_ref, gain_ref, gain_ffn_ref, conv_x_ref, conv_bc_ref,
    bias_ref, decay_ref, skip_ref,
):
    chips = late_ref.shape[0]
    heads = step_ref.shape[0] // chips
    inner = heads * SSM_DIM
    hid = ffn_gate_ref.shape[1] // chips

    def spread(source, begin, width):
        return jnp.concatenate(
            [source[k, :, begin : begin + width].astype(F32) for k in range(chips)], axis=1
        )

    def summed(source, begin, end):
        total = source[0, :, begin:end].astype(F32)
        for k in range(1, chips):
            total = total + source[k, :, begin:end].astype(F32)
        return total

    out_ref[...] = out_in_ref[...]
    grad_ref[...] = dx_ref[...]
    gate_ref[...] = spread(early_ref, 0, inner)
    query_ref[...] = spread(early_ref, inner, HEAD_DIM)
    keyval_ref[...] = summed(early_ref, 256, 384)
    x_ref[...] = spread(late_ref, 0, inner)
    bc_ref[...] = summed(bcs_ref, 0, 256)
    ffn_gate_ref[...] = spread(mid_ref, 0, hid)
    ffn_up_ref[...] = spread(mid_ref, hid, hid)
    ffn_down_ref[...] = spread(mid_ref, 2 * hid, hid)
    ssm_ref[...] = spread(outs_ref, 0, inner)
    attn_ref[...] = spread(outs_ref, inner, HEAD_DIM)

    @pl.when(pl.program_id(0) == 0)
    def _():
        step_ref[...] = spread(steps_ref, inner, heads).T
        everywhere = small_ref[0:16, :]
        for k in range(1, small_ref.shape[0] // 16):
            everywhere = everywhere + small_ref[16 * k : 16 * k + 16, :]
        gain_ref[...] = everywhere[0:1]
        gain_ffn_ref[...] = everywhere[1:2]
        conv_bc_ref[...] = everywhere[8 : 8 + CONV, 256:512]
        core = lax.axis_index("tensor")
        own = [
            small_ref[pl.ds(pl.multiple_of((2 * k + core) * 16, 16), 16), :] for k in range(chips)
        ]
        conv_x_ref[...] = jnp.concatenate([one[8 : 8 + CONV, :inner] for one in own], axis=1)
        for row, target in ((12, skip_ref), (13, bias_ref), (14, decay_ref)):
            target[...] = jnp.concatenate(
                [
                    jnp.sum(
                        one[row : row + 1, h * SSM_DIM : (h + 1) * SSM_DIM], axis=1, keepdims=True
                    )
                    for one in own
                    for h in range(heads)
                ],
                axis=1,
            )


def assemble(early, bcs, last, mid, outs, dx, out, small, widths, heads):
    chips = lax.axis_size("context")
    share = last.shape[0] // chips
    turns = 2
    rows = share // turns
    shape = jax.ShapeDtypeStruct
    block = lambda height, width: pl.BlockSpec((height, width), lambda i: (i, 0))
    fixed = lambda height, width: pl.BlockSpec((height, width), lambda i: (0, 0))
    slab = lambda width: pl.BlockSpec((chips, rows, width), lambda i: (0, i, 0))
    token_rows = dx.shape[0] // turns
    model = dx.shape[1]
    tiny = [
        (1, model), (1, model), (CONV, heads * SSM_DIM), (CONV, 2 * STATE), (1, heads), (1, heads),
        (1, heads),
    ]
    return pl.pallas_call(
        assemble_kernel,
        grid=(turns,),
        out_shape=(shape(out.shape, BF16), shape(dx.shape, BF16))
        + tuple(shape((share, w) if w > heads else (w, share), F32) for w in widths)
        + tuple(shape(one, F32) for one in tiny),
        in_specs=[
            slab(early.shape[1]), slab(bcs.shape[1]), slab(last.shape[1]), slab(mid.shape[1]), slab(outs.shape[1]),
            block(token_rows, model), block(token_rows, model), fixed(*small.shape),
            pl.BlockSpec((chips, share, last.shape[1]), lambda i: (0, 0, 0)),
        ],
        out_specs=(block(token_rows, model), block(token_rows, model))
        + tuple(block(rows, w) if w > heads else fixed(w, share) for w in widths)
        + tuple(fixed(*one) for one in tiny),
        compiler_params=pltpu.CompilerParams(vmem_limit_bytes=60 << 20),
    )(*[one.reshape(chips, share, -1) for one in (early, bcs, last, mid, outs)], dx, out, small,
      last.reshape(chips, share, -1))


def per_device(
    tokens, segments, deal, gain_mix, w_query, w_keyval, w_attn_out, w_gate_z, w_in_x, w_bc, w_step,
    conv_x, conv_bc, step_bias, decay_log, skip, w_ssm_out, gain_ffn, w_ffn_gate, w_ffn_up,
    w_ffn_down, cotangent,
):
    normed_t, u, w_all, wout_all, cot_all, table, head_rows, taps = opening(
        tokens,
        cotangent,
        (w_in_x, w_query, w_bc, w_gate_z, w_keyval, w_step.T, w_ssm_out, w_attn_out),
        gain_mix,
        segments,
        (conv_x, conv_bc),
        (step_bias, decay_log, skip),
    )
    ag, y, conv, states, keyval, kept, normed_t, keyval_t = mixer_forward(u, normed_t, table, head_rows, taps, deal[0])
    hidden, dag, mixed, dmixed, dgain, down, dffn, dout = middle(
        ag, wout_all, (w_ffn_gate, w_ffn_up, w_ffn_down), tokens, cotangent, cot_all, gain_ffn
    )
    dx, out, early, bcs, last, mids, outs, small = closing(
        (
            deal, dag, keyval, keyval_t, head_rows, taps, dmixed, gain_mix.reshape(1, -1), dffn,
            dgain, dout,
        ),
        (table, y, conv, kept, states),
        (normed_t, w_all, hidden, down, mixed, tokens),
        lax.axis_size("fsdp"),
    )
    weights = (
        w_query, w_keyval, w_attn_out, w_gate_z, w_in_x, w_bc, w_step, w_ssm_out, w_ffn_gate,
        w_ffn_up, w_ffn_down,
    )
    done = assemble(early, bcs, last, mids, outs, dx, out, small, [w.shape[1] for w in weights], skip.shape[0])
    grads = done[2:13]
    gain, gain_two, taps_x, taps_bc, bias, decay, skips = done[13:]
    return (
        done[0],
        done[1],
        gain.reshape(-1),
        *grads[:6],
        grads[6].T,
        taps_x,
        taps_bc,
        bias.reshape(-1),
        decay.reshape(-1),
        skips.reshape(-1),
        grads[7],
        gain_two.reshape(-1),
        *grads[8:],
    )


def solution(mesh):
    in_specs = (
        P(("fsdp", "context"), None),
        P("fsdp", None),
        P("fsdp", None),
        P(),
        P("fsdp", "tensor"),
        P("fsdp", "tensor"),
        P("fsdp", "tensor"),
        P("fsdp", "tensor"),
        P("fsdp", "tensor"),
        P("fsdp", None),
        P("fsdp", "tensor"),
        P(None, "tensor"),
        P(),
        P("tensor"),
        P("tensor"),
        P("tensor"),
        P("fsdp", "tensor"),
        P(),
        P("fsdp", "tensor"),
        P("fsdp", "tensor"),
        P("fsdp", "tensor"),
        P(("fsdp", "context"), None),
    )
    out_specs = (
        P(("fsdp", "context"), None),
        P(("fsdp", "context"), None),
        P(),
        P("fsdp", "tensor"),
        P("fsdp", "tensor"),
        P("fsdp", "tensor"),
        P("fsdp", "tensor"),
        P("fsdp", "tensor"),
        P("fsdp", None),
        P("fsdp", "tensor"),
        P(None, "tensor"),
        P(),
        P("tensor"),
        P("tensor"),
        P("tensor"),
        P("fsdp", "tensor"),
        P(),
        P("fsdp", "tensor"),
        P("fsdp", "tensor"),
        P("fsdp", "tensor"),
    )
    return jax.shard_map(
        per_device, mesh=mesh, in_specs=in_specs, out_specs=out_specs, check_vma=False
    )
```
